128 devices in a mesh: dp: 4 (over y), section: 4 (over x), mp: 8 (over z, core).
Axes of the slice: x: 4, y: 4, z: 4, core: 2. Of those that a mesh axis runs over, the one named last changes fastest.
Arguments:
- embeds: bfloat16 [8, 32, 8192], P('dp', 'mp'), may hold values from -22 to 22
- targets: int32 [8, 32], replicated, may hold values from 0 to 65535
- lengths: int32 [8], replicated, may hold values from 1 to 32, 192 in all
- source: int32 [8], replicated, may hold values from 0 to 7, each once
- attn_gain: float32 [4, 8192], P('section'), may hold values from 0.25 to 1.75
- w_query: bfloat16 [4, 8192, 4096], P('section', None, 'mp'), may hold values from -1 to 1
- w_key: bfloat16 [4, 8192, 1024], P('section', None, 'mp'), may hold values from -1 to 1
- w_value: bfloat16 [4, 8192, 1024], P('section', None, 'mp'), may hold values from -0.0625 to 0.0625
- w_out: bfloat16 [4, 4096, 8192], P('section', 'mp', 'dp'), may hold values from -0.09375 to 0.09375
- final_gain: float32 [8192], replicated, may hold values from 0.25 to 1.75
- head: bfloat16 [65536, 8192], P(('dp', 'section', 'mp')), may hold values from -3 to 3
Outputs:
- exit_logprobs: float32 [8, 32], P('dp')
- final_logprobs: float32 [8, 32], P('dp')
The draws below stay inside these ranges and needn't reach their ends.
Inputs may be any that keep to these rules, and one draw needn't show every extreme that they name: `source`: each trainer slot names a different decode slot; decode slot s lies with data group s // 2. `lengths`: positions at or beyond a rollout's length are padding.
All inputs are finite; a program needn't handle non-finite values.
Results may differ from the reference program's by a relative error of at most 0.0038.
Values may be sent and summed in bfloat16 or wider, within the bound.
A program may use at most 128 MiB of HBM per device.

```python
import math
import jax
import jax.numpy as jnp
import numpy as np
from jax import lax

D = 8192
HEADS = 32
HD = 128
KVH = 8
VOCAB = 65536
LEN = 32
LAYERS = 4
SLOTS = 8


def projection(key, columns):
    base = jnp.clip(jax.random.normal(key, (LAYERS, D, columns), jnp.float32), -6.0, 6.0) * D ** (-0.5)
    return base


def draw_embeds(key, part):
    key = jax.random.fold_in(key, 7)
    first = jax.random.fold_in(key, 0)
    noise = jnp.clip(jax.random.normal(first, (SLOTS, LEN, D), jnp.float32), -6.0, 6.0)
    values = noise
    return values.astype(jnp.bfloat16)


def draw_w_query(key, part):
    key = jax.random.fold_in(key, 5)
    return projection(key, HEADS * HD).astype(jnp.bfloat16)


def draw_w_key(key, part):
    key = jax.random.fold_in(key, 9)
    return projection(key, KVH * HD).astype(jnp.bfloat16)


def draw_head(key, part):
    key = jax.random.fold_in(key, 13)
    first = jax.random.fold_in(key, 0)
    base = jnp.clip(jax.random.normal(first, (VOCAB, D), jnp.float32), -6.0, 6.0) * (D // 9) ** (-0.5)
    values = base
    return values.astype(jnp.bfloat16)


def place_ends(values, rng, low, high):
    shape = values.shape
    index_at = [jax.random.randint(jax.random.fold_in(rng, axis), (), 0, shape[axis]) for axis in range(len(shape))]
    values = values.at[tuple(index_at)].set(low)
    longest = shape.index(max(shape))
    index_at[longest] = (index_at[longest] + 1) % shape[longest]
    return values.at[tuple(index_at)].set(high)


def steps_of(own_key, dims, cuts, smallest, top_value):
    level, own = 1.0, jax.random.fold_in(own_key, 6)
    for dim, blocks in cuts:
        heights = jnp.exp(jax.random.uniform(jax.random.fold_in(own, dim), (blocks,), jnp.float32, smallest / len(cuts), top_value / len(cuts)))
        level = level * jnp.repeat(heights, dims[dim] // blocks).reshape([-1 if axis == dim else 1 for axis in range(len(dims))])
    return level


def rank_table(count, slope):
    loads = [(1 << 20) // math.isqrt(standing ** slope) + 1 for standing in range(1, count + 1)]
    scale = 1 + sum(loads) // (1 << 30)
    return np.cumsum(np.array([max(1, weight // scale) for weight in loads]))


def skewed_ids(rng, extent, count, slope):
    listing = rank_table(count, slope)
    ticket = jax.random.randint(jax.random.fold_in(rng, 1), extent, 0, int(listing[count - 1]))
    grade = jnp.searchsorted(jnp.asarray(listing, jnp.int32), ticket, side="right")
    return jax.random.permutation(jax.random.fold_in(rng, 2), count)[grade].astype(jnp.int32)


def split_up(count, total, most, lean):
    portions = [(1 << 20) // math.isqrt(grade ** lean) + 1 for grade in range(2, count + 1)]
    spare, counts = total - most - (count - 1), [1] * (count - 1)
    while spare > 0:
        free = [i for i in range(count - 1) if counts[i] < most]
        pool, left = sum([portions[i] for i in free]), spare
        for i in free:
            more = min(most - counts[i], max(1, left * portions[i] // pool), spare)
            counts[i] = counts[i] + more
            spare = spare - more
    return np.array([most] + counts)


def ragged(own_key, amount, total, bound, skew):
    if amount == 2:
        one = jax.random.randint(own_key, (), max(1, total - bound), min(bound, total - 1) + 1)
        return jnp.stack([one, total - one])
    sizes = jnp.asarray(split_up(amount, total, bound, skew), jnp.int32)
    pairs = (amount - 1) // 2
    source_of, sink = sizes[1:1 + 2 * pairs:2], sizes[2:2 + 2 * pairs:2]
    room = jnp.minimum(source_of - 1, bound - sink)
    moved = jax.random.randint(jax.random.fold_in(own_key, 1), (pairs,), 0, 1 << 20) % (room + 1)
    sizes = sizes.at[1:1 + 2 * pairs:2].set(source_of - moved).at[2:2 + 2 * pairs:2].set(sink + moved)
    return sizes[jax.random.permutation(jax.random.fold_in(own_key, 2), amount)]


def scatter_about(stream_key, shape, scale, most, cuts=(), kind=jnp.bfloat16):
    loudness = steps_of(stream_key, shape, cuts, -0.22, 0.18) if cuts else 1.0
    array = jax.random.normal(stream_key, shape, jnp.float32) * scale * loudness
    return jnp.minimum(jnp.maximum(array, -most), most).astype(kind)


def setup_inputs(seed: int = 0) -> dict:
    arg_keys = jax.random.split(jax.random.key(seed), 12)
    embeds = draw_embeds(jax.random.fold_in(arg_keys[11], 71), 0)
    targets = place_ends(skewed_ids(arg_keys[1], (SLOTS, LEN), VOCAB, 2), jax.random.fold_in(arg_keys[1], 3), 0, VOCAB - 1).astype(jnp.int32)
    lengths = ragged(arg_keys[2], SLOTS, 3 * SLOTS * LEN // 4, LEN, 1).astype(jnp.int32)
    source = jax.random.permutation(arg_keys[3], SLOTS).astype(jnp.int32)
    attn_gain = jnp.clip(1.0 + 0.15 * jax.random.normal(arg_keys[4], (LAYERS, D), jnp.float32), 0.25, 1.75)
    w_query = draw_w_query(jax.random.fold_in(arg_keys[11], 71), 0)
    w_key = draw_w_key(jax.random.fold_in(arg_keys[11], 71), 0)
    w_value = scatter_about(arg_keys[7], (LAYERS, D, KVH * HD), D ** -0.5, 0.0625, ((0, 4), (2, 8)))
    w_out = scatter_about(arg_keys[8], (LAYERS, HEADS * HD, D), (HEADS * HD) ** -0.5, 0.09375, ((0, 4), (1, 8), (2, 4)))
    final_gain = jnp.clip(1.0 + 0.15 * jax.random.normal(arg_keys[9], (D,), jnp.float32), 0.25, 1.75)
    head = draw_head(jax.random.fold_in(arg_keys[11], 71), 0)
    return dict(embeds=embeds, targets=targets, lengths=lengths, source=source, attn_gain=attn_gain, w_query=w_query, w_key=w_key, w_value=w_value, w_out=w_out, final_gain=final_gain, head=head)


EPS = 1e-05
ROPE_BASE = 500000.0

def rotate(values, positions, count):
    rows = values.shape[0]
    split = values.reshape(rows, count, HD)
    halfway = HD // 2
    freqs = ROPE_BASE ** (-jnp.arange(halfway).astype(jnp.float32) * 2.0 / HD)
    angles = positions.astype(jnp.float32)[:, None] * freqs[None, :]
    cosine = jnp.cos(angles)[:, None, :]
    sine = jnp.sin(angles)[:, None, :]
    first = split[..., :halfway]
    second = split[..., halfway:]
    joined = jnp.concatenate([first * cosine - second * sine, second * cosine + first * sine], axis=-1)
    return joined.reshape(rows, count * HD)

def attend(query, keys, values, length, heads, kv_heads):
    rows = query.shape[0]
    grouped = heads // kv_heads
    query_f = query.reshape(rows, kv_heads, grouped, HD).astype(jnp.float32)
    keys_f = keys.reshape(rows, kv_heads, HD).astype(jnp.float32)
    values_f = values.reshape(rows, kv_heads, HD).astype(jnp.float32)
    scores = jnp.einsum('qkgd,skd->kgqs', query_f, keys_f) * HD ** (-0.5)
    places = jnp.arange(rows)
    allowed = (places[None, :] <= places[:, None]) & (places[None, :] < length)
    scores = jnp.where(allowed, scores, jnp.float32(-1e+30))
    highest = lax.optimization_barrier(jnp.max(scores, axis=-1, keepdims=True))
    weights = jnp.exp(scores - highest)
    probs = (weights / lax.optimization_barrier(jnp.sum(weights, axis=-1, keepdims=True))).astype(jnp.bfloat16)
    context = jnp.einsum('kgqs,skd->qkgd', probs.astype(jnp.float32), values_f)
    return context.astype(jnp.bfloat16).reshape(rows, heads * HD)

def block(hidden, length, gain, w_query, w_key, w_value, w_out):
    wide = hidden.astype(jnp.float32)
    normed = (wide * lax.rsqrt(lax.optimization_barrier(jnp.mean(wide * wide, axis=-1, keepdims=True)) + EPS) * gain).astype(jnp.bfloat16)
    positions = jnp.arange(LEN)
    query = rotate(jnp.dot(normed, w_query, preferred_element_type=jnp.float32), positions, HEADS).astype(jnp.bfloat16)
    keys = rotate(jnp.dot(normed, w_key, preferred_element_type=jnp.float32), positions, KVH).astype(jnp.bfloat16)
    values = jnp.dot(normed, w_value, preferred_element_type=jnp.float32).astype(jnp.bfloat16)
    context = attend(query, keys, values, length, HEADS, KVH)
    delta = jnp.dot(context, w_out, preferred_element_type=jnp.float32)
    return (wide + delta).astype(jnp.bfloat16)

def score(state, final_gain, head, sampled, live):
    wide = state.astype(jnp.float32).reshape(SLOTS * LEN, D)
    scaled = (wide * lax.rsqrt(lax.optimization_barrier(jnp.mean(wide * wide, axis=-1, keepdims=True)) + EPS) * final_gain).astype(jnp.bfloat16)
    logits = jnp.dot(scaled, head.T, preferred_element_type=jnp.float32)
    total = jax.nn.logsumexp(logits, axis=-1)
    picked = jnp.take_along_axis(logits, sampled.reshape(SLOTS * LEN, 1), axis=1)[:, 0]
    logprob = (picked - total).reshape(SLOTS, LEN)
    valid = jnp.arange(LEN)[None, :] < live[:, None]
    return jnp.where(valid, logprob, jnp.float32(0.0))

def reference(embeds, targets, lengths, source, attn_gain, w_query, w_key, w_value, w_out, final_gain, head):
    hidden = jnp.take(embeds, source, axis=0)
    live = jnp.take(lengths, source, axis=0)
    sampled = jnp.take(targets, source, axis=0)
    exit_state = hidden
    for level in range(LAYERS):
        hidden = jax.vmap(block, in_axes=(0, 0, None, None, None, None, None))(hidden, live, attn_gain[level], w_query[level], w_key[level], w_value[level], w_out[level])
        if level == LAYERS // 2 - 1:
            exit_state = hidden
    exit_logprobs = score(exit_state, final_gain, head, sampled, live)
    final_logprobs = score(hidden, final_gain, head, sampled, live)
    return (exit_logprobs, final_logprobs)
```

```python
import jax
import jax.numpy as jnp
import numpy as np
from jax import lax
from jax.experimental import pallas as pl
from jax.experimental.pallas import tpu as pltpu
from jax.sharding import PartitionSpec as P

HD = 128
EPS = 1e-05
ROPE_BASE = 500000.0
NY = 4
NX = 4
NZ = 4
NM = 8
ROWS = 64
D = 8192
QW = 512
MESH = pl.DeviceIdType.MESH
BF = jnp.bfloat16
F32 = jnp.float32


def lane(start, size):
    return pl.ds(pl.multiple_of(start, 128), size)


def kernel(
    emb, live, tgt, gain, fgain, cosine, sine, wq, wk, wv, wo, head, out,
    W, WO, HEAD, EB, X, XN, SS, QA, R, C, PS, PR, PO, ZS, ZR, HP, Y, LT, STO, SA, SB, SC,
    w_sem, eb_s, eb_r, hop_s, hop_r, ag_s, ag_r, res_s, res_r, ctx_s, ctx_r, ps_s, ps_r,
    zz_s, zz_r, y_s, y_r, st_s, st_r,
):
    d = lax.axis_index("dp")
    s = lax.axis_index("section")
    m = lax.axis_index("mp")
    z = m // 2
    c = m % 2
    sib = z * 2 + (1 - c)

    def ypeer(k):
        return (d + k) % NY

    def zpeer(k):
        return ((z + k) % NZ) * 2 + c

    def zother(k):
        return ((z + k) % NZ) * 2 + (1 - c)

    def rcopy(src, dst, ssem, rsem, dev):
        return pltpu.make_async_remote_copy(
            src_ref=src, dst_ref=dst, send_sem=ssem, recv_sem=rsem,
            device_id=dev, device_id_type=MESH,
        )

    here = (d, s, sib)

    loads = []
    for h in range(2):
        loads.append([
            pltpu.make_async_copy(wq.at[:, h], W.at[h, :, :, 0:512], w_sem.at[3 * h]),
            pltpu.make_async_copy(wk.at[:, h], W.at[h, :, :, 512:640], w_sem.at[3 * h + 1]),
            pltpu.make_async_copy(wv.at[:, h], W.at[h, :, :, 640:768], w_sem.at[3 * h + 2]),
        ])
    wo_loads = []
    for h in range(2):
        for mm in range(NM):
            wo_loads.append(pltpu.make_async_copy(
                wo.at[:, mm * 256 + h * 128: mm * 256 + h * 128 + 128],
                WO.at[h, :, mm * 128: mm * 128 + 128], w_sem.at[6 + h * NM + mm]))
    head_load = pltpu.make_async_copy(head, HEAD, w_sem.at[22])
    for group in loads:
        for copy in group:
            copy.start()
    for copy in wo_loads:
        copy.start()
    head_load.start()

    barrier = pltpu.get_barrier_semaphore()
    partners = []
    for k in range(1, 4):
        partners.append((ypeer(k), s, m))
        partners.append((d, (s + k) % NX, m))
        partners.append((d, s, zpeer(k)))
        partners.append((d, s, zother(k)))
        partners.append((ypeer(k), (s + 1) % NX, m))
        partners.append((ypeer(k), (s + 3) % NX, m))
    partners.append(here)
    for dev in partners:
        pl.semaphore_signal(barrier, inc=1, device_id=dev, device_id_type=MESH)
    pl.semaphore_wait(barrier, len(partners))

    def eb_z(k):
        return rcopy(EB.at[m], EB.at[m], eb_s.at[k], eb_r.at[m], (d, s, zpeer(k)))

    def eb_z_in(k):
        mk = zpeer(k)
        return rcopy(EB.at[mk], EB.at[mk], eb_s.at[k], eb_r.at[mk], (d, s, zpeer(k)))

    def eb_fwd(k):
        mk = zpeer(k)
        return rcopy(EB.at[mk], EB.at[mk], eb_s.at[4 + k], eb_r.at[mk], here)

    def eb_sib_in(k):
        mk = zother(k)
        return rcopy(EB.at[mk], EB.at[mk], eb_s.at[4 + k], eb_r.at[mk], here)

    def hop(h, g):
        return rcopy(HP.at[h, g], X.at[h, m, d], hop_s.at[h, g], hop_r.at[h, d],
                     (g, (s + 1) % NX, m))

    def hop_in(h, g):
        return rcopy(HP.at[h, g], X.at[h, m, g], hop_s.at[h, g], hop_r.at[h, g],
                     (g, (s + 1) % NX, m))

    def ag_z(h, k):
        return rcopy(X.at[h, m], X.at[h, m], ag_s.at[h, k], ag_r.at[h, m], (d, s, zpeer(k)))

    def ag_z_in(h, k):
        mk = zpeer(k)
        return rcopy(X.at[h, mk], X.at[h, mk], ag_s.at[h, k], ag_r.at[h, mk], (d, s, zpeer(k)))

    def ag_fwd(h, k):
        mk = zpeer(k)
        return rcopy(X.at[h, mk], X.at[h, mk], ag_s.at[h, 4 + k], ag_r.at[h, mk], here)

    def ag_sib_in(h, k):
        mk = zother(k)
        return rcopy(X.at[h, mk], X.at[h, mk], ag_s.at[h, 4 + k], ag_r.at[h, mk], here)

    def res(h, k):
        g = ypeer(k)
        return rcopy(X.at[h, m, g], R.at[h, d], res_s.at[h, k], res_r.at[h, d], (g, s, m))

    def res_in(h, k):
        g = ypeer(k)
        return rcopy(X.at[h, m, g], R.at[h, g], res_s.at[h, k], res_r.at[h, g], (g, s, m))

    def ctx(k):
        return rcopy(C.at[d], C.at[d], ctx_s.at[k], ctx_r.at[d], (ypeer(k), s, m))

    def ctx_in(k):
        g = ypeer(k)
        return rcopy(C.at[g], C.at[g], ctx_s.at[k], ctx_r.at[g], (g, s, m))

    def part(h, zz):
        return rcopy(PS.at[h, zz], PR.at[h, zz], ps_s.at[h, zz], ps_r.at[h, zz], here)

    def zred(h, k):
        zt = (z + k) % NZ
        return rcopy(ZS.at[h, zt], ZR.at[h, z], zz_s.at[h, k], zz_r.at[h, z], (d, s, zpeer(k)))

    def zred_in(h, k):
        zt = (z + k) % NZ
        return rcopy(ZS.at[h, zt], ZR.at[h, zt], zz_s.at[h, k], zz_r.at[h, zt], (d, s, zpeer(k)))

    def norm_block(h, g, mm, x):
        col = g * 2048 + mm * 256 + h * 128
        scaled = (x * gain[:, lane(col, 128)]).astype(BF)
        XN.at[h, g][:, lane(mm * 128, 128)] = scaled

    def layer():
        SS[...] = jnp.zeros_like(SS)

        @pl.when(s == 0)
        def _():
            EB.at[m][...] = emb[...]
            for k in (2, 1, 3, 0):
                (eb_z(k) if k else eb_fwd(0)).start()
            for k in (1, 3, 2):
                eb_z_in(k).wait_recv()
                eb_fwd(k).start()
            for k in range(4):
                eb_sib_in(k).wait_recv()

            def body(i, _):
                dl = i // 16
                mm = (i // 2) % 8
                h = i % 2
                x = EB[:, :, lane(dl * 2048 + mm * 256 + h * 128, 128)]
                xf = x.astype(F32)
                for half in range(2):
                    xs = xf[:, half * 8: half * 8 + 8, :].reshape(ROWS, 128)
                    g = half * 2 + dl
                    norm_block(h, g, mm, xs)
                    X.at[h, mm, g][...] = xs.astype(BF)
                    SS[...] += xs * xs
                return 0

            lax.fori_loop(0, 32, body, 0)
            for h in range(2):
                for k in (2, 1, 3):
                    res(h, k).start()

        @pl.when(s > 0)
        def _():
            for h in range(2):
                for g in range(NY):
                    hop_in(h, g).wait_recv()
                for k in (2, 1, 3, 0):
                    (ag_z(h, k) if k else ag_fwd(h, 0)).start()
            for h in range(2):
                for k in (2, 1, 3):
                    res(h, k).start()
            for h in range(2):
                for k in (1, 3, 2):
                    ag_z_in(h, k).wait_recv()
                    ag_fwd(h, k).start()

        QA[...] = jnp.zeros_like(QA)
        for h in range(2):
            @pl.when(s > 0)
            def _():
                for k in range(4):
                    ag_sib_in(h, k).wait_recv()

                def body(mm, _):
                    for g in range(NY):
                        xf = X[h, mm, g].astype(F32)
                        norm_block(h, g, mm, xf)
                        SS[...] += xf * xf
                    return 0

                lax.fori_loop(0, NM, body, 0)

            for copy in loads[h]:
                copy.wait()

            def dots(g, _):
                w = W[h, pl.ds(g * 8, 8)].reshape(1024, 768)
                QA[...] += jnp.dot(XN[h, g], w, preferred_element_type=F32)
                return 0

            lax.fori_loop(0, NY, dots, 0)

        r = lax.rsqrt(jnp.sum(SS[...], axis=1, keepdims=True) * (1.0 / D) + EPS)
        cos = cosine[...]
        sin = sine[...]

        def rope(x):
            return (x * cos + pltpu.roll(x, 64, 1) * sin).astype(BF)

        query = jnp.concatenate(
            [rope(QA[:, j * HD:(j + 1) * HD] * r) for j in range(4)], axis=0)
        key = rope(QA[:, 512:640] * r)
        value = (QA[:, 640:768] * r).astype(BF)
        scores = lax.dot_general(query, key, (((1,), (1,)), ((), ())),
                                 preferred_element_type=F32) * (HD ** -0.5)
        shape = (4 * ROWS, ROWS)
        rq = lax.broadcasted_iota(jnp.int32, shape, 0) % ROWS
        rk = lax.broadcasted_iota(jnp.int32, shape, 1)
        slot_q, slot_k = (rq // 4) % 2, (rk // 4) % 2
        pos_q, pos_k = (rq // 8) * 4 + rq % 4, (rk // 8) * 4 + rk % 4
        live_k = jnp.where(slot_k == 0, live[2 * d], live[2 * d + 1])
        allowed = (slot_q == slot_k) & (pos_k <= pos_q) & (pos_k < live_k)
        scores = jnp.where(allowed, scores, F32(-1e30))
        highest = jnp.max(scores, axis=-1, keepdims=True)
        weights = jnp.exp(scores - highest)
        probs = (weights / jnp.sum(weights, axis=-1, keepdims=True)).astype(BF)
        mixed = jnp.dot(probs, value, preferred_element_type=F32).astype(BF)
        for j in range(4):
            C.at[d][:, j * HD:(j + 1) * HD] = mixed[j * ROWS:(j + 1) * ROWS]
        for k in (2, 1, 3):
            ctx(k).start()

        for h in range(2):
            R.at[h, d][...] = X[h, m, d]
        for copy in wo_loads:
            copy.wait()
        for k in (1, 3, 2):
            ctx_in(k).wait_recv()

        context = C[...].reshape(NY * ROWS, QW)
        for h in range(2):
            def project(zz, _):
                p = jnp.dot(context, WO[h, :, lane(zz * 256, 256)], preferred_element_type=F32)
                low, high = p[:, :128], p[:, 128:]
                PO.at[h, zz][...] = jnp.where(c == 0, low, high)
                PS.at[h, zz][...] = jnp.where(c == 0, high, low).astype(BF)
                part(h, zz).start()
                return 0

            lax.fori_loop(0, NZ, project, 0)

        for h in range(2):
            for k in (2, 1, 3):
                zt = (z + k) % NZ
                part(h, zt).wait_recv()
                ZS.at[h, zt][...] = (PO[h, zt] + PR[h, zt].astype(F32)).astype(BF)
                zred(h, k).start()
        for h in range(2):
            part(h, z).wait_recv()
            total = PO[h, z] + PR[h, z].astype(F32)
            for k in (1, 3, 2):
                res_in(h, k).wait_recv()
            total = total + R[h].astype(F32).reshape(NY * ROWS, 128)
            for k in (1, 3, 2):
                zred_in(h, k).wait_recv()
                total = total + ZR[h, (z + k) % NZ].astype(F32)
            hidden = total.astype(BF)
            HP.at[h][...] = hidden.reshape(NY, ROWS, 128)

            @pl.when(s < NX - 1)
            def _():
                for k in (2, 1, 3, 0):
                    hop(h, ypeer(k)).start()

        @pl.when(s % 2 == 1)
        def _():
            b = s // 2
            sums = jnp.zeros((16, NY * ROWS), F32)
            ones = jnp.ones((16, 128), BF)
            nt = (((1,), (1,)), ((), ()))
            for h in range(2):
                wide = HP[h].astype(F32).reshape(NY * ROWS, 128)
                square = wide * wide
                top = square.astype(BF)
                rest = (square - top.astype(F32)).astype(BF)
                sums = sums + lax.dot_general(ones, top, nt, preferred_element_type=F32)
                sums = sums + lax.dot_general(ones, rest, nt, preferred_element_type=F32)
                col = d * 2048 + m * 256 + h * 128
                Y.at[b][0:256, lane(col, 128)] = (wide * fgain[:, lane(col, 128)]).astype(BF)
            top = sums.astype(BF).astype(F32)
            row = lax.broadcasted_iota(jnp.int32, (16, NY * ROWS), 0)
            packed = jnp.where(row == 0, top, jnp.where(row == 1, sums - top, 0.0))
            Y.at[b][256:272, lane(d * 2048 + m * 256, 256)] = packed.astype(BF)

    def piece(b, g, mm):
        return Y.at[b, :, lane(g * 2048 + mm * 256, 256)]

    def ycopy(b, g, mm, index, dev):
        ref = piece(b, g, mm)
        return rcopy(ref, ref, y_s.at[b, index], y_r.at[b, g * NM + mm], dev)

    def first_piece(k):
        return (jnp.where(c == 0, ypeer(k), d), jnp.where(c == 0, m, zpeer(k)))

    def second_piece(i, k):
        g0, m0 = first_piece(i)
        return (jnp.where(c == 0, g0, ypeer(k)), jnp.where(c == 0, zpeer(k), m0))

    def first_dev(k):
        g, mm = first_piece(k)
        return (g, s, mm)

    def second_dev(k):
        g, mm = second_piece(0, k)
        return (g, s, mm)

    def y_x(b, k):
        return ycopy(b, d, m, k, (d, (s + k) % NX, m))

    def y_first(b, k):
        return ycopy(b, d, m, 3 + k, first_dev(k))

    def y_second(b, i, k):
        g, mm = first_piece(i)
        return ycopy(b, g, mm, 7 + i * 3 + k - 1, second_dev(k))

    def y_fwd(b, i, k):
        g, mm = second_piece(i, k) if k else first_piece(i)
        return ycopy(b, g, mm, 19 + i * 4 + k, here)

    def y_in(b, g, mm):
        return ycopy(b, g, mm, 0, here)

    def score(b):
        source = 2 * b + 1

        @pl.when(s == source)
        def _():
            for k in (2, 1, 3):
                y_x(b, k).start()

        @pl.when(s != source)
        def _():
            y_in(b, d, m).wait_recv()

        for k in (2, 1, 3):
            y_first(b, k).start()
        for k in (2, 1, 3):
            y_second(b, 0, k).start()
        y_fwd(b, 0, 0).start()
        for i in (1, 3, 2):
            g, mm = first_piece(i)
            y_in(b, g, mm).wait_recv()
            for k in (2, 1, 3):
                y_second(b, i, k).start()
            y_fwd(b, i, 0).start()
        for i in (0, 1, 3, 2):
            for k in (1, 3, 2):
                g, mm = second_piece(i, k)
                y_in(b, g, mm).wait_recv()
                y_fwd(b, i, k).start()
        for g in range(NY):
            for zz in range(NZ):
                y_in(b, g, zz * 2 + (1 - c)).wait_recv()

        LT[...] = jnp.zeros_like(LT)

        def dots(g, _):
            cols = pl.ds(pl.multiple_of(g * 2048, 2048), 2048)
            LT[...] += lax.dot_general(HEAD[:, cols], Y[b, 0:256, cols],
                                       (((1,), (1,)), ((), ())), preferred_element_type=F32)
            return 0

        lax.fori_loop(0, NY, dots, 0)
        wide = jnp.sum(Y[b, 256:272, :].astype(F32), axis=0, keepdims=True)
        sums = wide[:, 0:256]
        for i in range(1, NY * NM):
            sums = sums + wide[:, i * 256:(i + 1) * 256]
        r = lax.rsqrt(sums * (1.0 / D) + EPS)
        logits = LT[...] * r
        highest = jnp.max(logits, axis=0, keepdims=True)
        summed = jnp.sum(jnp.exp(logits - highest), axis=0, keepdims=True)
        vocab = HEAD.shape[0]
        wanted = tgt[...] - ((d * NX + s) * NM + m) * vocab
        index = lax.broadcasted_iota(jnp.int32, logits.shape, 0)
        picked = jnp.sum(jnp.where(index == wanted, logits, 0.0), axis=0, keepdims=True)
        lanes = pl.ds(pl.multiple_of(b * 256, 256), 256)
        rows = lax.broadcasted_iota(jnp.int32, (8, 256), 0)
        STO[:, lanes] = jnp.where(rows == 0, highest,
                                  jnp.where(rows == 1, summed,
                                            jnp.where(rows == 2, picked, 0.0)))

    def step(t, _):
        place = jnp.where(s == NX - 1, 1, 0)

        @pl.when(t == place)
        def _():
            layer()

        @pl.when(t != place)
        def _():
            @pl.when((t == 0) | ((t == 1) & (s != NX - 1)))
            def _():
                head_load.wait()
            score(jnp.where(t == 2, 1, 0))
        return 0

    lax.fori_loop(0, 3, step, 0)

    def merge(ref, count):
        parts = [ref[j] for j in range(count)]
        highest = parts[0][0:1]
        for p in parts[1:]:
            highest = jnp.maximum(highest, p[0:1])
        summed = jnp.zeros_like(highest)
        picked = jnp.zeros_like(highest)
        for p in parts:
            summed = summed + p[1:2] * jnp.exp(p[0:1] - highest)
            picked = picked + p[2:3]
        return highest, summed, picked

    def stacked(highest, summed, picked):
        rows = lax.broadcasted_iota(jnp.int32, (8, 512), 0)
        return jnp.where(rows == 0, highest,
                         jnp.where(rows == 1, summed, jnp.where(rows == 2, picked, 0.0)))

    def st_y(k):
        return rcopy(SA.at[d], SA.at[d], st_s.at[0, k], st_r.at[0, d], (ypeer(k), s, m))

    def st_y_in(k):
        g = ypeer(k)
        return rcopy(SA.at[g], SA.at[g], st_s.at[0, k], st_r.at[0, g], (g, s, m))

    def m_of(k):
        return (m + k) % NM

    def st_m(k):
        return rcopy(SB.at[m], SB.at[m], st_s.at[1, k], st_r.at[1, m], (d, s, m_of(k)))

    def st_m_in(k):
        mm = m_of(k)
        return rcopy(SB.at[mm], SB.at[mm], st_s.at[1, k], st_r.at[1, mm], (d, s, mm))

    def st_x(k):
        return rcopy(SC.at[s], SC.at[s], st_s.at[2, k], st_r.at[2, s], (d, (s + k) % NX, m))

    def st_x_in(k):
        ss = (s + k) % NX
        return rcopy(SC.at[ss], SC.at[ss], st_s.at[2, k], st_r.at[2, ss], (d, ss, m))

    SA.at[d][...] = STO[...]
    for k in (2, 1, 3):
        st_y(k).start()
    for k in (1, 3, 2):
        st_y_in(k).wait_recv()
    SB.at[m][...] = stacked(*merge(SA, NY))
    for k in (4, 3, 5, 2, 6, 1, 7):
        st_m(k).start()
    for k in (1, 7, 2, 6, 3, 5, 4):
        st_m_in(k).wait_recv()
    SC.at[s][...] = stacked(*merge(SB, NM))
    for k in (2, 1, 3):
        st_x(k).start()
    for k in (1, 3, 2):
        st_x_in(k).wait_recv()
    highest, summed, picked = merge(SC, NX)
    out[...] = jnp.broadcast_to(picked - (highest + jnp.log(summed)), out.shape)

    @pl.when(s == 0)
    def _():
        for k in range(4):
            (eb_z(k) if k else eb_fwd(0)).wait_send()
        for k in range(1, 4):
            eb_fwd(k).wait_send()

    @pl.when(s > 0)
    def _():
        for h in range(2):
            for k in range(1, 4):
                ag_z(h, k).wait_send()
            for k in range(4):
                ag_fwd(h, k).wait_send()

    @pl.when(s < NX - 1)
    def _():
        for h in range(2):
            for k in range(4):
                hop(h, ypeer(k)).wait_send()

    for h in range(2):
        for k in range(1, 4):
            res(h, k).wait_send()
            zred(h, k).wait_send()
        for zz in range(NZ):
            part(h, zz).wait_send()
    for k in range(1, 4):
        ctx(k).wait_send()
        st_y(k).wait_send()
        st_x(k).wait_send()
    for k in range(1, 8):
        st_m(k).wait_send()
    for b in range(2):
        @pl.when(s == 2 * b + 1)
        def _():
            for k in range(1, 4):
                y_x(b, k).wait_send()
        for k in range(1, 4):
            y_first(b, k).wait_send()
        for i in range(4):
            for k in range(1, 4):
                y_second(b, i, k).wait_send()
            for k in range(4):
                y_fwd(b, i, k).wait_send()


def tables():
    row = np.arange(ROWS)
    position = (row // 8) * 4 + row % 4
    half = HD // 2
    freqs = (ROPE_BASE ** (-np.arange(half) * 2.0 / HD)).astype(np.float32)
    angles = (position.astype(np.float32)[:, None] * freqs[None, :]).astype(np.float64)
    cos, sin = np.cos(angles), np.sin(angles)
    return (np.concatenate([cos, cos], 1).astype(np.float32),
            np.concatenate([-sin, sin], 1).astype(np.float32))


def per_device(
    embeds, targets, lengths, source, attn_gain, w_query, w_key, w_value, w_out, final_gain, head
):
    d = lax.axis_index("dp")
    vocab = head.shape[0]
    emb = embeds.reshape(8, 2, 4096).transpose(1, 0, 2).reshape(16, 4096)
    tgt = targets.reshape(NY, 2, NM, 4).transpose(0, 2, 1, 3).reshape(1, NY * ROWS)
    cos, sin = tables()
    vmem = pl.BlockSpec(memory_space=pltpu.VMEM)
    hbm = pl.BlockSpec(memory_space=pl.ANY)
    smem = pl.BlockSpec(memory_space=pltpu.SMEM)
    dma = pltpu.SemaphoreType.DMA
    stats = pl.pallas_call(
        kernel,
        out_shape=jax.ShapeDtypeStruct((8, 512), F32),
        in_specs=[vmem, smem, vmem, vmem, vmem, vmem, vmem, hbm, hbm, hbm, hbm, hbm],
        out_specs=vmem,
        scratch_shapes=[
            pltpu.VMEM((2, 32, 128, 768), BF),
            pltpu.VMEM((2, QW, 1024), BF),
            pltpu.VMEM((vocab, D), BF),
            pltpu.VMEM((NM, 16, 4096), BF),
            pltpu.VMEM((2, NM, NY, ROWS, 128), BF),
            pltpu.VMEM((2, NY, ROWS, 1024), BF),
            pltpu.VMEM((ROWS, 128), F32),
            pltpu.VMEM((ROWS, 768), F32),
            pltpu.VMEM((2, NY, ROWS, 128), BF),
            pltpu.VMEM((NY, ROWS, QW), BF),
            pltpu.VMEM((2, NZ, NY * ROWS, 128), BF),
            pltpu.VMEM((2, NZ, NY * ROWS, 128), BF),
            pltpu.VMEM((2, NZ, NY * ROWS, 128), F32),
            pltpu.VMEM((2, NZ, NY * ROWS, 128), BF),
            pltpu.VMEM((2, NZ, NY * ROWS, 128), BF),
            pltpu.VMEM((2, NY, ROWS, 128), BF),
            pltpu.VMEM((2, 272, D), BF),
            pltpu.VMEM((vocab, 256), F32),
            pltpu.VMEM((8, 512), F32),
            pltpu.VMEM((NY, 8, 512), F32),
            pltpu.VMEM((NM, 8, 512), F32),
            pltpu.VMEM((NX, 8, 512), F32),
            dma((23,)),
            dma((8,)), dma((8,)),
            dma((2, 4)), dma((2, 4)),
            dma((2, 8)), dma((2, 8)),
            dma((2, 4)), dma((2, 4)),
            dma((4,)), dma((4,)),
            dma((2, 4)), dma((2, 4)),
            dma((2, 4)), dma((2, 4)),
            dma((2, 36)), dma((2, 32)),
            dma((3, 8)), dma((3, 8)),
        ],
        compiler_params=pltpu.CompilerParams(
            collective_id=0, has_side_effects=True, vmem_limit_bytes=60 * 1024 * 1024),
        cost_estimate=pl.CostEstimate(flops=8_000_000_000, bytes_accessed=24_000_000,
                                      transcendentals=300_000),
    )(
        emb, lengths, tgt, attn_gain, final_gain.reshape(1, D), jnp.asarray(cos), jnp.asarray(sin),
        w_query.reshape(32, 2, 128, 512), w_key.reshape(32, 2, 128, 128),
        w_value.reshape(32, 2, 128, 128), w_out.reshape(512, 2048), head,
    )
    slots = stats[0].reshape(2, NY, NM, 2, 4).transpose(0, 1, 3, 2, 4).reshape(2, 8, 32)
    chosen = lax.dynamic_slice_in_dim(source, d * 2, 2, 0)
    live = jnp.take(lengths, chosen, axis=0)
    picked = jnp.take(slots, chosen, axis=1)
    valid = jnp.arange(32)[None, :] < live[:, None]
    result = jnp.where(valid[None], picked, F32(0.0))
    return (result[0], result[1])


def solution(mesh):
    return jax.shard_map(
        per_device,
        mesh=mesh,
        in_specs=(
            P("dp", "mp", None),
            P(),
            P(),
            P(),
            P("section", None),
            P("section", None, "mp"),
            P("section", None, "mp"),
            P("section", None, "mp"),
            P("section", "mp", "dp"),
            P(),
            P(("dp", "section", "mp"), None),
        ),
        out_specs=(P("dp", None), P("dp", None)),
        check_vma=False,
    )
```

```python
import jax
import jax.numpy as jnp
import numpy as np
from jax import lax
from jax.experimental import pallas as pl
from jax.experimental.pallas import tpu as pltpu
from jax.sharding import PartitionSpec as P

HD = 128
EPS = 1e-05
ROPE_BASE = 500000.0
NY = 4
NX = 4
NZ = 4
NM = 8
ROWS = 64
D = 8192
QW = 512
MESH = pl.DeviceIdType.MESH
BF = jnp.bfloat16
F32 = jnp.float32


def lane(start, size):
    return pl.ds(pl.multiple_of(start, 128), size)


def kernel(
    emb, live, tgt, gain, fgain, cosine, sine, wq, wk, wv, wo, head, out,
    W, WO, HEAD, EB, X, XN, SS, QA, R, C, PS, PR, PO, ZS, ZR, HP, Y, LT, STO, SA, SB, SC,
    w_sem, eb_s, eb_r, hop_s, hop_r, ag_s, ag_r, res_s, res_r, ctx_s, ctx_r, ps_s, ps_r,
    zz_s, zz_r, y_s, y_r, st_s, st_r,
):
    d = lax.axis_index("dp")
    s = lax.axis_index("section")
    m = lax.axis_index("mp")
    z = m // 2
    c = m % 2
    sib = z * 2 + (1 - c)

    def ypeer(k):
        return (d + k) % NY

    def zpeer(k):
        return ((z + k) % NZ) * 2 + c

    def zother(k):
        return ((z + k) % NZ) * 2 + (1 - c)

    def rcopy(src, dst, ssem, rsem, dev):
        return pltpu.make_async_remote_copy(
            src_ref=src, dst_ref=dst, send_sem=ssem, recv_sem=rsem,
            device_id=dev, device_id_type=MESH,
        )

    here = (d, s, sib)

    loads = []
    for h in range(2):
        loads.append([
            pltpu.make_async_copy(wq.at[:, h], W.at[h, :, :, 0:512], w_sem.at[3 * h]),
            pltpu.make_async_copy(wk.at[:, h], W.at[h, :, :, 512:640], w_sem.at[3 * h + 1]),
            pltpu.make_async_copy(wv.at[:, h], W.at[h, :, :, 640:768], w_sem.at[3 * h + 2]),
        ])
    wo_loads = []
    for h in range(2):
        for mm in range(NM):
            wo_loads.append(pltpu.make_async_copy(
                wo.at[:, mm * 256 + h * 128: mm * 256 + h * 128 + 128],
                WO.at[h, :, mm * 128: mm * 128 + 128], w_sem.at[6 + h * NM + mm]))
    head_load = pltpu.make_async_copy(head, HEAD, w_sem.at[22])
    for group in loads:
        for copy in group:
            copy.start()
    for copy in wo_loads:
        copy.start()
    head_load.start()

    barrier = pltpu.get_barrier_semaphore()
    partners = []
    for k in range(1, 4):
        partners.append((ypeer(k), s, m))
        partners.append((d, (s + k) % NX, m))
        partners.append((d, s, zpeer(k)))
        partners.append((d, s, zother(k)))
        partners.append((ypeer(k), (s + 1) % NX, m))
        partners.append((ypeer(k), (s + 3) % NX, m))
    partners.append(here)
    for dev in partners:
        pl.semaphore_signal(barrier, inc=1, device_id=dev, device_id_type=MESH)
    pl.semaphore_wait(barrier, len(partners))

    ahead = jnp.where(c == 0, 1, 3)
    behind = jnp.where(c == 0, 3, 1)
    steps = {"behind": behind, "ahead": ahead, "far": 2, "own": 0}
    sends = {"own": 4, "behind": 5, "ahead": 6, "far": 7}

    def eb_z(k):
        return rcopy(EB.at[m], EB.at[m], eb_s.at[k], eb_r.at[m], (d, s, zpeer(k)))

    def eb_in(who):
        mk = zpeer(steps[who])
        return rcopy(EB.at[mk], EB.at[mk], eb_s.at[0], eb_r.at[mk], here)

    def eb_relay():
        mk = zpeer(behind)
        return rcopy(EB.at[mk], EB.at[mk], eb_s.at[2], eb_r.at[mk], (d, s, zpeer(ahead)))

    def eb_fwd(who):
        mk = zpeer(steps[who])
        return rcopy(EB.at[mk], EB.at[mk], eb_s.at[sends[who]], eb_r.at[mk], here)

    def eb_sib_in(k):
        mk = zother(k)
        return rcopy(EB.at[mk], EB.at[mk], eb_s.at[0], eb_r.at[mk], here)

    def hop(h, g):
        return rcopy(HP.at[h, g], X.at[h, m, d], hop_s.at[h, g], hop_r.at[h, d],
                     (g, (s + 1) % NX, m))

    def hop_in(h, g):
        return rcopy(HP.at[h, g], X.at[h, m, g], hop_s.at[h, g], hop_r.at[h, g],
                     (g, (s + 1) % NX, m))

    def ag_z(h, k):
        return rcopy(X.at[h, m], X.at[h, m], ag_s.at[h, k], ag_r.at[h, m], (d, s, zpeer(k)))

    def ag_in(h, who):
        mk = zpeer(steps[who])
        return rcopy(X.at[h, mk], X.at[h, mk], ag_s.at[h, 0], ag_r.at[h, mk], here)

    def ag_relay(h):
        mk = zpeer(behind)
        return rcopy(X.at[h, mk], X.at[h, mk], ag_s.at[h, 2], ag_r.at[h, mk],
                     (d, s, zpeer(ahead)))

    def ag_fwd(h, who):
        mk = zpeer(steps[who])
        return rcopy(X.at[h, mk], X.at[h, mk], ag_s.at[h, sends[who]], ag_r.at[h, mk], here)

    def ag_sib_in(h, k):
        mk = zother(k)
        return rcopy(X.at[h, mk], X.at[h, mk], ag_s.at[h, 0], ag_r.at[h, mk], here)

    def res(h, k):
        g = ypeer(k)
        return rcopy(X.at[h, m, g], R.at[h, d], res_s.at[h, k], res_r.at[h, d], (g, s, m))

    def res_in(h, k):
        g = ypeer(k)
        return rcopy(X.at[h, m, g], R.at[h, g], res_s.at[h, k], res_r.at[h, g], (g, s, m))

    def ctx(k):
        return rcopy(C.at[d], C.at[d], ctx_s.at[k], ctx_r.at[d], (ypeer(k), s, m))

    def ctx_in(k):
        g = ypeer(k)
        return rcopy(C.at[g], C.at[g], ctx_s.at[0], ctx_r.at[g], here)

    def ctx_relay():
        g = ypeer(behind)
        return rcopy(C.at[g], C.at[g], ctx_s.at[2], ctx_r.at[g], (ypeer(ahead), s, m))

    def part(h, zz):
        return rcopy(PS.at[h, zz], PR.at[h, zz], ps_s.at[h, zz], ps_r.at[h, zz], here)

    def zred(h, i):
        return rcopy(ZS.at[h, i], ZR.at[h, i], zz_s.at[h, i], zz_r.at[h, i],
                     (d, s, zpeer(behind if i == 1 else ahead)))

    def norm_block(h, g, mm, x):
        col = g * 2048 + mm * 256 + h * 128
        scaled = (x * gain[:, lane(col, 128)]).astype(BF)
        XN.at[h, g][:, lane(mm * 128, 128)] = scaled

    def layer():
        SS[...] = jnp.zeros_like(SS)

        @pl.when(s == 0)
        def _():
            EB.at[m][...] = emb[...]
            eb_z(1).start()
            eb_z(3).start()
            eb_fwd("own").start()
            eb_in("behind").wait_recv()
            eb_relay().start()
            eb_fwd("behind").start()
            eb_in("ahead").wait_recv()
            eb_fwd("ahead").start()
            eb_in("far").wait_recv()
            eb_fwd("far").start()
            for k in range(4):
                eb_sib_in(k).wait_recv()

            def body(i, _):
                dl = i // 16
                mm = (i // 2) % 8
                h = i % 2
                x = EB[:, :, lane(dl * 2048 + mm * 256 + h * 128, 128)]
                xf = x.astype(F32)
                for half in range(2):
                    xs = xf[:, half * 8: half * 8 + 8, :].reshape(ROWS, 128)
                    g = half * 2 + dl
                    norm_block(h, g, mm, xs)
                    X.at[h, mm, g][...] = xs.astype(BF)
                    SS[...] += xs * xs
                return 0

            lax.fori_loop(0, 32, body, 0)
            for h in range(2):
                for k in (2, 1, 3):
                    res(h, k).start()

        @pl.when(s > 0)
        def _():
            for h in range(2):
                for g in range(NY):
                    hop_in(h, g).wait_recv()
                ag_z(h, 1).start()
                ag_z(h, 3).start()
                ag_fwd(h, "own").start()
            for h in range(2):
                ag_in(h, "behind").wait_recv()
                ag_relay(h).start()
                ag_fwd(h, "behind").start()
            for h in range(2):
                ag_in(h, "ahead").wait_recv()
                ag_fwd(h, "ahead").start()
                for k in (2, 1, 3):
                    res(h, k).start()
            for h in range(2):
                ag_in(h, "far").wait_recv()
                ag_fwd(h, "far").start()

        QA[...] = jnp.zeros_like(QA)
        for h in range(2):
            @pl.when(s > 0)
            def _():
                for k in range(4):
                    ag_sib_in(h, k).wait_recv()

                def body(mm, _):
                    for g in range(NY):
                        xf = X[h, mm, g].astype(F32)
                        norm_block(h, g, mm, xf)
                        SS[...] += xf * xf
                    return 0

                lax.fori_loop(0, NM, body, 0)

            for copy in loads[h]:
                copy.wait()

            def dots(g, _):
                w = W[h, pl.ds(g * 8, 8)].reshape(1024, 768)
                QA[...] += jnp.dot(XN[h, g], w, preferred_element_type=F32)
                return 0

            lax.fori_loop(0, NY, dots, 0)

        r = lax.rsqrt(jnp.sum(SS[...], axis=1, keepdims=True) * (1.0 / D) + EPS)
        cos = cosine[...]
        sin = sine[...]

        def rope(x):
            return (x * cos + pltpu.roll(x, 64, 1) * sin).astype(BF)

        query = jnp.concatenate(
            [rope(QA[:, j * HD:(j + 1) * HD] * r) for j in range(4)], axis=0)
        key = rope(QA[:, 512:640] * r)
        value = (QA[:, 640:768] * r).astype(BF)
        scores = lax.dot_general(query, key, (((1,), (1,)), ((), ())),
                                 preferred_element_type=F32) * (HD ** -0.5)
        shape = (4 * ROWS, ROWS)
        rq = lax.broadcasted_iota(jnp.int32, shape, 0) % ROWS
        rk = lax.broadcasted_iota(jnp.int32, shape, 1)
        slot_q, slot_k = (rq // 4) % 2, (rk // 4) % 2
        pos_q, pos_k = (rq // 8) * 4 + rq % 4, (rk // 8) * 4 + rk % 4
        live_k = jnp.where(slot_k == 0, live[2 * d], live[2 * d + 1])
        allowed = (slot_q == slot_k) & (pos_k <= pos_q) & (pos_k < live_k)
        scores = jnp.where(allowed, scores, F32(-1e30))
        highest = jnp.max(scores, axis=-1, keepdims=True)
        weights = jnp.exp(scores - highest)
        probs = (weights / jnp.sum(weights, axis=-1, keepdims=True)).astype(BF)
        mixed = jnp.dot(probs, value, preferred_element_type=F32).astype(BF)
        for j in range(4):
            C.at[d][:, j * HD:(j + 1) * HD] = mixed[j * ROWS:(j + 1) * ROWS]
        ctx(1).start()
        ctx(3).start()
        for h in range(2):
            R.at[h, d][...] = X[h, m, d]
        for copy in wo_loads:
            copy.wait()
        ctx_in(behind).wait_recv()
        ctx_relay().start()
        ctx_in(ahead).wait_recv()
        ctx_in(2).wait_recv()

        context = C[...].reshape(NY * ROWS, QW)
        for h in range(2):
            def project(i, _):
                step = jnp.where(i == 0, 2, jnp.where(i == 1, behind, jnp.where(i == 2, ahead, 0)))
                zz = (z + step) % NZ
                p = jnp.dot(context, WO[h, :, lane(zz * 256, 256)], preferred_element_type=F32)
                low, high = p[:, :128], p[:, 128:]
                PO.at[h, zz][...] = jnp.where(c == 0, low, high)
                PS.at[h, zz][...] = jnp.where(c == 0, high, low).astype(BF)
                part(h, zz).start()
                return 0

            lax.fori_loop(0, NZ, project, 0)

        def pair(h, k):
            zt = (z + k) % NZ
            part(h, zt).wait_recv()
            return PO[h, zt] + PR[h, zt].astype(F32)

        for h in range(2):
            ZS.at[h, 0][...] = pair(h, 2).astype(BF)
            zred(h, 0).start()
            ZS.at[h, 1][...] = pair(h, behind).astype(BF)
            zred(h, 1).start()
        for h in range(2):
            both = pair(h, ahead)
            zred(h, 0).wait_recv()
            ZS.at[h, 2][...] = (both + ZR[h, 0].astype(F32)).astype(BF)
            zred(h, 2).start()
        for h in range(2):
            total = pair(h, 0)
            for k in (1, 3, 2):
                res_in(h, k).wait_recv()
            total = total + R[h].astype(F32).reshape(NY * ROWS, 128)
            for i in (1, 2):
                zred(h, i).wait_recv()
                total = total + ZR[h, i].astype(F32)
            HP.at[h][...] = total.astype(BF).reshape(NY, ROWS, 128)

            @pl.when(s < NX - 1)
            def _():
                for k in (2, 1, 3, 0):
                    hop(h, ypeer(k)).start()

            @pl.when(s == NX - 1)
            def _():
                emit(1, h)

        @pl.when(s == 1)
        def _():
            for h in range(2):
                emit(0, h)

    def emit(b, h):
        nt = (((1,), (1,)), ((), ()))
        wide = HP[h].astype(F32).reshape(NY * ROWS, 128)
        square = wide * wide
        top = square.astype(BF)
        rest = (square - top.astype(F32)).astype(BF)
        ones = jnp.ones((16, 128), BF)
        sums = (lax.dot_general(ones, top, nt, preferred_element_type=F32)
                + lax.dot_general(ones, rest, nt, preferred_element_type=F32))
        cols = lane(d * 2048 + m * 256 + h * 128, 128)
        Y.at[b][0:256, cols] = (wide * fgain[:, cols]).astype(BF)
        top = sums.astype(BF).astype(F32)
        low = sums - top
        row = lax.broadcasted_iota(jnp.int32, (16, 128), 0)
        packed = jnp.where(row == 0, top[:, :128], jnp.where(row == 1, low[:, :128],
                 jnp.where(row == 2, top[:, 128:], jnp.where(row == 3, low[:, 128:], 0.0))))
        Y.at[b][256:272, cols] = packed.astype(BF)
        y_x(b, h, 1).start()
        y_x(b, h, 3).start()
        spread_own(b, h)

    def ycopy(b, g, mm, h, index, dev):
        ref = Y.at[b, :, lane(g * 2048 + mm * 256 + h * 128, 128)]
        return rcopy(ref, ref, y_s.at[b, h, index], y_r.at[b, h, g * NM + mm], dev)

    def first_piece(k):
        return (jnp.where(c == 0, ypeer(k), d), jnp.where(c == 0, m, zpeer(k)))

    def second_piece(i, k):
        g0, m0 = first_piece(i)
        return (jnp.where(c == 0, g0, ypeer(k)), jnp.where(c == 0, zpeer(k), m0))

    def first_dev(k):
        g, mm = first_piece(k)
        return (g, s, mm)

    def second_dev(k):
        g, mm = second_piece(0, k)
        return (g, s, mm)

    back = (3, 1)

    def y_x(b, h, k):
        return ycopy(b, d, m, h, k, (d, (s + k) % NX, m))

    def y_x_relay(b, h):
        return ycopy(b, d, m, h, 2, (d, jnp.where(b == 0, 3, 1), m))

    def y_first(b, h, k):
        return ycopy(b, d, m, h, 3 + k, first_dev(k))

    def y_first_relay(b, h):
        g, mm = first_piece(back[h])
        return ycopy(b, g, mm, h, 5, first_dev(4 - back[h]))

    def y_second(b, h, i, k):
        g, mm = first_piece(i)
        return ycopy(b, g, mm, h, 7 + i * 3 + k, second_dev(k))

    def y_second_relay(b, h, i):
        g, mm = second_piece(i, back[h])
        return ycopy(b, g, mm, h, 9 + i * 3, second_dev(4 - back[h]))

    def y_fwd(b, h, i, k):
        g, mm = second_piece(i, k) if k else first_piece(i)
        return ycopy(b, g, mm, h, 20 + i * 4 + k, here)

    def y_in(b, g, mm, h):
        return ycopy(b, g, mm, h, 0, here)

    def spread_own(b, h):
        for k in (1, 3):
            y_first(b, h, k).start()
        for k in (1, 3):
            y_second(b, h, 0, k).start()
        y_fwd(b, h, 0, 0).start()

    def relays_x(b, h):
        from_zero = (s == 0) & ((b == 0) | (h == 0))
        return from_zero | ((s == 2) & (b == 1) & (h == 1))

    def score(b):
        source = 2 * b + 1

        @pl.when(s != source)
        def _():
            for h in range(2):
                y_in(b, d, m, h).wait_recv()

                @pl.when(relays_x(b, h))
                def _():
                    y_x_relay(b, h).start()

                spread_own(b, h)

        def arrived_first(i, h):
            g, mm = first_piece(i)
            y_in(b, g, mm, h).wait_recv()
            if i == back[h]:
                y_first_relay(b, h).start()
            for k in (1, 3):
                y_second(b, h, i, k).start()
            y_fwd(b, h, i, 0).start()

        def arrived_second(i, h, k):
            g, mm = second_piece(i, k)
            y_in(b, g, mm, h).wait_recv()
            if k == back[h]:
                y_second_relay(b, h, i).start()
            y_fwd(b, h, i, k).start()

        def arrived_ring(i):
            for h in range(2):
                arrived_second(i, h, back[h])
            for h in range(2):
                arrived_second(i, h, 4 - back[h])

        for h in range(2):
            arrived_first(back[h], h)
        for h in range(2):
            arrived_first(4 - back[h], h)
        arrived_ring(0)
        for h in range(2):
            arrived_first(2, h)
        for i in (1, 3, 2):
            arrived_ring(i)

        def dots(k):
            g = ypeer(k)
            for h in range(2):
                for zz in range(NZ):
                    y_in(b, g, zz * 2 + (1 - c), h).wait_recv()
            cols = pl.ds(pl.multiple_of(g * 2048, 2048), 2048)
            term = lax.dot_general(HEAD[:, cols], Y[b, 0:256, cols],
                                   (((1,), (1,)), ((), ())), preferred_element_type=F32)
            LT[...] = LT[...] + term if k else term

        def dots_of(j):
            for h in range(2):
                arrived_second(j, h, 2)
            dots(j)

        dots_of(0)
        for h in range(2):
            arrived_second(1, h, 2)
        for h in range(2):
            arrived_second(3, h, 2)
        dots(1)
        dots(3)
        dots_of(2)
        extra = Y[b, 256:272, :].astype(F32)
        halves = []
        for i in (0, 2):
            wide = extra[i:i + 1] + extra[i + 1:i + 2]
            total = wide[:, 0:128]
            for j in range(1, 2 * NY * NM):
                total = total + wide[:, j * 128:(j + 1) * 128]
            halves.append(total)
        sums = jnp.concatenate(halves, axis=1)
        r = lax.rsqrt(sums * (1.0 / D) + EPS)
        logits = LT[...] * r
        highest = jnp.max(logits, axis=0, keepdims=True)
        summed = jnp.sum(jnp.exp(logits - highest), axis=0, keepdims=True)
        vocab = HEAD.shape[0]
        wanted = tgt[...] - ((d * NX + s) * NM + m) * vocab
        index = lax.broadcasted_iota(jnp.int32, logits.shape, 0)
        picked = jnp.sum(jnp.where(index == wanted, logits, 0.0), axis=0, keepdims=True)
        lanes = pl.ds(pl.multiple_of(b * 256, 256), 256)
        rows = lax.broadcasted_iota(jnp.int32, (8, 256), 0)
        STO[:, lanes] = jnp.where(rows == 0, highest,
                                  jnp.where(rows == 1, summed,
                                            jnp.where(rows == 2, picked, 0.0)))

    def step(t, _):
        place = jnp.where(s == NX - 1, 1, 0)

        @pl.when(t == place)
        def _():
            layer()

        @pl.when(t != place)
        def _():
            @pl.when((t == 0) | ((t == 1) & (s != NX - 1)))
            def _():
                head_load.wait()
            score(jnp.where(t == 2, 1, 0))
        return 0

    lax.fori_loop(0, 3, step, 0)

    def merge(ref, count):
        parts = [ref[j] for j in range(count)]
        highest = parts[0][0:1]
        for p in parts[1:]:
            highest = jnp.maximum(highest, p[0:1])
        summed = jnp.zeros_like(highest)
        picked = jnp.zeros_like(highest)
        for p in parts:
            summed = summed + p[1:2] * jnp.exp(p[0:1] - highest)
            picked = picked + p[2:3]
        return highest, summed, picked

    def stacked(highest, summed, picked):
        rows = lax.broadcasted_iota(jnp.int32, (8, 512), 0)
        return jnp.where(rows == 0, highest,
                         jnp.where(rows == 1, summed, jnp.where(rows == 2, picked, 0.0)))

    def st_y(k):
        return rcopy(SA.at[d], SA.at[d], st_s.at[0, k], st_r.at[0, d], (ypeer(k), s, m))

    def st_y_in(k):
        g = ypeer(k)
        return rcopy(SA.at[g], SA.at[g], st_s.at[0, k], st_r.at[0, g], (g, s, m))

    def m_of(k):
        return (m + k) % NM

    def st_m(k):
        return rcopy(SB.at[m], SB.at[m], st_s.at[1, k], st_r.at[1, m], (d, s, m_of(k)))

    def st_m_in(k):
        mm = m_of(k)
        return rcopy(SB.at[mm], SB.at[mm], st_s.at[1, k], st_r.at[1, mm], (d, s, mm))

    def st_x(k):
        return rcopy(SC.at[s], SC.at[s], st_s.at[2, k], st_r.at[2, s], (d, (s + k) % NX, m))

    def st_x_in(k):
        ss = (s + k) % NX
        return rcopy(SC.at[ss], SC.at[ss], st_s.at[2, k], st_r.at[2, ss], (d, ss, m))

    SA.at[d][...] = STO[...]
    for k in (2, 1, 3):
        st_y(k).start()
    for k in (1, 3, 2):
        st_y_in(k).wait_recv()
    SB.at[m][...] = stacked(*merge(SA, NY))
    for k in (4, 3, 5, 2, 6, 1, 7):
        st_m(k).start()
    for k in (1, 7, 2, 6, 3, 5, 4):
        st_m_in(k).wait_recv()
    SC.at[s][...] = stacked(*merge(SB, NM))
    for k in (2, 1, 3):
        st_x(k).start()
    for k in (1, 3, 2):
        st_x_in(k).wait_recv()
    highest, summed, picked = merge(SC, NX)
    out[...] = jnp.broadcast_to(picked - (highest + jnp.log(summed)), out.shape)

    @pl.when(s == 0)
    def _():
        for k in (1, 3):
            eb_z(k).wait_send()
        eb_relay().wait_send()
        for who in sends:
            eb_fwd(who).wait_send()

    @pl.when(s > 0)
    def _():
        for h in range(2):
            for k in (1, 3):
                ag_z(h, k).wait_send()
            ag_relay(h).wait_send()
            for who in sends:
                ag_fwd(h, who).wait_send()

    @pl.when(s < NX - 1)
    def _():
        for h in range(2):
            for k in range(4):
                hop(h, ypeer(k)).wait_send()

    for h in range(2):
        for k in range(1, 4):
            res(h, k).wait_send()
        for i in range(3):
            zred(h, i).wait_send()
        for zz in range(NZ):
            part(h, zz).wait_send()
    for k in (1, 3):
        ctx(k).wait_send()
    ctx_relay().wait_send()
    for k in range(1, 4):
        st_y(k).wait_send()
        st_x(k).wait_send()
    for k in range(1, 8):
        st_m(k).wait_send()
    for b in range(2):
        for h in range(2):
            @pl.when(s == 2 * b + 1)
            def _():
                for k in (1, 3):
                    y_x(b, h, k).wait_send()

            @pl.when(relays_x(b, h))
            def _():
                y_x_relay(b, h).wait_send()

            for k in (1, 3):
                y_first(b, h, k).wait_send()
            y_first_relay(b, h).wait_send()
            for i in range(4):
                for k in (1, 3):
                    y_second(b, h, i, k).wait_send()
                y_second_relay(b, h, i).wait_send()
                for k in range(4):
                    y_fwd(b, h, i, k).wait_send()


def tables():
    row = np.arange(ROWS)
    position = (row // 8) * 4 + row % 4
    half = HD // 2
    freqs = (ROPE_BASE ** (-np.arange(half) * 2.0 / HD)).astype(np.float32)
    angles = (position.astype(np.float32)[:, None] * freqs[None, :]).astype(np.float64)
    cos, sin = np.cos(angles), np.sin(angles)
    return (np.concatenate([cos, cos], 1).astype(np.float32),
            np.concatenate([-sin, sin], 1).astype(np.float32))


def per_device(
    embeds, targets, lengths, source, attn_gain, w_query, w_key, w_value, w_out, final_gain, head
):
    d = lax.axis_index("dp")
    vocab = head.shape[0]
    emb = embeds.reshape(8, 2, 4096).transpose(1, 0, 2).reshape(16, 4096)
    tgt = targets.reshape(NY, 2, NM, 4).transpose(0, 2, 1, 3).reshape(1, NY * ROWS)
    cos, sin = tables()
    vmem = pl.BlockSpec(memory_space=pltpu.VMEM)
    hbm = pl.BlockSpec(memory_space=pl.ANY)
    smem = pl.BlockSpec(memory_space=pltpu.SMEM)
    dma = pltpu.SemaphoreType.DMA
    stats = pl.pallas_call(
        kernel,
        out_shape=jax.ShapeDtypeStruct((8, 512), F32),
        in_specs=[vmem, smem, vmem, vmem, vmem, vmem, vmem, hbm, hbm, hbm, hbm, hbm],
        out_specs=vmem,
        scratch_shapes=[
            pltpu.VMEM((2, 32, 128, 768), BF),
            pltpu.VMEM((2, QW, 1024), BF),
            pltpu.VMEM((vocab, D), BF),
            pltpu.VMEM((NM, 16, 4096), BF),
            pltpu.VMEM((2, NM, NY, ROWS, 128), BF),
            pltpu.VMEM((2, NY, ROWS, 1024), BF),
            pltpu.VMEM((ROWS, 128), F32),
            pltpu.VMEM((ROWS, 768), F32),
            pltpu.VMEM((2, NY, ROWS, 128), BF),
            pltpu.VMEM((NY, ROWS, QW), BF),
            pltpu.VMEM((2, NZ, NY * ROWS, 128), BF),
            pltpu.VMEM((2, NZ, NY * ROWS, 128), BF),
            pltpu.VMEM((2, NZ, NY * ROWS, 128), F32),
            pltpu.VMEM((2, 3, NY * ROWS, 128), BF),
            pltpu.VMEM((2, 3, NY * ROWS, 128), BF),
            pltpu.VMEM((2, NY, ROWS, 128), BF),
            pltpu.VMEM((2, 272, D), BF),
            pltpu.VMEM((vocab, 256), F32),
            pltpu.VMEM((8, 512), F32),
            pltpu.VMEM((NY, 8, 512), F32),
            pltpu.VMEM((NM, 8, 512), F32),
            pltpu.VMEM((NX, 8, 512), F32),
            dma((23,)),
            dma((8,)), dma((8,)),
            dma((2, 4)), dma((2, 4)),
            dma((2, 8)), dma((2, 8)),
            dma((2, 4)), dma((2, 4)),
            dma((4,)), dma((4,)),
            dma((2, 4)), dma((2, 4)),
            dma((2, 4)), dma((2, 4)),
            dma((2, 2, 36)), dma((2, 2, 32)),
            dma((3, 8)), dma((3, 8)),
        ],
        compiler_params=pltpu.CompilerParams(
            collective_id=0, has_side_effects=True, vmem_limit_bytes=60 * 1024 * 1024),
        cost_estimate=pl.CostEstimate(flops=8_000_000_000, bytes_accessed=24_000_000,
                                      transcendentals=300_000),
    )(
        emb, lengths, tgt, attn_gain, final_gain.reshape(1, D), jnp.asarray(cos), jnp.asarray(sin),
        w_query.reshape(32, 2, 128, 512), w_key.reshape(32, 2, 128, 128),
        w_value.reshape(32, 2, 128, 128), w_out.reshape(512, 2048), head,
    )
    slots = stats[0].reshape(2, NY, NM, 2, 4).transpose(0, 1, 3, 2, 4).reshape(2, 8, 32)
    chosen = lax.dynamic_slice_in_dim(source, d * 2, 2, 0)
    live = jnp.take(lengths, chosen, axis=0)
    picked = jnp.take(slots, chosen, axis=1)
    valid = jnp.arange(32)[None, :] < live[:, None]
    result = jnp.where(valid[None], picked, F32(0.0))
    return (result[0], result[1])


def solution(mesh):
    return jax.shard_map(
        per_device,
        mesh=mesh,
        in_specs=(
            P("dp", "mp", None),
            P(),
            P(),
            P(),
            P("section", None),
            P("section", None, "mp"),
            P("section", None, "mp"),
            P("section", None, "mp"),
            P("section", "mp", "dp"),
            P(),
            P(("dp", "section", "mp"), None),
        ),
        out_specs=(P("dp", None), P("dp", None)),
        check_vma=False,
    )
```

```python
import jax
import jax.numpy as jnp
import numpy as np
from jax import lax
from jax.experimental import pallas as pl
from jax.experimental.pallas import tpu as pltpu
from jax.sharding import PartitionSpec as P

HD = 128
EPS = 1e-05
ROPE_BASE = 500000.0
NY = 4
NX = 4
NZ = 4
NM = 8
ROWS = 64
D = 8192
QW = 512
MESH = pl.DeviceIdType.MESH
BF = jnp.bfloat16
F32 = jnp.float32


def lane(start, size):
    return pl.ds(pl.multiple_of(start, 128), size)


def kernel(
    emb, live, tgt, gain, fgain, cosine, sine, wq, wk, wv, wo, head, out,
    W, WO, HEAD, EB, X, XN, SS, QA, R, C, PS, PR, PO, ZS, ZR, HP, Y, LT, STO, SA, SB, SC,
    w_sem, eb_s, eb_r, hop_s, hop_r, ag_s, ag_r, res_s, res_r, ctx_s, ctx_r, ps_s, ps_r,
    zz_s, zz_r, y_s, y_r, st_s, st_r,
):
    d = lax.axis_index("dp")
    s = lax.axis_index("section")
    m = lax.axis_index("mp")
    z = m // 2
    c = m % 2
    sib = z * 2 + (1 - c)

    def ypeer(k):
        return (d + k) % NY

    def zpeer(k):
        return ((z + k) % NZ) * 2 + c

    def zother(k):
        return ((z + k) % NZ) * 2 + (1 - c)

    def rcopy(src, dst, ssem, rsem, dev):
        return pltpu.make_async_remote_copy(
            src_ref=src, dst_ref=dst, send_sem=ssem, recv_sem=rsem,
            device_id=dev, device_id_type=MESH,
        )

    here = (d, s, sib)

    loads = []
    for h in range(2):
        loads.append([
            pltpu.make_async_copy(wq.at[:, h], W.at[h, :, :, 0:512], w_sem.at[3 * h]),
            pltpu.make_async_copy(wk.at[:, h], W.at[h, :, :, 512:640], w_sem.at[3 * h + 1]),
            pltpu.make_async_copy(wv.at[:, h], W.at[h, :, :, 640:768], w_sem.at[3 * h + 2]),
        ])
    wo_loads = []
    for h in range(2):
        for mm in range(NM):
            wo_loads.append(pltpu.make_async_copy(
                wo.at[:, mm * 256 + h * 128: mm * 256 + h * 128 + 128],
                WO.at[h, :, mm * 128: mm * 128 + 128], w_sem.at[6 + h * NM + mm]))
    for group in loads:
        for copy in group:
            copy.start()
    for copy in wo_loads:
        copy.start()

    barrier = pltpu.get_barrier_semaphore()
    partners = []
    for k in range(1, 4):
        partners.append((ypeer(k), s, m))
        partners.append((d, (s + k) % NX, m))
        partners.append((d, s, zpeer(k)))
        partners.append((d, s, zother(k)))
        partners.append((ypeer(k), (s + 1) % NX, m))
        partners.append((ypeer(k), (s + 3) % NX, m))
    partners.append(here)
    for dev in partners:
        pl.semaphore_signal(barrier, inc=1, device_id=dev, device_id_type=MESH)
    offsets = (0, 3, 1, 2)
    for cc in range(2):
        for j in range(4):
            for i in range(4):
                g, zz = (offsets[i], offsets[j]) if cc == 0 else (offsets[j], offsets[i])
                col = ypeer(g) * 2048 + ((z + zz) % NZ) * 512 + cc * 256
                pltpu.make_async_copy(head.at[:, lane(col, 256)],
                                      HEAD.at[cc, j, :, i * 256:i * 256 + 256],
                                      w_sem.at[22]).start()
    head_load = pltpu.make_async_copy(HEAD, HEAD, w_sem.at[22])
    pl.semaphore_wait(barrier, len(partners))

    ahead = jnp.where(c == 0, 1, 3)
    behind = jnp.where(c == 0, 3, 1)
    steps = {"behind": behind, "ahead": ahead, "far": 2, "own": 0}
    sends = {"own": 4, "behind": 5, "ahead": 6, "far": 7}

    def eb_z(k):
        return rcopy(EB.at[m], EB.at[m], eb_s.at[k], eb_r.at[m], (d, s, zpeer(k)))

    def eb_in(who):
        mk = zpeer(steps[who])
        return rcopy(EB.at[mk], EB.at[mk], eb_s.at[0], eb_r.at[mk], here)

    def eb_relay():
        mk = zpeer(behind)
        return rcopy(EB.at[mk], EB.at[mk], eb_s.at[2], eb_r.at[mk], (d, s, zpeer(ahead)))

    def eb_fwd(who):
        mk = zpeer(steps[who])
        return rcopy(EB.at[mk], EB.at[mk], eb_s.at[sends[who]], eb_r.at[mk], here)

    def eb_sib_in(k):
        mk = zother(k)
        return rcopy(EB.at[mk], EB.at[mk], eb_s.at[0], eb_r.at[mk], here)

    def hop(h, g):
        return rcopy(HP.at[h, g], X.at[h, m, d], hop_s.at[h, g], hop_r.at[h, d],
                     (g, (s + 1) % NX, m))

    def hop_in(h, g):
        return rcopy(HP.at[h, g], X.at[h, m, g], hop_s.at[h, g], hop_r.at[h, g],
                     (g, (s + 1) % NX, m))

    def ag_z(h, k):
        return rcopy(X.at[h, m], X.at[h, m], ag_s.at[h, k], ag_r.at[h, m], (d, s, zpeer(k)))

    def ag_in(h, who):
        mk = zpeer(steps[who])
        return rcopy(X.at[h, mk], X.at[h, mk], ag_s.at[h, 0], ag_r.at[h, mk], here)

    def ag_relay(h):
        mk = zpeer(behind)
        return rcopy(X.at[h, mk], X.at[h, mk], ag_s.at[h, 2], ag_r.at[h, mk],
                     (d, s, zpeer(ahead)))

    def ag_fwd(h, who):
        mk = zpeer(steps[who])
        return rcopy(X.at[h, mk], X.at[h, mk], ag_s.at[h, sends[who]], ag_r.at[h, mk], here)

    def ag_sib_in(h, k):
        mk = zother(k)
        return rcopy(X.at[h, mk], X.at[h, mk], ag_s.at[h, 0], ag_r.at[h, mk], here)

    def res(h, k):
        g = ypeer(k)
        return rcopy(X.at[h, m, g], R.at[h, d], res_s.at[h, k], res_r.at[h, d], (g, s, m))

    def res_in(h, k):
        g = ypeer(k)
        return rcopy(X.at[h, m, g], R.at[h, g], res_s.at[h, k], res_r.at[h, g], (g, s, m))

    def ctx(k):
        return rcopy(C.at[d], C.at[d], ctx_s.at[k], ctx_r.at[d], (ypeer(k), s, m))

    def ctx_in(k):
        g = ypeer(k)
        return rcopy(C.at[g], C.at[g], ctx_s.at[0], ctx_r.at[g], here)

    def ctx_relay():
        g = ypeer(behind)
        return rcopy(C.at[g], C.at[g], ctx_s.at[2], ctx_r.at[g], (ypeer(ahead), s, m))

    def part(h, zz):
        return rcopy(PS.at[h, zz], PR.at[h, zz], ps_s.at[h, zz], ps_r.at[h, zz], here)

    def zred(h, i):
        return rcopy(ZS.at[h, i], ZR.at[h, i], zz_s.at[h, i], zz_r.at[h, i],
                     (d, s, zpeer(behind if i == 1 else ahead)))

    def norm_block(h, g, mm, x):
        col = g * 2048 + mm * 256 + h * 128
        scaled = (x * gain[:, lane(col, 128)]).astype(BF)
        XN.at[h, g][:, lane(mm * 128, 128)] = scaled

    def layer():
        SS[...] = jnp.zeros_like(SS)

        @pl.when(s == 0)
        def _():
            EB.at[m][...] = emb[...]
            eb_z(1).start()
            eb_z(3).start()
            eb_fwd("own").start()
            eb_in("behind").wait_recv()
            eb_relay().start()
            eb_fwd("behind").start()
            eb_in("ahead").wait_recv()
            eb_fwd("ahead").start()
            eb_in("far").wait_recv()
            eb_fwd("far").start()
            for k in range(4):
                eb_sib_in(k).wait_recv()

            def body(i, _):
                dl = i // 16
                mm = (i // 2) % 8
                h = i % 2
                x = EB[:, :, lane(dl * 2048 + mm * 256 + h * 128, 128)]
                xf = x.astype(F32)
                for half in range(2):
                    xs = xf[:, half * 8: half * 8 + 8, :].reshape(ROWS, 128)
                    g = half * 2 + dl
                    norm_block(h, g, mm, xs)
                    X.at[h, mm, g][...] = xs.astype(BF)
                    SS[...] += xs * xs
                return 0

            lax.fori_loop(0, 32, body, 0)
            for h in range(2):
                for k in (2, 1, 3):
                    res(h, k).start()

        @pl.when(s > 0)
        def _():
            for h in range(2):
                for g in range(NY):
                    hop_in(h, g).wait_recv()
                ag_z(h, 1).start()
                ag_z(h, 3).start()
                ag_fwd(h, "own").start()
            for h in range(2):
                ag_in(h, "behind").wait_recv()
                ag_relay(h).start()
                ag_fwd(h, "behind").start()
            for h in range(2):
                ag_in(h, "ahead").wait_recv()
                ag_fwd(h, "ahead").start()
                for k in (2, 1, 3):
                    res(h, k).start()
            for h in range(2):
                ag_in(h, "far").wait_recv()
                ag_fwd(h, "far").start()

        QA[...] = jnp.zeros_like(QA)
        for h in range(2):
            @pl.when(s > 0)
            def _():
                for k in range(4):
                    ag_sib_in(h, k).wait_recv()

                def body(mm, _):
                    for g in range(NY):
                        xf = X[h, mm, g].astype(F32)
                        norm_block(h, g, mm, xf)
                        SS[...] += xf * xf
                    return 0

                lax.fori_loop(0, NM, body, 0)

            for copy in loads[h]:
                copy.wait()

            def dots(g, _):
                w = W[h, pl.ds(g * 8, 8)].reshape(1024, 768)
                QA[...] += jnp.dot(XN[h, g], w, preferred_element_type=F32)
                return 0

            lax.fori_loop(0, NY, dots, 0)

        r = lax.rsqrt(jnp.sum(SS[...], axis=1, keepdims=True) * (1.0 / D) + EPS)
        cos = cosine[...]
        sin = sine[...]

        def rope(x):
            return (x * cos + pltpu.roll(x, 64, 1) * sin).astype(BF)

        query = jnp.concatenate(
            [rope(QA[:, j * HD:(j + 1) * HD] * r) for j in range(4)], axis=0)
        key = rope(QA[:, 512:640] * r)
        value = (QA[:, 640:768] * r).astype(BF)
        scores = lax.dot_general(query, key, (((1,), (1,)), ((), ())),
                                 preferred_element_type=F32) * (HD ** -0.5)
        shape = (4 * ROWS, ROWS)
        rq = lax.broadcasted_iota(jnp.int32, shape, 0) % ROWS
        rk = lax.broadcasted_iota(jnp.int32, shape, 1)
        slot_q, slot_k = (rq // 4) % 2, (rk // 4) % 2
        pos_q, pos_k = (rq // 8) * 4 + rq % 4, (rk // 8) * 4 + rk % 4
        live_k = jnp.where(slot_k == 0, live[2 * d], live[2 * d + 1])
        allowed = (slot_q == slot_k) & (pos_k <= pos_q) & (pos_k < live_k)
        scores = jnp.where(allowed, scores, F32(-1e30))
        highest = jnp.max(scores, axis=-1, keepdims=True)
        weights = jnp.exp(scores - highest)
        probs = (weights / jnp.sum(weights, axis=-1, keepdims=True)).astype(BF)
        mixed = jnp.dot(probs, value, preferred_element_type=F32).astype(BF)
        for j in range(4):
            C.at[d][:, j * HD:(j + 1) * HD] = mixed[j * ROWS:(j + 1) * ROWS]
        ctx(1).start()
        ctx(3).start()
        for h in range(2):
            R.at[h, d][...] = X[h, m, d]
        for copy in wo_loads:
            copy.wait()
        ctx_in(behind).wait_recv()
        ctx_relay().start()
        ctx_in(ahead).wait_recv()
        ctx_in(2).wait_recv()

        context = C[...].reshape(NY * ROWS, QW)
        for h in range(2):
            def project(i, _):
                step = jnp.where(i == 0, 2, jnp.where(i == 1, behind, jnp.where(i == 2, ahead, 0)))
                zz = (z + step) % NZ
                p = jnp.dot(context, WO[h, :, lane(zz * 256, 256)], preferred_element_type=F32)
                low, high = p[:, :128], p[:, 128:]
                PO.at[h, zz][...] = jnp.where(c == 0, low, high)
                PS.at[h, zz][...] = jnp.where(c == 0, high, low).astype(BF)
                part(h, zz).start()
                return 0

            lax.fori_loop(0, NZ, project, 0)

        def pair(h, k):
            zt = (z + k) % NZ
            part(h, zt).wait_recv()
            return PO[h, zt] + PR[h, zt].astype(F32)

        for h in range(2):
            ZS.at[h, 0][...] = pair(h, 2).astype(BF)
            zred(h, 0).start()
            ZS.at[h, 1][...] = pair(h, behind).astype(BF)
            zred(h, 1).start()
        for h in range(2):
            both = pair(h, ahead)
            zred(h, 0).wait_recv()
            ZS.at[h, 2][...] = (both + ZR[h, 0].astype(F32)).astype(BF)
            zred(h, 2).start()
        for h in range(2):
            total = pair(h, 0)
            for k in (1, 3, 2):
                res_in(h, k).wait_recv()
            total = total + R[h].astype(F32).reshape(NY * ROWS, 128)
            for i in (1, 2):
                zred(h, i).wait_recv()
                total = total + ZR[h, i].astype(F32)
            HP.at[h][...] = total.astype(BF).reshape(NY, ROWS, 128)

            @pl.when(s < NX - 1)
            def _():
                for k in (2, 1, 3, 0):
                    hop(h, ypeer(k)).start()

        @pl.when(s % 2 == 1)
        def _():
            emit(s // 2)

    def emit(b):
        nt = (((1,), (1,)), ((), ()))
        ones = jnp.ones((16, 128), BF)
        sums = jnp.zeros((16, NY * ROWS), F32)
        mine = Y.at[b, c, 0, 0]
        for h in range(2):
            wide = HP[h].astype(F32).reshape(NY * ROWS, 128)
            square = wide * wide
            top = square.astype(BF)
            rest = (square - top.astype(F32)).astype(BF)
            sums = sums + lax.dot_general(ones, top, nt, preferred_element_type=F32)
            sums = sums + lax.dot_general(ones, rest, nt, preferred_element_type=F32)
            cols = lane(d * 2048 + m * 256 + h * 128, 128)
            mine[0:256, h * 128:h * 128 + 128] = (wide * fgain[:, cols]).astype(BF)
        top = sums.astype(BF).astype(F32)
        row = lax.broadcasted_iota(jnp.int32, (16, NY * ROWS), 0)
        packed = jnp.where(row == 0, top, jnp.where(row == 1, sums - top, 0.0))
        mine[256:272, :] = packed.astype(BF)
        y_x(b, 1).start()
        y_x(b, 3).start()
        spread_own(b)

    def first_dev(k):
        return (jnp.where(c == 0, ypeer(k), d), s, jnp.where(c == 0, m, zpeer(k)))

    def second_dev(k):
        return (jnp.where(c == 0, d, ypeer(k)), s, jnp.where(c == 0, zpeer(k), m))

    def ycopy(src, dst, b, i, j, dev):
        return rcopy(src, dst, y_s.at[b, i], y_r.at[b, j], dev)

    def y_x(b, k):
        ref = Y.at[b, c, 0, 0]
        return ycopy(ref, ref, b, k, 0, (d, (s + k) % NX, m))

    cut = (pl.ds(0, 144), pl.ds(144, 128))

    def y_x_relay(b, half):
        ref = Y.at[b, c, 0, 0, cut[half]]
        return ycopy(ref, ref, b, 4 + half, 0, (d, jnp.where(b == 0, 3, 1), m))

    def relays_x(b, half):
        return (s == 0) if half == 0 else (s == jnp.where(b == 0, 0, 2))

    def y_first(b, k):
        slot = 1 if k == 1 else 2
        return ycopy(Y.at[b, c, 0, 0], Y.at[b, c, 0, slot], b, 5 + k, slot, first_dev(k))

    def y_first_relay(b, half):
        slot, k = ((1, 1), (2, 3))[half]
        return ycopy(Y.at[b, c, 0, slot, cut[half]], Y.at[b, c, 0, 3, cut[half]],
                     b, 9 + half, 3, first_dev(k))

    def y_opposite(b):
        ref = Y.at[b, c, 0, 3]
        return ycopy(ref, ref, b, 9, 3, here)

    sets = (pl.ds(0, 1), pl.ds(1, 2), pl.ds(3, 1))

    def y_second(b, part_no, k):
        slot = 1 if k == 1 else 2
        return ycopy(Y.at[b, c, 0, sets[part_no]], Y.at[b, c, slot, sets[part_no]],
                     b, 11 + part_no * 2 + (slot - 1), 1 + 3 * slot + part_no, second_dev(k))

    def y_second_relay(b, i):
        slot, k = (1, 1) if i < 2 else (2, 3)
        return ycopy(Y.at[b, c, slot, i], Y.at[b, c, 3, i], b, 17 + i, 10 + i, second_dev(k))

    forwards = ((0, 0, 1), (0, 1, 2), (0, 3, 1), (1, 0, 4), (2, 0, 4), (3, 0, 2), (3, 2, 2))

    def y_fwd(b, n, who):
        j, i, size = forwards[n]
        ref = Y.at[b, who, j, pl.ds(i, size)]
        return ycopy(ref, ref, b, 21 + n, 14 + n, here)

    def spread_own(b):
        for k in (1, 3):
            y_first(b, k).start()
        for k in (1, 3):
            y_second(b, 0, k).start()
        y_fwd(b, 0, c).start()

    def dots(b, cc, j, start):
        pieces = jnp.concatenate([Y[b, cc, j, i, 0:256, :] for i in range(4)], axis=1)
        term = lax.dot_general(HEAD[cc, j], pieces, (((1,), (1,)), ((), ())),
                               preferred_element_type=F32)
        LT[...] = term if start else LT[...] + term

    def score(b):
        source = 2 * b + 1

        @pl.when(s != source)
        def _():
            y_x(b, 1).wait_recv()
            for half in range(2):
                @pl.when(relays_x(b, half))
                def _():
                    y_x_relay(b, half).start()
            spread_own(b)

        y_first(b, 1).wait_recv()
        y_first_relay(b, 0).start()
        y_first(b, 3).wait_recv()
        y_first_relay(b, 1).start()
        for k in (1, 3):
            y_second(b, 1, k).start()
        y_fwd(b, 1, c).start()
        y_second(b, 0, 1).wait_recv()
        y_second_relay(b, 0).start()
        y_second(b, 0, 3).wait_recv()
        y_opposite(b).wait_recv()
        for k in (1, 3):
            y_second(b, 2, k).start()
        y_fwd(b, 2, c).start()
        y_second(b, 1, 1).wait_recv()
        y_second_relay(b, 1).start()
        y_second(b, 1, 3).wait_recv()
        y_second_relay(b, 2).start()
        y_second(b, 2, 3).wait_recv()
        y_second_relay(b, 3).start()
        y_fwd(b, 4, c).start()
        y_second(b, 2, 1).wait_recv()
        y_fwd(b, 3, c).start()

        dots(b, c, 0, True)
        for n in range(3):
            y_fwd(b, n, 1 - c).wait_recv()
        dots(b, 1 - c, 0, False)
        dots(b, c, 2, False)
        dots(b, c, 1, False)
        y_second_relay(b, 0).wait_recv()
        y_second_relay(b, 1).wait_recv()
        y_fwd(b, 5, c).start()
        y_fwd(b, 4, 1 - c).wait_recv()
        dots(b, 1 - c, 2, False)
        y_second_relay(b, 2).wait_recv()
        y_second_relay(b, 3).wait_recv()
        y_fwd(b, 6, c).start()
        y_fwd(b, 3, 1 - c).wait_recv()
        dots(b, 1 - c, 1, False)
        dots(b, c, 3, False)
        y_fwd(b, 5, 1 - c).wait_recv()
        y_fwd(b, 6, 1 - c).wait_recv()
        dots(b, 1 - c, 3, False)

        extra = jnp.zeros((16, 256), F32)
        for cc in range(2):
            for j in range(4):
                for i in range(4):
                    extra = extra + Y[b, cc, j, i, 256:272, :].astype(F32)
        sums = jnp.sum(extra, axis=0, keepdims=True)
        r = lax.rsqrt(sums * (1.0 / D) + EPS)
        logits = LT[...] * r
        highest = jnp.max(logits, axis=0, keepdims=True)
        summed = jnp.sum(jnp.exp(logits - highest), axis=0, keepdims=True)
        vocab = HEAD.shape[2]
        wanted = tgt[...] - ((d * NX + s) * NM + m) * vocab
        index = lax.broadcasted_iota(jnp.int32, logits.shape, 0)
        picked = jnp.sum(jnp.where(index == wanted, logits, 0.0), axis=0, keepdims=True)
        lanes = pl.ds(pl.multiple_of(b * 256, 256), 256)
        rows = lax.broadcasted_iota(jnp.int32, (8, 256), 0)
        STO[:, lanes] = jnp.where(rows == 0, highest,
                                  jnp.where(rows == 1, summed,
                                            jnp.where(rows == 2, picked, 0.0)))

    def step(t, _):
        place = jnp.where(s == NX - 1, 1, 0)

        @pl.when(t == place)
        def _():
            layer()

        @pl.when(t != place)
        def _():
            @pl.when((t == 0) | ((t == 1) & (s != NX - 1)))
            def _():
                head_load.wait()
            score(jnp.where(t == 2, 1, 0))
        return 0

    lax.fori_loop(0, 3, step, 0)

    def merge(ref, count):
        parts = [ref[j] for j in range(count)]
        highest = parts[0][0:1]
        for p in parts[1:]:
            highest = jnp.maximum(highest, p[0:1])
        summed = jnp.zeros_like(highest)
        picked = jnp.zeros_like(highest)
        for p in parts:
            summed = summed + p[1:2] * jnp.exp(p[0:1] - highest)
            picked = picked + p[2:3]
        return highest, summed, picked

    def stacked(highest, summed, picked):
        rows = lax.broadcasted_iota(jnp.int32, (8, 512), 0)
        return jnp.where(rows == 0, highest,
                         jnp.where(rows == 1, summed, jnp.where(rows == 2, picked, 0.0)))

    def st_y(k):
        return rcopy(SA.at[d], SA.at[d], st_s.at[0, k], st_r.at[0, d], (ypeer(k), s, m))

    def st_y_in(k):
        g = ypeer(k)
        return rcopy(SA.at[g], SA.at[g], st_s.at[0, k], st_r.at[0, g], (g, s, m))

    def m_of(k):
        return (m + k) % NM

    def st_m(k):
        return rcopy(SB.at[m], SB.at[m], st_s.at[1, k], st_r.at[1, m], (d, s, m_of(k)))

    def st_m_in(k):
        mm = m_of(k)
        return rcopy(SB.at[mm], SB.at[mm], st_s.at[1, k], st_r.at[1, mm], (d, s, mm))

    def st_x(k):
        return rcopy(SC.at[s], SC.at[s], st_s.at[2, k], st_r.at[2, s], (d, (s + k) % NX, m))

    def st_x_in(k):
        ss = (s + k) % NX
        return rcopy(SC.at[ss], SC.at[ss], st_s.at[2, k], st_r.at[2, ss], (d, ss, m))

    SA.at[d][...] = STO[...]
    for k in (2, 1, 3):
        st_y(k).start()
    for k in (1, 3, 2):
        st_y_in(k).wait_recv()
    SB.at[m][...] = stacked(*merge(SA, NY))
    for k in (4, 3, 5, 2, 6, 1, 7):
        st_m(k).start()
    for k in (1, 7, 2, 6, 3, 5, 4):
        st_m_in(k).wait_recv()
    SC.at[s][...] = stacked(*merge(SB, NM))
    for k in (2, 1, 3):
        st_x(k).start()
    for k in (1, 3, 2):
        st_x_in(k).wait_recv()
    highest, summed, picked = merge(SC, NX)
    out[...] = jnp.broadcast_to(picked - (highest + jnp.log(summed)), out.shape)

    @pl.when(s == 0)
    def _():
        for k in (1, 3):
            eb_z(k).wait_send()
        eb_relay().wait_send()
        for who in sends:
            eb_fwd(who).wait_send()

    @pl.when(s > 0)
    def _():
        for h in range(2):
            for k in (1, 3):
                ag_z(h, k).wait_send()
            ag_relay(h).wait_send()
            for who in sends:
                ag_fwd(h, who).wait_send()

    @pl.when(s < NX - 1)
    def _():
        for h in range(2):
            for k in range(4):
                hop(h, ypeer(k)).wait_send()

    for h in range(2):
        for k in range(1, 4):
            res(h, k).wait_send()
        for i in range(3):
            zred(h, i).wait_send()
        for zz in range(NZ):
            part(h, zz).wait_send()
    for k in (1, 3):
        ctx(k).wait_send()
    ctx_relay().wait_send()
    for k in range(1, 4):
        st_y(k).wait_send()
        st_x(k).wait_send()
    for k in range(1, 8):
        st_m(k).wait_send()
    for b in range(2):
        @pl.when(s == 2 * b + 1)
        def _():
            for k in (1, 3):
                y_x(b, k).wait_send()

        for half in range(2):
            @pl.when((s != 2 * b + 1) & relays_x(b, half))
            def _():
                y_x_relay(b, half).wait_send()

            y_first_relay(b, half).wait_send()
        for k in (1, 3):
            y_first(b, k).wait_send()
            for n in range(3):
                y_second(b, n, k).wait_send()
        for i in range(4):
            y_second_relay(b, i).wait_send()
        for n in range(7):
            y_fwd(b, n, c).wait_send()


def tables():
    row = np.arange(ROWS)
    position = (row // 8) * 4 + row % 4
    half = HD // 2
    freqs = (ROPE_BASE ** (-np.arange(half) * 2.0 / HD)).astype(np.float32)
    angles = (position.astype(np.float32)[:, None] * freqs[None, :]).astype(np.float64)
    cos, sin = np.cos(angles), np.sin(angles)
    return (np.concatenate([cos, cos], 1).astype(np.float32),
            np.concatenate([-sin, sin], 1).astype(np.float32))


def per_device(
    embeds, targets, lengths, source, attn_gain, w_query, w_key, w_value, w_out, final_gain, head
):
    d = lax.axis_index("dp")
    vocab = head.shape[0]
    emb = embeds.reshape(8, 2, 4096).transpose(1, 0, 2).reshape(16, 4096)
    tgt = targets.reshape(NY, 2, NM, 4).transpose(0, 2, 1, 3).reshape(1, NY * ROWS)
    cos, sin = tables()
    vmem = pl.BlockSpec(memory_space=pltpu.VMEM)
    hbm = pl.BlockSpec(memory_space=pl.ANY)
    smem = pl.BlockSpec(memory_space=pltpu.SMEM)
    dma = pltpu.SemaphoreType.DMA
    stats = pl.pallas_call(
        kernel,
        out_shape=jax.ShapeDtypeStruct((8, 512), F32),
        in_specs=[vmem, smem, vmem, vmem, vmem, vmem, vmem, hbm, hbm, hbm, hbm, hbm],
        out_specs=vmem,
        scratch_shapes=[
            pltpu.VMEM((2, 32, 128, 768), BF),
            pltpu.VMEM((2, QW, 1024), BF),
            pltpu.VMEM((2, 4, vocab, 1024), BF),
            pltpu.VMEM((NM, 16, 4096), BF),
            pltpu.VMEM((2, NM, NY, ROWS, 128), BF),
            pltpu.VMEM((2, NY, ROWS, 1024), BF),
            pltpu.VMEM((ROWS, 128), F32),
            pltpu.VMEM((ROWS, 768), F32),
            pltpu.VMEM((2, NY, ROWS, 128), BF),
            pltpu.VMEM((NY, ROWS, QW), BF),
            pltpu.VMEM((2, NZ, NY * ROWS, 128), BF),
            pltpu.VMEM((2, NZ, NY * ROWS, 128), BF),
            pltpu.VMEM((2, NZ, NY * ROWS, 128), F32),
            pltpu.VMEM((2, 3, NY * ROWS, 128), BF),
            pltpu.VMEM((2, 3, NY * ROWS, 128), BF),
            pltpu.VMEM((2, NY, ROWS, 128), BF),
            pltpu.VMEM((2, 2, 4, 4, 272, 256), BF),
            pltpu.VMEM((vocab, 256), F32),
            pltpu.VMEM((8, 512), F32),
            pltpu.VMEM((NY, 8, 512), F32),
            pltpu.VMEM((NM, 8, 512), F32),
            pltpu.VMEM((NX, 8, 512), F32),
            dma((23,)),
            dma((8,)), dma((8,)),
            dma((2, 4)), dma((2, 4)),
            dma((2, 8)), dma((2, 8)),
            dma((2, 4)), dma((2, 4)),
            dma((4,)), dma((4,)),
            dma((2, 4)), dma((2, 4)),
            dma((2, 4)), dma((2, 4)),
            dma((2, 28)), dma((2, 21)),
            dma((3, 8)), dma((3, 8)),
        ],
        compiler_params=pltpu.CompilerParams(
            collective_id=0, has_side_effects=True, vmem_limit_bytes=60 * 1024 * 1024),
        cost_estimate=pl.CostEstimate(flops=8_000_000_000, bytes_accessed=24_000_000,
                                      transcendentals=300_000),
    )(
        emb, lengths, tgt, attn_gain, final_gain.reshape(1, D), jnp.asarray(cos), jnp.asarray(sin),
        w_query.reshape(32, 2, 128, 512), w_key.reshape(32, 2, 128, 128),
        w_value.reshape(32, 2, 128, 128), w_out.reshape(512, 2048), head,
    )
    slots = stats[0].reshape(2, NY, NM, 2, 4).transpose(0, 1, 3, 2, 4).reshape(2, 8, 32)
    chosen = lax.dynamic_slice_in_dim(source, d * 2, 2, 0)
    live = jnp.take(lengths, chosen, axis=0)
    picked = jnp.take(slots, chosen, axis=1)
    valid = jnp.arange(32)[None, :] < live[:, None]
    result = jnp.where(valid[None], picked, F32(0.0))
    return (result[0], result[1])


def solution(mesh):
    return jax.shard_map(
        per_device,
        mesh=mesh,
        in_specs=(
            P("dp", "mp", None),
            P(),
            P(),
            P(),
            P("section", None),
            P("section", None, "mp"),
            P("section", None, "mp"),
            P("section", None, "mp"),
            P("section", "mp", "dp"),
            P(),
            P(("dp", "section", "mp"), None),
        ),
        out_specs=(P("dp", None), P("dp", None)),
        check_vma=False,
    )
```

```python
import jax
import jax.numpy as jnp
import numpy as np
from jax import lax
from jax.experimental import pallas as pl
from jax.experimental.pallas import tpu as pltpu
from jax.sharding import PartitionSpec as P

HD = 128
EPS = 1e-05
ROPE_BASE = 500000.0
NY = 4
NX = 4
NZ = 4
NM = 8
ROWS = 64
D = 8192
QW = 512
MESH = pl.DeviceIdType.MESH
BF = jnp.bfloat16
F32 = jnp.float32


def lane(start, size):
    return pl.ds(pl.multiple_of(start, 128), size)


def kernel(
    emb, live, source_of, targets, gain, fgain, cosine, sine, wq, wk, wv, wo, head,
    exit_out, final_out,
    W, WO, HEAD, EB, X, XN, SS, QA, R, C, PS, PR, PO, ZS, ZR, HP, Y, LT, STO, SA, SB, SC,
    w_sem, eb_s, eb_r, hop_s, hop_r, ag_s, ag_r, res_s, res_r, ctx_s, ctx_r, ps_s, ps_r,
    zz_s, zz_r, y_s, y_r, st_s, st_r,
):
    d = lax.axis_index("dp")
    s = lax.axis_index("section")
    m = lax.axis_index("mp")
    z = m // 2
    c = m % 2
    sib = z * 2 + (1 - c)

    def ypeer(k):
        return (d + k) % NY

    def zpeer(k):
        return ((z + k) % NZ) * 2 + c

    def zother(k):
        return ((z + k) % NZ) * 2 + (1 - c)

    def rcopy(src, dst, ssem, rsem, dev):
        return pltpu.make_async_remote_copy(
            src_ref=src, dst_ref=dst, send_sem=ssem, recv_sem=rsem,
            device_id=dev, device_id_type=MESH,
        )

    here = (d, s, sib)

    loads = []
    for h in range(2):
        loads.append([
            pltpu.make_async_copy(wq.at[:, h], W.at[h, :, :, 0:512], w_sem.at[3 * h]),
            pltpu.make_async_copy(wk.at[:, h], W.at[h, :, :, 512:640], w_sem.at[3 * h + 1]),
            pltpu.make_async_copy(wv.at[:, h], W.at[h, :, :, 640:768], w_sem.at[3 * h + 2]),
        ])
    wo_loads = []
    for h in range(2):
        for mm in range(NM):
            wo_loads.append(pltpu.make_async_copy(
                wo.at[:, mm * 256 + h * 128: mm * 256 + h * 128 + 128],
                WO.at[h, :, mm * 128: mm * 128 + 128], w_sem.at[6 + h * NM + mm]))
    for group in loads:
        for copy in group:
            copy.start()
    for copy in wo_loads:
        copy.start()

    barrier = pltpu.get_barrier_semaphore()
    partners = []
    for k in range(1, 4):
        partners.append((ypeer(k), s, m))
        partners.append((d, (s + k) % NX, m))
        partners.append((d, s, zpeer(k)))
        partners.append((d, s, zother(k)))
        partners.append((ypeer(k), (s + 1) % NX, m))
        partners.append((ypeer(k), (s + 3) % NX, m))
    partners.append(here)
    for dev in partners:
        pl.semaphore_signal(barrier, inc=1, device_id=dev, device_id_type=MESH)
    offsets = (0, 3, 1, 2)
    for cc in range(2):
        for j in range(4):
            for i in range(4):
                g, zz = (offsets[i], offsets[j]) if cc == 0 else (offsets[j], offsets[i])
                col = ypeer(g) * 2048 + ((z + zz) % NZ) * 512 + cc * 256
                pltpu.make_async_copy(head.at[:, lane(col, 256)],
                                      HEAD.at[cc, j, :, i * 256:i * 256 + 256],
                                      w_sem.at[22]).start()
    head_load = pltpu.make_async_copy(HEAD, HEAD, w_sem.at[22])
    pl.semaphore_wait(barrier, len(partners))

    def eb_z(k):
        return rcopy(EB.at[m], EB.at[m], eb_s.at[k], eb_r.at[m], (d, s, zpeer(k)))

    def eb_z_in(k):
        mk = zpeer(k)
        return rcopy(EB.at[mk], EB.at[mk], eb_s.at[k], eb_r.at[mk], (d, s, zpeer(k)))

    def eb_fwd(k):
        mk = zpeer(k)
        return rcopy(EB.at[mk], EB.at[mk], eb_s.at[4 + k], eb_r.at[mk], here)

    def eb_sib_in(k):
        mk = zother(k)
        return rcopy(EB.at[mk], EB.at[mk], eb_s.at[4 + k], eb_r.at[mk], here)

    def hop(h, g):
        return rcopy(HP.at[h, g], X.at[h, m, d], hop_s.at[h, g], hop_r.at[h, d],
                     (g, (s + 1) % NX, m))

    def hop_in(h, g):
        return rcopy(HP.at[h, g], X.at[h, m, g], hop_s.at[h, g], hop_r.at[h, g],
                     (g, (s + 1) % NX, m))

    def ag_z(h, k):
        return rcopy(X.at[h, m], X.at[h, m], ag_s.at[h, k], ag_r.at[h, m], (d, s, zpeer(k)))

    def ag_z_in(h, k):
        mk = zpeer(k)
        return rcopy(X.at[h, mk], X.at[h, mk], ag_s.at[h, k], ag_r.at[h, mk], (d, s, zpeer(k)))

    def ag_fwd(h, k):
        mk = zpeer(k)
        return rcopy(X.at[h, mk], X.at[h, mk], ag_s.at[h, 4 + k], ag_r.at[h, mk], here)

    def ag_sib_in(h, k):
        mk = zother(k)
        return rcopy(X.at[h, mk], X.at[h, mk], ag_s.at[h, 4 + k], ag_r.at[h, mk], here)

    def res(h, k):
        g = ypeer(k)
        return rcopy(X.at[h, m, g], R.at[h, d], res_s.at[h, k], res_r.at[h, d], (g, s, m))

    def res_in(h, k):
        g = ypeer(k)
        return rcopy(X.at[h, m, g], R.at[h, g], res_s.at[h, k], res_r.at[h, g], (g, s, m))

    def ctx(k):
        return rcopy(C.at[d], C.at[d], ctx_s.at[k], ctx_r.at[d], (ypeer(k), s, m))

    def ctx_in(k):
        g = ypeer(k)
        return rcopy(C.at[g], C.at[g], ctx_s.at[k], ctx_r.at[g], (g, s, m))

    def part(h, zz):
        return rcopy(PS.at[h, zz], PR.at[h, zz], ps_s.at[h, zz], ps_r.at[h, zz], here)

    def zred(h, k):
        return rcopy(ZS.at[h, k], ZR.at[h, k], zz_s.at[h, k], zz_r.at[h, k], (d, s, zpeer(k)))

    def norm_block(h, g, mm, x):
        col = g * 2048 + mm * 256 + h * 128
        scaled = (x * gain[:, lane(col, 128)]).astype(BF)
        XN.at[h, g][:, lane(mm * 128, 128)] = scaled

    def layer():
        SS[...] = jnp.zeros_like(SS)

        @pl.when(s == 0)
        def _():
            rows = jnp.concatenate([emb[0], emb[1]], axis=0).astype(F32)
            EB.at[m][...] = jnp.concatenate([rows[:, :4096], rows[:, 4096:]], axis=0).astype(BF)
            for k in (2, 1, 3, 0):
                (eb_z(k) if k else eb_fwd(0)).start()
            for k in (1, 3, 2):
                eb_z_in(k).wait_recv()
                eb_fwd(k).start()
            for k in range(4):
                eb_sib_in(k).wait_recv()

            def body(i, _):
                dl = i // 16
                mm = (i // 2) % 8
                h = i % 2
                x = EB[:, :, lane(dl * 2048 + mm * 256 + h * 128, 128)]
                xf = x.astype(F32)
                for half in range(2):
                    xs = xf[:, half * 8: half * 8 + 8, :].reshape(ROWS, 128)
                    g = half * 2 + dl
                    norm_block(h, g, mm, xs)
                    X.at[h, mm, g][...] = xs.astype(BF)
                    SS[...] += xs * xs
                return 0

            lax.fori_loop(0, 32, body, 0)
            for h in range(2):
                for k in (2, 1, 3):
                    res(h, k).start()

        @pl.when(s > 0)
        def _():
            for h in range(2):
                for g in range(NY):
                    hop_in(h, g).wait_recv()
                for k in (2, 1, 3, 0):
                    (ag_z(h, k) if k else ag_fwd(h, 0)).start()
            for h in range(2):
                for k in (2, 1, 3):
                    res(h, k).start()
            for h in range(2):
                for k in (1, 3, 2):
                    ag_z_in(h, k).wait_recv()
                    ag_fwd(h, k).start()

        QA[...] = jnp.zeros_like(QA)
        for h in range(2):
            @pl.when(s > 0)
            def _():
                for k in range(4):
                    ag_sib_in(h, k).wait_recv()

                def body(mm, _):
                    for g in range(NY):
                        xf = X[h, mm, g].astype(F32)
                        norm_block(h, g, mm, xf)
                        SS[...] += xf * xf
                    return 0

                lax.fori_loop(0, NM, body, 0)

            for copy in loads[h]:
                copy.wait()

            def dots(g, _):
                w = W[h, pl.ds(g * 8, 8)].reshape(1024, 768)
                QA[...] += jnp.dot(XN[h, g], w, preferred_element_type=F32)
                return 0

            lax.fori_loop(0, NY, dots, 0)

        r = lax.rsqrt(jnp.sum(SS[...], axis=1, keepdims=True) * (1.0 / D) + EPS)
        cos = cosine[...]
        sin = sine[...]

        def rope(x):
            return (x * cos + pltpu.roll(x, 64, 1) * sin).astype(BF)

        query = jnp.concatenate(
            [rope(QA[:, j * HD:(j + 1) * HD] * r) for j in range(4)], axis=0)
        key = rope(QA[:, 512:640] * r)
        value = (QA[:, 640:768] * r).astype(BF)
        scores = lax.dot_general(query, key, (((1,), (1,)), ((), ())),
                                 preferred_element_type=F32) * (HD ** -0.5)
        shape = (4 * ROWS, ROWS)
        rq = lax.broadcasted_iota(jnp.int32, shape, 0) % ROWS
        rk = lax.broadcasted_iota(jnp.int32, shape, 1)
        slot_q, slot_k = (rq // 4) % 2, (rk // 4) % 2
        pos_q, pos_k = (rq // 8) * 4 + rq % 4, (rk // 8) * 4 + rk % 4
        live_k = jnp.where(slot_k == 0, live[2 * d], live[2 * d + 1])
        allowed = (slot_q == slot_k) & (pos_k <= pos_q) & (pos_k < live_k)
        scores = jnp.where(allowed, scores, F32(-1e30))
        highest = jnp.max(scores, axis=-1, keepdims=True)
        weights = jnp.exp(scores - highest)
        probs = (weights / jnp.sum(weights, axis=-1, keepdims=True)).astype(BF)
        mixed = jnp.dot(probs, value, preferred_element_type=F32).astype(BF)
        for j in range(4):
            C.at[d][:, j * HD:(j + 1) * HD] = mixed[j * ROWS:(j + 1) * ROWS]
        for k in (2, 1, 3):
            ctx(k).start()

        for h in range(2):
            R.at[h, d][...] = X[h, m, d]
        for copy in wo_loads:
            copy.wait()
        for k in (1, 3, 2):
            ctx_in(k).wait_recv()

        context = C[...].reshape(NY * ROWS, QW)
        for h in range(2):
            def project(i, _):
                zz = (z + jnp.where(i == 0, 2, jnp.where(i == 1, 1, jnp.where(i == 2, 3, 0)))) % NZ
                p = jnp.dot(context, WO[h, :, lane(zz * 256, 256)], preferred_element_type=F32)
                low, high = p[:, :128], p[:, 128:]
                PO.at[h, zz][...] = jnp.where(c == 0, low, high)
                PS.at[h, zz][...] = jnp.where(c == 0, high, low).astype(BF)
                part(h, zz).start()
                return 0

            lax.fori_loop(0, NZ, project, 0)

        def pair(h, k):
            zt = (z + k) % NZ
            part(h, zt).wait_recv()
            return PO[h, zt] + PR[h, zt].astype(F32)

        for h in range(2):
            for k in (2, 1, 3):
                ZS.at[h, k][...] = pair(h, k).astype(BF)
                zred(h, k).start()
        for h in range(2):
            total = pair(h, 0)
            for k in (1, 3, 2):
                res_in(h, k).wait_recv()
            total = total + R[h].astype(F32).reshape(NY * ROWS, 128)
            for k in (1, 3, 2):
                zred(h, k).wait_recv()
                total = total + ZR[h, k].astype(F32)
            HP.at[h][...] = total.astype(BF).reshape(NY, ROWS, 128)

            @pl.when(s < NX - 1)
            def _():
                for k in (2, 1, 3, 0):
                    hop(h, ypeer(k)).start()

        @pl.when(s % 2 == 1)
        def _():
            emit(s // 2)

    def emit(b):
        nt = (((1,), (1,)), ((), ()))
        ones = jnp.ones((16, 128), BF)
        sums = jnp.zeros((16, NY * ROWS), F32)
        mine = Y.at[b, c, 0, 0]
        for h in range(2):
            wide = HP[h].astype(F32).reshape(NY * ROWS, 128)
            square = wide * wide
            top = square.astype(BF)
            rest = (square - top.astype(F32)).astype(BF)
            sums = sums + lax.dot_general(ones, top, nt, preferred_element_type=F32)
            sums = sums + lax.dot_general(ones, rest, nt, preferred_element_type=F32)
            cols = lane(d * 2048 + m * 256 + h * 128, 128)
            mine[0:256, h * 128:h * 128 + 128] = (wide * fgain[:, cols]).astype(BF)
        top = sums.astype(BF).astype(F32)
        row = lax.broadcasted_iota(jnp.int32, (16, NY * ROWS), 0)
        packed = jnp.where(row == 0, top, jnp.where(row == 1, sums - top, 0.0))
        mine[256:272, :] = packed.astype(BF)
        y_x(b, 1).start()
        y_x(b, 3).start()
        spread_own(b)

    def first_dev(k):
        return (jnp.where(c == 0, ypeer(k), d), s, jnp.where(c == 0, m, zpeer(k)))

    def second_dev(k):
        return (jnp.where(c == 0, d, ypeer(k)), s, jnp.where(c == 0, zpeer(k), m))

    def ycopy(src, dst, b, i, j, dev):
        return rcopy(src, dst, y_s.at[b, i], y_r.at[b, j], dev)

    def y_x(b, k):
        ref = Y.at[b, c, 0, 0]
        return ycopy(ref, ref, b, k, 0, (d, (s + k) % NX, m))

    cut = (pl.ds(0, 144), pl.ds(144, 128))

    def y_x_relay(b, half):
        ref = Y.at[b, c, 0, 0, cut[half]]
        return ycopy(ref, ref, b, 4 + half, 0, (d, jnp.where(b == 0, 3, 1), m))

    def relays_x(b, half):
        return (s == 0) if half == 0 else (s == jnp.where(b == 0, 0, 2))

    def y_first(b, k):
        slot = 1 if k == 1 else 2
        return ycopy(Y.at[b, c, 0, 0], Y.at[b, c, 0, slot], b, 5 + k, slot, first_dev(k))

    def y_first_relay(b, half):
        slot, k = ((1, 1), (2, 3))[half]
        return ycopy(Y.at[b, c, 0, slot, cut[half]], Y.at[b, c, 0, 3, cut[half]],
                     b, 9 + half, 3, first_dev(k))

    def y_opposite(b):
        ref = Y.at[b, c, 0, 3]
        return ycopy(ref, ref, b, 9, 3, here)

    sets = (pl.ds(0, 1), pl.ds(1, 2), pl.ds(3, 1))

    def y_second(b, part_no, k):
        slot = 1 if k == 1 else 2
        return ycopy(Y.at[b, c, 0, sets[part_no]], Y.at[b, c, slot, sets[part_no]],
                     b, 11 + part_no * 2 + (slot - 1), 1 + 3 * slot + part_no, second_dev(k))

    def y_second_relay(b, i):
        slot, k = (1, 1) if i < 2 else (2, 3)
        return ycopy(Y.at[b, c, slot, i], Y.at[b, c, 3, i], b, 17 + i, 10 + i, second_dev(k))

    forwards = ((0, 0, 1), (0, 1, 2), (0, 3, 1), (1, 0, 4), (2, 0, 4), (3, 0, 2), (3, 2, 2))

    def y_fwd(b, n, who):
        j, i, size = forwards[n]
        ref = Y.at[b, who, j, pl.ds(i, size)]
        return ycopy(ref, ref, b, 21 + n, 14 + n, here)

    def spread_own(b):
        for k in (1, 3):
            y_first(b, k).start()
        for k in (1, 3):
            y_second(b, 0, k).start()
        y_fwd(b, 0, c).start()

    def dots(b, cc, j, start):
        pieces = jnp.concatenate([Y[b, cc, j, i, 0:256, :] for i in range(4)], axis=1)
        term = lax.dot_general(HEAD[cc, j], pieces, (((1,), (1,)), ((), ())),
                               preferred_element_type=F32)
        LT[...] = term if start else LT[...] + term

    def row_slot(lanes):
        return (lanes // 64) * 2 + (lanes // 4) % 2, ((lanes // 8) % 8) * 4 + lanes % 4

    def wanted_rows():
        slot, position = row_slot(lax.broadcasted_iota(jnp.int32, (32, 256), 1))
        place = (position == lax.broadcasted_iota(jnp.int32, (32, 256), 0)).astype(BF)
        tokens = targets[...]
        top = jnp.dot((tokens // 256).astype(F32).astype(BF), place, preferred_element_type=F32)
        low = jnp.dot((tokens % 256).astype(F32).astype(BF), place, preferred_element_type=F32)
        every = top * 256.0 + low
        keep = slot[0:8] == lax.broadcasted_iota(jnp.int32, (8, 256), 0)
        return jnp.sum(jnp.where(keep, every, 0.0), axis=0, keepdims=True)

    def score(b):
        source = 2 * b + 1

        @pl.when(s != source)
        def _():
            y_x(b, 1).wait_recv()
            for half in range(2):
                @pl.when(relays_x(b, half))
                def _():
                    y_x_relay(b, half).start()
            spread_own(b)

        y_first(b, 1).wait_recv()
        y_first_relay(b, 0).start()
        y_first(b, 3).wait_recv()
        y_first_relay(b, 1).start()
        for k in (1, 3):
            y_second(b, 1, k).start()
        y_fwd(b, 1, c).start()
        y_second(b, 0, 1).wait_recv()
        y_second_relay(b, 0).start()
        y_second(b, 0, 3).wait_recv()
        y_opposite(b).wait_recv()
        for k in (1, 3):
            y_second(b, 2, k).start()
        y_fwd(b, 2, c).start()
        y_second(b, 1, 1).wait_recv()
        y_second_relay(b, 1).start()
        y_second(b, 1, 3).wait_recv()
        y_second_relay(b, 2).start()
        y_second(b, 2, 3).wait_recv()
        y_second_relay(b, 3).start()
        y_fwd(b, 4, c).start()
        y_second(b, 2, 1).wait_recv()
        y_fwd(b, 3, c).start()

        dots(b, c, 0, True)
        for n in range(3):
            y_fwd(b, n, 1 - c).wait_recv()
        dots(b, 1 - c, 0, False)
        dots(b, c, 2, False)
        dots(b, c, 1, False)
        y_second_relay(b, 0).wait_recv()
        y_second_relay(b, 1).wait_recv()
        y_fwd(b, 5, c).start()
        y_fwd(b, 4, 1 - c).wait_recv()
        dots(b, 1 - c, 2, False)
        y_second_relay(b, 2).wait_recv()
        y_second_relay(b, 3).wait_recv()
        y_fwd(b, 6, c).start()
        y_fwd(b, 3, 1 - c).wait_recv()
        dots(b, 1 - c, 1, False)
        dots(b, c, 3, False)
        y_fwd(b, 5, 1 - c).wait_recv()
        y_fwd(b, 6, 1 - c).wait_recv()
        dots(b, 1 - c, 3, False)

        extra = jnp.zeros((16, 256), F32)
        for cc in range(2):
            for j in range(4):
                for i in range(4):
                    extra = extra + Y[b, cc, j, i, 256:272, :].astype(F32)
        sums = jnp.sum(extra, axis=0, keepdims=True)
        r = lax.rsqrt(sums * (1.0 / D) + EPS)
        logits = LT[...] * r
        highest = jnp.max(logits, axis=0, keepdims=True)
        summed = jnp.sum(jnp.exp(logits - highest), axis=0, keepdims=True)
        vocab = HEAD.shape[2]
        first = ((d * NX + s) * NM + m) * vocab
        index = (lax.broadcasted_iota(jnp.int32, logits.shape, 0) + first).astype(F32)
        wanted = wanted_rows()
        picked = jnp.sum(jnp.where(index == wanted, logits, 0.0), axis=0, keepdims=True)
        lanes = pl.ds(pl.multiple_of(b * 256, 256), 256)
        rows = lax.broadcasted_iota(jnp.int32, (8, 256), 0)
        STO[:, lanes] = jnp.where(rows == 0, highest,
                                  jnp.where(rows == 1, summed,
                                            jnp.where(rows == 2, picked, 0.0)))

    def step(t, _):
        place = jnp.where(s == NX - 1, 1, 0)

        @pl.when(t == place)
        def _():
            layer()

        @pl.when(t != place)
        def _():
            @pl.when((t == 0) | ((t == 1) & (s != NX - 1)))
            def _():
                head_load.wait()
            score(jnp.where(t == 2, 1, 0))
        return 0

    lax.fori_loop(0, 3, step, 0)

    def merge(ref, count):
        parts = [ref[j] for j in range(count)]
        highest = parts[0][0:1]
        for p in parts[1:]:
            highest = jnp.maximum(highest, p[0:1])
        summed = jnp.zeros_like(highest)
        picked = jnp.zeros_like(highest)
        for p in parts:
            summed = summed + p[1:2] * jnp.exp(p[0:1] - highest)
            picked = picked + p[2:3]
        return highest, summed, picked

    def stacked(highest, summed, picked):
        rows = lax.broadcasted_iota(jnp.int32, (8, 512), 0)
        return jnp.where(rows == 0, highest,
                         jnp.where(rows == 1, summed, jnp.where(rows == 2, picked, 0.0)))

    def st_y(k):
        return rcopy(SA.at[d], SA.at[d], st_s.at[0, k], st_r.at[0, d], (ypeer(k), s, m))

    def st_y_in(k):
        g = ypeer(k)
        return rcopy(SA.at[g], SA.at[g], st_s.at[0, k], st_r.at[0, g], (g, s, m))

    def m_of(k):
        return (m + k) % NM

    def st_m(k):
        return rcopy(SB.at[m], SB.at[m], st_s.at[1, k], st_r.at[1, m], (d, s, m_of(k)))

    def st_m_in(k):
        mm = m_of(k)
        return rcopy(SB.at[mm], SB.at[mm], st_s.at[1, k], st_r.at[1, mm], (d, s, mm))

    def st_x(k):
        return rcopy(SC.at[s], SC.at[s], st_s.at[2, k], st_r.at[2, s], (d, (s + k) % NX, m))

    def st_x_in(k):
        ss = (s + k) % NX
        return rcopy(SC.at[ss], SC.at[ss], st_s.at[2, k], st_r.at[2, ss], (d, ss, m))

    SA.at[d][...] = STO[...]
    for k in (2, 1, 3):
        st_y(k).start()
    for k in (1, 3, 2):
        st_y_in(k).wait_recv()
    SB.at[m][...] = stacked(*merge(SA, NY))
    for k in (4, 3, 5, 2, 6, 1, 7):
        st_m(k).start()
    for k in (1, 7, 2, 6, 3, 5, 4):
        st_m_in(k).wait_recv()
    SC.at[s][...] = stacked(*merge(SB, NM))
    for k in (2, 1, 3):
        st_x(k).start()
    for k in (1, 3, 2):
        st_x_in(k).wait_recv()
    highest, summed, picked = merge(SC, NX)
    logprob = picked - (highest + jnp.log(summed))
    terms = []
    for e in range(2):
        rest = logprob[:, e * 256:e * 256 + 256]
        for _ in range(3):
            term = rest.astype(BF).astype(F32)
            terms.append(term)
            rest = rest - term
    row = lax.broadcasted_iota(jnp.int32, (16, 256), 0)
    stack = jnp.zeros((16, 256), F32)
    for j, term in enumerate(terms):
        stack = jnp.where(row == j, term, stack)
    stack = stack.astype(BF)
    slot, position = row_slot(lax.broadcasted_iota(jnp.int32, (256, 32), 0))
    place = lax.broadcasted_iota(jnp.int32, (256, 32), 1)
    results = []
    for i in range(2):
        chosen = source_of[2 * d + i]
        take = ((slot == chosen) & (position == place)).astype(BF)
        got = jnp.dot(stack, take, preferred_element_type=F32)
        alive = lax.broadcasted_iota(jnp.int32, (1, 32), 1) < live[chosen]
        results.append([jnp.where(alive, got[j:j + 1] + got[j + 1:j + 2] + got[j + 2:j + 3], 0.0)
                        for j in (0, 3)])
    for e, ref in enumerate((exit_out, final_out)):
        first = lax.broadcasted_iota(jnp.int32, (2, 32), 0) == 0
        ref[...] = jnp.where(first, results[0][e], results[1][e])

    @pl.when(s == 0)
    def _():
        for k in range(4):
            (eb_z(k) if k else eb_fwd(0)).wait_send()
        for k in range(1, 4):
            eb_fwd(k).wait_send()

    @pl.when(s > 0)
    def _():
        for h in range(2):
            for k in range(1, 4):
                ag_z(h, k).wait_send()
            for k in range(4):
                ag_fwd(h, k).wait_send()

    @pl.when(s < NX - 1)
    def _():
        for h in range(2):
            for k in range(4):
                hop(h, ypeer(k)).wait_send()

    for h in range(2):
        for k in range(1, 4):
            res(h, k).wait_send()
            zred(h, k).wait_send()
        for zz in range(NZ):
            part(h, zz).wait_send()
    for k in range(1, 4):
        ctx(k).wait_send()
        st_y(k).wait_send()
        st_x(k).wait_send()
    for k in range(1, 8):
        st_m(k).wait_send()
    for b in range(2):
        @pl.when(s == 2 * b + 1)
        def _():
            for k in (1, 3):
                y_x(b, k).wait_send()

        for half in range(2):
            @pl.when((s != 2 * b + 1) & relays_x(b, half))
            def _():
                y_x_relay(b, half).wait_send()

            y_first_relay(b, half).wait_send()
        for k in (1, 3):
            y_first(b, k).wait_send()
            for n in range(3):
                y_second(b, n, k).wait_send()
        for i in range(4):
            y_second_relay(b, i).wait_send()
        for n in range(7):
            y_fwd(b, n, c).wait_send()


def tables():
    row = np.arange(ROWS)
    position = (row // 8) * 4 + row % 4
    half = HD // 2
    freqs = (ROPE_BASE ** (-np.arange(half) * 2.0 / HD)).astype(np.float32)
    angles = (position.astype(np.float32)[:, None] * freqs[None, :]).astype(np.float64)
    cos, sin = np.cos(angles), np.sin(angles)
    return (np.concatenate([cos, cos], 1).astype(np.float32),
            np.concatenate([-sin, sin], 1).astype(np.float32))


def per_device(
    embeds, targets, lengths, source, attn_gain, w_query, w_key, w_value, w_out, final_gain, head
):
    vocab = head.shape[0]
    cos, sin = tables()
    vmem = pl.BlockSpec(memory_space=pltpu.VMEM)
    hbm = pl.BlockSpec(memory_space=pl.ANY)
    smem = pl.BlockSpec(memory_space=pltpu.SMEM)
    dma = pltpu.SemaphoreType.DMA
    return pl.pallas_call(
        kernel,
        out_shape=[jax.ShapeDtypeStruct((2, 32), F32)] * 2,
        in_specs=[vmem, smem, smem, vmem, vmem, vmem, vmem, vmem, hbm, hbm, hbm, hbm, hbm],
        out_specs=[vmem, vmem],
        scratch_shapes=[
            pltpu.VMEM((2, 32, 128, 768), BF),
            pltpu.VMEM((2, QW, 1024), BF),
            pltpu.VMEM((2, 4, vocab, 1024), BF),
            pltpu.VMEM((NM, 16, 4096), BF),
            pltpu.VMEM((2, NM, NY, ROWS, 128), BF),
            pltpu.VMEM((2, NY, ROWS, 1024), BF),
            pltpu.VMEM((ROWS, 128), F32),
            pltpu.VMEM((ROWS, 768), F32),
            pltpu.VMEM((2, NY, ROWS, 128), BF),
            pltpu.VMEM((NY, ROWS, QW), BF),
            pltpu.VMEM((2, NZ, NY * ROWS, 128), BF),
            pltpu.VMEM((2, NZ, NY * ROWS, 128), BF),
            pltpu.VMEM((2, NZ, NY * ROWS, 128), F32),
            pltpu.VMEM((2, NZ, NY * ROWS, 128), BF),
            pltpu.VMEM((2, NZ, NY * ROWS, 128), BF),
            pltpu.VMEM((2, NY, ROWS, 128), BF),
            pltpu.VMEM((2, 2, 4, 4, 272, 256), BF),
            pltpu.VMEM((vocab, 256), F32),
            pltpu.VMEM((8, 512), F32),
            pltpu.VMEM((NY, 8, 512), F32),
            pltpu.VMEM((NM, 8, 512), F32),
            pltpu.VMEM((NX, 8, 512), F32),
            dma((23,)),
            dma((8,)), dma((8,)),
            dma((2, 4)), dma((2, 4)),
            dma((2, 8)), dma((2, 8)),
            dma((2, 4)), dma((2, 4)),
            dma((4,)), dma((4,)),
            dma((2, 4)), dma((2, 4)),
            dma((2, 4)), dma((2, 4)),
            dma((2, 28)), dma((2, 21)),
            dma((3, 8)), dma((3, 8)),
        ],
        compiler_params=pltpu.CompilerParams(
            collective_id=0, has_side_effects=True, vmem_limit_bytes=60 * 1024 * 1024),
        cost_estimate=pl.CostEstimate(flops=8_000_000_000, bytes_accessed=24_000_000,
                                      transcendentals=300_000),
    )(
        embeds, lengths, source, targets, attn_gain, final_gain.reshape(1, D), jnp.asarray(cos), jnp.asarray(sin),
        w_query.reshape(32, 2, 128, 512), w_key.reshape(32, 2, 128, 128),
        w_value.reshape(32, 2, 128, 128), w_out.reshape(512, 2048), head,
    )


def solution(mesh):
    return jax.shard_map(
        per_device,
        mesh=mesh,
        in_specs=(
            P("dp", "mp", None),
            P(),
            P(),
            P(),
            P("section", None),
            P("section", None, "mp"),
            P("section", None, "mp"),
            P("section", None, "mp"),
            P("section", "mp", "dp"),
            P(),
            P(("dp", "section", "mp"), None),
        ),
        out_specs=(P("dp", None), P("dp", None)),
        check_vma=False,
    )
```

```python
import jax
import jax.numpy as jnp
import numpy as np
from jax import lax
from jax.experimental import pallas as pl
from jax.experimental.pallas import tpu as pltpu
from jax.sharding import PartitionSpec as P

HD = 128
EPS = 1e-05
ROPE_BASE = 500000.0
NY = 4
NX = 4
NZ = 4
NM = 8
ROWS = 64
D = 8192
QW = 512
MESH = pl.DeviceIdType.MESH
BF = jnp.bfloat16
F32 = jnp.float32


def lane(start, size):
    return pl.ds(pl.multiple_of(start, 128), size)


def kernel(
    emb, live, source_of, targets, gain, fgain, cosine, sine, wq, wk, wv, wo, head,
    exit_out, final_out,
    W, WO, HEAD, EB, X, G, NG, RX, MASK, SS, QA, R, C, PS, PR, PO, ZS, ZR, HP, SUMS, Y, LT, STO, SA, SB, SC,
    w_sem, ng_s, ng_r, eb_s, eb_r, hop_s, hop_r, ag_s, ag_r, res_s, res_r, ctx_s, ctx_r, ps_s, ps_r,
    zz_s, zz_r, y_s, y_r, st_s, st_r,
):
    d = lax.axis_index("dp")
    s = lax.axis_index("section")
    m = lax.axis_index("mp")
    z = m // 2
    c = m % 2
    sib = z * 2 + (1 - c)

    def ypeer(k):
        return (d + k) % NY

    def zpeer(k):
        return ((z + k) % NZ) * 2 + c

    def zother(k):
        return ((z + k) % NZ) * 2 + (1 - c)

    def rcopy(src, dst, ssem, rsem, dev):
        return pltpu.make_async_remote_copy(
            src_ref=src, dst_ref=dst, send_sem=ssem, recv_sem=rsem,
            device_id=dev, device_id_type=MESH,
        )

    here = (d, s, sib)

    loads = []
    for h in range(2):
        loads.append([
            pltpu.make_async_copy(wq.at[:, h], W.at[h, :, :, 0:512], w_sem.at[3 * h]),
            pltpu.make_async_copy(wk.at[:, h], W.at[h, :, :, 512:640], w_sem.at[3 * h + 1]),
            pltpu.make_async_copy(wv.at[:, h], W.at[h, :, :, 640:768], w_sem.at[3 * h + 2]),
        ])
    wo_loads = []
    for h in range(2):
        for mm in range(NM):
            wo_loads.append(pltpu.make_async_copy(
                wo.at[:, mm * 256 + h * 128: mm * 256 + h * 128 + 128],
                WO.at[h, :, mm * 128: mm * 128 + 128], w_sem.at[6 + h * NM + mm]))
    for group in loads:
        for copy in group:
            copy.start()
    for copy in wo_loads:
        copy.start()

    barrier = pltpu.get_barrier_semaphore()
    partners = []
    for k in range(1, 4):
        partners.append((ypeer(k), s, m))
        partners.append((d, (s + k) % NX, m))
        partners.append((d, s, zpeer(k)))
        partners.append((d, s, zother(k)))
        partners.append((ypeer(k), (s + 1) % NX, m))
        partners.append((ypeer(k), (s + 3) % NX, m))
    partners.append(here)
    for dev in partners:
        pl.semaphore_signal(barrier, inc=1, device_id=dev, device_id_type=MESH)
    offsets = (0, 3, 1, 2)
    for cc in range(2):
        for j in range(4):
            for i in range(4):
                g, zz = (offsets[i], offsets[j]) if cc == 0 else (offsets[j], offsets[i])
                col = ypeer(g) * 2048 + ((z + zz) % NZ) * 512 + cc * 256
                pltpu.make_async_copy(head.at[:, lane(col, 256)],
                                      HEAD.at[cc, j, :, i * 256:i * 256 + 256],
                                      w_sem.at[22]).start()
    head_load = pltpu.make_async_copy(HEAD, HEAD, w_sem.at[22])
    shape = (4 * ROWS, ROWS)
    rq = lax.broadcasted_iota(jnp.int32, shape, 0) % ROWS
    rk = lax.broadcasted_iota(jnp.int32, shape, 1)
    slot_q, slot_k = (rq // 4) % 2, (rk // 4) % 2
    pos_q, pos_k = (rq // 8) * 4 + rq % 4, (rk // 8) * 4 + rk % 4
    live_k = jnp.where(slot_k == 0, live[2 * d], live[2 * d + 1])
    allowed = (slot_q == slot_k) & (pos_k <= pos_q) & (pos_k < live_k)
    MASK[...] = jnp.where(allowed, F32(0.0), F32(-1e30))
    pl.semaphore_wait(barrier, len(partners))

    def next_gain():
        return rcopy(gain.at[:, lane(d * 2048 + m * 256, 256)], NG, ng_s, ng_r,
                     (d, (s + 3) % NX, m))

    @pl.when(s > 0)
    def _():
        next_gain().start()

    def eb_z(k):
        return rcopy(EB.at[m], EB.at[m], eb_s.at[k], eb_r.at[m], (d, s, zpeer(k)))

    def eb_z_in(k):
        mk = zpeer(k)
        return rcopy(EB.at[mk], EB.at[mk], eb_s.at[k], eb_r.at[mk], (d, s, zpeer(k)))

    def eb_fwd(k):
        mk = zpeer(k)
        return rcopy(EB.at[mk], EB.at[mk], eb_s.at[4 + k], eb_r.at[mk], here)

    def eb_sib_in(k):
        mk = zother(k)
        return rcopy(EB.at[mk], EB.at[mk], eb_s.at[4 + k], eb_r.at[mk], here)

    rows_of = (pl.ds(0, ROWS), pl.ds(0, ROWS + 16))

    def hop(h, g):
        return rcopy(G.at[h, g, rows_of[h]], X.at[h, m, d, rows_of[h]], hop_s.at[h, g],
                     hop_r.at[h, d], (g, (s + 1) % NX, m))

    def hop_in(h, g):
        return rcopy(G.at[h, g, rows_of[h]], X.at[h, m, g, rows_of[h]], hop_s.at[h, g],
                     hop_r.at[h, g], (g, (s + 1) % NX, m))

    def hop_raw(h):
        return rcopy(HP.at[h], R.at[h], hop_s.at[h, 4], hop_r.at[h, 4], (d, (s + 1) % NX, m))

    def slab(h, mm):
        return X.at[h, mm, :, rows_of[h]]

    def ag_z(h, k):
        return rcopy(slab(h, m), slab(h, m), ag_s.at[h, k], ag_r.at[h, m], (d, s, zpeer(k)))

    def ag_z_in(h, k):
        mk = zpeer(k)
        return rcopy(slab(h, mk), slab(h, mk), ag_s.at[h, k], ag_r.at[h, mk], (d, s, zpeer(k)))

    def ag_fwd(h, k):
        mk = zpeer(k)
        return rcopy(slab(h, mk), slab(h, mk), ag_s.at[h, 4 + k], ag_r.at[h, mk], here)

    def ag_sib_in(h, k):
        mk = zother(k)
        return rcopy(slab(h, mk), slab(h, mk), ag_s.at[h, 4 + k], ag_r.at[h, mk], here)

    def res(h, k):
        g = ypeer(k)
        return rcopy(RX.at[h, g], R.at[h, d], res_s.at[h, k], res_r.at[h, d], (g, s, m))

    def res_in(h, k):
        g = ypeer(k)
        return rcopy(RX.at[h, g], R.at[h, g], res_s.at[h, k], res_r.at[h, g], (g, s, m))

    def ctx(k):
        return rcopy(C.at[d], C.at[d], ctx_s.at[k], ctx_r.at[d], (ypeer(k), s, m))

    def ctx_in(k):
        g = ypeer(k)
        return rcopy(C.at[g], C.at[g], ctx_s.at[k], ctx_r.at[g], (g, s, m))

    def part(h, zz):
        return rcopy(PS.at[h, zz], PR.at[h, zz], ps_s.at[h, zz], ps_r.at[h, zz], here)

    def zred(h, k):
        return rcopy(ZS.at[h, k], ZR.at[h, k], zz_s.at[h, k], zz_r.at[h, k], (d, s, zpeer(k)))

    def layer():
        @pl.when(s == 0)
        def _():
            rows = jnp.concatenate([emb[0], emb[1]], axis=0).astype(F32)
            EB.at[m][...] = jnp.concatenate([rows[:, :4096], rows[:, 4096:]], axis=0).astype(BF)
            for k in (2, 1, 3, 0):
                (eb_z(k) if k else eb_fwd(0)).start()
            for k in (1, 3, 2):
                eb_z_in(k).wait_recv()
                eb_fwd(k).start()
            for k in range(4):
                eb_sib_in(k).wait_recv()

            def block(dl, mm, h):
                return EB[:, :, lane(dl * 2048 + mm * 256 + h * 128, 128)].astype(F32)

            def body(mm, total):
                for dl in range(2):
                    for h in range(2):
                        xf = block(dl, mm, h)
                        for half in range(2):
                            xs = xf[:, half * 8: half * 8 + 8, :].reshape(ROWS, 128)
                            g = half * 2 + dl
                            cols = lane(g * 2048 + mm * 256 + h * 128, 128)
                            X.at[h, mm, g][0:ROWS, :] = (xs * gain[:, cols]).astype(BF)
                            total = total + xs * xs
                return total

            SS[...] = lax.fori_loop(0, NM, body, jnp.zeros((ROWS, 128), F32))
            for dl in range(2):
                for h in range(2):
                    xf = block(dl, m, h)
                    for half in range(2):
                        xs = xf[:, half * 8: half * 8 + 8, :].reshape(ROWS, 128)
                        RX.at[h, half * 2 + dl][...] = xs.astype(BF)
            for h in range(2):
                for k in (2, 1, 3):
                    res(h, k).start()
                R.at[h, d][...] = RX[h, d]

        @pl.when(s > 0)
        def _():
            for h in range(2):
                for g in range(NY):
                    hop_in(h, g).wait_recv()
                for k in (2, 1, 3, 0):
                    (ag_z(h, k) if k else ag_fwd(h, 0)).start()
            for h in range(2):
                for k in (1, 3, 2):
                    ag_z_in(h, k).wait_recv()
                    ag_fwd(h, k).start()

        def multiply(h, who, start):
            term = None
            for g in range(NY):
                x = jnp.concatenate([X[h, 2 * zz + who, g, 0:ROWS] for zz in range(NZ)], axis=1)
                w = jnp.concatenate([W[h, g * 8 + 2 * zz + who] for zz in range(NZ)], axis=0)
                one = jnp.dot(x, w, preferred_element_type=F32)
                term = one if term is None else term + one
            QA[...] = term if start else QA[...] + term

        for h in range(2):
            for copy in loads[h]:
                copy.wait()
            multiply(h, c, h == 0)

            @pl.when(s > 0)
            def _():
                for k in range(4):
                    ag_sib_in(h, k).wait_recv()

            multiply(h, 1 - c, False)

        @pl.when(s > 0)
        def _():
            total = jnp.zeros((16, 128), F32)
            for mm in range(NM):
                for g in range(NY):
                    total = total + X[1, mm, g, ROWS:ROWS + 16].astype(F32)
            total = total[0:1] + total[1:2]
            mine = (lax.broadcasted_iota(jnp.int32, (ROWS, 128), 1)
                    == lax.broadcasted_iota(jnp.int32, (ROWS, 128), 0) + (d % 2) * ROWS)
            SS[...] = jnp.where(mine, total, 0.0)

        r = lax.rsqrt(jnp.sum(SS[...], axis=1, keepdims=True) * (1.0 / D) + EPS)
        cos = cosine[...]
        sin = sine[...]

        def rope(x):
            return (x * cos + pltpu.roll(x, 64, 1) * sin).astype(BF)

        query = jnp.concatenate(
            [rope(QA[:, j * HD:(j + 1) * HD] * r) for j in range(4)], axis=0)
        key = rope(QA[:, 512:640] * r)
        value = (QA[:, 640:768] * r).astype(BF)
        scores = lax.dot_general(query, key, (((1,), (1,)), ((), ())),
                                 preferred_element_type=F32) * (HD ** -0.5)
        scores = scores + MASK[...]
        highest = jnp.max(scores, axis=-1, keepdims=True)
        weights = jnp.exp(scores - highest)
        probs = (weights / jnp.sum(weights, axis=-1, keepdims=True)).astype(BF)
        mixed = jnp.dot(probs, value, preferred_element_type=F32).astype(BF)
        for j in range(4):
            C.at[d][:, j * HD:(j + 1) * HD] = mixed[j * ROWS:(j + 1) * ROWS]
        for k in (2, 1, 3):
            ctx(k).start()

        for copy in wo_loads:
            copy.wait()
        for k in (1, 3, 2):
            ctx_in(k).wait_recv()

        context = C[...].reshape(NY * ROWS, QW)
        for h in range(2):
            for k in (2, 1, 3, 0):
                zz = (z + k) % NZ
                p = jnp.dot(context, WO[h, :, lane(zz * 256, 256)], preferred_element_type=F32)
                low, high = p[:, :128], p[:, 128:]
                PO.at[h, zz][...] = jnp.where(c == 0, low, high)
                PS.at[h, zz][...] = jnp.where(c == 0, high, low).astype(BF)
                part(h, zz).start()

        def pair(h, k):
            zt = (z + k) % NZ
            part(h, zt).wait_recv()
            return PO[h, zt] + PR[h, zt].astype(F32)

        for h in range(2):
            for k in (2, 1, 3):
                ZS.at[h, k][...] = pair(h, k).astype(BF)
                zred(h, k).start()
        @pl.when(s == 0)
        def _():
            for h in range(2):
                for k in (1, 3, 2):
                    res_in(h, k).wait_recv()

        @pl.when(s > 0)
        def _():
            for h in range(2):
                hop_raw(h).wait_recv()

        @pl.when(s < NX - 1)
        def _():
            next_gain().wait_recv()

        sums = jnp.zeros((16, NY * ROWS), F32)
        for h in range(2):
            total = pair(h, 0)
            total = total + R[h].astype(F32).reshape(NY * ROWS, 128)
            for k in (1, 3, 2):
                zred(h, k).wait_recv()
                total = total + ZR[h, k].astype(F32)
            hidden = total.astype(BF)
            HP.at[h][...] = hidden.reshape(NY, ROWS, 128)
            wide = hidden.astype(F32)
            scaled = (wide * NG[:, h * 128:h * 128 + 128]).astype(BF)
            G.at[h][:, 0:ROWS, :] = scaled.reshape(NY, ROWS, 128)
            square = wide * wide
            top = square.astype(BF)
            rest = (square - top.astype(F32)).astype(BF)
            ones = jnp.ones((16, 128), BF)
            nt = (((1,), (1,)), ((), ()))
            sums = sums + lax.dot_general(ones, top, nt, preferred_element_type=F32)
            sums = sums + lax.dot_general(ones, rest, nt, preferred_element_type=F32)
            if h == 1:
                top = sums.astype(BF).astype(F32)
                row = lax.broadcasted_iota(jnp.int32, (16, NY * ROWS), 0)
                packed = jnp.where(row == 0, top, jnp.where(row == 1, sums - top, 0.0)).astype(BF)
                for g in range(NY):
                    tile = g // 2 * 128
                    G.at[1, g][ROWS:ROWS + 16, :] = packed[:, tile:tile + 128]
                SUMS[...] = packed

            @pl.when(s < NX - 1)
            def _():
                for k in (2, 1, 3, 0):
                    hop(h, ypeer(k)).start()

        @pl.when(s < NX - 1)
        def _():
            for h in range(2):
                hop_raw(h).start()

        @pl.when(s % 2 == 1)
        def _():
            emit(s // 2)

    def emit(b):
        mine = Y.at[b, c, 0, 0]
        for h in range(2):
            wide = HP[h].astype(F32).reshape(NY * ROWS, 128)
            cols = lane(d * 2048 + m * 256 + h * 128, 128)
            mine[0:256, h * 128:h * 128 + 128] = (wide * fgain[:, cols]).astype(BF)
        mine[256:272, :] = SUMS[...]
        y_x(b, 1).start()
        y_x(b, 3).start()
        spread_own(b)

    def first_dev(k):
        return (jnp.where(c == 0, ypeer(k), d), s, jnp.where(c == 0, m, zpeer(k)))

    def second_dev(k):
        return (jnp.where(c == 0, d, ypeer(k)), s, jnp.where(c == 0, zpeer(k), m))

    def ycopy(src, dst, b, i, j, dev):
        return rcopy(src, dst, y_s.at[b, i], y_r.at[b, j], dev)

    def y_x(b, k):
        ref = Y.at[b, c, 0, 0]
        return ycopy(ref, ref, b, k, 0, (d, (s + k) % NX, m))

    cut = (pl.ds(0, 144), pl.ds(144, 128))

    def y_x_relay(b, half):
        ref = Y.at[b, c, 0, 0, cut[half]]
        return ycopy(ref, ref, b, 4 + half, 0, (d, jnp.where(b == 0, 3, 1), m))

    def relays_x(b, half):
        return (s == 0) if half == 0 else (s == jnp.where(b == 0, 0, 2))

    def y_first(b, k):
        slot = 1 if k == 1 else 2
        return ycopy(Y.at[b, c, 0, 0], Y.at[b, c, 0, slot], b, 5 + k, slot, first_dev(k))

    def y_first_relay(b, half):
        slot, k = ((1, 1), (2, 3))[half]
        return ycopy(Y.at[b, c, 0, slot, cut[half]], Y.at[b, c, 0, 3, cut[half]],
                     b, 9 + half, 3, first_dev(k))

    def y_opposite(b):
        ref = Y.at[b, c, 0, 3]
        return ycopy(ref, ref, b, 9, 3, here)

    sets = (pl.ds(0, 1), pl.ds(1, 2), pl.ds(3, 1))

    def y_second(b, part_no, k):
        slot = 1 if k == 1 else 2
        return ycopy(Y.at[b, c, 0, sets[part_no]], Y.at[b, c, slot, sets[part_no]],
                     b, 11 + part_no * 2 + (slot - 1), 1 + 3 * slot + part_no, second_dev(k))

    def y_second_relay(b, i):
        slot, k = (1, 1) if i < 2 else (2, 3)
        return ycopy(Y.at[b, c, slot, i], Y.at[b, c, 3, i], b, 17 + i, 10 + i, second_dev(k))

    forwards = ((0, 0, 1), (0, 1, 2), (0, 3, 1), (1, 0, 4), (2, 0, 4), (3, 0, 2), (3, 2, 2))

    def y_fwd(b, n, who):
        j, i, size = forwards[n]
        ref = Y.at[b, who, j, pl.ds(i, size)]
        return ycopy(ref, ref, b, 21 + n, 14 + n, here)

    def spread_own(b):
        for k in (1, 3):
            y_first(b, k).start()
        for k in (1, 3):
            y_second(b, 0, k).start()
        y_fwd(b, 0, c).start()

    def dots(b, cc, j, start):
        pieces = jnp.concatenate([Y[b, cc, j, i, 0:256, :] for i in range(4)], axis=1)
        term = lax.dot_general(HEAD[cc, j], pieces, (((1,), (1,)), ((), ())),
                               preferred_element_type=F32)
        LT[...] = term if start else LT[...] + term

    def row_slot(lanes):
        return (lanes // 64) * 2 + (lanes // 4) % 2, ((lanes // 8) % 8) * 4 + lanes % 4

    def wanted_rows():
        slot, position = row_slot(lax.broadcasted_iota(jnp.int32, (32, 256), 1))
        place = (position == lax.broadcasted_iota(jnp.int32, (32, 256), 0)).astype(BF)
        tokens = targets[...]
        top = jnp.dot((tokens // 256).astype(F32).astype(BF), place, preferred_element_type=F32)
        low = jnp.dot((tokens % 256).astype(F32).astype(BF), place, preferred_element_type=F32)
        every = top * 256.0 + low
        keep = slot[0:8] == lax.broadcasted_iota(jnp.int32, (8, 256), 0)
        return jnp.sum(jnp.where(keep, every, 0.0), axis=0, keepdims=True)

    def score(b):
        source = 2 * b + 1

        @pl.when(s != source)
        def _():
            y_x(b, 1).wait_recv()
            for half in range(2):
                @pl.when(relays_x(b, half))
                def _():
                    y_x_relay(b, half).start()
            spread_own(b)

        y_first(b, 1).wait_recv()
        y_first_relay(b, 0).start()
        y_first(b, 3).wait_recv()
        y_first_relay(b, 1).start()
        for k in (1, 3):
            y_second(b, 1, k).start()
        y_fwd(b, 1, c).start()
        y_second(b, 0, 1).wait_recv()
        y_second_relay(b, 0).start()
        y_second(b, 0, 3).wait_recv()
        y_opposite(b).wait_recv()
        for k in (1, 3):
            y_second(b, 2, k).start()
        y_fwd(b, 2, c).start()
        y_second(b, 1, 1).wait_recv()
        y_second_relay(b, 1).start()
        y_second(b, 1, 3).wait_recv()
        y_second_relay(b, 2).start()
        y_second(b, 2, 3).wait_recv()
        y_second_relay(b, 3).start()
        y_fwd(b, 4, c).start()
        y_second(b, 2, 1).wait_recv()
        y_fwd(b, 3, c).start()

        dots(b, c, 0, True)
        for n in range(3):
            y_fwd(b, n, 1 - c).wait_recv()
        dots(b, 1 - c, 0, False)
        dots(b, c, 2, False)
        dots(b, c, 1, False)
        y_second_relay(b, 0).wait_recv()
        y_second_relay(b, 1).wait_recv()
        y_fwd(b, 5, c).start()
        y_fwd(b, 4, 1 - c).wait_recv()
        dots(b, 1 - c, 2, False)
        y_second_relay(b, 2).wait_recv()
        y_second_relay(b, 3).wait_recv()
        y_fwd(b, 6, c).start()
        y_fwd(b, 3, 1 - c).wait_recv()
        dots(b, 1 - c, 1, False)
        dots(b, c, 3, False)
        y_fwd(b, 5, 1 - c).wait_recv()
        y_fwd(b, 6, 1 - c).wait_recv()
        dots(b, 1 - c, 3, False)

        extra = jnp.zeros((16, 256), F32)
        for cc in range(2):
            for j in range(4):
                for i in range(4):
                    extra = extra + Y[b, cc, j, i, 256:272, :].astype(F32)
        sums = jnp.sum(extra, axis=0, keepdims=True)
        r = lax.rsqrt(sums * (1.0 / D) + EPS)
        logits = LT[...] * r
        highest = jnp.max(logits, axis=0, keepdims=True)
        summed = jnp.sum(jnp.exp(logits - highest), axis=0, keepdims=True)
        vocab = HEAD.shape[2]
        first = ((d * NX + s) * NM + m) * vocab
        index = (lax.broadcasted_iota(jnp.int32, logits.shape, 0) + first).astype(F32)
        wanted = wanted_rows()
        picked = jnp.sum(jnp.where(index == wanted, logits, 0.0), axis=0, keepdims=True)
        lanes = pl.ds(pl.multiple_of(b * 256, 256), 256)
        rows = lax.broadcasted_iota(jnp.int32, (8, 256), 0)
        STO[:, lanes] = jnp.where(rows == 0, highest,
                                  jnp.where(rows == 1, summed,
                                            jnp.where(rows == 2, picked, 0.0)))

    def step(t, _):
        place = jnp.where(s == NX - 1, 1, 0)

        @pl.when(t == place)
        def _():
            layer()

        @pl.when(t != place)
        def _():
            @pl.when((t == 0) | ((t == 1) & (s != NX - 1)))
            def _():
                head_load.wait()
            score(jnp.where(t == 2, 1, 0))
        return 0

    lax.fori_loop(0, 3, step, 0)

    def merge(ref, count):
        parts = [ref[j] for j in range(count)]
        highest = parts[0][0:1]
        for p in parts[1:]:
            highest = jnp.maximum(highest, p[0:1])
        summed = jnp.zeros_like(highest)
        picked = jnp.zeros_like(highest)
        for p in parts:
            summed = summed + p[1:2] * jnp.exp(p[0:1] - highest)
            picked = picked + p[2:3]
        return highest, summed, picked

    def stacked(highest, summed, picked):
        rows = lax.broadcasted_iota(jnp.int32, (8, 512), 0)
        return jnp.where(rows == 0, highest,
                         jnp.where(rows == 1, summed, jnp.where(rows == 2, picked, 0.0)))

    def st_y(k):
        return rcopy(SA.at[d], SA.at[d], st_s.at[0, k], st_r.at[0, d], (ypeer(k), s, m))

    def st_y_in(k):
        g = ypeer(k)
        return rcopy(SA.at[g], SA.at[g], st_s.at[0, k], st_r.at[0, g], (g, s, m))

    def m_of(k):
        return (m + k) % NM

    def st_m(k):
        return rcopy(SB.at[m], SB.at[m], st_s.at[1, k], st_r.at[1, m], (d, s, m_of(k)))

    def st_m_in(k):
        mm = m_of(k)
        return rcopy(SB.at[mm], SB.at[mm], st_s.at[1, k], st_r.at[1, mm], (d, s, mm))

    def st_x(k):
        return rcopy(SC.at[s], SC.at[s], st_s.at[2, k], st_r.at[2, s], (d, (s + k) % NX, m))

    def st_x_in(k):
        ss = (s + k) % NX
        return rcopy(SC.at[ss], SC.at[ss], st_s.at[2, k], st_r.at[2, ss], (d, ss, m))

    SA.at[d][...] = STO[...]
    for k in (2, 1, 3):
        st_y(k).start()
    for k in (1, 3, 2):
        st_y_in(k).wait_recv()
    SB.at[m][...] = stacked(*merge(SA, NY))
    for k in (4, 3, 5, 2, 6, 1, 7):
        st_m(k).start()
    for k in (1, 7, 2, 6, 3, 5, 4):
        st_m_in(k).wait_recv()
    SC.at[s][...] = stacked(*merge(SB, NM))
    for k in (2, 1, 3):
        st_x(k).start()
    for k in (1, 3, 2):
        st_x_in(k).wait_recv()
    highest, summed, picked = merge(SC, NX)
    logprob = picked - (highest + jnp.log(summed))
    terms = []
    for e in range(2):
        rest = logprob[:, e * 256:e * 256 + 256]
        for _ in range(3):
            term = rest.astype(BF).astype(F32)
            terms.append(term)
            rest = rest - term
    row = lax.broadcasted_iota(jnp.int32, (16, 256), 0)
    stack = jnp.zeros((16, 256), F32)
    for j, term in enumerate(terms):
        stack = jnp.where(row == j, term, stack)
    stack = stack.astype(BF)
    slot, position = row_slot(lax.broadcasted_iota(jnp.int32, (256, 32), 0))
    place = lax.broadcasted_iota(jnp.int32, (256, 32), 1)
    results = []
    for i in range(2):
        chosen = source_of[2 * d + i]
        take = ((slot == chosen) & (position == place)).astype(BF)
        got = jnp.dot(stack, take, preferred_element_type=F32)
        alive = lax.broadcasted_iota(jnp.int32, (1, 32), 1) < live[chosen]
        results.append([jnp.where(alive, got[j:j + 1] + got[j + 1:j + 2] + got[j + 2:j + 3], 0.0)
                        for j in (0, 3)])
    for e, ref in enumerate((exit_out, final_out)):
        first = lax.broadcasted_iota(jnp.int32, (2, 32), 0) == 0
        ref[...] = jnp.where(first, results[0][e], results[1][e])

    @pl.when(s == 0)
    def _():
        for k in range(4):
            (eb_z(k) if k else eb_fwd(0)).wait_send()
        for k in range(1, 4):
            eb_fwd(k).wait_send()

    @pl.when(s > 0)
    def _():
        for h in range(2):
            for k in range(1, 4):
                ag_z(h, k).wait_send()
            for k in range(4):
                ag_fwd(h, k).wait_send()

    @pl.when(s < NX - 1)
    def _():
        for h in range(2):
            for k in range(4):
                hop(h, ypeer(k)).wait_send()
            hop_raw(h).wait_send()

    @pl.when(s == 0)
    def _():
        for h in range(2):
            for k in range(1, 4):
                res(h, k).wait_send()

    @pl.when(s > 0)
    def _():
        next_gain().wait_send()

    for h in range(2):
        for k in range(1, 4):
            zred(h, k).wait_send()
        for zz in range(NZ):
            part(h, zz).wait_send()
    for k in range(1, 4):
        ctx(k).wait_send()
        st_y(k).wait_send()
        st_x(k).wait_send()
    for k in range(1, 8):
        st_m(k).wait_send()
    for b in range(2):
        @pl.when(s == 2 * b + 1)
        def _():
            for k in (1, 3):
                y_x(b, k).wait_send()

        for half in range(2):
            @pl.when((s != 2 * b + 1) & relays_x(b, half))
            def _():
                y_x_relay(b, half).wait_send()

            y_first_relay(b, half).wait_send()
        for k in (1, 3):
            y_first(b, k).wait_send()
            for n in range(3):
                y_second(b, n, k).wait_send()
        for i in range(4):
            y_second_relay(b, i).wait_send()
        for n in range(7):
            y_fwd(b, n, c).wait_send()


def tables():
    row = np.arange(ROWS)
    position = (row // 8) * 4 + row % 4
    half = HD // 2
    freqs = (ROPE_BASE ** (-np.arange(half) * 2.0 / HD)).astype(np.float32)
    angles = (position.astype(np.float32)[:, None] * freqs[None, :]).astype(np.float64)
    cos, sin = np.cos(angles), np.sin(angles)
    return (np.concatenate([cos, cos], 1).astype(np.float32),
            np.concatenate([-sin, sin], 1).astype(np.float32))


def per_device(
    embeds, targets, lengths, source, attn_gain, w_query, w_key, w_value, w_out, final_gain, head
):
    vocab = head.shape[0]
    cos, sin = tables()
    vmem = pl.BlockSpec(memory_space=pltpu.VMEM)
    hbm = pl.BlockSpec(memory_space=pl.ANY)
    smem = pl.BlockSpec(memory_space=pltpu.SMEM)
    dma = pltpu.SemaphoreType.DMA
    return pl.pallas_call(
        kernel,
        out_shape=[jax.ShapeDtypeStruct((2, 32), F32)] * 2,
        in_specs=[vmem, smem, smem, vmem, vmem, vmem, vmem, vmem, hbm, hbm, hbm, hbm, hbm],
        out_specs=[vmem, vmem],
        scratch_shapes=[
            pltpu.VMEM((2, 32, 128, 768), BF),
            pltpu.VMEM((2, QW, 1024), BF),
            pltpu.VMEM((2, 4, vocab, 1024), BF),
            pltpu.VMEM((NM, 16, 4096), BF),
            pltpu.VMEM((2, NM, NY, ROWS + 16, 128), BF),
            pltpu.VMEM((2, NY, ROWS + 16, 128), BF),
            pltpu.VMEM((1, 256), F32),
            pltpu.VMEM((2, NY, ROWS, 128), BF),
            pltpu.VMEM((4 * ROWS, ROWS), F32),
            pltpu.VMEM((ROWS, 128), F32),
            pltpu.VMEM((ROWS, 768), F32),
            pltpu.VMEM((2, NY, ROWS, 128), BF),
            pltpu.VMEM((NY, ROWS, QW), BF),
            pltpu.VMEM((2, NZ, NY * ROWS, 128), BF),
            pltpu.VMEM((2, NZ, NY * ROWS, 128), BF),
            pltpu.VMEM((2, NZ, NY * ROWS, 128), F32),
            pltpu.VMEM((2, NZ, NY * ROWS, 128), BF),
            pltpu.VMEM((2, NZ, NY * ROWS, 128), BF),
            pltpu.VMEM((2, NY, ROWS, 128), BF),
            pltpu.VMEM((16, NY * ROWS), BF),
            pltpu.VMEM((2, 2, 4, 4, 272, 256), BF),
            pltpu.VMEM((vocab, 256), F32),
            pltpu.VMEM((8, 512), F32),
            pltpu.VMEM((NY, 8, 512), F32),
            pltpu.VMEM((NM, 8, 512), F32),
            pltpu.VMEM((NX, 8, 512), F32),
            dma((23,)),
            dma, dma,
            dma((8,)), dma((8,)),
            dma((2, 5)), dma((2, 5)),
            dma((2, 8)), dma((2, 8)),
            dma((2, 4)), dma((2, 4)),
            dma((4,)), dma((4,)),
            dma((2, 4)), dma((2, 4)),
            dma((2, 4)), dma((2, 4)),
            dma((2, 28)), dma((2, 21)),
            dma((3, 8)), dma((3, 8)),
        ],
        compiler_params=pltpu.CompilerParams(
            collective_id=0, has_side_effects=True, vmem_limit_bytes=60 * 1024 * 1024),
        cost_estimate=pl.CostEstimate(flops=8_000_000_000, bytes_accessed=24_000_000,
                                      transcendentals=300_000),
    )(
        embeds, lengths, source, targets, attn_gain, final_gain.reshape(1, D), jnp.asarray(cos), jnp.asarray(sin),
        w_query.reshape(32, 2, 128, 512), w_key.reshape(32, 2, 128, 128),
        w_value.reshape(32, 2, 128, 128), w_out.reshape(512, 2048), head,
    )


def solution(mesh):
    return jax.shard_map(
        per_device,
        mesh=mesh,
        in_specs=(
            P("dp", "mp", None),
            P(),
            P(),
            P(),
            P("section", None),
            P("section", None, "mp"),
            P("section", None, "mp"),
            P("section", None, "mp"),
            P("section", "mp", "dp"),
            P(),
            P(("dp", "section", "mp"), None),
        ),
        out_specs=(P("dp", None), P("dp", None)),
        check_vma=False,
    )
```

```python
import jax
import jax.numpy as jnp
import numpy as np
from jax import lax
from jax.experimental import pallas as pl
from jax.experimental.pallas import tpu as pltpu
from jax.sharding import PartitionSpec as P

HD = 128
EPS = 1e-05
ROPE_BASE = 500000.0
NY = 4
NX = 4
NZ = 4
NM = 8
ROWS = 64
LIVE = 192
PIECE = LIVE + 16
D = 8192
QW = 512
MESH = pl.DeviceIdType.MESH
BF = jnp.bfloat16
F32 = jnp.float32


def lane(start, size):
    return pl.ds(pl.multiple_of(start, 128), size)


def kernel(
    emb, live, source_of, targets, gain, fgain, cosine, sine, wq, wk, wv, wo, head,
    out,
    W, WO, HEAD, EB, X, G, NG, RX, MASK, SEL, SS, QA, R, C, PS, PR, PO, ZS, ZR, HP, SUMS, Y, LT, STO, SA, SB, SC,
    w_sem, ng_s, ng_r, eb_s, eb_r, hop_s, hop_r, ag_s, ag_r, res_s, res_r, ctx_s, ctx_r, ps_s, ps_r,
    zz_s, zz_r, y_s, y_r, st_s, st_r,
):
    d = lax.axis_index("dp")
    s = lax.axis_index("section")
    m = lax.axis_index("mp")
    z = m // 2
    c = m % 2
    sib = z * 2 + (1 - c)

    def ypeer(k):
        return (d + k) % NY

    def zpeer(k):
        return ((z + k) % NZ) * 2 + c

    def zother(k):
        return ((z + k) % NZ) * 2 + (1 - c)

    def rcopy(src, dst, ssem, rsem, dev):
        return pltpu.make_async_remote_copy(
            src_ref=src, dst_ref=dst, send_sem=ssem, recv_sem=rsem,
            device_id=dev, device_id_type=MESH,
        )

    here = (d, s, sib)

    loads = []
    for h in range(2):
        loads.append([
            pltpu.make_async_copy(wq.at[:, h], W.at[h, :, :, 0:512], w_sem.at[3 * h]),
            pltpu.make_async_copy(wk.at[:, h], W.at[h, :, :, 512:640], w_sem.at[3 * h + 1]),
            pltpu.make_async_copy(wv.at[:, h], W.at[h, :, :, 640:768], w_sem.at[3 * h + 2]),
        ])
    wo_loads = []
    for h in range(2):
        for mm in range(NM):
            wo_loads.append(pltpu.make_async_copy(
                wo.at[:, mm * 256 + h * 128: mm * 256 + h * 128 + 128],
                WO.at[h, :, mm * 128: mm * 128 + 128], w_sem.at[6 + h * NM + mm]))
    for group in loads:
        for copy in group:
            copy.start()
    for copy in wo_loads:
        copy.start()

    barrier = pltpu.get_barrier_semaphore()
    partners = []
    for k in range(1, 4):
        partners.append((ypeer(k), s, m))
        partners.append((d, (s + k) % NX, m))
        partners.append((d, s, zpeer(k)))
        partners.append((d, s, zother(k)))
        partners.append((ypeer(k), (s + 1) % NX, m))
        partners.append((ypeer(k), (s + 3) % NX, m))
    partners.append(here)
    for dev in partners:
        pl.semaphore_signal(barrier, inc=1, device_id=dev, device_id_type=MESH)
    offsets = (0, 3, 1, 2)
    for cc in range(2):
        for j in range(4):
            for i in range(4):
                g, zz = (offsets[i], offsets[j]) if cc == 0 else (offsets[j], offsets[i])
                col = ypeer(g) * 2048 + ((z + zz) % NZ) * 512 + cc * 256
                pltpu.make_async_copy(head.at[:, lane(col, 256)],
                                      HEAD.at[cc, j, :, i * 256:i * 256 + 256],
                                      w_sem.at[22]).start()
    head_load = pltpu.make_async_copy(HEAD, HEAD, w_sem.at[22])
    shape = (4 * ROWS, ROWS)
    rq = lax.broadcasted_iota(jnp.int32, shape, 0) % ROWS
    rk = lax.broadcasted_iota(jnp.int32, shape, 1)
    slot_q, slot_k = (rq // 4) % 2, (rk // 4) % 2
    pos_q, pos_k = (rq // 8) * 4 + rq % 4, (rk // 8) * 4 + rk % 4
    live_k = jnp.where(slot_k == 0, live[2 * d], live[2 * d + 1])
    allowed = (slot_q == slot_k) & (pos_k <= pos_q) & (pos_k < live_k)
    MASK[...] = jnp.where(allowed, F32(0.0), F32(-1e30))

    def row_slot(lanes):
        return (lanes // 64) * 2 + (lanes // 4) % 2, ((lanes // 8) % 8) * 4 + lanes % 4

    def first_row(slot):
        start = jnp.zeros_like(slot)
        for other in range(8):
            start = start + jnp.where(slot > other, live[other], 0)
        return start

    def live_of(slot):
        count = jnp.zeros_like(slot)
        for other in range(8):
            count = count + jnp.where(slot == other, live[other], 0)
        return count

    slot, position = row_slot(lax.broadcasted_iota(jnp.int32, (8, 256), 1))
    packed_at = jnp.where(position < live_of(slot), first_row(slot) + position, 999)[0:1]
    SEL[...] = (lax.broadcasted_iota(jnp.int32, (256, 256), 0) == packed_at).astype(F32).astype(BF)
    pl.semaphore_wait(barrier, len(partners))

    def next_gain():
        return rcopy(gain.at[:, lane(d * 2048 + m * 256, 256)], NG, ng_s, ng_r,
                     (d, (s + 3) % NX, m))

    @pl.when(s > 0)
    def _():
        next_gain().start()

    def eb_z(k):
        return rcopy(EB.at[m], EB.at[m], eb_s.at[k], eb_r.at[m], (d, s, zpeer(k)))

    def eb_z_in(k):
        mk = zpeer(k)
        return rcopy(EB.at[mk], EB.at[mk], eb_s.at[k], eb_r.at[mk], (d, s, zpeer(k)))

    def eb_fwd(k):
        mk = zpeer(k)
        return rcopy(EB.at[mk], EB.at[mk], eb_s.at[4 + k], eb_r.at[mk], here)

    def eb_sib_in(k):
        mk = zother(k)
        return rcopy(EB.at[mk], EB.at[mk], eb_s.at[4 + k], eb_r.at[mk], here)

    rows_of = (pl.ds(0, ROWS), pl.ds(0, ROWS + 16))

    def hop(h, g):
        return rcopy(G.at[h, g, rows_of[h]], X.at[h, m, d, rows_of[h]], hop_s.at[h, g],
                     hop_r.at[h, d], (g, (s + 1) % NX, m))

    def hop_in(h, g):
        return rcopy(G.at[h, g, rows_of[h]], X.at[h, m, g, rows_of[h]], hop_s.at[h, g],
                     hop_r.at[h, g], (g, (s + 1) % NX, m))

    def hop_raw(h):
        return rcopy(HP.at[h], R.at[h], hop_s.at[h, 4], hop_r.at[h, 4], (d, (s + 1) % NX, m))

    def slab(h, mm):
        return X.at[h, mm, :, rows_of[h]]

    def ag_z(h, k):
        return rcopy(slab(h, m), slab(h, m), ag_s.at[h, k], ag_r.at[h, m], (d, s, zpeer(k)))

    def ag_z_in(h, k):
        mk = zpeer(k)
        return rcopy(slab(h, mk), slab(h, mk), ag_s.at[h, k], ag_r.at[h, mk], (d, s, zpeer(k)))

    def ag_fwd(h, k):
        mk = zpeer(k)
        return rcopy(slab(h, mk), slab(h, mk), ag_s.at[h, 4 + k], ag_r.at[h, mk], here)

    def ag_sib_in(h, k):
        mk = zother(k)
        return rcopy(slab(h, mk), slab(h, mk), ag_s.at[h, 4 + k], ag_r.at[h, mk], here)

    def res(h, k):
        g = ypeer(k)
        return rcopy(RX.at[h, g], R.at[h, d], res_s.at[h, k], res_r.at[h, d], (g, s, m))

    def res_in(h, k):
        g = ypeer(k)
        return rcopy(RX.at[h, g], R.at[h, g], res_s.at[h, k], res_r.at[h, g], (g, s, m))

    def ctx(k):
        return rcopy(C.at[d], C.at[d], ctx_s.at[k], ctx_r.at[d], (ypeer(k), s, m))

    def ctx_in(k):
        g = ypeer(k)
        return rcopy(C.at[g], C.at[g], ctx_s.at[k], ctx_r.at[g], (g, s, m))

    def part(h, zz):
        return rcopy(PS.at[h, zz], PR.at[h, zz], ps_s.at[h, zz], ps_r.at[h, zz], here)

    def zred(h, k):
        return rcopy(ZS.at[h, k], ZR.at[h, k], zz_s.at[h, k], zz_r.at[h, k], (d, s, zpeer(k)))

    def layer():
        @pl.when(s == 0)
        def _():
            rows = jnp.concatenate([emb[0], emb[1]], axis=0).astype(F32)
            EB.at[m][...] = jnp.concatenate([rows[:, :4096], rows[:, 4096:]], axis=0).astype(BF)
            for k in (2, 1, 3, 0):
                (eb_z(k) if k else eb_fwd(0)).start()
            for k in (1, 3, 2):
                eb_z_in(k).wait_recv()
                eb_fwd(k).start()
            for k in range(4):
                eb_sib_in(k).wait_recv()

            def block(dl, mm, h):
                return EB[:, :, lane(dl * 2048 + mm * 256 + h * 128, 128)].astype(F32)

            def body(mm, total):
                for dl in range(2):
                    for h in range(2):
                        xf = block(dl, mm, h)
                        for half in range(2):
                            xs = xf[:, half * 8: half * 8 + 8, :].reshape(ROWS, 128)
                            g = half * 2 + dl
                            cols = lane(g * 2048 + mm * 256 + h * 128, 128)
                            X.at[h, mm, g][0:ROWS, :] = (xs * gain[:, cols]).astype(BF)
                            total = total + xs * xs
                return total

            SS[...] = lax.fori_loop(0, NM, body, jnp.zeros((ROWS, 128), F32))
            for dl in range(2):
                for h in range(2):
                    xf = block(dl, m, h)
                    for half in range(2):
                        xs = xf[:, half * 8: half * 8 + 8, :].reshape(ROWS, 128)
                        RX.at[h, half * 2 + dl][...] = xs.astype(BF)
            for h in range(2):
                for k in (2, 1, 3):
                    res(h, k).start()
                R.at[h, d][...] = RX[h, d]

        @pl.when(s > 0)
        def _():
            for h in range(2):
                for g in range(NY):
                    hop_in(h, g).wait_recv()
                for k in (2, 1, 3, 0):
                    (ag_z(h, k) if k else ag_fwd(h, 0)).start()
            for h in range(2):
                for k in (1, 3, 2):
                    ag_z_in(h, k).wait_recv()
                    ag_fwd(h, k).start()

        def multiply(h, who, start):
            term = None
            for g in range(NY):
                x = jnp.concatenate([X[h, 2 * zz + who, g, 0:ROWS] for zz in range(NZ)], axis=1)
                w = jnp.concatenate([W[h, g * 8 + 2 * zz + who] for zz in range(NZ)], axis=0)
                one = jnp.dot(x, w, preferred_element_type=F32)
                term = one if term is None else term + one
            QA[...] = term if start else QA[...] + term

        for h in range(2):
            for copy in loads[h]:
                copy.wait()
            multiply(h, c, h == 0)

            @pl.when(s > 0)
            def _():
                for k in range(4):
                    ag_sib_in(h, k).wait_recv()

            multiply(h, 1 - c, False)

        @pl.when(s > 0)
        def _():
            total = jnp.zeros((16, 128), F32)
            for mm in range(NM):
                for g in range(NY):
                    total = total + X[1, mm, g, ROWS:ROWS + 16].astype(F32)
            total = total[0:1] + total[1:2]
            mine = (lax.broadcasted_iota(jnp.int32, (ROWS, 128), 1)
                    == lax.broadcasted_iota(jnp.int32, (ROWS, 128), 0) + (d % 2) * ROWS)
            SS[...] = jnp.where(mine, total, 0.0)

        r = lax.rsqrt(jnp.sum(SS[...], axis=1, keepdims=True) * (1.0 / D) + EPS)
        cos = cosine[...]
        sin = sine[...]

        def rope(x):
            return (x * cos + pltpu.roll(x, 64, 1) * sin).astype(BF)

        query = jnp.concatenate(
            [rope(QA[:, j * HD:(j + 1) * HD] * r) for j in range(4)], axis=0)
        key = rope(QA[:, 512:640] * r)
        value = (QA[:, 640:768] * r).astype(BF)
        scores = lax.dot_general(query, key, (((1,), (1,)), ((), ())),
                                 preferred_element_type=F32) * (HD ** -0.5)
        scores = scores + MASK[...]
        highest = jnp.max(scores, axis=-1, keepdims=True)
        weights = jnp.exp(scores - highest)
        probs = (weights / jnp.sum(weights, axis=-1, keepdims=True)).astype(BF)
        mixed = jnp.dot(probs, value, preferred_element_type=F32).astype(BF)
        for j in range(4):
            C.at[d][:, j * HD:(j + 1) * HD] = mixed[j * ROWS:(j + 1) * ROWS]
        for k in (2, 1, 3):
            ctx(k).start()

        for copy in wo_loads:
            copy.wait()
        for k in (1, 3, 2):
            ctx_in(k).wait_recv()

        context = C[...].reshape(NY * ROWS, QW)
        for h in range(2):
            for k in (2, 1, 3, 0):
                zz = (z + k) % NZ
                p = jnp.dot(context, WO[h, :, lane(zz * 256, 256)], preferred_element_type=F32)
                low, high = p[:, :128], p[:, 128:]
                PO.at[h, zz][...] = jnp.where(c == 0, low, high)
                PS.at[h, zz][...] = jnp.where(c == 0, high, low).astype(BF)
                part(h, zz).start()

        def pair(h, k):
            zt = (z + k) % NZ
            part(h, zt).wait_recv()
            return PO[h, zt] + PR[h, zt].astype(F32)

        for h in range(2):
            for k in (2, 1, 3):
                ZS.at[h, k][...] = pair(h, k).astype(BF)
                zred(h, k).start()
        @pl.when(s == 0)
        def _():
            for h in range(2):
                for k in (1, 3, 2):
                    res_in(h, k).wait_recv()

        @pl.when(s > 0)
        def _():
            for h in range(2):
                hop_raw(h).wait_recv()

        @pl.when(s < NX - 1)
        def _():
            next_gain().wait_recv()

        sums = jnp.zeros((16, NY * ROWS), F32)
        for h in range(2):
            total = pair(h, 0)
            total = total + R[h].astype(F32).reshape(NY * ROWS, 128)
            for k in (1, 3, 2):
                zred(h, k).wait_recv()
                total = total + ZR[h, k].astype(F32)
            hidden = total.astype(BF)
            HP.at[h][...] = hidden.reshape(NY, ROWS, 128)
            wide = hidden.astype(F32)
            scaled = (wide * NG[:, h * 128:h * 128 + 128]).astype(BF)
            G.at[h][:, 0:ROWS, :] = scaled.reshape(NY, ROWS, 128)
            square = wide * wide
            top = square.astype(BF)
            rest = (square - top.astype(F32)).astype(BF)
            ones = jnp.ones((16, 128), BF)
            nt = (((1,), (1,)), ((), ()))
            sums = sums + lax.dot_general(ones, top, nt, preferred_element_type=F32)
            sums = sums + lax.dot_general(ones, rest, nt, preferred_element_type=F32)
            if h == 1:
                top = sums.astype(BF).astype(F32)
                row = lax.broadcasted_iota(jnp.int32, (16, NY * ROWS), 0)
                packed = jnp.where(row == 0, top, jnp.where(row == 1, sums - top, 0.0)).astype(BF)
                for g in range(NY):
                    tile = g // 2 * 128
                    G.at[1, g][ROWS:ROWS + 16, :] = packed[:, tile:tile + 128]
                SUMS[...] = packed

            @pl.when(s < NX - 1)
            def _():
                for k in (2, 1, 3, 0):
                    hop(h, ypeer(k)).start()

        @pl.when(s < NX - 1)
        def _():
            for h in range(2):
                hop_raw(h).start()

        @pl.when(s % 2 == 1)
        def _():
            emit(s // 2)

    def emit(b):
        mine = Y.at[b, c, 0, 0]
        nt = (((1,), (1,)), ((), ()))
        for h in range(2):
            wide = HP[h].astype(F32).reshape(NY * ROWS, 128)
            cols = lane(d * 2048 + m * 256 + h * 128, 128)
            scaled = (wide * fgain[:, cols]).astype(BF)
            live_rows = jnp.dot(SEL[0:LIVE], scaled, preferred_element_type=F32)
            mine[0:LIVE, h * 128:h * 128 + 128] = live_rows.astype(BF)
        squares = lax.dot_general(SUMS[...], SEL[...], nt, preferred_element_type=F32)
        mine[LIVE:PIECE, :] = squares.astype(BF)
        for half in range(2):
            y_x(b, half, 1).start()
            y_x(b, 1 - half, 3).start()
        spread_own(b)

    def first_dev(k):
        return (jnp.where(c == 0, ypeer(k), d), s, jnp.where(c == 0, m, zpeer(k)))

    def second_dev(k):
        return (jnp.where(c == 0, d, ypeer(k)), s, jnp.where(c == 0, zpeer(k), m))

    def ycopy(src, dst, b, i, j, dev):
        return rcopy(src, dst, y_s.at[b, i], y_r.at[b, j], dev)

    cut = (pl.ds(0, 96), pl.ds(96, PIECE - 96))

    def own(b, rows):
        return Y.at[b, c, 0, 0, rows]

    def y_x(b, half, k):
        ref = own(b, cut[half])
        return ycopy(ref, ref, b, k + half, (0, 21)[half], (d, (s + k) % NX, m))

    def y_x_relay(b, half):
        ref = own(b, cut[half])
        return ycopy(ref, ref, b, 28 + half, (0, 21)[half], (d, jnp.where(b == 0, 3, 1), m))

    def relays_x(b, half):
        return (s == 0) if half == 0 else (s == jnp.where(b == 0, 0, 2))

    whole = pl.ds(0, PIECE)

    def y_first(b, k):
        slot = 1 if k == 1 else 2
        return ycopy(own(b, whole), Y.at[b, c, 0, slot, whole], b, 5 + k, slot, first_dev(k))

    def y_first_relay(b, half):
        slot, k = ((1, 1), (2, 3))[half]
        return ycopy(Y.at[b, c, 0, slot, cut[half]], Y.at[b, c, 0, 3, cut[half]],
                     b, 9 + half, 3, first_dev(k))

    def y_opposite(b):
        ref = Y.at[b, c, 0, 3, whole]
        return ycopy(ref, ref, b, 9, 3, here)

    sets = (pl.ds(0, 1), pl.ds(1, 2), pl.ds(3, 1))

    def y_second(b, part_no, k):
        slot = 1 if k == 1 else 2
        return ycopy(Y.at[b, c, 0, sets[part_no], whole], Y.at[b, c, slot, sets[part_no], whole],
                     b, 11 + part_no * 2 + (slot - 1), 1 + 3 * slot + part_no, second_dev(k))

    def y_second_relay(b, i):
        slot, k = (1, 1) if i < 2 else (2, 3)
        return ycopy(Y.at[b, c, slot, i, whole], Y.at[b, c, 3, i, whole],
                     b, 17 + i, 10 + i, second_dev(k))

    forwards = ((0, 0, 1), (0, 1, 2), (0, 3, 1), (1, 0, 4), (2, 0, 4), (3, 0, 2), (3, 2, 2))

    def y_fwd(b, n, who):
        j, i, size = forwards[n]
        ref = Y.at[b, who, j, pl.ds(i, size), whole]
        return ycopy(ref, ref, b, 21 + n, 14 + n, here)

    def spread_own(b):
        for k in (1, 3):
            y_first(b, k).start()
        for k in (1, 3):
            y_second(b, 0, k).start()
        y_fwd(b, 0, c).start()

    def dots(b, cc, j, start):
        pieces = jnp.concatenate([Y[b, cc, j, i, 0:256, :] for i in range(4)], axis=1)
        term = lax.dot_general(HEAD[cc, j], pieces, (((1,), (1,)), ((), ())),
                               preferred_element_type=F32)
        LT[...] = term if start else LT[...] + term

    def wanted_rows():
        slot, position = row_slot(lax.broadcasted_iota(jnp.int32, (32, 256), 1))
        place = (position == lax.broadcasted_iota(jnp.int32, (32, 256), 0)).astype(BF)
        tokens = targets[...]
        nt = (((1,), (1,)), ((), ()))
        keep = slot[0:8] == lax.broadcasted_iota(jnp.int32, (8, 256), 0)
        parts = []
        for term in (tokens // 256, tokens % 256):
            every = jnp.dot(term.astype(F32).astype(BF), place, preferred_element_type=F32)
            mine = jnp.sum(jnp.where(keep, every, 0.0), axis=0, keepdims=True)
            spread = jnp.broadcast_to(mine, (16, 256)).astype(BF)
            parts.append(lax.dot_general(spread, SEL[...], nt, preferred_element_type=F32)[0:1])
        return parts[0] * 256.0 + parts[1]

    def gather(b):
        source = 2 * b + 1

        @pl.when(s != source)
        def _():
            def take(half):
                y_x(b, half, 1).wait_recv()

                @pl.when(relays_x(b, half))
                def _():
                    y_x_relay(b, half).start()

            @pl.when(s == 2)
            def _():
                take(1)
                take(0)

            @pl.when(s != 2)
            def _():
                take(0)
                take(1)

            spread_own(b)

        y_first(b, 1).wait_recv()
        y_first_relay(b, 0).start()
        y_first(b, 3).wait_recv()
        y_first_relay(b, 1).start()
        for k in (1, 3):
            y_second(b, 1, k).start()
        y_fwd(b, 1, c).start()
        y_second(b, 0, 1).wait_recv()
        y_second_relay(b, 0).start()
        y_second(b, 0, 3).wait_recv()
        y_opposite(b).wait_recv()
        for k in (1, 3):
            y_second(b, 2, k).start()
        y_fwd(b, 2, c).start()
        y_second(b, 1, 1).wait_recv()
        y_second_relay(b, 1).start()
        y_second(b, 1, 3).wait_recv()
        y_second_relay(b, 2).start()
        y_second(b, 2, 3).wait_recv()
        y_second_relay(b, 3).start()
        y_fwd(b, 4, c).start()
        y_second(b, 2, 1).wait_recv()
        y_fwd(b, 3, c).start()

    def finish(b):
        dots(b, c, 0, True)
        for n in range(3):
            y_fwd(b, n, 1 - c).wait_recv()
        dots(b, 1 - c, 0, False)
        dots(b, c, 2, False)
        dots(b, c, 1, False)
        y_second_relay(b, 0).wait_recv()
        y_second_relay(b, 1).wait_recv()
        y_fwd(b, 5, c).start()
        y_fwd(b, 4, 1 - c).wait_recv()
        dots(b, 1 - c, 2, False)
        y_second_relay(b, 2).wait_recv()
        y_second_relay(b, 3).wait_recv()
        y_fwd(b, 6, c).start()
        y_fwd(b, 3, 1 - c).wait_recv()
        dots(b, 1 - c, 1, False)
        dots(b, c, 3, False)
        y_fwd(b, 5, 1 - c).wait_recv()
        y_fwd(b, 6, 1 - c).wait_recv()
        dots(b, 1 - c, 3, False)

        extra = jnp.zeros((16, 256), F32)
        for cc in range(2):
            for j in range(4):
                for i in range(4):
                    extra = extra + Y[b, cc, j, i, LIVE:PIECE, :].astype(F32)
        sums = jnp.sum(extra, axis=0, keepdims=True)
        r = lax.rsqrt(sums * (1.0 / D) + EPS)
        logits = LT[...] * r
        highest = jnp.max(logits, axis=0, keepdims=True)
        summed = jnp.sum(jnp.exp(logits - highest), axis=0, keepdims=True)
        vocab = HEAD.shape[2]
        first = ((d * NX + s) * NM + m) * vocab
        index = (lax.broadcasted_iota(jnp.int32, logits.shape, 0) + first).astype(F32)
        wanted = wanted_rows()
        picked = jnp.sum(jnp.where(index == wanted, logits, 0.0), axis=0, keepdims=True)
        alive = lax.broadcasted_iota(jnp.int32, (1, 256), 1) < LIVE
        for n, value in enumerate((highest, summed, picked)):
            value = jnp.where(alive, value, 1.0)
            for half in range(2):
                STO[pl.ds(n * 4 + b * 2 + half, 1), :] = value[:, half * 128:half * 128 + 128]

    def step(t, _):
        last = s == NX - 1
        place = jnp.where(last, 1, 0)

        @pl.when(t == place)
        def _():
            layer()

        @pl.when(jnp.where(last, (t == 0) | (t == 2), (t == 1) | (t == 3)))
        def _():
            gather(jnp.where(t < 2, 0, 1))

        @pl.when(jnp.where(last, t >= 3, (t == 2) | (t == 4)))
        def _():
            @pl.when(t == jnp.where(last, 3, 2))
            def _():
                head_load.wait()
            finish(jnp.where(t == 4, 1, 0))
        return 0

    STO[...] = jnp.zeros_like(STO)
    lax.fori_loop(0, 5, step, 0)

    def merge(ref, count):
        parts = [ref[j] for j in range(count)]
        highest = parts[0][0:4]
        for p in parts[1:]:
            highest = jnp.maximum(highest, p[0:4])
        summed = jnp.zeros_like(highest)
        picked = jnp.zeros_like(highest)
        for p in parts:
            summed = summed + p[4:8] * jnp.exp(p[0:4] - highest)
            picked = picked + p[8:12]
        return highest, summed, picked

    def stacked(highest, summed, picked):
        return jnp.concatenate([highest, summed, picked, jnp.zeros_like(picked)], axis=0)

    def st_y(k):
        return rcopy(SA.at[d], SA.at[d], st_s.at[0, k], st_r.at[0, d], (ypeer(k), s, m))

    def st_y_in(k):
        g = ypeer(k)
        return rcopy(SA.at[g], SA.at[g], st_s.at[0, k], st_r.at[0, g], (g, s, m))

    def m_of(k):
        return (m + k) % NM

    def st_m(k):
        return rcopy(SB.at[m], SB.at[m], st_s.at[1, k], st_r.at[1, m], (d, s, m_of(k)))

    def st_m_in(k):
        mm = m_of(k)
        return rcopy(SB.at[mm], SB.at[mm], st_s.at[1, k], st_r.at[1, mm], (d, s, mm))

    def st_x(k):
        return rcopy(SC.at[s], SC.at[s], st_s.at[2, k], st_r.at[2, s], (d, (s + k) % NX, m))

    def st_x_in(k):
        ss = (s + k) % NX
        return rcopy(SC.at[ss], SC.at[ss], st_s.at[2, k], st_r.at[2, ss], (d, ss, m))

    SA.at[d][...] = STO[...]
    for k in (2, 1, 3):
        st_y(k).start()
    for k in (1, 3, 2):
        st_y_in(k).wait_recv()
    SB.at[m][...] = stacked(*merge(SA, NY))
    for k in (4, 3, 5, 2, 6, 1, 7):
        st_m(k).start()
    for k in (1, 7, 2, 6, 3, 5, 4):
        st_m_in(k).wait_recv()
    SC.at[s][...] = stacked(*merge(SB, NM))
    for k in (2, 1, 3):
        st_x(k).start()
    for k in (1, 3, 2):
        st_x_in(k).wait_recv()
    highest, summed, picked = merge(SC, NX)
    logprob = picked - (highest + jnp.log(summed))
    terms = []
    for e in range(2):
        rest = jnp.concatenate([logprob[2 * e:2 * e + 1], logprob[2 * e + 1:2 * e + 2]], axis=1)
        for _ in range(3):
            term = rest.astype(BF).astype(F32)
            terms.append(term)
            rest = rest - term
    row = lax.broadcasted_iota(jnp.int32, (16, 256), 0)
    stack = jnp.zeros((16, 256), F32)
    for j, term in enumerate(terms):
        stack = jnp.where(row == j, term, stack)
    stack = stack.astype(BF)
    index = lax.broadcasted_iota(jnp.int32, (256, 32), 0)
    place = lax.broadcasted_iota(jnp.int32, (256, 32), 1)
    results = []
    for i in range(2):
        chosen = source_of[2 * d + i]
        start = 0
        for other in range(8):
            start = start + jnp.where(chosen > other, live[other], 0)
        take = ((index == start + place) & (place < live[chosen])).astype(F32).astype(BF)
        got = jnp.dot(stack, take, preferred_element_type=F32)
        results.append([got[j:j + 1] + got[j + 1:j + 2] + got[j + 2:j + 3] for j in (0, 3)])
    for e in range(2):
        first = lax.broadcasted_iota(jnp.int32, (2, 32), 0) == 0
        out.at[e][...] = jnp.where(first, results[0][e], results[1][e])

    @pl.when(s == 0)
    def _():
        for k in range(4):
            (eb_z(k) if k else eb_fwd(0)).wait_send()
        for k in range(1, 4):
            eb_fwd(k).wait_send()

    @pl.when(s > 0)
    def _():
        for h in range(2):
            for k in range(1, 4):
                ag_z(h, k).wait_send()
            for k in range(4):
                ag_fwd(h, k).wait_send()

    @pl.when(s < NX - 1)
    def _():
        for h in range(2):
            for k in range(4):
                hop(h, ypeer(k)).wait_send()
            hop_raw(h).wait_send()

    @pl.when(s == 0)
    def _():
        for h in range(2):
            for k in range(1, 4):
                res(h, k).wait_send()

    @pl.when(s > 0)
    def _():
        next_gain().wait_send()

    for h in range(2):
        for k in range(1, 4):
            zred(h, k).wait_send()
        for zz in range(NZ):
            part(h, zz).wait_send()
    for k in range(1, 4):
        ctx(k).wait_send()
        st_y(k).wait_send()
        st_x(k).wait_send()
    for k in range(1, 8):
        st_m(k).wait_send()
    for b in range(2):
        @pl.when(s == 2 * b + 1)
        def _():
            for half in range(2):
                for k in (1, 3):
                    y_x(b, half, k).wait_send()

        for half in range(2):
            @pl.when((s != 2 * b + 1) & relays_x(b, half))
            def _():
                y_x_relay(b, half).wait_send()

            y_first_relay(b, half).wait_send()
        for k in (1, 3):
            y_first(b, k).wait_send()
            for n in range(3):
                y_second(b, n, k).wait_send()
        for i in range(4):
            y_second_relay(b, i).wait_send()
        for n in range(7):
            y_fwd(b, n, c).wait_send()


def tables():
    row = np.arange(ROWS)
    position = (row // 8) * 4 + row % 4
    half = HD // 2
    freqs = (ROPE_BASE ** (-np.arange(half) * 2.0 / HD)).astype(np.float32)
    angles = (position.astype(np.float32)[:, None] * freqs[None, :]).astype(np.float64)
    cos, sin = np.cos(angles), np.sin(angles)
    return (np.concatenate([cos, cos], 1).astype(np.float32),
            np.concatenate([-sin, sin], 1).astype(np.float32))


def per_device(
    embeds, targets, lengths, source, attn_gain, w_query, w_key, w_value, w_out, final_gain, head
):
    vocab = head.shape[0]
    cos, sin = tables()
    vmem = pl.BlockSpec(memory_space=pltpu.VMEM)
    hbm = pl.BlockSpec(memory_space=pl.ANY)
    smem = pl.BlockSpec(memory_space=pltpu.SMEM)
    dma = pltpu.SemaphoreType.DMA
    stats = pl.pallas_call(
        kernel,
        out_shape=jax.ShapeDtypeStruct((2, 2, 32), F32),
        in_specs=[vmem, smem, smem, vmem, vmem, vmem, vmem, vmem, hbm, hbm, hbm, hbm, hbm],
        out_specs=vmem,
        scratch_shapes=[
            pltpu.VMEM((2, 32, 128, 768), BF),
            pltpu.VMEM((2, QW, 1024), BF),
            pltpu.VMEM((2, 4, vocab, 1024), BF),
            pltpu.VMEM((NM, 16, 4096), BF),
            pltpu.VMEM((2, NM, NY, ROWS + 16, 128), BF),
            pltpu.VMEM((2, NY, ROWS + 16, 128), BF),
            pltpu.VMEM((1, 256), F32),
            pltpu.VMEM((2, NY, ROWS, 128), BF),
            pltpu.VMEM((4 * ROWS, ROWS), F32),
            pltpu.VMEM((256, 256), BF),
            pltpu.VMEM((ROWS, 128), F32),
            pltpu.VMEM((ROWS, 768), F32),
            pltpu.VMEM((2, NY, ROWS, 128), BF),
            pltpu.VMEM((NY, ROWS, QW), BF),
            pltpu.VMEM((2, NZ, NY * ROWS, 128), BF),
            pltpu.VMEM((2, NZ, NY * ROWS, 128), BF),
            pltpu.VMEM((2, NZ, NY * ROWS, 128), F32),
            pltpu.VMEM((2, NZ, NY * ROWS, 128), BF),
            pltpu.VMEM((2, NZ, NY * ROWS, 128), BF),
            pltpu.VMEM((2, NY, ROWS, 128), BF),
            pltpu.VMEM((16, NY * ROWS), BF),
            pltpu.VMEM((2, 2, 4, 4, 256, 256), BF),
            pltpu.VMEM((vocab, 256), F32),
            pltpu.VMEM((16, 128), F32),
            pltpu.VMEM((NY, 16, 128), F32),
            pltpu.VMEM((NM, 16, 128), F32),
            pltpu.VMEM((NX, 16, 128), F32),
            dma((23,)),
            dma, dma,
            dma((8,)), dma((8,)),
            dma((2, 5)), dma((2, 5)),
            dma((2, 8)), dma((2, 8)),
            dma((2, 4)), dma((2, 4)),
            dma((4,)), dma((4,)),
            dma((2, 4)), dma((2, 4)),
            dma((2, 4)), dma((2, 4)),
            dma((2, 30)), dma((2, 22)),
            dma((3, 8)), dma((3, 8)),
        ],
        compiler_params=pltpu.CompilerParams(
            collective_id=0, has_side_effects=True, vmem_limit_bytes=60 * 1024 * 1024),
        cost_estimate=pl.CostEstimate(flops=8_000_000_000, bytes_accessed=24_000_000,
                                      transcendentals=300_000),
    )(
        embeds, lengths, source, targets, attn_gain, final_gain.reshape(1, D), jnp.asarray(cos), jnp.asarray(sin),
        w_query.reshape(32, 2, 128, 512), w_key.reshape(32, 2, 128, 128),
        w_value.reshape(32, 2, 128, 128), w_out.reshape(512, 2048), head,
    )
    return (stats[0], stats[1])


def solution(mesh):
    return jax.shard_map(
        per_device,
        mesh=mesh,
        in_specs=(
            P("dp", "mp", None),
            P(),
            P(),
            P(),
            P("section", None),
            P("section", None, "mp"),
            P("section", None, "mp"),
            P("section", None, "mp"),
            P("section", "mp", "dp"),
            P(),
            P(("dp", "section", "mp"), None),
        ),
        out_specs=(P("dp", None), P("dp", None)),
        check_vma=False,
    )
```

```python
import jax
import jax.numpy as jnp
import numpy as np
from jax import lax
from jax.experimental import pallas as pl
from jax.experimental.pallas import tpu as pltpu
from jax.sharding import PartitionSpec as P

HD = 128
EPS = 1e-05
ROPE_BASE = 500000.0
NY = 4
NX = 4
NZ = 4
NM = 8
ROWS = 64
LIVE = 192
PIECE = LIVE + 16
D = 8192
QW = 512
MESH = pl.DeviceIdType.MESH
BF = jnp.bfloat16
F32 = jnp.float32


def lane(start, size):
    return pl.ds(pl.multiple_of(start, 128), size)


def kernel(
    emb, live, source_of, targets, gain, fgain, cosine, sine, wq, wk, wv, wo, head,
    out,
    W, WO, HEAD, EB, X, G, NG, RX, MASK, SEL, SS, QA, R, C, PS, PR, PO, ZS, ZR, HP, Y, LT, STO, SA, SB, SC,
    w_sem, ng_s, ng_r, eb_s, eb_r, hop_s, hop_r, ag_s, ag_r, res_s, res_r, ctx_s, ctx_r, ps_s, ps_r,
    zz_s, zz_r, y_s, y_r, st_s, st_r,
):
    d = lax.axis_index("dp")
    s = lax.axis_index("section")
    m = lax.axis_index("mp")
    z = m // 2
    c = m % 2
    sib = z * 2 + (1 - c)

    def ypeer(k):
        return (d + k) % NY

    def zpeer(k):
        return ((z + k) % NZ) * 2 + c

    def zother(k):
        return ((z + k) % NZ) * 2 + (1 - c)

    def rcopy(src, dst, ssem, rsem, dev):
        return pltpu.make_async_remote_copy(
            src_ref=src, dst_ref=dst, send_sem=ssem, recv_sem=rsem,
            device_id=dev, device_id_type=MESH,
        )

    here = (d, s, sib)

    loads = []
    for g in range(NY):
        blocks = pl.ds(g * NM, NM)
        loads.append([
            pltpu.make_async_copy(wq.at[blocks], W.at[blocks, :, 0:512], w_sem.at[3 * g]),
            pltpu.make_async_copy(wk.at[blocks], W.at[blocks, :, 512:640], w_sem.at[3 * g + 1]),
            pltpu.make_async_copy(wv.at[blocks], W.at[blocks, :, 640:768], w_sem.at[3 * g + 2]),
        ])
    wo_load = pltpu.make_async_copy(wo, WO, w_sem.at[12])
    for group in loads:
        for copy in group:
            copy.start()
    wo_load.start()

    barrier = pltpu.get_barrier_semaphore()
    partners = []
    for k in range(1, 4):
        partners.append((ypeer(k), s, m))
        partners.append((d, (s + k) % NX, m))
        partners.append((d, s, zpeer(k)))
        partners.append((d, s, zother(k)))
        partners.append((ypeer(k), (s + 1) % NX, m))
        partners.append((ypeer(k), (s + 3) % NX, m))
    partners.append(here)
    for dev in partners:
        pl.semaphore_signal(barrier, inc=1, device_id=dev, device_id_type=MESH)
    offsets = (0, 3, 1, 2)
    for cc in range(2):
        for j in range(4):
            for i in range(4):
                g, zz = (offsets[i], offsets[j]) if cc == 0 else (offsets[j], offsets[i])
                col = ypeer(g) * 2048 + ((z + zz) % NZ) * 512 + cc * 256
                pltpu.make_async_copy(head.at[:, lane(col, 256)],
                                      HEAD.at[cc, j, :, i * 256:i * 256 + 256],
                                      w_sem.at[13]).start()
    head_load = pltpu.make_async_copy(HEAD, HEAD, w_sem.at[13])
    shape = (4 * ROWS, ROWS)
    rq = lax.broadcasted_iota(jnp.int32, shape, 0) % ROWS
    rk = lax.broadcasted_iota(jnp.int32, shape, 1)
    slot_q, slot_k = (rq // 4) % 2, (rk // 4) % 2
    pos_q, pos_k = (rq // 8) * 4 + rq % 4, (rk // 8) * 4 + rk % 4
    live_k = jnp.where(slot_k == 0, live[2 * d], live[2 * d + 1])
    allowed = (slot_q == slot_k) & (pos_k <= pos_q) & (pos_k < live_k)
    MASK[...] = jnp.where(allowed, F32(0.0), F32(-1e30))

    def row_slot(lanes):
        return (lanes // 64) * 2 + (lanes // 4) % 2, ((lanes // 8) % 8) * 4 + lanes % 4

    def first_row(slot):
        start = jnp.zeros_like(slot)
        for other in range(8):
            start = start + jnp.where(slot > other, live[other], 0)
        return start

    def live_of(slot):
        count = jnp.zeros_like(slot)
        for other in range(8):
            count = count + jnp.where(slot == other, live[other], 0)
        return count

    slot, position = row_slot(lax.broadcasted_iota(jnp.int32, (8, 256), 1))
    packed_at = jnp.where(position < live_of(slot), first_row(slot) + position, 999)[0:1]
    SEL[...] = (lax.broadcasted_iota(jnp.int32, (256, 256), 0) == packed_at).astype(F32).astype(BF)
    pl.semaphore_wait(barrier, len(partners))

    def next_gain():
        return rcopy(gain.at[:, lane(d * 2048 + m * 256, 256)], NG, ng_s, ng_r,
                     (d, (s + 3) % NX, m))

    @pl.when(s > 0)
    def _():
        next_gain().start()

    def eb_z(q, k):
        return rcopy(EB.at[q, m], EB.at[q, m], eb_s.at[q, k], eb_r.at[q, m], (d, s, zpeer(k)))

    def eb_z_in(q, k):
        mk = zpeer(k)
        return rcopy(EB.at[q, mk], EB.at[q, mk], eb_s.at[q, k], eb_r.at[q, mk], here)

    def eb_fwd(q, k):
        mk = zpeer(k)
        return rcopy(EB.at[q, mk], EB.at[q, mk], eb_s.at[q, 4 + k], eb_r.at[q, mk], here)

    def eb_sib_in(q, k):
        mk = zother(k)
        return rcopy(EB.at[q, mk], EB.at[q, mk], eb_s.at[q, 4 + k], eb_r.at[q, mk], here)

    def hop(g):
        return rcopy(G.at[g], X.at[d, m], hop_s.at[g], hop_r.at[d], (g, (s + 1) % NX, m))

    def hop_in(g):
        return rcopy(G.at[g], X.at[g, m], hop_s.at[g], hop_r.at[g], (g, (s + 1) % NX, m))

    def hop_raw():
        return rcopy(HP, R, hop_s.at[4], hop_r.at[4], (d, (s + 1) % NX, m))

    def ag_z(g, k):
        return rcopy(X.at[g, m], X.at[g, m], ag_s.at[g, k], ag_r.at[g, m], (d, s, zpeer(k)))

    def ag_z_in(g, k):
        mk = zpeer(k)
        return rcopy(X.at[g, mk], X.at[g, mk], ag_s.at[g, k], ag_r.at[g, mk], here)

    def ag_fwd(g, k):
        mk = zpeer(k)
        return rcopy(X.at[g, mk], X.at[g, mk], ag_s.at[g, 4 + k], ag_r.at[g, mk], here)

    def ag_sib_in(g, k):
        mk = zother(k)
        return rcopy(X.at[g, mk], X.at[g, mk], ag_s.at[g, 4 + k], ag_r.at[g, mk], here)

    def res(k):
        g = ypeer(k)
        return rcopy(RX.at[g], R.at[d], res_s.at[k], res_r.at[d], (g, s, m))

    def res_in(k):
        g = ypeer(k)
        return rcopy(RX.at[g], R.at[g], res_s.at[k], res_r.at[g], here)

    def ctx(k):
        return rcopy(C.at[d], C.at[d], ctx_s.at[k], ctx_r.at[d], (ypeer(k), s, m))

    def ctx_in(k):
        g = ypeer(k)
        return rcopy(C.at[g], C.at[g], ctx_s.at[k], ctx_r.at[g], here)

    def part(g):
        return rcopy(PS.at[g], PR.at[g], ps_s.at[g], ps_r.at[g], here)

    def zred(g, k):
        return rcopy(ZS.at[g, k], ZR.at[g, k], zz_s.at[g, k], zz_r.at[g, k], (d, s, zpeer(k)))

    def layer():
        def multiply(g, who, start=False):
            x = jnp.concatenate([X[g, 2 * zz + who, 0:ROWS] for zz in range(NZ)], axis=1)
            w = jnp.concatenate([W[g * NM + 2 * zz + who] for zz in range(NZ)], axis=0)
            term = jnp.dot(x, w, preferred_element_type=F32)
            QA[...] = term if start else QA[...] + term

        @pl.when(s == 0)
        def _():
            rows = jnp.concatenate([emb[0], emb[1]], axis=0).astype(F32)
            for q in range(2):
                EB.at[q, m][...] = jnp.concatenate(
                    [rows[:, q * 2048:q * 2048 + 2048], rows[:, q * 2048 + 4096:q * 2048 + 6144]],
                    axis=0).astype(BF)
                for k in (2, 1, 3, 0):
                    (eb_z(q, k) if k else eb_fwd(q, 0)).start()
            for q in range(2):
                for k in (1, 3, 2):
                    eb_z_in(q, k).wait_recv()
                    eb_fwd(q, k).start()
            SS[...] = jnp.zeros_like(SS)
            for q in range(2):
                for k in range(4):
                    eb_sib_in(q, k).wait_recv()

                def blocks(mm):
                    x = EB[q, :, :, lane(mm * 256, 256)].astype(F32)
                    return [x[:, i * 8:i * 8 + 8, :].reshape(ROWS, 256) for i in range(2)]

                def body(mm, total):
                    for half, xs in enumerate(blocks(mm)):
                        g = half * 2 + q
                        cols = lane(g * 2048 + mm * 256, 256)
                        X.at[g, mm][0:ROWS, :] = (xs * gain[:, cols]).astype(BF)
                        square = xs * xs
                        total = total + square[:, 0:128] + square[:, 128:256]
                    return total

                SS[...] = lax.fori_loop(0, NM, body, SS[...])
                for half, xs in enumerate(blocks(m)):
                    RX.at[half * 2 + q][...] = xs.astype(BF)
            for k in (2, 1, 3):
                res(k).start()
            R.at[d][...] = RX[d]
            for group in loads:
                for copy in group:
                    copy.wait()
            QA[...] = jnp.zeros_like(QA)

            def both(g, _):
                multiply(g, 0)
                multiply(g, 1)
                return 0

            lax.fori_loop(0, NY, both, 0)

        @pl.when(s > 0)
        def _():
            def arrived(k):
                g = ypeer(k)
                hop_in(g).wait_recv()
                for j in (2, 1, 3, 0):
                    (ag_z(g, j) if j else ag_fwd(g, 0)).start()

            def hand_on(k):
                g = ypeer(k)
                for j in (1, 3, 2):
                    ag_z_in(g, j).wait_recv()
                    ag_fwd(g, j).start()

            def other_half(k):
                g = ypeer(k)
                for j in range(4):
                    ag_sib_in(g, j).wait_recv()
                multiply(g, 1 - c)

            for group in loads:
                for copy in group:
                    copy.wait()
            arrived(0)
            arrived(3)
            arrived(1)
            hand_on(0)
            arrived(2)
            multiply(d, c, True)
            hand_on(3)
            hand_on(1)
            other_half(0)
            multiply(ypeer(3), c)
            multiply(ypeer(1), c)
            hand_on(2)
            other_half(3)
            other_half(1)
            multiply(ypeer(2), c)
            other_half(2)
            total = jnp.zeros((16, 256), F32)
            for mm in range(NM):
                for g in range(NY):
                    total = total + X[g, mm, ROWS:ROWS + 16].astype(F32)
            total = total[0:1, 0:128] + total[1:2, 0:128]
            mine = (lax.broadcasted_iota(jnp.int32, (ROWS, 128), 1)
                    == lax.broadcasted_iota(jnp.int32, (ROWS, 128), 0))
            SS[...] = jnp.where(mine, total, 0.0)

        r = lax.rsqrt(jnp.sum(SS[...], axis=1, keepdims=True) * (1.0 / D) + EPS)
        cos = cosine[...]
        sin = sine[...]

        def rope(x):
            return (x * cos + pltpu.roll(x, 64, 1) * sin).astype(BF)

        query = jnp.concatenate(
            [rope(QA[:, j * HD:(j + 1) * HD] * r) for j in range(4)], axis=0)
        key = rope(QA[:, 512:640] * r)
        value = (QA[:, 640:768] * r).astype(BF)
        scores = lax.dot_general(query, key, (((1,), (1,)), ((), ())),
                                 preferred_element_type=F32) * (HD ** -0.5)
        scores = scores + MASK[...]
        highest = jnp.max(scores, axis=-1, keepdims=True)
        weights = jnp.exp(scores - highest)
        probs = (weights / jnp.sum(weights, axis=-1, keepdims=True)).astype(BF)
        mixed = jnp.dot(probs, value, preferred_element_type=F32).astype(BF)
        for j in range(4):
            C.at[d][:, j * HD:(j + 1) * HD] = mixed[j * ROWS:(j + 1) * ROWS]
        for k in (2, 1, 3):
            ctx(k).start()

        wo_load.wait()

        def project(g):
            for zz in range(NZ):
                p = jnp.dot(C[g], WO[:, zz * 512:zz * 512 + 512], preferred_element_type=F32)
                low, high = p[:, :256], p[:, 256:]
                PO.at[g, zz][...] = jnp.where(c == 0, low, high)
                PS.at[g, zz][...] = jnp.where(c == 0, high, low).astype(BF)
            part(g).start()

        def pair(g):
            part(g).wait_recv()
            for k in (2, 1, 3):
                zt = (z + k) % NZ
                ZS.at[g, k][...] = (PO[g, zt] + PR[g, zt].astype(F32)).astype(BF)
                zred(g, k).start()

        def total_of(g):
            total = PO[g, z] + PR[g, z].astype(F32) + R[g].astype(F32)
            for k in (1, 3, 2):
                zred(g, k).wait_recv()
                total = total + ZR[g, k].astype(F32)
            hidden = total.astype(BF)
            HP.at[g][...] = hidden
            wide = hidden.astype(F32)
            G.at[g][0:ROWS, :] = (wide * NG[...]).astype(BF)
            square = wide * wide
            top = square.astype(BF)
            rest = (square - top.astype(F32)).astype(BF)
            ones = jnp.ones((16, 256), BF)
            nt = (((1,), (1,)), ((), ()))
            sums = (lax.dot_general(ones, top, nt, preferred_element_type=F32)
                    + lax.dot_general(ones, rest, nt, preferred_element_type=F32))
            top = sums.astype(BF).astype(F32)
            row = lax.broadcasted_iota(jnp.int32, (16, ROWS), 0)
            packed = jnp.where(row == 0, top, jnp.where(row == 1, sums - top, 0.0))
            packed = jnp.concatenate([packed, jnp.zeros_like(packed)], axis=1).astype(BF)
            G.at[g][ROWS:ROWS + 16, 0:128] = packed

            @pl.when(s < NX - 1)
            def _():
                hop(g).start()

        project(d)

        @pl.when(s == 0)
        def _():
            for k in (1, 3, 2):
                res_in(k).wait_recv()

        @pl.when(s > 0)
        def _():
            hop_raw().wait_recv()

        @pl.when(s < NX - 1)
        def _():
            next_gain().wait_recv()

        pair(d)
        for k in (1, 3):
            ctx_in(k).wait_recv()
            project(ypeer(k))
        pair(ypeer(1))
        pair(ypeer(3))
        total_of(d)
        ctx_in(2).wait_recv()
        project(ypeer(2))
        total_of(ypeer(1))
        pair(ypeer(2))
        total_of(ypeer(3))
        total_of(ypeer(2))

        @pl.when(s < NX - 1)
        def _():
            hop_raw().start()

        @pl.when(s % 2 == 1)
        def _():
            emit(s // 2)

    def emit(b):
        mine = Y.at[b, c, 0, 0]
        nt = (((1,), (1,)), ((), ()))
        wide = HP[...].reshape(NY * ROWS, 256).astype(F32)
        cols = lane(d * 2048 + m * 256, 256)
        scaled = (wide * fgain[:, cols]).astype(BF)
        live_rows = jnp.dot(SEL[0:LIVE], scaled, preferred_element_type=F32)
        mine[0:LIVE, :] = live_rows.astype(BF)
        square = wide * wide
        top = square.astype(BF)
        rest = (square - top.astype(F32)).astype(BF)
        ones = jnp.ones((16, 256), BF)
        sums = (lax.dot_general(ones, top, nt, preferred_element_type=F32)
                + lax.dot_general(ones, rest, nt, preferred_element_type=F32))
        top = sums.astype(BF).astype(F32)
        row = lax.broadcasted_iota(jnp.int32, (16, NY * ROWS), 0)
        packed = jnp.where(row == 0, top, jnp.where(row == 1, sums - top, 0.0)).astype(BF)
        squares = lax.dot_general(packed, SEL[...], nt, preferred_element_type=F32)
        mine[LIVE:PIECE, :] = squares.astype(BF)
        for half in range(2):
            y_x(b, half, 1).start()
            y_x(b, 1 - half, 3).start()
        spread_own(b)

    def first_dev(k):
        return (jnp.where(c == 0, ypeer(k), d), s, jnp.where(c == 0, m, zpeer(k)))

    def second_dev(k):
        return (jnp.where(c == 0, d, ypeer(k)), s, jnp.where(c == 0, zpeer(k), m))

    def ycopy(src, dst, b, i, j, dev):
        return rcopy(src, dst, y_s.at[b, i], y_r.at[b, j], dev)

    cut = (pl.ds(0, 96), pl.ds(96, PIECE - 96))

    def own(b, rows):
        return Y.at[b, c, 0, 0, rows]

    def y_x(b, half, k):
        ref = own(b, cut[half])
        return ycopy(ref, ref, b, k + half, (0, 21)[half], (d, (s + k) % NX, m))

    def y_x_relay(b, half):
        ref = own(b, cut[half])
        return ycopy(ref, ref, b, 28 + half, (0, 21)[half], (d, jnp.where(b == 0, 3, 1), m))

    def relays_x(b, half):
        return (s == 0) if half == 0 else (s == jnp.where(b == 0, 0, 2))

    whole = pl.ds(0, PIECE)

    def y_first(b, k):
        slot = 1 if k == 1 else 2
        return ycopy(own(b, whole), Y.at[b, c, 0, slot, whole], b, 5 + k, slot, first_dev(k))

    def y_first_relay(b, half):
        slot, k = ((1, 1), (2, 3))[half]
        return ycopy(Y.at[b, c, 0, slot, cut[half]], Y.at[b, c, 0, 3, cut[half]],
                     b, 9 + half, 3, first_dev(k))

    def y_opposite(b):
        ref = Y.at[b, c, 0, 3, whole]
        return ycopy(ref, ref, b, 9, 3, here)

    sets = (pl.ds(0, 1), pl.ds(1, 2), pl.ds(3, 1))

    def y_second(b, part_no, k):
        slot = 1 if k == 1 else 2
        return ycopy(Y.at[b, c, 0, sets[part_no], whole], Y.at[b, c, slot, sets[part_no], whole],
                     b, 11 + part_no * 2 + (slot - 1), 1 + 3 * slot + part_no, second_dev(k))

    def y_second_relay(b, i):
        slot, k = (1, 1) if i < 2 else (2, 3)
        return ycopy(Y.at[b, c, slot, i, whole], Y.at[b, c, 3, i, whole],
                     b, 17 + i, 10 + i, second_dev(k))

    forwards = ((0, 0, 1), (0, 1, 2), (0, 3, 1), (1, 0, 4), (2, 0, 4), (3, 0, 2), (3, 2, 2))

    def y_fwd(b, n, who):
        j, i, size = forwards[n]
        ref = Y.at[b, who, j, pl.ds(i, size), whole]
        return ycopy(ref, ref, b, 21 + n, 14 + n, here)

    def spread_own(b):
        for k in (1, 3):
            y_first(b, k).start()
        for k in (1, 3):
            y_second(b, 0, k).start()
        y_fwd(b, 0, c).start()

    def dots(b, cc, j, start):
        pieces = jnp.concatenate([Y[b, cc, j, i, 0:256, :] for i in range(4)], axis=1)
        term = lax.dot_general(HEAD[cc, j], pieces, (((1,), (1,)), ((), ())),
                               preferred_element_type=F32)
        LT[...] = term if start else LT[...] + term

    def wanted_rows():
        slot, position = row_slot(lax.broadcasted_iota(jnp.int32, (32, 256), 1))
        place = (position == lax.broadcasted_iota(jnp.int32, (32, 256), 0)).astype(BF)
        tokens = targets[...]
        nt = (((1,), (1,)), ((), ()))
        keep = slot[0:8] == lax.broadcasted_iota(jnp.int32, (8, 256), 0)
        parts = []
        for term in (tokens // 256, tokens % 256):
            every = jnp.dot(term.astype(F32).astype(BF), place, preferred_element_type=F32)
            mine = jnp.sum(jnp.where(keep, every, 0.0), axis=0, keepdims=True)
            spread = jnp.broadcast_to(mine, (16, 256)).astype(BF)
            parts.append(lax.dot_general(spread, SEL[...], nt, preferred_element_type=F32)[0:1])
        return parts[0] * 256.0 + parts[1]

    def gather(b):
        source = 2 * b + 1

        @pl.when(s != source)
        def _():
            def take(half):
                y_x(b, half, 1).wait_recv()

                @pl.when(relays_x(b, half))
                def _():
                    y_x_relay(b, half).start()

            @pl.when(s == 2)
            def _():
                take(1)
                take(0)

            @pl.when(s != 2)
            def _():
                take(0)
                take(1)

            spread_own(b)

        y_first(b, 1).wait_recv()
        y_first_relay(b, 0).start()
        y_first(b, 3).wait_recv()
        y_first_relay(b, 1).start()
        for k in (1, 3):
            y_second(b, 1, k).start()
        y_fwd(b, 1, c).start()
        y_second(b, 0, 1).wait_recv()
        y_second_relay(b, 0).start()
        y_second(b, 0, 3).wait_recv()
        y_opposite(b).wait_recv()
        for k in (1, 3):
            y_second(b, 2, k).start()
        y_fwd(b, 2, c).start()
        y_second(b, 1, 1).wait_recv()
        y_second_relay(b, 1).start()
        y_second(b, 1, 3).wait_recv()
        y_second_relay(b, 2).start()
        y_second(b, 2, 3).wait_recv()
        y_second_relay(b, 3).start()
        y_fwd(b, 4, c).start()
        y_second(b, 2, 1).wait_recv()
        y_fwd(b, 3, c).start()

    def finish(b):
        dots(b, c, 0, True)
        for n in range(3):
            y_fwd(b, n, 1 - c).wait_recv()
        dots(b, 1 - c, 0, False)
        dots(b, c, 2, False)
        dots(b, c, 1, False)
        y_second_relay(b, 0).wait_recv()
        y_second_relay(b, 1).wait_recv()
        y_fwd(b, 5, c).start()
        y_fwd(b, 4, 1 - c).wait_recv()
        dots(b, 1 - c, 2, False)
        y_second_relay(b, 2).wait_recv()
        y_second_relay(b, 3).wait_recv()
        y_fwd(b, 6, c).start()
        y_fwd(b, 3, 1 - c).wait_recv()
        dots(b, 1 - c, 1, False)
        dots(b, c, 3, False)
        y_fwd(b, 5, 1 - c).wait_recv()
        y_fwd(b, 6, 1 - c).wait_recv()
        dots(b, 1 - c, 3, False)

        extra = jnp.zeros((16, 256), F32)
        for cc in range(2):
            for j in range(4):
                for i in range(4):
                    extra = extra + Y[b, cc, j, i, LIVE:PIECE, :].astype(F32)
        sums = jnp.sum(extra, axis=0, keepdims=True)
        r = lax.rsqrt(sums * (1.0 / D) + EPS)
        logits = LT[...] * r
        highest = jnp.max(logits, axis=0, keepdims=True)
        summed = jnp.sum(jnp.exp(logits - highest), axis=0, keepdims=True)
        vocab = HEAD.shape[2]
        first = ((d * NX + s) * NM + m) * vocab
        index = (lax.broadcasted_iota(jnp.int32, logits.shape, 0) + first).astype(F32)
        wanted = wanted_rows()
        picked = jnp.sum(jnp.where(index == wanted, logits, 0.0), axis=0, keepdims=True)
        alive = lax.broadcasted_iota(jnp.int32, (1, 256), 1) < LIVE
        for n, value in enumerate((highest, summed, picked)):
            value = jnp.where(alive, value, 1.0)
            for half in range(2):
                STO[pl.ds(n * 4 + b * 2 + half, 1), :] = value[:, half * 128:half * 128 + 128]

    def step(t, _):
        last = s == NX - 1
        place = jnp.where(last, 1, 0)

        @pl.when(t == place)
        def _():
            layer()

        @pl.when(jnp.where(last, (t == 0) | (t == 2), (t == 1) | (t == 3)))
        def _():
            gather(jnp.where(t < 2, 0, 1))

        @pl.when(jnp.where(last, t >= 3, (t == 2) | (t == 4)))
        def _():
            @pl.when(t == jnp.where(last, 3, 2))
            def _():
                head_load.wait()
            finish(jnp.where(t == 4, 1, 0))
        return 0

    STO[...] = jnp.zeros_like(STO)
    lax.fori_loop(0, 5, step, 0)

    def merge(ref, count):
        parts = [ref[j] for j in range(count)]
        highest = parts[0][0:4]
        for p in parts[1:]:
            highest = jnp.maximum(highest, p[0:4])
        summed = jnp.zeros_like(highest)
        picked = jnp.zeros_like(highest)
        for p in parts:
            summed = summed + p[4:8] * jnp.exp(p[0:4] - highest)
            picked = picked + p[8:12]
        return highest, summed, picked

    def stacked(highest, summed, picked):
        return jnp.concatenate([highest, summed, picked, jnp.zeros_like(picked)], axis=0)

    def st_y(k):
        return rcopy(SA.at[d], SA.at[d], st_s.at[0, k], st_r.at[0, d], (ypeer(k), s, m))

    def st_y_in(k):
        g = ypeer(k)
        return rcopy(SA.at[g], SA.at[g], st_s.at[0, k], st_r.at[0, g], (g, s, m))

    def m_of(k):
        return (m + k) % NM

    def st_m(k):
        return rcopy(SB.at[m], SB.at[m], st_s.at[1, k], st_r.at[1, m], (d, s, m_of(k)))

    def st_m_in(k):
        mm = m_of(k)
        return rcopy(SB.at[mm], SB.at[mm], st_s.at[1, k], st_r.at[1, mm], (d, s, mm))

    def st_x(k):
        return rcopy(SC.at[s], SC.at[s], st_s.at[2, k], st_r.at[2, s], (d, (s + k) % NX, m))

    def st_x_in(k):
        ss = (s + k) % NX
        return rcopy(SC.at[ss], SC.at[ss], st_s.at[2, k], st_r.at[2, ss], (d, ss, m))

    SA.at[d][...] = STO[...]
    for k in (2, 1, 3):
        st_y(k).start()
    for k in (1, 3, 2):
        st_y_in(k).wait_recv()
    SB.at[m][...] = stacked(*merge(SA, NY))
    for k in (4, 3, 5, 2, 6, 1, 7):
        st_m(k).start()
    for k in (1, 7, 2, 6, 3, 5, 4):
        st_m_in(k).wait_recv()
    SC.at[s][...] = stacked(*merge(SB, NM))
    for k in (2, 1, 3):
        st_x(k).start()
    for k in (1, 3, 2):
        st_x_in(k).wait_recv()
    highest, summed, picked = merge(SC, NX)
    logprob = picked - (highest + jnp.log(summed))
    terms = []
    for e in range(2):
        rest = jnp.concatenate([logprob[2 * e:2 * e + 1], logprob[2 * e + 1:2 * e + 2]], axis=1)
        for _ in range(3):
            term = rest.astype(BF).astype(F32)
            terms.append(term)
            rest = rest - term
    row = lax.broadcasted_iota(jnp.int32, (16, 256), 0)
    stack = jnp.zeros((16, 256), F32)
    for j, term in enumerate(terms):
        stack = jnp.where(row == j, term, stack)
    stack = stack.astype(BF)
    index = lax.broadcasted_iota(jnp.int32, (256, 32), 0)
    place = lax.broadcasted_iota(jnp.int32, (256, 32), 1)
    results = []
    for i in range(2):
        chosen = source_of[2 * d + i]
        start = 0
        for other in range(8):
            start = start + jnp.where(chosen > other, live[other], 0)
        take = ((index == start + place) & (place < live[chosen])).astype(F32).astype(BF)
        got = jnp.dot(stack, take, preferred_element_type=F32)
        results.append([got[j:j + 1] + got[j + 1:j + 2] + got[j + 2:j + 3] for j in (0, 3)])
    for e in range(2):
        first = lax.broadcasted_iota(jnp.int32, (2, 32), 0) == 0
        out.at[e][...] = jnp.where(first, results[0][e], results[1][e])

    @pl.when(s == 0)
    def _():
        for q in range(2):
            for k in range(1, 4):
                eb_z(q, k).wait_send()
            for k in range(4):
                eb_fwd(q, k).wait_send()
        for k in range(1, 4):
            res(k).wait_send()

    @pl.when(s > 0)
    def _():
        for g in range(NY):
            for k in range(1, 4):
                ag_z(g, k).wait_send()
            for k in range(4):
                ag_fwd(g, k).wait_send()
        next_gain().wait_send()

    @pl.when(s < NX - 1)
    def _():
        for g in range(NY):
            hop(g).wait_send()
        hop_raw().wait_send()

    for g in range(NY):
        for k in range(1, 4):
            zred(g, k).wait_send()
        part(g).wait_send()
    for k in range(1, 4):
        ctx(k).wait_send()
        st_y(k).wait_send()
        st_x(k).wait_send()
    for k in range(1, 8):
        st_m(k).wait_send()
    for b in range(2):
        @pl.when(s == 2 * b + 1)
        def _():
            for half in range(2):
                for k in (1, 3):
                    y_x(b, half, k).wait_send()

        for half in range(2):
            @pl.when((s != 2 * b + 1) & relays_x(b, half))
            def _():
                y_x_relay(b, half).wait_send()

            y_first_relay(b, half).wait_send()
        for k in (1, 3):
            y_first(b, k).wait_send()
            for n in range(3):
                y_second(b, n, k).wait_send()
        for i in range(4):
            y_second_relay(b, i).wait_send()
        for n in range(7):
            y_fwd(b, n, c).wait_send()


def tables():
    row = np.arange(ROWS)
    position = (row // 8) * 4 + row % 4
    half = HD // 2
    freqs = (ROPE_BASE ** (-np.arange(half) * 2.0 / HD)).astype(np.float32)
    angles = (position.astype(np.float32)[:, None] * freqs[None, :]).astype(np.float64)
    cos, sin = np.cos(angles), np.sin(angles)
    return (np.concatenate([cos, cos], 1).astype(np.float32),
            np.concatenate([-sin, sin], 1).astype(np.float32))


def per_device(
    embeds, targets, lengths, source, attn_gain, w_query, w_key, w_value, w_out, final_gain, head
):
    vocab = head.shape[0]
    cos, sin = tables()
    vmem = pl.BlockSpec(memory_space=pltpu.VMEM)
    hbm = pl.BlockSpec(memory_space=pl.ANY)
    smem = pl.BlockSpec(memory_space=pltpu.SMEM)
    dma = pltpu.SemaphoreType.DMA
    stats = pl.pallas_call(
        kernel,
        out_shape=jax.ShapeDtypeStruct((2, 2, 32), F32),
        in_specs=[vmem, smem, smem, vmem, vmem, vmem, vmem, vmem, hbm, hbm, hbm, hbm, hbm],
        out_specs=vmem,
        scratch_shapes=[
            pltpu.VMEM((32, 256, 768), BF),
            pltpu.VMEM((QW, 2048), BF),
            pltpu.VMEM((2, 4, vocab, 1024), BF),
            pltpu.VMEM((2, NM, 16, 2048), BF),
            pltpu.VMEM((NY, NM, ROWS + 16, 256), BF),
            pltpu.VMEM((NY, ROWS + 16, 256), BF),
            pltpu.VMEM((1, 256), F32),
            pltpu.VMEM((NY, ROWS, 256), BF),
            pltpu.VMEM((4 * ROWS, ROWS), F32),
            pltpu.VMEM((256, 256), BF),
            pltpu.VMEM((ROWS, 128), F32),
            pltpu.VMEM((ROWS, 768), F32),
            pltpu.VMEM((NY, ROWS, 256), BF),
            pltpu.VMEM((NY, ROWS, QW), BF),
            pltpu.VMEM((NY, NZ, ROWS, 256), BF),
            pltpu.VMEM((NY, NZ, ROWS, 256), BF),
            pltpu.VMEM((NY, NZ, ROWS, 256), F32),
            pltpu.VMEM((NY, NZ, ROWS, 256), BF),
            pltpu.VMEM((NY, NZ, ROWS, 256), BF),
            pltpu.VMEM((NY, ROWS, 256), BF),
            pltpu.VMEM((2, 2, 4, 4, 256, 256), BF),
            pltpu.VMEM((vocab, 256), F32),
            pltpu.VMEM((16, 128), F32),
            pltpu.VMEM((NY, 16, 128), F32),
            pltpu.VMEM((NM, 16, 128), F32),
            pltpu.VMEM((NX, 16, 128), F32),
            dma((14,)),
            dma, dma,
            dma((2, 8)), dma((2, 8)),
            dma((5,)), dma((5,)),
            dma((4, 8)), dma((4, 8)),
            dma((4,)), dma((4,)),
            dma((4,)), dma((4,)),
            dma((4,)), dma((4,)),
            dma((4, 4)), dma((4, 4)),
            dma((2, 30)), dma((2, 22)),
            dma((3, 8)), dma((3, 8)),
        ],
        compiler_params=pltpu.CompilerParams(
            collective_id=0, has_side_effects=True, vmem_limit_bytes=60 * 1024 * 1024),
        cost_estimate=pl.CostEstimate(flops=8_000_000_000, bytes_accessed=24_000_000,
                                      transcendentals=300_000),
    )(
        embeds, lengths, source, targets, attn_gain, final_gain.reshape(1, D), jnp.asarray(cos), jnp.asarray(sin),
        w_query.reshape(32, 256, 512), w_key.reshape(32, 256, 128),
        w_value.reshape(32, 256, 128), w_out.reshape(512, 2048), head,
    )
    return (stats[0], stats[1])


def solution(mesh):
    return jax.shard_map(
        per_device,
        mesh=mesh,
        in_specs=(
            P("dp", "mp", None),
            P(),
            P(),
            P(),
            P("section", None),
            P("section", None, "mp"),
            P("section", None, "mp"),
            P("section", None, "mp"),
            P("section", "mp", "dp"),
            P(),
            P(("dp", "section", "mp"), None),
        ),
        out_specs=(P("dp", None), P("dp", None)),
        check_vma=False,
    )
```

```python
import jax
import jax.numpy as jnp
import numpy as np
from jax import lax
from jax.experimental import pallas as pl
from jax.experimental.pallas import tpu as pltpu
from jax.sharding import PartitionSpec as P

HD = 128
EPS = 1e-05
ROPE_BASE = 500000.0
NY = 4
NX = 4
NZ = 4
NM = 8
ROWS = 64
LIVE = 192
PIECE = LIVE + 16
D = 8192
QW = 512
MESH = pl.DeviceIdType.MESH
BF = jnp.bfloat16
F32 = jnp.float32


def lane(start, size):
    return pl.ds(pl.multiple_of(start, 128), size)


def kernel(
    emb_in, live, source_of, targets_in, gain, fgain_in, cosine_in, sine_in, wq, wk, wv, wo, head,
    out,
    emb, targets, gains, fgain, cosine, sine, W, WO, HEAD, EB, X, G, NG, RX, MASK, SEL, SS, QA, R, C, PS, PR, PO, ZS, ZR, HP, Y, LT, STO, SA, SB, SC,
    w_sem, ng_s, ng_r, eb_s, eb_r, hop_s, hop_r, ag_s, ag_r, res_s, res_r, ctx_s, ctx_r, ps_s, ps_r,
    zz_s, zz_r, y_s, y_r, st_s, st_r,
):
    d = lax.axis_index("dp")
    s = lax.axis_index("section")
    m = lax.axis_index("mp")
    z = m // 2
    c = m % 2
    sib = z * 2 + (1 - c)

    def ypeer(k):
        return (d + k) % NY

    def zpeer(k):
        return ((z + k) % NZ) * 2 + c

    def zother(k):
        return ((z + k) % NZ) * 2 + (1 - c)

    def rcopy(src, dst, ssem, rsem, dev):
        return pltpu.make_async_remote_copy(
            src_ref=src, dst_ref=dst, send_sem=ssem, recv_sem=rsem,
            device_id=dev, device_id_type=MESH,
        )

    here = (d, s, sib)

    barrier = pltpu.get_barrier_semaphore()
    partners = []
    for k in range(1, 4):
        partners.append((ypeer(k), s, m))
        partners.append((d, (s + k) % NX, m))
        partners.append((d, s, zpeer(k)))
        partners.append((d, s, zother(k)))
        partners.append((ypeer(k), (s + 1) % NX, m))
        partners.append((ypeer(k), (s + 3) % NX, m))
    partners.append(here)
    for dev in partners:
        pl.semaphore_signal(barrier, inc=1, device_id=dev, device_id_type=MESH)
    small = [
        pltpu.make_async_copy(src, dst, w_sem.at[14 + n])
        for n, (src, dst) in enumerate((
            (emb_in, emb), (gain, gains), (cosine_in, cosine), (sine_in, sine),
            (fgain_in, fgain), (targets_in, targets)))
    ]
    for copy in small:
        copy.start()
    loads = []
    for g in range(NY):
        blocks = pl.ds(g * NM, NM)
        loads.append([
            pltpu.make_async_copy(wq.at[blocks], W.at[blocks, :, 0:512], w_sem.at[3 * g]),
            pltpu.make_async_copy(wk.at[blocks], W.at[blocks, :, 512:640], w_sem.at[3 * g + 1]),
            pltpu.make_async_copy(wv.at[blocks], W.at[blocks, :, 640:768], w_sem.at[3 * g + 2]),
        ])
    wo_load = pltpu.make_async_copy(wo, WO, w_sem.at[12])
    for group in loads:
        for copy in group:
            copy.start()

    head_load = pltpu.make_async_copy(HEAD, HEAD, w_sem.at[13])

    def prepare():
        wo_load.start()
        offsets = (0, 3, 1, 2)
        for cc in range(2):
            for j in range(4):
                for i in range(4):
                    g, zz = (offsets[i], offsets[j]) if cc == 0 else (offsets[j], offsets[i])
                    col = ypeer(g) * 2048 + ((z + zz) % NZ) * 512 + cc * 256
                    pltpu.make_async_copy(head.at[:, lane(col, 256)],
                                          HEAD.at[cc, j, :, i * 256:i * 256 + 256],
                                          w_sem.at[13]).start()
        shape = (4 * ROWS, ROWS)
        rq = lax.broadcasted_iota(jnp.int32, shape, 0) % ROWS
        rk = lax.broadcasted_iota(jnp.int32, shape, 1)
        slot_q, slot_k = (rq // 4) % 2, (rk // 4) % 2
        pos_q, pos_k = (rq // 8) * 4 + rq % 4, (rk // 8) * 4 + rk % 4
        live_k = jnp.where(slot_k == 0, live[2 * d], live[2 * d + 1])
        allowed = (slot_q == slot_k) & (pos_k <= pos_q) & (pos_k < live_k)
        MASK[...] = jnp.where(allowed, F32(0.0), F32(-1e30))

        def first_row(slot):
            start = jnp.zeros_like(slot)
            for other in range(8):
                start = start + jnp.where(slot > other, live[other], 0)
            return start

        def live_of(slot):
            count = jnp.zeros_like(slot)
            for other in range(8):
                count = count + jnp.where(slot == other, live[other], 0)
            return count

        slot, position = row_slot(lax.broadcasted_iota(jnp.int32, (8, 256), 1))
        packed_at = jnp.where(position < live_of(slot), first_row(slot) + position, 999)[0:1]
        SEL[...] = (lax.broadcasted_iota(jnp.int32, (256, 256), 0) == packed_at).astype(F32).astype(BF)

    def row_slot(lanes):
        return (lanes // 64) * 2 + (lanes // 4) % 2, ((lanes // 8) % 8) * 4 + lanes % 4

    small[0].wait()

    @pl.when(s == 0)
    def _():
        rows = jnp.concatenate([emb[0], emb[1]], axis=0).astype(F32)
        for q in range(2):
            EB.at[q, m][...] = jnp.concatenate(
                [rows[:, q * 2048:q * 2048 + 2048], rows[:, q * 2048 + 4096:q * 2048 + 6144]],
                axis=0).astype(BF)

    pl.semaphore_wait(barrier, len(partners))

    def next_gain():
        return rcopy(gain.at[:, lane(d * 2048 + m * 256, 256)], NG, ng_s, ng_r,
                     (d, (s + 3) % NX, m))

    @pl.when(s > 0)
    def _():
        next_gain().start()

    def eb_z(q, k):
        return rcopy(EB.at[q, m], EB.at[q, m], eb_s.at[q, k], eb_r.at[q, m], (d, s, zpeer(k)))

    def eb_z_in(q, k):
        mk = zpeer(k)
        return rcopy(EB.at[q, mk], EB.at[q, mk], eb_s.at[q, k], eb_r.at[q, mk], here)

    def eb_fwd(q, k):
        mk = zpeer(k)
        return rcopy(EB.at[q, mk], EB.at[q, mk], eb_s.at[q, 4 + k], eb_r.at[q, mk], here)

    def eb_sib_in(q, k):
        mk = zother(k)
        return rcopy(EB.at[q, mk], EB.at[q, mk], eb_s.at[q, 4 + k], eb_r.at[q, mk], here)

    def hop(g):
        return rcopy(G.at[g], X.at[d, m], hop_s.at[g], hop_r.at[d], (g, (s + 1) % NX, m))

    def hop_in(g):
        return rcopy(G.at[g], X.at[g, m], hop_s.at[g], hop_r.at[g], (g, (s + 1) % NX, m))

    def hop_raw():
        return rcopy(HP, R, hop_s.at[4], hop_r.at[4], (d, (s + 1) % NX, m))

    def ag_z(g, k):
        return rcopy(X.at[g, m], X.at[g, m], ag_s.at[g, k], ag_r.at[g, m], (d, s, zpeer(k)))

    def ag_z_in(g, k):
        mk = zpeer(k)
        return rcopy(X.at[g, mk], X.at[g, mk], ag_s.at[g, k], ag_r.at[g, mk], here)

    def ag_fwd(g, k):
        mk = zpeer(k)
        return rcopy(X.at[g, mk], X.at[g, mk], ag_s.at[g, 4 + k], ag_r.at[g, mk], here)

    def ag_sib_in(g, k):
        mk = zother(k)
        return rcopy(X.at[g, mk], X.at[g, mk], ag_s.at[g, 4 + k], ag_r.at[g, mk], here)

    def res(k):
        g = ypeer(k)
        return rcopy(RX.at[g], R.at[d], res_s.at[k], res_r.at[d], (g, s, m))

    def res_in(k):
        g = ypeer(k)
        return rcopy(RX.at[g], R.at[g], res_s.at[k], res_r.at[g], here)

    def ctx(k):
        return rcopy(C.at[d], C.at[d], ctx_s.at[k], ctx_r.at[d], (ypeer(k), s, m))

    def ctx_in(k):
        g = ypeer(k)
        return rcopy(C.at[g], C.at[g], ctx_s.at[k], ctx_r.at[g], here)

    def part(g):
        return rcopy(PS.at[g], PR.at[g], ps_s.at[g], ps_r.at[g], here)

    def zred(g, k):
        return rcopy(ZS.at[g, k], ZR.at[g, k], zz_s.at[g, k], zz_r.at[g, k], (d, s, zpeer(k)))

    def layer():
        def multiply(g, who, start=False):
            x = jnp.concatenate([X[g, 2 * zz + who, 0:ROWS] for zz in range(NZ)], axis=1)
            w = jnp.concatenate([W[g * NM + 2 * zz + who] for zz in range(NZ)], axis=0)
            term = jnp.dot(x, w, preferred_element_type=F32)
            QA[...] = term if start else QA[...] + term

        @pl.when(s == 0)
        def _():
            for q in range(2):
                for k in (1, 3, 2):
                    eb_z_in(q, k).wait_recv()
                    eb_fwd(q, k).start()
            QA[...] = jnp.zeros_like(QA)
            SS[...] = jnp.zeros_like(SS)
            for q in range(2):
                for k in range(4):
                    eb_sib_in(q, k).wait_recv()

                def blocks(mm):
                    x = EB[q, :, :, lane(mm * 256, 256)].astype(F32)
                    return [x[:, i * 8:i * 8 + 8, :].reshape(ROWS, 256) for i in range(2)]

                def body(mm, total):
                    for half, xs in enumerate(blocks(mm)):
                        g = half * 2 + q
                        cols = lane(g * 2048 + mm * 256, 256)
                        X.at[g, mm][0:ROWS, :] = (xs * gains[:, cols]).astype(BF)
                        square = xs * xs
                        total = total + square[:, 0:128] + square[:, 128:256]
                    return total

                SS[...] = lax.fori_loop(0, NM, body, SS[...])
                for half, xs in enumerate(blocks(m)):
                    RX.at[half * 2 + q][...] = xs.astype(BF)
                for g in (q, q + 2):
                    for copy in loads[g]:
                        copy.wait()

                def both(i, _):
                    multiply(2 * i + q, 0)
                    multiply(2 * i + q, 1)
                    return 0

                lax.fori_loop(0, 2, both, 0)
            for k in (2, 1, 3):
                res(k).start()
            R.at[d][...] = RX[d]

        @pl.when(s > 0)
        def _():
            def arrived(k):
                g = ypeer(k)
                hop_in(g).wait_recv()
                for j in (2, 1, 3, 0):
                    (ag_z(g, j) if j else ag_fwd(g, 0)).start()

            def hand_on(k):
                g = ypeer(k)
                for j in (1, 3, 2):
                    ag_z_in(g, j).wait_recv()
                    ag_fwd(g, j).start()

            def other_half(k):
                g = ypeer(k)
                for j in range(4):
                    ag_sib_in(g, j).wait_recv()
                multiply(g, 1 - c)

            for group in loads:
                for copy in group:
                    copy.wait()
            arrived(0)
            arrived(3)
            arrived(1)
            hand_on(0)
            arrived(2)
            multiply(d, c, True)
            hand_on(3)
            hand_on(1)
            other_half(0)
            multiply(ypeer(3), c)
            multiply(ypeer(1), c)
            hand_on(2)
            other_half(3)
            other_half(1)
            multiply(ypeer(2), c)
            other_half(2)
            total = jnp.zeros((16, 256), F32)
            for mm in range(NM):
                for g in range(NY):
                    total = total + X[g, mm, ROWS:ROWS + 16].astype(F32)
            total = total[0:1, 0:128] + total[1:2, 0:128]
            mine = (lax.broadcasted_iota(jnp.int32, (ROWS, 128), 1)
                    == lax.broadcasted_iota(jnp.int32, (ROWS, 128), 0))
            SS[...] = jnp.where(mine, total, 0.0)

        r = lax.rsqrt(jnp.sum(SS[...], axis=1, keepdims=True) * (1.0 / D) + EPS)
        cos = cosine[...]
        sin = sine[...]

        def rope(x):
            return (x * cos + pltpu.roll(x, 64, 1) * sin).astype(BF)

        query = jnp.concatenate(
            [rope(QA[:, j * HD:(j + 1) * HD] * r) for j in range(4)], axis=0)
        key = rope(QA[:, 512:640] * r)
        value = (QA[:, 640:768] * r).astype(BF)
        scores = lax.dot_general(query, key, (((1,), (1,)), ((), ())),
                                 preferred_element_type=F32) * (HD ** -0.5)
        scores = scores + MASK[...]
        highest = jnp.max(scores, axis=-1, keepdims=True)
        weights = jnp.exp(scores - highest)
        probs = (weights / jnp.sum(weights, axis=-1, keepdims=True)).astype(BF)
        mixed = jnp.dot(probs, value, preferred_element_type=F32).astype(BF)
        for j in range(4):
            C.at[d][:, j * HD:(j + 1) * HD] = mixed[j * ROWS:(j + 1) * ROWS]
        for k in (2, 1, 3):
            ctx(k).start()

        wo_load.wait()

        def project(g):
            for zz in range(NZ):
                p = jnp.dot(C[g], WO[:, zz * 512:zz * 512 + 512], preferred_element_type=F32)
                low, high = p[:, :256], p[:, 256:]
                PO.at[g, zz][...] = jnp.where(c == 0, low, high)
                PS.at[g, zz][...] = jnp.where(c == 0, high, low).astype(BF)
            part(g).start()

        def pair(g):
            part(g).wait_recv()
            for k in (2, 1, 3):
                zt = (z + k) % NZ
                ZS.at[g, k][...] = (PO[g, zt] + PR[g, zt].astype(F32)).astype(BF)
                zred(g, k).start()

        def total_of(g):
            total = PO[g, z] + PR[g, z].astype(F32) + R[g].astype(F32)
            for k in (1, 3, 2):
                zred(g, k).wait_recv()
                total = total + ZR[g, k].astype(F32)
            hidden = total.astype(BF)
            HP.at[g][...] = hidden
            wide = hidden.astype(F32)
            G.at[g][0:ROWS, :] = (wide * NG[...]).astype(BF)
            square = wide * wide
            top = square.astype(BF)
            rest = (square - top.astype(F32)).astype(BF)
            ones = jnp.ones((16, 256), BF)
            nt = (((1,), (1,)), ((), ()))
            sums = (lax.dot_general(ones, top, nt, preferred_element_type=F32)
                    + lax.dot_general(ones, rest, nt, preferred_element_type=F32))
            top = sums.astype(BF).astype(F32)
            row = lax.broadcasted_iota(jnp.int32, (16, ROWS), 0)
            packed = jnp.where(row == 0, top, jnp.where(row == 1, sums - top, 0.0))
            packed = jnp.concatenate([packed, jnp.zeros_like(packed)], axis=1).astype(BF)
            G.at[g][ROWS:ROWS + 16, 0:128] = packed

            @pl.when(s < NX - 1)
            def _():
                hop(g).start()

        project(d)

        @pl.when(s == 0)
        def _():
            for k in (1, 3, 2):
                res_in(k).wait_recv()

        @pl.when(s > 0)
        def _():
            hop_raw().wait_recv()

        @pl.when(s < NX - 1)
        def _():
            next_gain().wait_recv()

        pair(d)
        for k in (1, 3):
            ctx_in(k).wait_recv()
            project(ypeer(k))
        pair(ypeer(1))
        pair(ypeer(3))
        total_of(d)
        ctx_in(2).wait_recv()
        project(ypeer(2))
        total_of(ypeer(1))
        pair(ypeer(2))
        total_of(ypeer(3))
        total_of(ypeer(2))

        @pl.when(s < NX - 1)
        def _():
            hop_raw().start()

        @pl.when(s % 2 == 1)
        def _():
            emit(s // 2)

    def emit(b):
        mine = Y.at[b, c, 0, 0]
        nt = (((1,), (1,)), ((), ()))
        wide = HP[...].reshape(NY * ROWS, 256).astype(F32)
        cols = lane(d * 2048 + m * 256, 256)
        scaled = (wide * fgain[:, cols]).astype(BF)
        live_rows = jnp.dot(SEL[0:LIVE], scaled, preferred_element_type=F32)
        mine[0:LIVE, :] = live_rows.astype(BF)
        square = wide * wide
        top = square.astype(BF)
        rest = (square - top.astype(F32)).astype(BF)
        ones = jnp.ones((16, 256), BF)
        sums = (lax.dot_general(ones, top, nt, preferred_element_type=F32)
                + lax.dot_general(ones, rest, nt, preferred_element_type=F32))
        top = sums.astype(BF).astype(F32)
        row = lax.broadcasted_iota(jnp.int32, (16, NY * ROWS), 0)
        packed = jnp.where(row == 0, top, jnp.where(row == 1, sums - top, 0.0)).astype(BF)
        squares = lax.dot_general(packed, SEL[...], nt, preferred_element_type=F32)
        mine[LIVE:PIECE, :] = squares.astype(BF)
        for k in (2, 1, 3):
            y_x(b, k).start()
        spread_own(b)

    def first_dev(k):
        return (jnp.where(c == 0, ypeer(k), d), s, jnp.where(c == 0, m, zpeer(k)))

    def second_dev(k):
        return (jnp.where(c == 0, d, ypeer(k)), s, jnp.where(c == 0, zpeer(k), m))

    def ycopy(src, dst, b, i, j, dev):
        return rcopy(src, dst, y_s.at[b, i], y_r.at[b, j], dev)

    def own(b, rows):
        return Y.at[b, c, 0, 0, rows]

    def y_x(b, k):
        return ycopy(own(b, whole), own(b, whole), b, k, 0, (d, (s + k) % NX, m))

    whole = pl.ds(0, PIECE)

    def y_first(b, k):
        slot = (1, 3, 2)[k - 1]
        return ycopy(own(b, whole), Y.at[b, c, 0, slot, whole], b, 5 + k, slot, first_dev(k))

    sets = (pl.ds(0, 1), pl.ds(1, 2), pl.ds(3, 1))

    def y_second(b, part_no, k):
        slot = 1 if k == 1 else 2
        return ycopy(Y.at[b, c, 0, sets[part_no], whole], Y.at[b, c, slot, sets[part_no], whole],
                     b, 11 + part_no * 2 + (slot - 1), 1 + 3 * slot + part_no, second_dev(k))

    def y_second_relay(b, i):
        slot, k = (1, 1) if i < 2 else (2, 3)
        return ycopy(Y.at[b, c, slot, i, whole], Y.at[b, c, 3, i, whole],
                     b, 17 + i, 10 + i, second_dev(k))

    forwards = ((0, 0, 1), (0, 1, 2), (0, 3, 1), (1, 0, 4), (2, 0, 4), (3, 0, 2), (3, 2, 2))

    def y_fwd(b, n, who):
        j, i, size = forwards[n]
        ref = Y.at[b, who, j, pl.ds(i, size), whole]
        return ycopy(ref, ref, b, 21 + n, 14 + n, here)

    def spread_own(b):
        for k in (2, 1, 3):
            y_first(b, k).start()
        for k in (1, 3):
            y_second(b, 0, k).start()
        y_fwd(b, 0, c).start()

    def dots(b, cc, j, start):
        pieces = jnp.concatenate([Y[b, cc, j, i, 0:256, :] for i in range(4)], axis=1)
        term = lax.dot_general(HEAD[cc, j], pieces, (((1,), (1,)), ((), ())),
                               preferred_element_type=F32)
        LT[...] = term if start else LT[...] + term

    def wanted_rows():
        slot, position = row_slot(lax.broadcasted_iota(jnp.int32, (32, 256), 1))
        place = (position == lax.broadcasted_iota(jnp.int32, (32, 256), 0)).astype(BF)
        tokens = targets[...]
        nt = (((1,), (1,)), ((), ()))
        keep = slot[0:8] == lax.broadcasted_iota(jnp.int32, (8, 256), 0)
        parts = []
        for term in (tokens // 256, tokens % 256):
            every = jnp.dot(term.astype(F32).astype(BF), place, preferred_element_type=F32)
            mine = jnp.sum(jnp.where(keep, every, 0.0), axis=0, keepdims=True)
            spread = jnp.broadcast_to(mine, (16, 256)).astype(BF)
            parts.append(lax.dot_general(spread, SEL[...], nt, preferred_element_type=F32)[0:1])
        return parts[0] * 256.0 + parts[1]

    def gather(b):
        source = 2 * b + 1

        @pl.when(s != source)
        def _():
            y_x(b, 1).wait_recv()
            spread_own(b)

        y_first(b, 1).wait_recv()
        y_first(b, 3).wait_recv()
        for k in (1, 3):
            y_second(b, 1, k).start()
        y_fwd(b, 1, c).start()
        y_second(b, 0, 1).wait_recv()
        y_second_relay(b, 0).start()
        y_second(b, 0, 3).wait_recv()
        y_first(b, 2).wait_recv()
        for k in (1, 3):
            y_second(b, 2, k).start()
        y_fwd(b, 2, c).start()
        y_second(b, 1, 1).wait_recv()
        y_second_relay(b, 1).start()
        y_second(b, 1, 3).wait_recv()
        y_second_relay(b, 2).start()
        y_second(b, 2, 3).wait_recv()
        y_second_relay(b, 3).start()
        y_fwd(b, 4, c).start()
        y_second(b, 2, 1).wait_recv()
        y_fwd(b, 3, c).start()

    def finish(b):
        dots(b, c, 0, True)
        for n in range(3):
            y_fwd(b, n, 1 - c).wait_recv()
        dots(b, 1 - c, 0, False)
        dots(b, c, 2, False)
        dots(b, c, 1, False)
        y_second_relay(b, 0).wait_recv()
        y_second_relay(b, 1).wait_recv()
        y_fwd(b, 5, c).start()
        y_fwd(b, 4, 1 - c).wait_recv()
        dots(b, 1 - c, 2, False)
        y_second_relay(b, 2).wait_recv()
        y_second_relay(b, 3).wait_recv()
        y_fwd(b, 6, c).start()
        y_fwd(b, 3, 1 - c).wait_recv()
        dots(b, 1 - c, 1, False)
        dots(b, c, 3, False)
        y_fwd(b, 5, 1 - c).wait_recv()
        y_fwd(b, 6, 1 - c).wait_recv()
        dots(b, 1 - c, 3, False)

        extra = jnp.zeros((16, 256), F32)
        for cc in range(2):
            for j in range(4):
                for i in range(4):
                    extra = extra + Y[b, cc, j, i, LIVE:PIECE, :].astype(F32)
        sums = jnp.sum(extra, axis=0, keepdims=True)
        r = lax.rsqrt(sums * (1.0 / D) + EPS)
        logits = LT[...] * r
        highest = jnp.max(logits, axis=0, keepdims=True)
        summed = jnp.sum(jnp.exp(logits - highest), axis=0, keepdims=True)
        vocab = HEAD.shape[2]
        first = ((d * NX + s) * NM + m) * vocab
        index = (lax.broadcasted_iota(jnp.int32, logits.shape, 0) + first).astype(F32)
        wanted = wanted_rows()
        picked = jnp.sum(jnp.where(index == wanted, logits, 0.0), axis=0, keepdims=True)
        alive = lax.broadcasted_iota(jnp.int32, (1, 256), 1) < LIVE
        for n, value in enumerate((highest, summed, picked)):
            value = jnp.where(alive, value, 1.0)
            for half in range(2):
                STO[pl.ds(n * 4 + b * 2 + half, 1), :] = value[:, half * 128:half * 128 + 128]

    def step(t, _):
        last = s == NX - 1
        place = jnp.where(last, 1, 0)

        @pl.when(t == place)
        def _():
            layer()

        @pl.when(jnp.where(last, (t == 0) | (t == 2), (t == 1) | (t == 3)))
        def _():
            gather(jnp.where(t < 2, 0, 1))

        @pl.when(jnp.where(last, t >= 3, (t == 2) | (t == 4)))
        def _():
            @pl.when(t == jnp.where(last, 3, 2))
            def _():
                head_load.wait()
            finish(jnp.where(t == 4, 1, 0))
        return 0

    @pl.when(s == 0)
    def _():
        for q in range(2):
            for k in (2, 1, 3, 0):
                (eb_z(q, k) if k else eb_fwd(q, 0)).start()

    prepare()
    for copy in small[1:]:
        copy.wait()
    STO[...] = jnp.zeros_like(STO)
    lax.fori_loop(0, 5, step, 0)

    def merge(ref, count):
        parts = [ref[j] for j in range(count)]
        highest = parts[0][0:4]
        for p in parts[1:]:
            highest = jnp.maximum(highest, p[0:4])
        summed = jnp.zeros_like(highest)
        picked = jnp.zeros_like(highest)
        for p in parts:
            summed = summed + p[4:8] * jnp.exp(p[0:4] - highest)
            picked = picked + p[8:12]
        return highest, summed, picked

    def stacked(highest, summed, picked):
        return jnp.concatenate([highest, summed, picked, jnp.zeros_like(picked)], axis=0)

    def st_y(k):
        return rcopy(SA.at[d], SA.at[d], st_s.at[0, k], st_r.at[0, d], (ypeer(k), s, m))

    def st_y_in(k):
        g = ypeer(k)
        return rcopy(SA.at[g], SA.at[g], st_s.at[0, k], st_r.at[0, g], (g, s, m))

    def m_of(k):
        return (m + k) % NM

    def st_m(k):
        return rcopy(SB.at[m], SB.at[m], st_s.at[1, k], st_r.at[1, m], (d, s, m_of(k)))

    def st_m_in(k):
        mm = m_of(k)
        return rcopy(SB.at[mm], SB.at[mm], st_s.at[1, k], st_r.at[1, mm], (d, s, mm))

    def st_x(k):
        return rcopy(SC.at[s], SC.at[s], st_s.at[2, k], st_r.at[2, s], (d, (s + k) % NX, m))

    def st_x_in(k):
        ss = (s + k) % NX
        return rcopy(SC.at[ss], SC.at[ss], st_s.at[2, k], st_r.at[2, ss], (d, ss, m))

    SA.at[d][...] = STO[...]
    for k in (2, 1, 3):
        st_y(k).start()
    for k in (1, 3, 2):
        st_y_in(k).wait_recv()
    SB.at[m][...] = stacked(*merge(SA, NY))
    for k in (4, 3, 5, 2, 6, 1, 7):
        st_m(k).start()
    for k in (1, 7, 2, 6, 3, 5, 4):
        st_m_in(k).wait_recv()
    SC.at[s][...] = stacked(*merge(SB, NM))
    for k in (2, 1, 3):
        st_x(k).start()
    for k in (1, 3, 2):
        st_x_in(k).wait_recv()
    highest, summed, picked = merge(SC, NX)
    logprob = picked - (highest + jnp.log(summed))
    terms = []
    for e in range(2):
        rest = jnp.concatenate([logprob[2 * e:2 * e + 1], logprob[2 * e + 1:2 * e + 2]], axis=1)
        for _ in range(3):
            term = rest.astype(BF).astype(F32)
            terms.append(term)
            rest = rest - term
    row = lax.broadcasted_iota(jnp.int32, (16, 256), 0)
    stack = jnp.zeros((16, 256), F32)
    for j, term in enumerate(terms):
        stack = jnp.where(row == j, term, stack)
    stack = stack.astype(BF)
    index = lax.broadcasted_iota(jnp.int32, (256, 32), 0)
    place = lax.broadcasted_iota(jnp.int32, (256, 32), 1)
    results = []
    for i in range(2):
        chosen = source_of[2 * d + i]
        start = 0
        for other in range(8):
            start = start + jnp.where(chosen > other, live[other], 0)
        take = ((index == start + place) & (place < live[chosen])).astype(F32).astype(BF)
        got = jnp.dot(stack, take, preferred_element_type=F32)
        results.append([got[j:j + 1] + got[j + 1:j + 2] + got[j + 2:j + 3] for j in (0, 3)])
    for e in range(2):
        first = lax.broadcasted_iota(jnp.int32, (2, 32), 0) == 0
        out.at[e][...] = jnp.where(first, results[0][e], results[1][e])

    @pl.when(s == 0)
    def _():
        for q in range(2):
            for k in range(1, 4):
                eb_z(q, k).wait_send()
            for k in range(4):
                eb_fwd(q, k).wait_send()
        for k in range(1, 4):
            res(k).wait_send()

    @pl.when(s > 0)
    def _():
        for g in range(NY):
            for k in range(1, 4):
                ag_z(g, k).wait_send()
            for k in range(4):
                ag_fwd(g, k).wait_send()
        next_gain().wait_send()

    @pl.when(s < NX - 1)
    def _():
        for g in range(NY):
            hop(g).wait_send()
        hop_raw().wait_send()

    for g in range(NY):
        for k in range(1, 4):
            zred(g, k).wait_send()
        part(g).wait_send()
    for k in range(1, 4):
        ctx(k).wait_send()
        st_y(k).wait_send()
        st_x(k).wait_send()
    for k in range(1, 8):
        st_m(k).wait_send()
    for b in range(2):
        @pl.when(s == 2 * b + 1)
        def _():
            for k in (1, 2, 3):
                y_x(b, k).wait_send()

        for k in (1, 2, 3):
            y_first(b, k).wait_send()
        for k in (1, 3):
            for n in range(3):
                y_second(b, n, k).wait_send()
        for i in range(4):
            y_second_relay(b, i).wait_send()
        for n in range(7):
            y_fwd(b, n, c).wait_send()


def tables():
    row = np.arange(ROWS)
    position = (row // 8) * 4 + row % 4
    half = HD // 2
    freqs = (ROPE_BASE ** (-np.arange(half) * 2.0 / HD)).astype(np.float32)
    angles = (position.astype(np.float32)[:, None] * freqs[None, :]).astype(np.float64)
    cos, sin = np.cos(angles), np.sin(angles)
    return (np.concatenate([cos, cos], 1).astype(np.float32),
            np.concatenate([-sin, sin], 1).astype(np.float32))


def per_device(
    embeds, targets, lengths, source, attn_gain, w_query, w_key, w_value, w_out, final_gain, head
):
    vocab = head.shape[0]
    cos, sin = tables()
    vmem = pl.BlockSpec(memory_space=pltpu.VMEM)
    hbm = pl.BlockSpec(memory_space=pl.ANY)
    smem = pl.BlockSpec(memory_space=pltpu.SMEM)
    dma = pltpu.SemaphoreType.DMA
    stats = pl.pallas_call(
        kernel,
        out_shape=jax.ShapeDtypeStruct((2, 2, 32), F32),
        in_specs=[hbm, smem, smem] + [hbm] * 10,
        out_specs=vmem,
        scratch_shapes=[
            pltpu.VMEM((2, 4, D), BF),
            pltpu.VMEM((8, 32), jnp.int32),
            pltpu.VMEM((1, D), F32),
            pltpu.VMEM((1, D), F32),
            pltpu.VMEM((ROWS, HD), F32),
            pltpu.VMEM((ROWS, HD), F32),
            pltpu.VMEM((32, 256, 768), BF),
            pltpu.VMEM((QW, 2048), BF),
            pltpu.VMEM((2, 4, vocab, 1024), BF),
            pltpu.VMEM((2, NM, 16, 2048), BF),
            pltpu.VMEM((NY, NM, ROWS + 16, 256), BF),
            pltpu.VMEM((NY, ROWS + 16, 256), BF),
            pltpu.VMEM((1, 256), F32),
            pltpu.VMEM((NY, ROWS, 256), BF),
            pltpu.VMEM((4 * ROWS, ROWS), F32),
            pltpu.VMEM((256, 256), BF),
            pltpu.VMEM((ROWS, 128), F32),
            pltpu.VMEM((ROWS, 768), F32),
            pltpu.VMEM((NY, ROWS, 256), BF),
            pltpu.VMEM((NY, ROWS, QW), BF),
            pltpu.VMEM((NY, NZ, ROWS, 256), BF),
            pltpu.VMEM((NY, NZ, ROWS, 256), BF),
            pltpu.VMEM((NY, NZ, ROWS, 256), F32),
            pltpu.VMEM((NY, NZ, ROWS, 256), BF),
            pltpu.VMEM((NY, NZ, ROWS, 256), BF),
            pltpu.VMEM((NY, ROWS, 256), BF),
            pltpu.VMEM((2, 2, 4, 4, 256, 256), BF),
            pltpu.VMEM((vocab, 256), F32),
            pltpu.VMEM((16, 128), F32),
            pltpu.VMEM((NY, 16, 128), F32),
            pltpu.VMEM((NM, 16, 128), F32),
            pltpu.VMEM((NX, 16, 128), F32),
            dma((20,)),
            dma, dma,
            dma((2, 8)), dma((2, 8)),
            dma((5,)), dma((5,)),
            dma((4, 8)), dma((4, 8)),
            dma((4,)), dma((4,)),
            dma((4,)), dma((4,)),
            dma((4,)), dma((4,)),
            dma((4, 4)), dma((4, 4)),
            dma((2, 30)), dma((2, 22)),
            dma((3, 8)), dma((3, 8)),
        ],
        compiler_params=pltpu.CompilerParams(
            collective_id=0, has_side_effects=True, vmem_limit_bytes=60 * 1024 * 1024),
        cost_estimate=pl.CostEstimate(flops=8_000_000_000, bytes_accessed=24_000_000,
                                      transcendentals=300_000),
    )(
        embeds, lengths, source, targets, attn_gain, final_gain.reshape(1, D), jnp.asarray(cos), jnp.asarray(sin),
        w_query.reshape(32, 256, 512), w_key.reshape(32, 256, 128),
        w_value.reshape(32, 256, 128), w_out.reshape(512, 2048), head,
    )
    return (stats[0], stats[1])


def solution(mesh):
    return jax.shard_map(
        per_device,
        mesh=mesh,
        in_specs=(
            P("dp", "mp", None),
            P(),
            P(),
            P(),
            P("section", None),
            P("section", None, "mp"),
            P("section", None, "mp"),
            P("section", None, "mp"),
            P("section", "mp", "dp"),
            P(),
            P(("dp", "section", "mp"), None),
        ),
        out_specs=(P("dp", None), P("dp", None)),
        check_vma=False,
    )
```

```python
import jax
import jax.numpy as jnp
import numpy as np
from jax import lax
from jax.experimental import pallas as pl
from jax.experimental.pallas import tpu as pltpu
from jax.sharding import PartitionSpec as P

HD = 128
EPS = 1e-05
ROPE_BASE = 500000.0
NY = 4
NX = 4
NZ = 4
NM = 8
ROWS = 64
LIVE = 192
PIECE = LIVE + 16
D = 8192
QW = 512
MESH = pl.DeviceIdType.MESH
BF = jnp.bfloat16
F32 = jnp.float32


def lane(start, size):
    return pl.ds(pl.multiple_of(start, 128), size)


def kernel(
    emb_in, live, source_of, targets_in, gain, fgain_in, cosine_in, sine_in, wq, wk, wv, wo, head,
    out,
    emb, targets, gains, fgain, cosine, sine, W, WO, HEAD, EB, XE, X, G, NG, RX, MASK, SEL, SS, QA, QR, R, C, PS, PR, PO, ZS, ZR, HP, Y, LT, STO, SA, SB, SC,
    w_sem, sw_s, sw_r, qr_s, qr_r, ng_s, ng_r, eb_s, eb_r, hop_s, hop_r, ag_s, ag_r, res_s, res_r, ctx_s, ctx_r, ps_s, ps_r,
    zz_s, zz_r, y_s, y_r, st_s, st_r,
):
    d = lax.axis_index("dp")
    s = lax.axis_index("section")
    m = lax.axis_index("mp")
    z = m // 2
    c = m % 2
    sib = z * 2 + (1 - c)

    def ypeer(k):
        return (d + k) % NY

    def zpeer(k):
        return ((z + k) % NZ) * 2 + c

    def zother(k):
        return ((z + k) % NZ) * 2 + (1 - c)

    def rcopy(src, dst, ssem, rsem, dev):
        return pltpu.make_async_remote_copy(
            src_ref=src, dst_ref=dst, send_sem=ssem, recv_sem=rsem,
            device_id=dev, device_id_type=MESH,
        )

    here = (d, s, sib)

    barrier = pltpu.get_barrier_semaphore()
    partners = []
    for k in range(1, 4):
        partners.append((ypeer(k), s, m))
        partners.append((d, (s + k) % NX, m))
        partners.append((d, s, zpeer(k)))
        partners.append((d, s, zother(k)))
        partners.append((ypeer(k), (s + 1) % NX, m))
        partners.append((ypeer(k), (s + 3) % NX, m))
    partners.append(here)
    for dev in partners:
        pl.semaphore_signal(barrier, inc=1, device_id=dev, device_id_type=MESH)
    small = [
        pltpu.make_async_copy(src, dst, w_sem.at[14 + n])
        for n, (src, dst) in enumerate((
            (emb_in, emb), (gain, gains), (cosine_in, cosine), (sine_in, sine),
            (fgain_in, fgain), (targets_in, targets)))
    ]
    for copy in small:
        copy.start()
    parts = ((wq, pl.ds(0, 512)), (wk, pl.ds(512, 128)), (wv, pl.ds(640, 128)))

    def load(n, first):
        src, lanes = parts[n]
        take = 1 if first else jnp.where(s == 0, 0, c)
        return pltpu.make_async_copy(src.at[:, take], W.at[first, :, :, lanes],
                                     w_sem.at[3 * first + n])

    def swap(n):
        src, lanes = parts[n]
        return rcopy(src.at[:, 1 - c], W.at[1, :, :, lanes], sw_s.at[n], sw_r.at[n], here)

    wo_load = pltpu.make_async_copy(wo, WO, w_sem.at[12])
    for n in range(3):
        load(n, 0).start()

    @pl.when(s == 0)
    def _():
        for n in range(3):
            load(n, 1).start()

    head_load = pltpu.make_async_copy(HEAD, HEAD, w_sem.at[13])

    def prepare():
        wo_load.start()
        offsets = (0, 3, 1, 2)
        for cc in range(2):
            for j in range(4):
                for i in range(4):
                    g, zz = (offsets[i], offsets[j]) if cc == 0 else (offsets[j], offsets[i])
                    col = ypeer(g) * 2048 + ((z + zz) % NZ) * 512 + cc * 256
                    pltpu.make_async_copy(head.at[:, lane(col, 256)],
                                          HEAD.at[cc, j, :, i * 256:i * 256 + 256],
                                          w_sem.at[13]).start()
        shape = (4 * ROWS, ROWS)
        rq = lax.broadcasted_iota(jnp.int32, shape, 0) % ROWS
        rk = lax.broadcasted_iota(jnp.int32, shape, 1)
        slot_q, slot_k = (rq // 4) % 2, (rk // 4) % 2
        pos_q, pos_k = (rq // 8) * 4 + rq % 4, (rk // 8) * 4 + rk % 4
        live_k = jnp.where(slot_k == 0, live[2 * d], live[2 * d + 1])
        allowed = (slot_q == slot_k) & (pos_k <= pos_q) & (pos_k < live_k)
        MASK[...] = jnp.where(allowed, F32(0.0), F32(-1e30))

        def first_row(slot):
            start = jnp.zeros_like(slot)
            for other in range(8):
                start = start + jnp.where(slot > other, live[other], 0)
            return start

        def live_of(slot):
            count = jnp.zeros_like(slot)
            for other in range(8):
                count = count + jnp.where(slot == other, live[other], 0)
            return count

        slot, position = row_slot(lax.broadcasted_iota(jnp.int32, (8, 256), 1))
        packed_at = jnp.where(position < live_of(slot), first_row(slot) + position, 999)[0:1]
        SEL[...] = (lax.broadcasted_iota(jnp.int32, (256, 256), 0) == packed_at).astype(F32).astype(BF)

    def row_slot(lanes):
        return (lanes // 64) * 2 + (lanes // 4) % 2, ((lanes // 8) % 8) * 4 + lanes % 4

    small[0].wait()

    @pl.when(s == 0)
    def _():
        rows = jnp.concatenate([emb[0], emb[1]], axis=0).astype(F32)
        for q in range(2):
            EB.at[q, m][...] = jnp.concatenate(
                [rows[:, q * 2048:q * 2048 + 2048], rows[:, q * 2048 + 4096:q * 2048 + 6144]],
                axis=0).astype(BF)

    pl.semaphore_wait(barrier, len(partners))

    def next_gain():
        return rcopy(gain.at[:, lane(d * 2048 + m * 256, 256)], NG, ng_s, ng_r,
                     (d, (s + 3) % NX, m))

    @pl.when(s > 0)
    def _():
        next_gain().start()
        for n in range(3):
            swap(n).start()

    def eb_z(q, k):
        return rcopy(EB.at[q, m], EB.at[q, m], eb_s.at[q, k], eb_r.at[q, m], (d, s, zpeer(k)))

    def eb_z_in(q, k):
        mk = zpeer(k)
        return rcopy(EB.at[q, mk], EB.at[q, mk], eb_s.at[q, k], eb_r.at[q, mk], here)

    def eb_fwd(q, k):
        mk = zpeer(k)
        return rcopy(EB.at[q, mk], EB.at[q, mk], eb_s.at[q, 4 + k], eb_r.at[q, mk], here)

    def eb_sib_in(q, k):
        mk = zother(k)
        return rcopy(EB.at[q, mk], EB.at[q, mk], eb_s.at[q, 4 + k], eb_r.at[q, mk], here)

    def hop(g):
        return rcopy(G.at[g], X.at[d, z], hop_s.at[g], hop_r.at[d], (g, (s + 1) % NX, m))

    def hop_in(g):
        return rcopy(G.at[g], X.at[g, z], hop_s.at[g], hop_r.at[g], (g, (s + 1) % NX, m))

    def hop_raw():
        return rcopy(HP, R, hop_s.at[4], hop_r.at[4], (d, (s + 1) % NX, m))

    def ag_z(g, k):
        return rcopy(X.at[g, z], X.at[g, z], ag_s.at[g, k], ag_r.at[g, z], (d, s, zpeer(k)))

    def ag_z_in(g, k):
        zk = (z + k) % NZ
        return rcopy(X.at[g, zk], X.at[g, zk], ag_s.at[g, k], ag_r.at[g, zk], here)

    def sums_out():
        return rcopy(QA.at[1], QR, qr_s, qr_r, here)

    def res(k):
        g = ypeer(k)
        return rcopy(RX.at[g], R.at[d], res_s.at[k], res_r.at[d], (g, s, m))

    def res_in(k):
        g = ypeer(k)
        return rcopy(RX.at[g], R.at[g], res_s.at[k], res_r.at[g], here)

    def ctx(k):
        return rcopy(C.at[d], C.at[d], ctx_s.at[k], ctx_r.at[d], (ypeer(k), s, m))

    def ctx_in(k):
        g = ypeer(k)
        return rcopy(C.at[g], C.at[g], ctx_s.at[k], ctx_r.at[g], here)

    def part(g):
        return rcopy(PS.at[g], PR.at[g], ps_s.at[g], ps_r.at[g], here)

    def zred(g, k):
        return rcopy(ZS.at[g, k], ZR.at[g, k], zz_s.at[g, k], zz_r.at[g, k], (d, s, zpeer(k)))

    def layer():
        def multiply(x, which, rows, n, start=False):
            w = W[which, pl.ds(rows * NZ, NZ)].reshape(4 * 256, 768)
            term = jnp.dot(x, w, preferred_element_type=F32)
            QA.at[n][:, 0:768] = term if start else QA[n, :, 0:768] + term

        @pl.when(s == 0)
        def _():
            for q in range(2):
                for k in (1, 3, 2):
                    eb_z_in(q, k).wait_recv()
                    eb_fwd(q, k).start()
            QA[...] = jnp.zeros_like(QA)
            QR[...] = jnp.zeros_like(QR)
            SS[...] = jnp.zeros_like(SS)
            for q in range(2):
                for k in range(4):
                    eb_sib_in(q, k).wait_recv()

                def blocks(mm):
                    x = EB[q, :, :, lane(mm * 256, 256)].astype(F32)
                    return [x[:, i * 8:i * 8 + 8, :].reshape(ROWS, 256) for i in range(2)]

                def body(mm, total):
                    for half, xs in enumerate(blocks(mm)):
                        g = half * 2 + q
                        cols = lane(g * 2048 + mm * 256, 256)
                        XE.at[g, mm][...] = (xs * gains[:, cols]).astype(BF)
                        square = xs * xs
                        total = total + square[:, 0:128] + square[:, 128:256]
                    return total

                SS[...] = lax.fori_loop(0, NM, body, SS[...])
                for half, xs in enumerate(blocks(m)):
                    RX.at[half * 2 + q][...] = xs.astype(BF)
                if q == 0:
                    for n in range(3):
                        load(n, 0).wait()
                        load(n, 1).wait()

                def both(i, _):
                    g = 2 * i + q
                    for who in range(2):
                        x = jnp.concatenate([XE[g, 2 * zz + who] for zz in range(NZ)], axis=1)
                        multiply(x, who, g, 0)
                    return 0

                lax.fori_loop(0, 2, both, 0)
            for k in (2, 1, 3):
                res(k).start()
            R.at[d][...] = RX[d]

        @pl.when(s > 0)
        def _():
            def arrived(k):
                g = ypeer(k)
                hop_in(g).wait_recv()
                for j in (2, 1, 3):
                    ag_z(g, j).start()

            def columns(k):
                g = ypeer(k)
                for j in (1, 3, 2):
                    ag_z_in(g, j).wait_recv()
                return jnp.concatenate([X[g, zz, 0:ROWS] for zz in range(NZ)], axis=1)

            def both(k, start=False):
                x = columns(k)
                multiply(x, 1, ypeer(k), 1, start)
                multiply(x, 0, ypeer(k), 0, start)

            for n in range(3):
                load(n, 0).wait()
                swap(n).wait_recv()
            arrived(0)
            arrived(3)
            arrived(1)
            arrived(2)
            both(0, True)
            both(3)
            both(1)
            x = columns(2)
            multiply(x, 1, ypeer(2), 1)
            total = jnp.zeros((16, 256), F32)
            for zz in range(NZ):
                for g in range(NY):
                    total = total + X[g, zz, ROWS:ROWS + 16].astype(F32)
            total = total[0:1, 0:128] + total[1:2, 0:128]
            mine = (lax.broadcasted_iota(jnp.int32, (ROWS, 128), 1)
                    == lax.broadcasted_iota(jnp.int32, (ROWS, 128), 0))
            squares = jnp.where(mine, total, 0.0)
            QA.at[1][:, 768:896] = squares
            sums_out().start()
            multiply(x, 0, ypeer(2), 0)
            sums_out().wait_recv()
            SS[...] = squares + QR[:, 768:896]

        r = lax.rsqrt(jnp.sum(SS[...], axis=1, keepdims=True) * (1.0 / D) + EPS)
        cos = cosine[...]
        sin = sine[...]

        def summed(first, last):
            return QA[0, :, first:last] + QR[:, first:last]

        def rope(x):
            return (x * cos + pltpu.roll(x, 64, 1) * sin).astype(BF)

        query = jnp.concatenate(
            [rope(summed(j * HD, (j + 1) * HD) * r) for j in range(4)], axis=0)
        key = rope(summed(512, 640) * r)
        value = (summed(640, 768) * r).astype(BF)
        scores = lax.dot_general(query, key, (((1,), (1,)), ((), ())),
                                 preferred_element_type=F32) * (HD ** -0.5)
        scores = scores + MASK[...]
        highest = jnp.max(scores, axis=-1, keepdims=True)
        weights = jnp.exp(scores - highest)
        probs = (weights / jnp.sum(weights, axis=-1, keepdims=True)).astype(BF)
        mixed = jnp.dot(probs, value, preferred_element_type=F32).astype(BF)
        for j in range(4):
            C.at[d][:, j * HD:(j + 1) * HD] = mixed[j * ROWS:(j + 1) * ROWS]
        for k in (2, 1, 3):
            ctx(k).start()

        wo_load.wait()

        def project(g):
            for zz in range(NZ):
                p = jnp.dot(C[g], WO[:, zz * 512:zz * 512 + 512], preferred_element_type=F32)
                low, high = p[:, :256], p[:, 256:]
                PO.at[g, zz][...] = jnp.where(c == 0, low, high)
                PS.at[g, zz][...] = jnp.where(c == 0, high, low).astype(BF)
            part(g).start()

        def pair(g):
            part(g).wait_recv()
            for k in (2, 1, 3):
                zt = (z + k) % NZ
                ZS.at[g, k][...] = (PO[g, zt] + PR[g, zt].astype(F32)).astype(BF)
                zred(g, k).start()

        def total_of(g):
            total = PO[g, z] + PR[g, z].astype(F32) + R[g].astype(F32)
            for k in (1, 3, 2):
                zred(g, k).wait_recv()
                total = total + ZR[g, k].astype(F32)
            hidden = total.astype(BF)
            HP.at[g][...] = hidden
            wide = hidden.astype(F32)
            G.at[g][0:ROWS, :] = (wide * NG[...]).astype(BF)
            square = wide * wide
            top = square.astype(BF)
            rest = (square - top.astype(F32)).astype(BF)
            ones = jnp.ones((16, 256), BF)
            nt = (((1,), (1,)), ((), ()))
            sums = (lax.dot_general(ones, top, nt, preferred_element_type=F32)
                    + lax.dot_general(ones, rest, nt, preferred_element_type=F32))
            top = sums.astype(BF).astype(F32)
            row = lax.broadcasted_iota(jnp.int32, (16, ROWS), 0)
            packed = jnp.where(row == 0, top, jnp.where(row == 1, sums - top, 0.0))
            packed = jnp.concatenate([packed, jnp.zeros_like(packed)], axis=1).astype(BF)
            G.at[g][ROWS:ROWS + 16, 0:128] = packed

            @pl.when(s < NX - 1)
            def _():
                hop(g).start()

        project(d)

        @pl.when(s == 0)
        def _():
            for k in (1, 3, 2):
                res_in(k).wait_recv()

        @pl.when(s > 0)
        def _():
            hop_raw().wait_recv()

        @pl.when(s < NX - 1)
        def _():
            next_gain().wait_recv()

        pair(d)
        for k in (1, 3):
            ctx_in(k).wait_recv()
            project(ypeer(k))
        pair(ypeer(1))
        pair(ypeer(3))
        total_of(d)
        ctx_in(2).wait_recv()
        project(ypeer(2))
        total_of(ypeer(1))
        pair(ypeer(2))
        total_of(ypeer(3))
        total_of(ypeer(2))

        @pl.when(s < NX - 1)
        def _():
            hop_raw().start()

        @pl.when(s % 2 == 1)
        def _():
            emit(s // 2)

    def emit(b):
        mine = Y.at[b, c, 0, 0]
        nt = (((1,), (1,)), ((), ()))
        wide = HP[...].reshape(NY * ROWS, 256).astype(F32)
        cols = lane(d * 2048 + m * 256, 256)
        scaled = (wide * fgain[:, cols]).astype(BF)
        live_rows = jnp.dot(SEL[0:LIVE], scaled, preferred_element_type=F32)
        mine[0:LIVE, :] = live_rows.astype(BF)
        square = wide * wide
        top = square.astype(BF)
        rest = (square - top.astype(F32)).astype(BF)
        ones = jnp.ones((16, 256), BF)
        sums = (lax.dot_general(ones, top, nt, preferred_element_type=F32)
                + lax.dot_general(ones, rest, nt, preferred_element_type=F32))
        top = sums.astype(BF).astype(F32)
        row = lax.broadcasted_iota(jnp.int32, (16, NY * ROWS), 0)
        packed = jnp.where(row == 0, top, jnp.where(row == 1, sums - top, 0.0)).astype(BF)
        squares = lax.dot_general(packed, SEL[...], nt, preferred_element_type=F32)
        mine[LIVE:PIECE, :] = squares.astype(BF)
        for k in (2, 1, 3):
            y_x(b, k).start()
        spread_own(b)

    def first_dev(k):
        return (jnp.where(c == 0, ypeer(k), d), s, jnp.where(c == 0, m, zpeer(k)))

    def second_dev(k):
        return (jnp.where(c == 0, d, ypeer(k)), s, jnp.where(c == 0, zpeer(k), m))

    def ycopy(src, dst, b, i, j, dev):
        return rcopy(src, dst, y_s.at[b, i], y_r.at[b, j], dev)

    def own(b, rows):
        return Y.at[b, c, 0, 0, rows]

    def y_x(b, k):
        return ycopy(own(b, whole), own(b, whole), b, k, 0, (d, (s + k) % NX, m))

    whole = pl.ds(0, PIECE)

    def y_first(b, k):
        slot = (1, 3, 2)[k - 1]
        return ycopy(own(b, whole), Y.at[b, c, 0, slot, whole], b, 5 + k, slot, first_dev(k))

    sets = (pl.ds(0, 1), pl.ds(1, 2), pl.ds(3, 1))

    def y_second(b, part_no, k):
        slot = 1 if k == 1 else 2
        return ycopy(Y.at[b, c, 0, sets[part_no], whole], Y.at[b, c, slot, sets[part_no], whole],
                     b, 11 + part_no * 2 + (slot - 1), 1 + 3 * slot + part_no, second_dev(k))

    def y_second_relay(b, i):
        slot, k = (1, 1) if i < 2 else (2, 3)
        return ycopy(Y.at[b, c, slot, i, whole], Y.at[b, c, 3, i, whole],
                     b, 17 + i, 10 + i, second_dev(k))

    forwards = ((0, 0, 1), (0, 1, 2), (0, 3, 1), (1, 0, 4), (2, 0, 4), (3, 0, 2), (3, 2, 2))

    def y_fwd(b, n, who):
        j, i, size = forwards[n]
        ref = Y.at[b, who, j, pl.ds(i, size), whole]
        return ycopy(ref, ref, b, 21 + n, 14 + n, here)

    def spread_own(b):
        for k in (2, 1, 3):
            y_first(b, k).start()
        for k in (1, 3):
            y_second(b, 0, k).start()
        y_fwd(b, 0, c).start()

    def dots(b, cc, j, start):
        pieces = jnp.concatenate([Y[b, cc, j, i, 0:256, :] for i in range(4)], axis=1)
        term = lax.dot_general(HEAD[cc, j], pieces, (((1,), (1,)), ((), ())),
                               preferred_element_type=F32)
        LT[...] = term if start else LT[...] + term

    def wanted_rows():
        slot, position = row_slot(lax.broadcasted_iota(jnp.int32, (32, 256), 1))
        place = (position == lax.broadcasted_iota(jnp.int32, (32, 256), 0)).astype(BF)
        tokens = targets[...]
        nt = (((1,), (1,)), ((), ()))
        keep = slot[0:8] == lax.broadcasted_iota(jnp.int32, (8, 256), 0)
        parts = []
        for term in (tokens // 256, tokens % 256):
            every = jnp.dot(term.astype(F32).astype(BF), place, preferred_element_type=F32)
            mine = jnp.sum(jnp.where(keep, every, 0.0), axis=0, keepdims=True)
            spread = jnp.broadcast_to(mine, (16, 256)).astype(BF)
            parts.append(lax.dot_general(spread, SEL[...], nt, preferred_element_type=F32)[0:1])
        return parts[0] * 256.0 + parts[1]

    def gather(b):
        source = 2 * b + 1

        @pl.when(s != source)
        def _():
            y_x(b, 1).wait_recv()
            spread_own(b)

        y_first(b, 1).wait_recv()
        y_first(b, 3).wait_recv()
        for k in (1, 3):
            y_second(b, 1, k).start()
        y_fwd(b, 1, c).start()
        y_second(b, 0, 1).wait_recv()
        y_second_relay(b, 0).start()
        y_second(b, 0, 3).wait_recv()
        y_first(b, 2).wait_recv()
        for k in (1, 3):
            y_second(b, 2, k).start()
        y_fwd(b, 2, c).start()
        y_second(b, 1, 1).wait_recv()
        y_second_relay(b, 1).start()
        y_second(b, 1, 3).wait_recv()
        y_second_relay(b, 2).start()
        y_second(b, 2, 3).wait_recv()
        y_second_relay(b, 3).start()
        y_fwd(b, 4, c).start()
        y_second(b, 2, 1).wait_recv()
        y_fwd(b, 3, c).start()

    def finish(b):
        dots(b, c, 0, True)
        for n in range(3):
            y_fwd(b, n, 1 - c).wait_recv()
        dots(b, 1 - c, 0, False)
        dots(b, c, 2, False)
        dots(b, c, 1, False)
        y_second_relay(b, 0).wait_recv()
        y_second_relay(b, 1).wait_recv()
        y_fwd(b, 5, c).start()
        y_fwd(b, 4, 1 - c).wait_recv()
        dots(b, 1 - c, 2, False)
        y_second_relay(b, 2).wait_recv()
        y_second_relay(b, 3).wait_recv()
        y_fwd(b, 6, c).start()
        y_fwd(b, 3, 1 - c).wait_recv()
        dots(b, 1 - c, 1, False)
        dots(b, c, 3, False)
        y_fwd(b, 5, 1 - c).wait_recv()
        y_fwd(b, 6, 1 - c).wait_recv()
        dots(b, 1 - c, 3, False)

        extra = jnp.zeros((16, 256), F32)
        for cc in range(2):
            for j in range(4):
                for i in range(4):
                    extra = extra + Y[b, cc, j, i, LIVE:PIECE, :].astype(F32)
        sums = jnp.sum(extra, axis=0, keepdims=True)
        r = lax.rsqrt(sums * (1.0 / D) + EPS)
        logits = LT[...] * r
        highest = jnp.max(logits, axis=0, keepdims=True)
        summed = jnp.sum(jnp.exp(logits - highest), axis=0, keepdims=True)
        vocab = HEAD.shape[2]
        first = ((d * NX + s) * NM + m) * vocab
        index = (lax.broadcasted_iota(jnp.int32, logits.shape, 0) + first).astype(F32)
        wanted = wanted_rows()
        picked = jnp.sum(jnp.where(index == wanted, logits, 0.0), axis=0, keepdims=True)
        alive = lax.broadcasted_iota(jnp.int32, (1, 256), 1) < LIVE
        for n, value in enumerate((highest, summed, picked)):
            value = jnp.where(alive, value, 1.0)
            for half in range(2):
                STO[pl.ds(n * 4 + b * 2 + half, 1), :] = value[:, half * 128:half * 128 + 128]

    def step(t, _):
        last = s == NX - 1
        place = jnp.where(last, 1, 0)

        @pl.when(t == place)
        def _():
            layer()

        @pl.when(jnp.where(last, (t == 0) | (t == 2), (t == 1) | (t == 3)))
        def _():
            gather(jnp.where(t < 2, 0, 1))

        @pl.when(jnp.where(last, t >= 3, (t == 2) | (t == 4)))
        def _():
            @pl.when(t == jnp.where(last, 3, 2))
            def _():
                head_load.wait()
            finish(jnp.where(t == 4, 1, 0))
        return 0

    @pl.when(s == 0)
    def _():
        for q in range(2):
            for k in (2, 1, 3, 0):
                (eb_z(q, k) if k else eb_fwd(q, 0)).start()

    prepare()
    for copy in small[1:]:
        copy.wait()
    STO[...] = jnp.zeros_like(STO)
    lax.fori_loop(0, 5, step, 0)

    def merge(ref, count):
        parts = [ref[j] for j in range(count)]
        highest = parts[0][0:4]
        for p in parts[1:]:
            highest = jnp.maximum(highest, p[0:4])
        summed = jnp.zeros_like(highest)
        picked = jnp.zeros_like(highest)
        for p in parts:
            summed = summed + p[4:8] * jnp.exp(p[0:4] - highest)
            picked = picked + p[8:12]
        return highest, summed, picked

    def stacked(highest, summed, picked):
        return jnp.concatenate([highest, summed, picked, jnp.zeros_like(picked)], axis=0)

    def st_y(k):
        return rcopy(SA.at[d], SA.at[d], st_s.at[0, k], st_r.at[0, d], (ypeer(k), s, m))

    def st_y_in(k):
        g = ypeer(k)
        return rcopy(SA.at[g], SA.at[g], st_s.at[0, k], st_r.at[0, g], (g, s, m))

    def m_of(k):
        return (m + k) % NM

    def st_m(k):
        return rcopy(SB.at[m], SB.at[m], st_s.at[1, k], st_r.at[1, m], (d, s, m_of(k)))

    def st_m_in(k):
        mm = m_of(k)
        return rcopy(SB.at[mm], SB.at[mm], st_s.at[1, k], st_r.at[1, mm], (d, s, mm))

    def st_x(k):
        return rcopy(SC.at[s], SC.at[s], st_s.at[2, k], st_r.at[2, s], (d, (s + k) % NX, m))

    def st_x_in(k):
        ss = (s + k) % NX
        return rcopy(SC.at[ss], SC.at[ss], st_s.at[2, k], st_r.at[2, ss], (d, ss, m))

    SA.at[d][...] = STO[...]
    for k in (2, 1, 3):
        st_y(k).start()
    for k in (1, 3, 2):
        st_y_in(k).wait_recv()
    SB.at[m][...] = stacked(*merge(SA, NY))
    for k in (4, 3, 5, 2, 6, 1, 7):
        st_m(k).start()
    for k in (1, 7, 2, 6, 3, 5, 4):
        st_m_in(k).wait_recv()
    SC.at[s][...] = stacked(*merge(SB, NM))
    for k in (2, 1, 3):
        st_x(k).start()
    for k in (1, 3, 2):
        st_x_in(k).wait_recv()
    highest, summed, picked = merge(SC, NX)
    logprob = picked - (highest + jnp.log(summed))
    terms = []
    for e in range(2):
        rest = jnp.concatenate([logprob[2 * e:2 * e + 1], logprob[2 * e + 1:2 * e + 2]], axis=1)
        for _ in range(3):
            term = rest.astype(BF).astype(F32)
            terms.append(term)
            rest = rest - term
    row = lax.broadcasted_iota(jnp.int32, (16, 256), 0)
    stack = jnp.zeros((16, 256), F32)
    for j, term in enumerate(terms):
        stack = jnp.where(row == j, term, stack)
    stack = stack.astype(BF)
    index = lax.broadcasted_iota(jnp.int32, (256, 32), 0)
    place = lax.broadcasted_iota(jnp.int32, (256, 32), 1)
    results = []
    for i in range(2):
        chosen = source_of[2 * d + i]
        start = 0
        for other in range(8):
            start = start + jnp.where(chosen > other, live[other], 0)
        take = ((index == start + place) & (place < live[chosen])).astype(F32).astype(BF)
        got = jnp.dot(stack, take, preferred_element_type=F32)
        results.append([got[j:j + 1] + got[j + 1:j + 2] + got[j + 2:j + 3] for j in (0, 3)])
    for e in range(2):
        first = lax.broadcasted_iota(jnp.int32, (2, 32), 0) == 0
        out.at[e][...] = jnp.where(first, results[0][e], results[1][e])

    @pl.when(s == 0)
    def _():
        for q in range(2):
            for k in range(1, 4):
                eb_z(q, k).wait_send()
            for k in range(4):
                eb_fwd(q, k).wait_send()
        for k in range(1, 4):
            res(k).wait_send()

    @pl.when(s > 0)
    def _():
        for g in range(NY):
            for k in range(1, 4):
                ag_z(g, k).wait_send()
        sums_out().wait_send()
        for n in range(3):
            swap(n).wait_send()
        next_gain().wait_send()

    @pl.when(s < NX - 1)
    def _():
        for g in range(NY):
            hop(g).wait_send()
        hop_raw().wait_send()

    for g in range(NY):
        for k in range(1, 4):
            zred(g, k).wait_send()
        part(g).wait_send()
    for k in range(1, 4):
        ctx(k).wait_send()
        st_y(k).wait_send()
        st_x(k).wait_send()
    for k in range(1, 8):
        st_m(k).wait_send()
    for b in range(2):
        @pl.when(s == 2 * b + 1)
        def _():
            for k in (1, 2, 3):
                y_x(b, k).wait_send()

        for k in (1, 2, 3):
            y_first(b, k).wait_send()
        for k in (1, 3):
            for n in range(3):
                y_second(b, n, k).wait_send()
        for i in range(4):
            y_second_relay(b, i).wait_send()
        for n in range(7):
            y_fwd(b, n, c).wait_send()


def tables():
    row = np.arange(ROWS)
    position = (row // 8) * 4 + row % 4
    half = HD // 2
    freqs = (ROPE_BASE ** (-np.arange(half) * 2.0 / HD)).astype(np.float32)
    angles = (position.astype(np.float32)[:, None] * freqs[None, :]).astype(np.float64)
    cos, sin = np.cos(angles), np.sin(angles)
    return (np.concatenate([cos, cos], 1).astype(np.float32),
            np.concatenate([-sin, sin], 1).astype(np.float32))


def per_device(
    embeds, targets, lengths, source, attn_gain, w_query, w_key, w_value, w_out, final_gain, head
):
    vocab = head.shape[0]
    cos, sin = tables()
    vmem = pl.BlockSpec(memory_space=pltpu.VMEM)
    hbm = pl.BlockSpec(memory_space=pl.ANY)
    smem = pl.BlockSpec(memory_space=pltpu.SMEM)
    dma = pltpu.SemaphoreType.DMA
    stats = pl.pallas_call(
        kernel,
        out_shape=jax.ShapeDtypeStruct((2, 2, 32), F32),
        in_specs=[hbm, smem, smem] + [hbm] * 10,
        out_specs=vmem,
        scratch_shapes=[
            pltpu.VMEM((2, 4, D), BF),
            pltpu.VMEM((8, 32), jnp.int32),
            pltpu.VMEM((1, D), F32),
            pltpu.VMEM((1, D), F32),
            pltpu.VMEM((ROWS, HD), F32),
            pltpu.VMEM((ROWS, HD), F32),
            pltpu.VMEM((2, 16, 256, 768), BF),
            pltpu.VMEM((QW, 2048), BF),
            pltpu.VMEM((2, 4, vocab, 1024), BF),
            pltpu.VMEM((2, NM, 16, 2048), BF),
            pltpu.VMEM((NY, NM, ROWS, 256), BF),
            pltpu.VMEM((NY, NZ, ROWS + 16, 256), BF),
            pltpu.VMEM((NY, ROWS + 16, 256), BF),
            pltpu.VMEM((1, 256), F32),
            pltpu.VMEM((NY, ROWS, 256), BF),
            pltpu.VMEM((4 * ROWS, ROWS), F32),
            pltpu.VMEM((256, 256), BF),
            pltpu.VMEM((ROWS, 128), F32),
            pltpu.VMEM((2, ROWS, 896), F32),
            pltpu.VMEM((ROWS, 896), F32),
            pltpu.VMEM((NY, ROWS, 256), BF),
            pltpu.VMEM((NY, ROWS, QW), BF),
            pltpu.VMEM((NY, NZ, ROWS, 256), BF),
            pltpu.VMEM((NY, NZ, ROWS, 256), BF),
            pltpu.VMEM((NY, NZ, ROWS, 256), F32),
            pltpu.VMEM((NY, NZ, ROWS, 256), BF),
            pltpu.VMEM((NY, NZ, ROWS, 256), BF),
            pltpu.VMEM((NY, ROWS, 256), BF),
            pltpu.VMEM((2, 2, 4, 4, 256, 256), BF),
            pltpu.VMEM((vocab, 256), F32),
            pltpu.VMEM((16, 128), F32),
            pltpu.VMEM((NY, 16, 128), F32),
            pltpu.VMEM((NM, 16, 128), F32),
            pltpu.VMEM((NX, 16, 128), F32),
            dma((20,)),
            dma((3,)), dma((3,)),
            dma, dma,
            dma, dma,
            dma((2, 8)), dma((2, 8)),
            dma((5,)), dma((5,)),
            dma((4, 8)), dma((4, 8)),
            dma((4,)), dma((4,)),
            dma((4,)), dma((4,)),
            dma((4,)), dma((4,)),
            dma((4, 4)), dma((4, 4)),
            dma((2, 30)), dma((2, 22)),
            dma((3, 8)), dma((3, 8)),
        ],
        compiler_params=pltpu.CompilerParams(
            collective_id=0, has_side_effects=True, vmem_limit_bytes=60 * 1024 * 1024),
        cost_estimate=pl.CostEstimate(flops=8_000_000_000, bytes_accessed=24_000_000,
                                      transcendentals=300_000),
    )(
        embeds, lengths, source, targets, attn_gain, final_gain.reshape(1, D), jnp.asarray(cos), jnp.asarray(sin),
        w_query.reshape(16, 2, 256, 512), w_key.reshape(16, 2, 256, 128),
        w_value.reshape(16, 2, 256, 128), w_out.reshape(512, 2048), head,
    )
    return (stats[0], stats[1])


def solution(mesh):
    return jax.shard_map(
        per_device,
        mesh=mesh,
        in_specs=(
            P("dp", "mp", None),
            P(),
            P(),
            P(),
            P("section", None),
            P("section", None, "mp"),
            P("section", None, "mp"),
            P("section", None, "mp"),
            P("section", "mp", "dp"),
            P(),
            P(("dp", "section", "mp"), None),
        ),
        out_specs=(P("dp", None), P("dp", None)),
        check_vma=False,
    )
```

```python
import jax
import jax.numpy as jnp
import numpy as np
from jax import lax
from jax.experimental import pallas as pl
from jax.experimental.pallas import tpu as pltpu
from jax.sharding import PartitionSpec as P

HD = 128
EPS = 1e-05
ROPE_BASE = 500000.0
NY = 4
NX = 4
NZ = 4
NM = 8
ROWS = 64
LIVE = 192
PIECE = LIVE + 16
D = 8192
QW = 512
MESH = pl.DeviceIdType.MESH
BF = jnp.bfloat16
F32 = jnp.float32


def lane(start, size):
    return pl.ds(pl.multiple_of(start, 128), size)


def kernel(
    emb_in, live, source_of, targets_in, gain, fgain_in, cosine_in, sine_in, wq, wk, wv, wo, head,
    out,
    emb, targets, gains, fgain, cosine, sine, W, WO, HEAD, EB, XE, X, RX, MASK, SEL, SS, QA, QR, R, C, PS, PR, PO, ZS, ZR, HP, Y, LT, STO, SA, SB,
    w_sem, sw_s, sw_r, qr_s, qr_r, eb_s, eb_r, hop_s, hop_r, ag_s, ag_r, res_s, res_r, ctx_s, ctx_r, ps_s, ps_r,
    zz_s, zz_r, y_s, y_r, st_s, st_r,
):
    d = lax.axis_index("dp")
    s = lax.axis_index("section")
    m = lax.axis_index("mp")
    z = m // 2
    c = m % 2
    sib = z * 2 + (1 - c)

    def ypeer(k):
        return (d + k) % NY

    def zpeer(k):
        return ((z + k) % NZ) * 2 + c

    def zother(k):
        return ((z + k) % NZ) * 2 + (1 - c)

    def rcopy(src, dst, ssem, rsem, dev):
        return pltpu.make_async_remote_copy(
            src_ref=src, dst_ref=dst, send_sem=ssem, recv_sem=rsem,
            device_id=dev, device_id_type=MESH,
        )

    here = (d, s, sib)

    barrier = pltpu.get_barrier_semaphore()
    partners = []
    for k in range(1, 4):
        partners.append((ypeer(k), s, m))
        partners.append((d, (s + k) % NX, m))
        partners.append((d, s, zpeer(k)))
        partners.append((d, s, zother(k)))
        partners.append((ypeer(k), (s + 1) % NX, m))
        partners.append((ypeer(k), (s + 3) % NX, m))
        partners.append((ypeer(k), (s + 2) % NX, m))
    partners.append(here)
    for dev in partners:
        pl.semaphore_signal(barrier, inc=1, device_id=dev, device_id_type=MESH)
    small = [
        pltpu.make_async_copy(src, dst, w_sem.at[14 + n])
        for n, (src, dst) in enumerate((
            (emb_in, emb), (gain, gains), (cosine_in, cosine), (sine_in, sine),
            (fgain_in, fgain), (targets_in, targets)))
    ]
    for copy in small:
        copy.start()
    parts = ((wq, pl.ds(0, 512)), (wk, pl.ds(512, 128)), (wv, pl.ds(640, 128)))

    def load(n, first):
        src, lanes = parts[n]
        take = 1 if first else jnp.where(s == 0, 0, c)
        return pltpu.make_async_copy(src.at[:, take], W.at[first, :, :, lanes],
                                     w_sem.at[3 * first + n])

    def swap(n):
        src, lanes = parts[n]
        return rcopy(src.at[:, 1 - c], W.at[1, :, :, lanes], sw_s.at[n], sw_r.at[n], here)

    wo_load = pltpu.make_async_copy(wo, WO, w_sem.at[12])
    for n in range(3):
        load(n, 0).start()

    @pl.when(s == 0)
    def _():
        for n in range(3):
            load(n, 1).start()

    head_load = pltpu.make_async_copy(HEAD, HEAD, w_sem.at[13])

    def prepare():
        wo_load.start()
        offsets = (0, 3, 1, 2)
        for cc in range(2):
            for j in range(4):
                for i in range(4):
                    g, zz = (offsets[i], offsets[j]) if cc == 0 else (offsets[j], offsets[i])
                    col = ypeer(g) * 2048 + ((z + zz) % NZ) * 512 + cc * 256
                    pltpu.make_async_copy(head.at[:, lane(col, 256)],
                                          HEAD.at[cc, j, :, i * 256:i * 256 + 256],
                                          w_sem.at[13]).start()
        shape = (4 * ROWS, ROWS)
        rq = lax.broadcasted_iota(jnp.int32, shape, 0) % ROWS
        rk = lax.broadcasted_iota(jnp.int32, shape, 1)
        slot_q, slot_k = (rq // 4) % 2, (rk // 4) % 2
        pos_q, pos_k = (rq // 8) * 4 + rq % 4, (rk // 8) * 4 + rk % 4
        live_k = jnp.where(slot_k == 0, live[2 * d], live[2 * d + 1])
        allowed = (slot_q == slot_k) & (pos_k <= pos_q) & (pos_k < live_k)
        MASK[...] = jnp.where(allowed, F32(0.0), F32(-1e30))

        def first_row(slot):
            start = jnp.zeros_like(slot)
            for other in range(8):
                start = start + jnp.where(slot > other, live[other], 0)
            return start

        def live_of(slot):
            count = jnp.zeros_like(slot)
            for other in range(8):
                count = count + jnp.where(slot == other, live[other], 0)
            return count

        slot, position = row_slot(lax.broadcasted_iota(jnp.int32, (8, 256), 1))
        packed_at = jnp.where(position < live_of(slot), first_row(slot) + position, 999)[0:1]
        SEL[...] = (lax.broadcasted_iota(jnp.int32, (256, 256), 0) == packed_at).astype(F32).astype(BF)

        @pl.when(s > 0)
        def _():
            for n in range(3):
                load(n, 0).wait()
                swap(n).wait_recv()
            for copy in small[1:2]:
                copy.wait()
            diagonal = (lax.broadcasted_iota(jnp.int32, (256, 256), 0)
                        == lax.broadcasted_iota(jnp.int32, (256, 256), 1))

            def scale(i, _):
                cols = lane((i // NZ) * 2048 + ((i % NZ) * 2 + c) * 256, 256)
                column = jnp.sum(jnp.where(diagonal, gains[:, cols], 0.0), axis=1, keepdims=True)
                for which in range(2):
                    W.at[which, i][...] = (W[which, i].astype(F32) * column).astype(BF)
                return 0

            lax.fori_loop(0, 16, scale, 0)

        @pl.when(s == 0)
        def _():
            for copy in small[1:2]:
                copy.wait()
        for copy in small[2:]:
            copy.wait()

    def row_slot(lanes):
        return (lanes // 64) * 2 + (lanes // 4) % 2, ((lanes // 8) % 8) * 4 + lanes % 4

    small[0].wait()

    @pl.when(s == 0)
    def _():
        rows = jnp.concatenate([emb[0], emb[1]], axis=0).astype(F32)
        for q in range(2):
            EB.at[q, m][...] = jnp.concatenate(
                [rows[:, q * 2048:q * 2048 + 2048], rows[:, q * 2048 + 4096:q * 2048 + 6144]],
                axis=0).astype(BF)

    pl.semaphore_wait(barrier, len(partners))

    @pl.when(s > 0)
    def _():
        for n in range(3):
            swap(n).start()

    def eb_z(q, k):
        return rcopy(EB.at[q, m], EB.at[q, m], eb_s.at[q, k], eb_r.at[q, m], (d, s, zpeer(k)))

    def eb_z_in(q, k):
        mk = zpeer(k)
        return rcopy(EB.at[q, mk], EB.at[q, mk], eb_s.at[q, k], eb_r.at[q, mk], here)

    def eb_fwd(q, k):
        mk = zpeer(k)
        return rcopy(EB.at[q, mk], EB.at[q, mk], eb_s.at[q, 4 + k], eb_r.at[q, mk], here)

    def eb_sib_in(q, k):
        mk = zother(k)
        return rcopy(EB.at[q, mk], EB.at[q, mk], eb_s.at[q, 4 + k], eb_r.at[q, mk], here)

    def hop(g):
        return rcopy(HP.at[g], X.at[d, z], hop_s.at[g], hop_r.at[d], (g, (s + 1) % NX, m))

    def hop_in(g):
        return rcopy(HP.at[g], X.at[g, z], hop_s.at[g], hop_r.at[g], here)

    def hop_raw():
        return rcopy(HP, R, hop_s.at[4], hop_r.at[4], (d, (s + 1) % NX, m))

    def ag_z(g, k):
        return rcopy(X.at[g, z], X.at[g, z], ag_s.at[g, k], ag_r.at[g, z], (d, s, zpeer(k)))

    def ag_z_in(g, k):
        zk = (z + k) % NZ
        return rcopy(X.at[g, zk], X.at[g, zk], ag_s.at[g, k], ag_r.at[g, zk], here)

    def sums_out():
        return rcopy(QA.at[1], QR, qr_s, qr_r, here)

    def res(k):
        g = ypeer(k)
        return rcopy(RX.at[g], R.at[d], res_s.at[k], res_r.at[d], (g, s, m))

    def res_in(k):
        g = ypeer(k)
        return rcopy(RX.at[g], R.at[g], res_s.at[k], res_r.at[g], here)

    def ctx(k):
        return rcopy(C.at[d], C.at[d], ctx_s.at[k], ctx_r.at[d], (ypeer(k), s, m))

    def ctx_in(k):
        g = ypeer(k)
        return rcopy(C.at[g], C.at[g], ctx_s.at[k], ctx_r.at[g], here)

    def part(g):
        return rcopy(PS.at[g], PR.at[g], ps_s.at[g], ps_r.at[g], here)

    def zred(g, k):
        return rcopy(ZS.at[g, k], ZR.at[g, k], zz_s.at[g, k], zz_r.at[g, k], (d, s, zpeer(k)))

    def layer():
        def multiply(x, which, rows, n, start=False):
            w = W[which, pl.ds(rows * NZ, NZ)].reshape(4 * 256, 768)
            term = jnp.dot(x, w, preferred_element_type=F32)
            QA.at[n][:, 0:768] = term if start else QA[n, :, 0:768] + term

        @pl.when(s == 0)
        def _():
            for q in range(2):
                for k in (1, 3, 2):
                    eb_z_in(q, k).wait_recv()
                    eb_fwd(q, k).start()
            QA[...] = jnp.zeros_like(QA)
            QR[...] = jnp.zeros_like(QR)
            SS[...] = jnp.zeros_like(SS)
            for q in range(2):
                for k in range(4):
                    eb_sib_in(q, k).wait_recv()

                def blocks(mm):
                    x = EB[q, :, :, lane(mm * 256, 256)].astype(F32)
                    return [x[:, i * 8:i * 8 + 8, :].reshape(ROWS, 256) for i in range(2)]

                def body(mm, total):
                    for half, xs in enumerate(blocks(mm)):
                        g = half * 2 + q
                        cols = lane(g * 2048 + mm * 256, 256)
                        XE.at[g, mm][...] = (xs * gains[:, cols]).astype(BF)
                        square = xs * xs
                        total = total + square[:, 0:128] + square[:, 128:256]
                    return total

                SS[...] = lax.fori_loop(0, NM, body, SS[...])
                for half, xs in enumerate(blocks(m)):
                    RX.at[half * 2 + q][...] = xs.astype(BF)
                if q == 0:
                    for n in range(3):
                        load(n, 0).wait()
                        load(n, 1).wait()

                def both(i, _):
                    g = 2 * i + q
                    for who in range(2):
                        x = jnp.concatenate([XE[g, 2 * zz + who] for zz in range(NZ)], axis=1)
                        multiply(x, who, g, 0)
                    return 0

                lax.fori_loop(0, 2, both, 0)
            for k in (2, 1, 3):
                res(k).start()
            R.at[d][...] = RX[d]

        @pl.when(s > 0)
        def _():
            def arrived(k):
                g = ypeer(k)
                hop_in(g).wait_recv()
                for j in (2, 1, 3):
                    ag_z(g, j).start()

            def columns(k):
                g = ypeer(k)
                for j in (1, 3, 2):
                    ag_z_in(g, j).wait_recv()
                return jnp.concatenate([X[g, zz] for zz in range(NZ)], axis=1)

            def both(k, start=False):
                x = columns(k)
                multiply(x, 1, ypeer(k), 1, start)
                multiply(x, 0, ypeer(k), 0, start)

            def squares_of(k):
                total = jnp.zeros((ROWS, 128), F32)
                for zz in range(NZ):
                    x = X[ypeer(k), zz].astype(F32)
                    square = x * x
                    total = total + square[:, 0:128] + square[:, 128:256]
                return total

            arrived(0)
            arrived(3)
            arrived(1)
            arrived(2)
            both(0, True)
            squares = squares_of(0)
            both(3)
            squares = squares + squares_of(3)
            both(1)
            squares = squares + squares_of(1)
            x = columns(2)
            multiply(x, 1, ypeer(2), 1)
            squares = squares + squares_of(2)
            QA.at[1][:, 768:896] = squares
            sums_out().start()
            multiply(x, 0, ypeer(2), 0)
            sums_out().wait_recv()
            SS[...] = squares + QR[:, 768:896]

        r = lax.rsqrt(jnp.sum(SS[...], axis=1, keepdims=True) * (1.0 / D) + EPS)
        cos = cosine[...]
        sin = sine[...]

        def summed(first, last):
            return QA[0, :, first:last] + QR[:, first:last]

        def rope(x):
            return (x * cos + pltpu.roll(x, 64, 1) * sin).astype(BF)

        query = jnp.concatenate(
            [rope(summed(j * HD, (j + 1) * HD) * r) for j in range(4)], axis=0)
        key = rope(summed(512, 640) * r)
        value = (summed(640, 768) * r).astype(BF)
        scores = lax.dot_general(query, key, (((1,), (1,)), ((), ())),
                                 preferred_element_type=F32) * (HD ** -0.5)
        scores = scores + MASK[...]
        highest = jnp.max(scores, axis=-1, keepdims=True)
        weights = jnp.exp(scores - highest)
        probs = (weights / jnp.sum(weights, axis=-1, keepdims=True)).astype(BF)
        mixed = jnp.dot(probs, value, preferred_element_type=F32).astype(BF)
        for j in range(4):
            C.at[d][:, j * HD:(j + 1) * HD] = mixed[j * ROWS:(j + 1) * ROWS]
        for k in (2, 1, 3):
            ctx(k).start()

        wo_load.wait()

        def project(g):
            for zz in range(NZ):
                p = jnp.dot(C[g], WO[:, zz * 512:zz * 512 + 512], preferred_element_type=F32)
                low, high = p[:, :256], p[:, 256:]
                PO.at[g, zz][...] = jnp.where(c == 0, low, high)
                PS.at[g, zz][...] = jnp.where(c == 0, high, low).astype(BF)
            part(g).start()

        def pair(g):
            part(g).wait_recv()
            for k in (2, 1, 3):
                zt = (z + k) % NZ
                ZS.at[g, k][...] = (PO[g, zt] + PR[g, zt].astype(F32)).astype(BF)
                zred(g, k).start()

        def total_of(g):
            total = PO[g, z] + PR[g, z].astype(F32) + R[g].astype(F32)
            for k in (1, 3, 2):
                zred(g, k).wait_recv()
                total = total + ZR[g, k].astype(F32)
            HP.at[g][...] = total.astype(BF)

            @pl.when(s < NX - 1)
            def _():
                hop(g).start()

        project(d)

        @pl.when(s == 0)
        def _():
            for k in (1, 3, 2):
                res_in(k).wait_recv()

        @pl.when(s > 0)
        def _():
            hop_raw().wait_recv()

        pair(d)
        for k in (1, 3):
            ctx_in(k).wait_recv()
            project(ypeer(k))
        pair(ypeer(1))
        pair(ypeer(3))
        total_of(d)
        ctx_in(2).wait_recv()
        project(ypeer(2))
        total_of(ypeer(1))
        pair(ypeer(2))
        total_of(ypeer(3))
        total_of(ypeer(2))

        @pl.when(s < NX - 1)
        def _():
            hop_raw().start()

        @pl.when(s % 2 == 1)
        def _():
            emit(s // 2)

    def emit(b):
        mine = Y.at[b, c, 0, 0]
        nt = (((1,), (1,)), ((), ()))
        wide = HP[...].reshape(NY * ROWS, 256).astype(F32)
        cols = lane(d * 2048 + m * 256, 256)
        scaled = (wide * fgain[:, cols]).astype(BF)
        live_rows = jnp.dot(SEL[0:LIVE], scaled, preferred_element_type=F32)
        mine[0:LIVE, :] = live_rows.astype(BF)
        square = wide * wide
        top = square.astype(BF)
        rest = (square - top.astype(F32)).astype(BF)
        ones = jnp.ones((16, 256), BF)
        sums = (lax.dot_general(ones, top, nt, preferred_element_type=F32)
                + lax.dot_general(ones, rest, nt, preferred_element_type=F32))
        top = sums.astype(BF).astype(F32)
        row = lax.broadcasted_iota(jnp.int32, (16, NY * ROWS), 0)
        packed = jnp.where(row == 0, top, jnp.where(row == 1, sums - top, 0.0)).astype(BF)
        squares = lax.dot_general(packed, SEL[...], nt, preferred_element_type=F32)
        mine[LIVE:PIECE, :] = squares.astype(BF)
        for k in (2, 1, 3):
            y_x(b, k).start()
        spread_own(b)

    def first_dev(k):
        return (jnp.where(c == 0, ypeer(k), d), s, jnp.where(c == 0, m, zpeer(k)))

    def second_dev(k):
        return (jnp.where(c == 0, d, ypeer(k)), s, jnp.where(c == 0, zpeer(k), m))

    def ycopy(src, dst, b, i, j, dev):
        return rcopy(src, dst, y_s.at[b, i], y_r.at[b, j], dev)

    def own(b, rows):
        return Y.at[b, c, 0, 0, rows]

    def y_x(b, k):
        return ycopy(own(b, whole), own(b, whole), b, k, 0, (d, (s + k) % NX, m))

    whole = pl.ds(0, PIECE)

    def y_first(b, k):
        slot = (1, 3, 2)[k - 1]
        return ycopy(own(b, whole), Y.at[b, c, 0, slot, whole], b, 5 + k, slot, first_dev(k))

    sets = (pl.ds(0, 1), pl.ds(1, 2), pl.ds(3, 1))

    def y_second(b, part_no, k):
        slot = 1 if k == 1 else 2
        return ycopy(Y.at[b, c, 0, sets[part_no], whole], Y.at[b, c, slot, sets[part_no], whole],
                     b, 11 + part_no * 2 + (slot - 1), 1 + 3 * slot + part_no, second_dev(k))

    def y_second_relay(b, i):
        slot, k = (1, 1) if i < 2 else (2, 3)
        return ycopy(Y.at[b, c, slot, i, whole], Y.at[b, c, 3, i, whole],
                     b, 17 + i, 10 + i, second_dev(k))

    forwards = ((0, 0, 1), (0, 1, 2), (0, 3, 1), (1, 0, 4), (2, 0, 4), (3, 0, 2), (3, 2, 2))

    def y_fwd(b, n, who):
        j, i, size = forwards[n]
        ref = Y.at[b, who, j, pl.ds(i, size), whole]
        return ycopy(ref, ref, b, 21 + n, 14 + n, here)

    def spread_own(b):
        for k in (2, 1, 3):
            y_first(b, k).start()
        for k in (1, 3):
            y_second(b, 0, k).start()
        y_fwd(b, 0, c).start()

    def dots(b, cc, j, start):
        pieces = jnp.concatenate([Y[b, cc, j, i, 0:256, :] for i in range(4)], axis=1)
        term = lax.dot_general(HEAD[cc, j], pieces, (((1,), (1,)), ((), ())),
                               preferred_element_type=F32)
        LT[...] = term if start else LT[...] + term

    def wanted_rows():
        slot, position = row_slot(lax.broadcasted_iota(jnp.int32, (32, 256), 1))
        place = (position == lax.broadcasted_iota(jnp.int32, (32, 256), 0)).astype(BF)
        tokens = targets[...]
        nt = (((1,), (1,)), ((), ()))
        keep = slot[0:8] == lax.broadcasted_iota(jnp.int32, (8, 256), 0)
        parts = []
        for term in (tokens // 256, tokens % 256):
            every = jnp.dot(term.astype(F32).astype(BF), place, preferred_element_type=F32)
            mine = jnp.sum(jnp.where(keep, every, 0.0), axis=0, keepdims=True)
            spread = jnp.broadcast_to(mine, (16, 256)).astype(BF)
            parts.append(lax.dot_general(spread, SEL[...], nt, preferred_element_type=F32)[0:1])
        return parts[0] * 256.0 + parts[1]

    def gather(b):
        source = 2 * b + 1

        @pl.when(s != source)
        def _():
            y_x(b, 1).wait_recv()
            spread_own(b)

        y_first(b, 1).wait_recv()
        y_first(b, 3).wait_recv()
        for k in (1, 3):
            y_second(b, 1, k).start()
        y_fwd(b, 1, c).start()
        y_second(b, 0, 1).wait_recv()
        y_second_relay(b, 0).start()
        y_second(b, 0, 3).wait_recv()
        y_first(b, 2).wait_recv()
        for k in (1, 3):
            y_second(b, 2, k).start()
        y_fwd(b, 2, c).start()
        y_second(b, 1, 1).wait_recv()
        y_second_relay(b, 1).start()
        y_second(b, 1, 3).wait_recv()
        y_second_relay(b, 2).start()
        y_second(b, 2, 3).wait_recv()
        y_second_relay(b, 3).start()
        y_fwd(b, 4, c).start()
        y_second(b, 2, 1).wait_recv()
        y_fwd(b, 3, c).start()

    def finish(b):
        dots(b, c, 0, True)
        for n in range(3):
            y_fwd(b, n, 1 - c).wait_recv()
        dots(b, 1 - c, 0, False)
        dots(b, c, 2, False)
        dots(b, c, 1, False)
        y_second_relay(b, 0).wait_recv()
        y_second_relay(b, 1).wait_recv()
        y_fwd(b, 5, c).start()
        y_fwd(b, 4, 1 - c).wait_recv()
        dots(b, 1 - c, 2, False)
        y_second_relay(b, 2).wait_recv()
        y_second_relay(b, 3).wait_recv()
        y_fwd(b, 6, c).start()
        y_fwd(b, 3, 1 - c).wait_recv()
        dots(b, 1 - c, 1, False)
        dots(b, c, 3, False)
        y_fwd(b, 5, 1 - c).wait_recv()
        y_fwd(b, 6, 1 - c).wait_recv()
        dots(b, 1 - c, 3, False)

        extra = jnp.zeros((16, 256), F32)
        for cc in range(2):
            for j in range(4):
                for i in range(4):
                    extra = extra + Y[b, cc, j, i, LIVE:PIECE, :].astype(F32)
        sums = jnp.sum(extra, axis=0, keepdims=True)
        r = lax.rsqrt(sums * (1.0 / D) + EPS)
        logits = LT[...] * r
        highest = jnp.max(logits, axis=0, keepdims=True)
        summed = jnp.sum(jnp.exp(logits - highest), axis=0, keepdims=True)
        vocab = HEAD.shape[2]
        first = ((d * NX + s) * NM + m) * vocab
        index = (lax.broadcasted_iota(jnp.int32, logits.shape, 0) + first).astype(F32)
        wanted = wanted_rows()
        picked = jnp.sum(jnp.where(index == wanted, logits, 0.0), axis=0, keepdims=True)
        alive = lax.broadcasted_iota(jnp.int32, (1, 256), 1) < LIVE
        for n, value in enumerate((highest, summed, picked)):
            value = jnp.where(alive, value, 1.0)
            for half in range(2):
                STO[pl.ds(n * 4 + b * 2 + half, 1), :] = value[:, half * 128:half * 128 + 128]

    def step(t, _):
        last = s == NX - 1
        place = jnp.where(last, 1, 0)

        @pl.when(t == place)
        def _():
            layer()

        @pl.when(jnp.where(last, (t == 0) | (t == 2), (t == 1) | (t == 3)))
        def _():
            gather(jnp.where(t < 2, 0, 1))

        @pl.when(jnp.where(last, t >= 3, (t == 2) | (t == 4)))
        def _():
            @pl.when(t == jnp.where(last, 3, 2))
            def _():
                head_load.wait()
            finish(jnp.where(t == 4, 1, 0))
        return 0

    @pl.when(s == 0)
    def _():
        for q in range(2):
            for k in (2, 1, 3, 0):
                (eb_z(q, k) if k else eb_fwd(q, 0)).start()

    prepare()
    STO[...] = jnp.zeros_like(STO)
    lax.fori_loop(0, 5, step, 0)

    def merge(ref, count):
        parts = [ref[j] for j in range(count)]
        highest = parts[0][0:4]
        for p in parts[1:]:
            highest = jnp.maximum(highest, p[0:4])
        summed = jnp.zeros_like(highest)
        picked = jnp.zeros_like(highest)
        for p in parts:
            summed = summed + p[4:8] * jnp.exp(p[0:4] - highest)
            picked = picked + p[8:12]
        return highest, summed, picked

    def stacked(highest, summed, picked):
        return jnp.concatenate([highest, summed, picked, jnp.zeros_like(picked)], axis=0)

    pairs = [(j, k) for j in range(NX) for k in range(NY) if j or k]

    def st_yx(n):
        j, k = pairs[n]
        mine = s * NY + d
        return rcopy(SA.at[mine], SA.at[mine], st_s.at[0, n], st_r.at[0, mine],
                     (ypeer(k), (s + j) % NX, m))

    def st_yx_in(n):
        j, k = pairs[n]
        other = ((s + j) % NX) * NY + ypeer(k)
        return rcopy(SA.at[other], SA.at[other], st_s.at[0, n], st_r.at[0, other], here)

    def m_of(k):
        return (m + k) % NM

    def st_m(k):
        return rcopy(SB.at[m], SB.at[m], st_s.at[1, k], st_r.at[1, m], (d, s, m_of(k)))

    def st_m_in(k):
        mm = m_of(k)
        return rcopy(SB.at[mm], SB.at[mm], st_s.at[1, k], st_r.at[1, mm], (d, s, mm))

    SA.at[s * NY + d][...] = STO[...]
    for n in range(15):
        st_yx(n).start()
    for n in range(15):
        st_yx_in(n).wait_recv()
    SB.at[m][...] = stacked(*merge(SA, NX * NY))
    for k in (4, 3, 5, 2, 6, 1, 7):
        st_m(k).start()
    for k in (1, 7, 2, 6, 3, 5, 4):
        st_m_in(k).wait_recv()
    highest, summed, picked = merge(SB, NM)
    logprob = picked - (highest + jnp.log(summed))
    terms = []
    for e in range(2):
        rest = jnp.concatenate([logprob[2 * e:2 * e + 1], logprob[2 * e + 1:2 * e + 2]], axis=1)
        for _ in range(3):
            term = rest.astype(BF).astype(F32)
            terms.append(term)
            rest = rest - term
    row = lax.broadcasted_iota(jnp.int32, (16, 256), 0)
    stack = jnp.zeros((16, 256), F32)
    for j, term in enumerate(terms):
        stack = jnp.where(row == j, term, stack)
    stack = stack.astype(BF)
    index = lax.broadcasted_iota(jnp.int32, (256, 32), 0)
    place = lax.broadcasted_iota(jnp.int32, (256, 32), 1)
    results = []
    for i in range(2):
        chosen = source_of[2 * d + i]
        start = 0
        for other in range(8):
            start = start + jnp.where(chosen > other, live[other], 0)
        take = ((index == start + place) & (place < live[chosen])).astype(F32).astype(BF)
        got = jnp.dot(stack, take, preferred_element_type=F32)
        results.append([got[j:j + 1] + got[j + 1:j + 2] + got[j + 2:j + 3] for j in (0, 3)])
    for e in range(2):
        first = lax.broadcasted_iota(jnp.int32, (2, 32), 0) == 0
        out.at[e][...] = jnp.where(first, results[0][e], results[1][e])

    @pl.when(s == 0)
    def _():
        for q in range(2):
            for k in range(1, 4):
                eb_z(q, k).wait_send()
            for k in range(4):
                eb_fwd(q, k).wait_send()
        for k in range(1, 4):
            res(k).wait_send()

    @pl.when(s > 0)
    def _():
        for g in range(NY):
            for k in range(1, 4):
                ag_z(g, k).wait_send()
        sums_out().wait_send()
        for n in range(3):
            swap(n).wait_send()

    @pl.when(s < NX - 1)
    def _():
        for g in range(NY):
            hop(g).wait_send()
        hop_raw().wait_send()

    for g in range(NY):
        for k in range(1, 4):
            zred(g, k).wait_send()
        part(g).wait_send()
    for k in range(1, 4):
        ctx(k).wait_send()
    for n in range(15):
        st_yx(n).wait_send()
    for k in range(1, 8):
        st_m(k).wait_send()
    for b in range(2):
        @pl.when(s == 2 * b + 1)
        def _():
            for k in (1, 2, 3):
                y_x(b, k).wait_send()

        for k in (1, 2, 3):
            y_first(b, k).wait_send()
        for k in (1, 3):
            for n in range(3):
                y_second(b, n, k).wait_send()
        for i in range(4):
            y_second_relay(b, i).wait_send()
        for n in range(7):
            y_fwd(b, n, c).wait_send()


def tables():
    row = np.arange(ROWS)
    position = (row // 8) * 4 + row % 4
    half = HD // 2
    freqs = (ROPE_BASE ** (-np.arange(half) * 2.0 / HD)).astype(np.float32)
    angles = (position.astype(np.float32)[:, None] * freqs[None, :]).astype(np.float64)
    cos, sin = np.cos(angles), np.sin(angles)
    return (np.concatenate([cos, cos], 1).astype(np.float32),
            np.concatenate([-sin, sin], 1).astype(np.float32))


def per_device(
    embeds, targets, lengths, source, attn_gain, w_query, w_key, w_value, w_out, final_gain, head
):
    vocab = head.shape[0]
    cos, sin = tables()
    vmem = pl.BlockSpec(memory_space=pltpu.VMEM)
    hbm = pl.BlockSpec(memory_space=pl.ANY)
    smem = pl.BlockSpec(memory_space=pltpu.SMEM)
    dma = pltpu.SemaphoreType.DMA
    stats = pl.pallas_call(
        kernel,
        out_shape=jax.ShapeDtypeStruct((2, 2, 32), F32),
        in_specs=[hbm, smem, smem] + [hbm] * 10,
        out_specs=vmem,
        scratch_shapes=[
            pltpu.VMEM((2, 4, D), BF),
            pltpu.VMEM((8, 32), jnp.int32),
            pltpu.VMEM((1, D), F32),
            pltpu.VMEM((1, D), F32),
            pltpu.VMEM((ROWS, HD), F32),
            pltpu.VMEM((ROWS, HD), F32),
            pltpu.VMEM((2, 16, 256, 768), BF),
            pltpu.VMEM((QW, 2048), BF),
            pltpu.VMEM((2, 4, vocab, 1024), BF),
            pltpu.VMEM((2, NM, 16, 2048), BF),
            pltpu.VMEM((NY, NM, ROWS, 256), BF),
            pltpu.VMEM((NY, NZ, ROWS, 256), BF),
            pltpu.VMEM((NY, ROWS, 256), BF),
            pltpu.VMEM((4 * ROWS, ROWS), F32),
            pltpu.VMEM((256, 256), BF),
            pltpu.VMEM((ROWS, 128), F32),
            pltpu.VMEM((2, ROWS, 896), F32),
            pltpu.VMEM((ROWS, 896), F32),
            pltpu.VMEM((NY, ROWS, 256), BF),
            pltpu.VMEM((NY, ROWS, QW), BF),
            pltpu.VMEM((NY, NZ, ROWS, 256), BF),
            pltpu.VMEM((NY, NZ, ROWS, 256), BF),
            pltpu.VMEM((NY, NZ, ROWS, 256), F32),
            pltpu.VMEM((NY, NZ, ROWS, 256), BF),
            pltpu.VMEM((NY, NZ, ROWS, 256), BF),
            pltpu.VMEM((NY, ROWS, 256), BF),
            pltpu.VMEM((2, 2, 4, 4, 256, 256), BF),
            pltpu.VMEM((vocab, 256), F32),
            pltpu.VMEM((16, 128), F32),
            pltpu.VMEM((NX * NY, 16, 128), F32),
            pltpu.VMEM((NM, 16, 128), F32),
            dma((20,)),
            dma((3,)), dma((3,)),
            dma, dma,
            dma((2, 8)), dma((2, 8)),
            dma((5,)), dma((5,)),
            dma((4, 8)), dma((4, 8)),
            dma((4,)), dma((4,)),
            dma((4,)), dma((4,)),
            dma((4,)), dma((4,)),
            dma((4, 4)), dma((4, 4)),
            dma((2, 30)), dma((2, 22)),
            dma((2, 16)), dma((2, 16)),
        ],
        compiler_params=pltpu.CompilerParams(
            collective_id=0, has_side_effects=True, vmem_limit_bytes=60 * 1024 * 1024),
        cost_estimate=pl.CostEstimate(flops=8_000_000_000, bytes_accessed=24_000_000,
                                      transcendentals=300_000),
    )(
        embeds, lengths, source, targets, attn_gain, final_gain.reshape(1, D), jnp.asarray(cos), jnp.asarray(sin),
        w_query.reshape(16, 2, 256, 512), w_key.reshape(16, 2, 256, 128),
        w_value.reshape(16, 2, 256, 128), w_out.reshape(512, 2048), head,
    )
    return (stats[0], stats[1])


def solution(mesh):
    return jax.shard_map(
        per_device,
        mesh=mesh,
        in_specs=(
            P("dp", "mp", None),
            P(),
            P(),
            P(),
            P("section", None),
            P("section", None, "mp"),
            P("section", None, "mp"),
            P("section", None, "mp"),
            P("section", "mp", "dp"),
            P(),
            P(("dp", "section", "mp"), None),
        ),
        out_specs=(P("dp", None), P("dp", None)),
        check_vma=False,
    )
```

```python
import jax
import jax.numpy as jnp
import numpy as np
from jax import lax
from jax.experimental import pallas as pl
from jax.experimental.pallas import tpu as pltpu
from jax.sharding import PartitionSpec as P

HD = 128
EPS = 1e-05
ROPE_BASE = 500000.0
NY = 4
NX = 4
NZ = 4
NM = 8
ROWS = 64
D = 8192
QW = 512
MESH = pl.DeviceIdType.MESH
BF = jnp.bfloat16
F32 = jnp.float32


def lane(start, size):
    return pl.ds(pl.multiple_of(start, 128), size)


def kernel(
    emb_in, live, source_of, targets_in, gain, fgain_in, cosine_in, sine_in, wq, wk, wv, wo, head,
    out,
    emb, targets, gains, fgain, cosine, sine, W, WO, HEAD, EB, XE, X, RX, MASK, SS, QA, QR, R, C, PS, PR, PO, ZS, ZR, HP, Y, LT, SQ, STO, SA, SB,
    w_sem, sw_s, sw_r, qr_s, qr_r, eb_s, eb_r, hop_s, hop_r, ag_s, ag_r, res_s, res_r, ctx_s, ctx_r, ps_s, ps_r,
    zz_s, zz_r, y_s, y_r, st_s, st_r,
):
    d = lax.axis_index("dp")
    s = lax.axis_index("section")
    m = lax.axis_index("mp")
    z = m // 2
    c = m % 2
    sib = z * 2 + (1 - c)

    def ypeer(k):
        return (d + k) % NY

    def zpeer(k):
        return ((z + k) % NZ) * 2 + c

    def zother(k):
        return ((z + k) % NZ) * 2 + (1 - c)

    def rcopy(src, dst, ssem, rsem, dev):
        return pltpu.make_async_remote_copy(
            src_ref=src, dst_ref=dst, send_sem=ssem, recv_sem=rsem,
            device_id=dev, device_id_type=MESH,
        )

    here = (d, s, sib)

    barrier = pltpu.get_barrier_semaphore()
    partners = []
    for k in range(1, 4):
        partners.append((ypeer(k), s, m))
        partners.append((d, (s + k) % NX, m))
        partners.append((d, s, zpeer(k)))
        partners.append((d, s, zother(k)))
        partners.append((ypeer(k), (s + 1) % NX, m))
        partners.append((ypeer(k), (s + 3) % NX, m))
        partners.append((ypeer(k), (s + 2) % NX, m))
    partners.append(here)
    for dev in partners:
        pl.semaphore_signal(barrier, inc=1, device_id=dev, device_id_type=MESH)
    small = [
        pltpu.make_async_copy(src, dst, w_sem.at[14 + n])
        for n, (src, dst) in enumerate((
            (emb_in, emb), (gain, gains), (cosine_in, cosine), (sine_in, sine),
            (fgain_in, fgain), (targets_in, targets)))
    ]
    for copy in small:
        copy.start()
    parts = ((wq, pl.ds(0, 512)), (wk, pl.ds(512, 128)), (wv, pl.ds(640, 128)))

    def load(n, first):
        src, lanes = parts[n]
        take = 1 if first else jnp.where(s == 0, 0, c)
        return pltpu.make_async_copy(src.at[:, take], W.at[first, :, :, lanes],
                                     w_sem.at[3 * first + n])

    def swap(n):
        src, lanes = parts[n]
        return rcopy(src.at[:, 1 - c], W.at[1, :, :, lanes], sw_s.at[n], sw_r.at[n], here)

    wo_load = pltpu.make_async_copy(wo, WO, w_sem.at[12])
    for n in range(3):
        load(n, 0).start()

    @pl.when(s == 0)
    def _():
        for n in range(3):
            load(n, 1).start()

    head_load = pltpu.make_async_copy(HEAD, HEAD, w_sem.at[13])

    def prepare():
        wo_load.start()
        offsets = (0, 3, 1, 2)
        for cc in range(2):
            for j in range(4):
                for i in range(4):
                    g, zz = (offsets[i], offsets[j]) if cc == 0 else (offsets[j], offsets[i])
                    col = ypeer(g) * 2048 + ((z + zz) % NZ) * 512 + cc * 256
                    pltpu.make_async_copy(head.at[:, lane(col, 256)],
                                          HEAD.at[cc, j, :, i * 256:i * 256 + 256],
                                          w_sem.at[13]).start()
        shape = (4 * ROWS, ROWS)
        rq = lax.broadcasted_iota(jnp.int32, shape, 0) % ROWS
        rk = lax.broadcasted_iota(jnp.int32, shape, 1)
        slot_q, slot_k = (rq // 4) % 2, (rk // 4) % 2
        pos_q, pos_k = (rq // 8) * 4 + rq % 4, (rk // 8) * 4 + rk % 4
        live_k = jnp.where(slot_k == 0, live[2 * d], live[2 * d + 1])
        allowed = (slot_q == slot_k) & (pos_k <= pos_q) & (pos_k < live_k)
        MASK[...] = jnp.where(allowed, F32(0.0), F32(-1e30))

        @pl.when(s > 0)
        def _():
            for n in range(3):
                load(n, 0).wait()
                swap(n).wait_recv()
            for copy in small[1:2]:
                copy.wait()
            diagonal = (lax.broadcasted_iota(jnp.int32, (256, 256), 0)
                        == lax.broadcasted_iota(jnp.int32, (256, 256), 1))

            def scale(i, _):
                cols = lane((i // NZ) * 2048 + ((i % NZ) * 2 + c) * 256, 256)
                column = jnp.sum(jnp.where(diagonal, gains[:, cols], 0.0), axis=1, keepdims=True)
                for which in range(2):
                    W.at[which, i][...] = (W[which, i].astype(F32) * column).astype(BF)
                return 0

            lax.fori_loop(0, 16, scale, 0)

        @pl.when(s == 0)
        def _():
            for copy in small[1:2]:
                copy.wait()
        for copy in small[2:]:
            copy.wait()

        @pl.when(s > 0)
        def _():
            scale_head()

    def scale_head():
        head_load.wait()

        def off(n):
            return jnp.where(n == 0, 0, jnp.where(n == 1, 3, jnp.where(n == 2, 1, 2)))

        def scale(n, _):
            cc, j, i = n // 16, (n // 4) % 4, n % 4
            g = jnp.where(cc == 0, off(i), off(j))
            zz = jnp.where(cc == 0, off(j), off(i))
            col = ((d + g) % NY) * 2048 + ((z + zz) % NZ) * 512 + cc * 256
            block = HEAD.at[cc, j, :, lane(i * 256, 256)]
            block[...] = (block[...].astype(F32) * fgain[:, lane(col, 256)]).astype(BF)
            return 0

        lax.fori_loop(0, 32, scale, 0)

    def row_slot(lanes):
        return (lanes // 64) * 2 + (lanes // 4) % 2, ((lanes // 8) % 8) * 4 + lanes % 4

    small[0].wait()

    @pl.when(s == 0)
    def _():
        rows = jnp.concatenate([emb[0], emb[1]], axis=0).astype(F32)
        for q in range(2):
            EB.at[q, m][...] = jnp.concatenate(
                [rows[:, q * 2048:q * 2048 + 2048], rows[:, q * 2048 + 4096:q * 2048 + 6144]],
                axis=0).astype(BF)

    pl.semaphore_wait(barrier, len(partners))

    @pl.when(s > 0)
    def _():
        for n in range(3):
            swap(n).start()

    def eb_z(q, k):
        return rcopy(EB.at[q, m], EB.at[q, m], eb_s.at[q, k], eb_r.at[q, m], (d, s, zpeer(k)))

    def eb_z_in(q, k):
        mk = zpeer(k)
        return rcopy(EB.at[q, mk], EB.at[q, mk], eb_s.at[q, k], eb_r.at[q, mk], here)

    def eb_fwd(q, k):
        mk = zpeer(k)
        return rcopy(EB.at[q, mk], EB.at[q, mk], eb_s.at[q, 4 + k], eb_r.at[q, mk], here)

    def eb_sib_in(q, k):
        mk = zother(k)
        return rcopy(EB.at[q, mk], EB.at[q, mk], eb_s.at[q, 4 + k], eb_r.at[q, mk], here)

    def hop(g):
        return rcopy(HP.at[g], X.at[d, z], hop_s.at[g], hop_r.at[d], (g, (s + 1) % NX, m))

    def hop_in(g):
        return rcopy(HP.at[g], X.at[g, z], hop_s.at[g], hop_r.at[g], here)

    def hop_raw():
        return rcopy(HP, R, hop_s.at[4], hop_r.at[4], (d, (s + 1) % NX, m))

    def ag_z(g, k):
        return rcopy(X.at[g, z], X.at[g, z], ag_s.at[g, k], ag_r.at[g, z], (d, s, zpeer(k)))

    def ag_z_in(g, k):
        zk = (z + k) % NZ
        return rcopy(X.at[g, zk], X.at[g, zk], ag_s.at[g, k], ag_r.at[g, zk], here)

    def sums_out():
        return rcopy(QA.at[1], QR, qr_s, qr_r, here)

    def res(k):
        g = ypeer(k)
        return rcopy(RX.at[g], R.at[d], res_s.at[k], res_r.at[d], (g, s, m))

    def res_in(k):
        g = ypeer(k)
        return rcopy(RX.at[g], R.at[g], res_s.at[k], res_r.at[g], here)

    def ctx(k):
        return rcopy(C.at[d], C.at[d], ctx_s.at[k], ctx_r.at[d], (ypeer(k), s, m))

    def ctx_in(k):
        g = ypeer(k)
        return rcopy(C.at[g], C.at[g], ctx_s.at[k], ctx_r.at[g], here)

    def part(g):
        return rcopy(PS.at[g], PR.at[g], ps_s.at[g], ps_r.at[g], here)

    def zred(g, k):
        return rcopy(ZS.at[g, k], ZR.at[g, k], zz_s.at[g, k], zz_r.at[g, k], (d, s, zpeer(k)))

    def layer():
        def multiply(x, which, rows, n, start=False):
            w = W[which, pl.ds(rows * NZ, NZ)].reshape(4 * 256, 768)
            term = jnp.dot(x, w, preferred_element_type=F32)
            QA.at[n][:, 0:768] = term if start else QA[n, :, 0:768] + term

        @pl.when(s == 0)
        def _():
            for q in range(2):
                for k in (1, 3, 2):
                    eb_z_in(q, k).wait_recv()
                    eb_fwd(q, k).start()
            QA[...] = jnp.zeros_like(QA)
            QR[...] = jnp.zeros_like(QR)
            SS[...] = jnp.zeros_like(SS)
            for q in range(2):
                for k in range(4):
                    eb_sib_in(q, k).wait_recv()

                def blocks(mm):
                    x = EB[q, :, :, lane(mm * 256, 256)].astype(F32)
                    return [x[:, i * 8:i * 8 + 8, :].reshape(ROWS, 256) for i in range(2)]

                def body(mm, total):
                    for half, xs in enumerate(blocks(mm)):
                        g = half * 2 + q
                        cols = lane(g * 2048 + mm * 256, 256)
                        XE.at[g, mm][...] = (xs * gains[:, cols]).astype(BF)
                        square = xs * xs
                        total = total + square[:, 0:128] + square[:, 128:256]
                    return total

                SS[...] = lax.fori_loop(0, NM, body, SS[...])
                for half, xs in enumerate(blocks(m)):
                    RX.at[half * 2 + q][...] = xs.astype(BF)
                if q == 0:
                    for n in range(3):
                        load(n, 0).wait()
                        load(n, 1).wait()

                def both(i, _):
                    g = 2 * i + q
                    for who in range(2):
                        x = jnp.concatenate([XE[g, 2 * zz + who] for zz in range(NZ)], axis=1)
                        multiply(x, who, g, 0)
                    return 0

                lax.fori_loop(0, 2, both, 0)
            for k in (2, 1, 3):
                res(k).start()
            R.at[d][...] = RX[d]

        @pl.when(s > 0)
        def _():
            def arrived(k):
                g = ypeer(k)
                hop_in(g).wait_recv()
                for j in (2, 1, 3):
                    ag_z(g, j).start()

            def columns(k):
                g = ypeer(k)
                for j in (1, 3, 2):
                    ag_z_in(g, j).wait_recv()
                return jnp.concatenate([X[g, zz] for zz in range(NZ)], axis=1)

            def both(k, start=False):
                x = columns(k)
                multiply(x, 1, ypeer(k), 1, start)
                multiply(x, 0, ypeer(k), 0, start)

            def squares_of(k):
                total = jnp.zeros((ROWS, 128), F32)
                for zz in range(NZ):
                    x = X[ypeer(k), zz].astype(F32)
                    square = x * x
                    total = total + square[:, 0:128] + square[:, 128:256]
                return total

            arrived(0)
            arrived(3)
            arrived(1)
            arrived(2)
            both(0, True)
            squares = squares_of(0)
            both(3)
            squares = squares + squares_of(3)
            both(1)
            squares = squares + squares_of(1)
            x = columns(2)
            multiply(x, 1, ypeer(2), 1)
            squares = squares + squares_of(2)
            QA.at[1][:, 768:896] = squares
            sums_out().start()
            multiply(x, 0, ypeer(2), 0)
            sums_out().wait_recv()
            SS[...] = squares + QR[:, 768:896]

        r = lax.rsqrt(jnp.sum(SS[...], axis=1, keepdims=True) * (1.0 / D) + EPS)
        cos = cosine[...]
        sin = sine[...]

        def summed(first, last):
            return QA[0, :, first:last] + QR[:, first:last]

        def rope(x):
            return (x * cos + pltpu.roll(x, 64, 1) * sin).astype(BF)

        query = jnp.concatenate(
            [rope(summed(j * HD, (j + 1) * HD) * r) for j in range(4)], axis=0)
        key = rope(summed(512, 640) * r)
        value = (summed(640, 768) * r).astype(BF)
        scores = lax.dot_general(query, key, (((1,), (1,)), ((), ())),
                                 preferred_element_type=F32) * (HD ** -0.5)
        scores = scores + MASK[...]
        highest = jnp.max(scores, axis=-1, keepdims=True)
        weights = jnp.exp(scores - highest)
        probs = (weights / jnp.sum(weights, axis=-1, keepdims=True)).astype(BF)
        mixed = jnp.dot(probs, value, preferred_element_type=F32).astype(BF)
        for j in range(4):
            C.at[d][:, j * HD:(j + 1) * HD] = mixed[j * ROWS:(j + 1) * ROWS]
        for k in (2, 1, 3):
            ctx(k).start()

        wo_load.wait()

        def project(g):
            for zz in range(NZ):
                p = jnp.dot(C[g], WO[:, zz * 512:zz * 512 + 512], preferred_element_type=F32)
                low, high = p[:, :256], p[:, 256:]
                PO.at[g, zz][...] = jnp.where(c == 0, low, high)
                PS.at[g, zz][...] = jnp.where(c == 0, high, low).astype(BF)
            part(g).start()

        def pair(g):
            part(g).wait_recv()
            for k in (2, 1, 3):
                zt = (z + k) % NZ
                ZS.at[g, k][...] = (PO[g, zt] + PR[g, zt].astype(F32)).astype(BF)
                zred(g, k).start()

        def total_of(g):
            total = PO[g, z] + PR[g, z].astype(F32) + R[g].astype(F32)
            for k in (1, 3, 2):
                zred(g, k).wait_recv()
                total = total + ZR[g, k].astype(F32)
            HP.at[g][...] = total.astype(BF)

            @pl.when(s < NX - 1)
            def _():
                hop(g).start()

        project(d)

        @pl.when(s == 0)
        def _():
            for k in (1, 3, 2):
                res_in(k).wait_recv()

        @pl.when(s > 0)
        def _():
            hop_raw().wait_recv()

        pair(d)
        for k in (1, 3):
            ctx_in(k).wait_recv()
            project(ypeer(k))
        pair(ypeer(1))
        pair(ypeer(3))
        def own_chunk(k):
            @pl.when(s == NX - 1)
            def _():
                stage_own(1, k, True)
                if k >= 1:
                    stage_first(1, k - 1)
                if k >= 2:
                    stage_second(1, k - 2)

        total_of(d)
        own_chunk(0)
        ctx_in(2).wait_recv()
        project(ypeer(2))
        total_of(ypeer(1))
        pair(ypeer(2))
        own_chunk(1)
        total_of(ypeer(3))
        own_chunk(2)
        total_of(ypeer(2))
        own_chunk(3)

        @pl.when(s < NX - 1)
        def _():
            hop_raw().start()

        @pl.when(s == 1)
        def _():
            def body(k, _):
                stage_own(0, k, True)
                return 0

            lax.fori_loop(0, 4, body, 0)

    def first_dev(k):
        return (jnp.where(c == 0, ypeer(k), d), s, jnp.where(c == 0, m, zpeer(k)))

    def second_dev(k):
        return (jnp.where(c == 0, d, ypeer(k)), s, jnp.where(c == 0, zpeer(k), m))

    def ycopy(src, dst, b, k, i, j, dev):
        return rcopy(src, dst, y_s.at[b, k, i], y_r.at[b, k, j], dev)

    def y_x(b, k, n):
        ref = Y.at[b, k, c, 0, 0]
        return ycopy(ref, ref, b, k, n, 0, (d, (s + n) % NX, m))

    def y_first(b, k, n):
        slot = (1, 3, 2)[n - 1]
        return ycopy(Y.at[b, k, c, 0, 0], Y.at[b, k, c, 0, slot], b, k, 3 + n, slot, first_dev(n))

    sets = (pl.ds(0, 1), pl.ds(1, 2), pl.ds(3, 1))

    def y_second(b, k, part_no, n):
        slot = 1 if n == 1 else 2
        return ycopy(Y.at[b, k, c, 0, sets[part_no]], Y.at[b, k, c, slot, sets[part_no]], b, k,
                     7 + part_no * 2 + (slot - 1), 1 + 3 * slot + part_no, second_dev(n))

    def y_relay(b, k, half):
        slot, n = ((1, 1), (2, 3))[half]
        two = pl.ds(2 * half, 2)
        return ycopy(Y.at[b, k, c, slot, two], Y.at[b, k, c, 3, two], b, k, 13 + half, 10 + half,
                     second_dev(n))

    forwards = ((0, 0, 1), (0, 1, 2), (0, 3, 1), (1, 0, 4), (2, 0, 4), (3, 0, 2), (3, 2, 2))

    def y_fwd(b, k, n, who):
        j, i, size = forwards[n]
        ref = Y.at[b, k, who, j, pl.ds(i, size)]
        return ycopy(ref, ref, b, k, 15 + n, 12 + n, here)

    def chunk_order(step):
        return jnp.where(step == 3, 2, jnp.where(step == 2, 3, step))

    def stage_own(b, k, source):
        if source:
            Y.at[b, k, c, 0, 0][...] = HP[(d + chunk_order(k)) % NY]
            for n in (2, 1, 3):
                y_x(b, k, n).start()
        else:
            y_x(b, k, 1).wait_recv()
        for n in (2, 1, 3):
            y_first(b, k, n).start()
        for n in (1, 3):
            y_second(b, k, 0, n).start()
        y_fwd(b, k, 0, c).start()

    def stage_first(b, k):
        y_first(b, k, 1).wait_recv()
        y_first(b, k, 3).wait_recv()
        for n in (1, 3):
            y_second(b, k, 1, n).start()
        y_fwd(b, k, 1, c).start()
        y_first(b, k, 2).wait_recv()
        for n in (1, 3):
            y_second(b, k, 2, n).start()
        y_fwd(b, k, 2, c).start()

    def stage_second(b, k):
        for part_no in (0, 1):
            y_second(b, k, part_no, 1).wait_recv()
        y_relay(b, k, 0).start()
        for part_no in (1, 2):
            y_second(b, k, part_no, 3).wait_recv()
        y_relay(b, k, 1).start()
        y_second(b, k, 2, 1).wait_recv()
        y_fwd(b, k, 3, c).start()
        y_second(b, k, 0, 3).wait_recv()
        y_fwd(b, k, 4, c).start()

    def stage_last(b, k):
        for half in range(2):
            y_relay(b, k, half).wait_recv()
            y_fwd(b, k, 5 + half, c).start()
        for n in range(7):
            y_fwd(b, k, n, 1 - c).wait_recv()

    def dots(b, cc, j):
        blocks = []
        for g in range(NY):
            row = []
            total = jnp.zeros((ROWS, 128), F32)
            for i in range(4):
                off_j = jnp.where(j == 0, 0, jnp.where(j == 1, 3, jnp.where(j == 2, 1, 2)))
                sender = (d + jnp.where(cc == 0, (0, 3, 1, 2)[i], off_j)) % NY
                k = chunk_order((g - sender + NY) % NY)
                x = Y[b, k, cc, j, i]
                row.append(x)
                wide = x.astype(F32)
                square = wide * wide
                total = total + square[:, 0:128] + square[:, 128:256]
            SQ.at[b, g][...] += total
            blocks.append(jnp.concatenate(row, axis=1))
        pieces = jnp.concatenate(blocks, axis=0)
        LT.at[b][...] += lax.dot_general(HEAD[cc, j], pieces, (((1,), (1,)), ((), ())),
                                         preferred_element_type=F32)

    def wanted_rows():
        slot, position = row_slot(lax.broadcasted_iota(jnp.int32, (32, 256), 1))
        place = (position == lax.broadcasted_iota(jnp.int32, (32, 256), 0)).astype(BF)
        tokens = targets[...]
        keep = slot[0:8] == lax.broadcasted_iota(jnp.int32, (8, 256), 0)
        parts = []
        for term in (tokens // 256, tokens % 256):
            every = jnp.dot(term.astype(F32).astype(BF), place, preferred_element_type=F32)
            parts.append(jnp.sum(jnp.where(keep, every, 0.0), axis=0, keepdims=True))
        return parts[0] * 256.0 + parts[1]

    def gather(b):
        source = 2 * b + 1
        final = (b == 1) & (s == NX - 1)
        late = (b == 1) & (s >= 2)

        def body(t, _):
            @pl.when((t < 4) & (s != source))
            def _():
                stage_own(b, t, False)

            @pl.when((t >= 1) & (t < 5) & ((t == 4) | jnp.logical_not(final)))
            def _():
                stage_first(b, t - 1)

            @pl.when((t >= 2) & (t < 6) & ((t >= 4) | jnp.logical_not(final)))
            def _():
                stage_second(b, t - 2)

            @pl.when(t >= 3)
            def _():
                stage_last(b, t - 3)

            @pl.when(late & (t == 0))
            def _():
                stage_last(0, 3)

            @pl.when(late & (t >= 1) & (t < 5))
            def _():
                j = chunk_order(t - 1)
                dots(0, c, j)
                dots(0, 1 - c, j)
            return 0

        lax.fori_loop(0, 6, body, 0)

    def finish(b):
        @pl.when((b == 1) | (s < 2))
        def _():
            dots(b, c, 0)
            for n in range(3):
                y_fwd(b, 3, n, 1 - c).wait_recv()
            dots(b, 1 - c, 0)
            dots(b, c, 1)
            dots(b, c, 2)
            for half in range(2):
                y_relay(b, 3, half).wait_recv()
                y_fwd(b, 3, 5 + half, c).start()
            for n in (3, 4):
                y_fwd(b, 3, n, 1 - c).wait_recv()
            dots(b, 1 - c, 1)
            dots(b, 1 - c, 2)
            dots(b, c, 3)
            for n in (5, 6):
                y_fwd(b, 3, n, 1 - c).wait_recv()
            dots(b, 1 - c, 3)

        squares = SQ[b].reshape(NY * ROWS, 128)
        top = squares.astype(BF)
        rest = (squares - top.astype(F32)).astype(BF)
        ones = jnp.ones((16, 128), BF)
        nt = (((1,), (1,)), ((), ()))
        sums = (lax.dot_general(ones, top, nt, preferred_element_type=F32)
                + lax.dot_general(ones, rest, nt, preferred_element_type=F32))[0:1]
        r = lax.rsqrt(sums * (1.0 / D) + EPS)
        logits = LT[b] * r
        highest = jnp.max(logits, axis=0, keepdims=True)
        summed = jnp.sum(jnp.exp(logits - highest), axis=0, keepdims=True)
        vocab = HEAD.shape[2]
        first = ((d * NX + s) * NM + m) * vocab
        index = (lax.broadcasted_iota(jnp.int32, logits.shape, 0) + first).astype(F32)
        wanted = wanted_rows()
        picked = jnp.sum(jnp.where(index == wanted, logits, 0.0), axis=0, keepdims=True)
        for n, value in enumerate((highest, summed, picked)):
            for half in range(2):
                STO[pl.ds(n * 4 + b * 2 + half, 1), :] = value[:, half * 128:half * 128 + 128]

    def step(t, _):
        last = s == NX - 1
        place = jnp.where(last, 1, 0)

        @pl.when(t == place)
        def _():
            layer()

        @pl.when(jnp.where(last, (t == 0) | (t == 2), (t == 1) | (t == jnp.where(s < 2, 3, 2))))
        def _():
            gather(jnp.where((t == 0) | (t == 1), 0, 1))

        @pl.when((t == 4) | (t == jnp.where(s < 2, 2, 3)))
        def _():
            @pl.when((t == 2) & (s == 0))
            def _():
                scale_head()
            finish(jnp.where(t == 4, 1, 0))
        return 0

    @pl.when(s == 0)
    def _():
        for q in range(2):
            for k in (2, 1, 3, 0):
                (eb_z(q, k) if k else eb_fwd(q, 0)).start()

    prepare()
    STO[...] = jnp.zeros_like(STO)
    SQ[...] = jnp.zeros_like(SQ)
    LT[...] = jnp.zeros_like(LT)
    lax.fori_loop(0, 5, step, 0)

    def merge(ref, count):
        parts = [ref[j] for j in range(count)]
        highest = parts[0][0:4]
        for p in parts[1:]:
            highest = jnp.maximum(highest, p[0:4])
        summed = jnp.zeros_like(highest)
        picked = jnp.zeros_like(highest)
        for p in parts:
            summed = summed + p[4:8] * jnp.exp(p[0:4] - highest)
            picked = picked + p[8:12]
        return highest, summed, picked

    def stacked(highest, summed, picked):
        return jnp.concatenate([highest, summed, picked, jnp.zeros_like(picked)], axis=0)

    pairs = [(j, k) for j in range(NX) for k in range(NY) if j or k]

    def st_yx(n):
        j, k = pairs[n]
        mine = s * NY + d
        return rcopy(SA.at[mine], SA.at[mine], st_s.at[0, n], st_r.at[0, mine],
                     (ypeer(k), (s + j) % NX, m))

    def st_yx_in(n):
        j, k = pairs[n]
        other = ((s + j) % NX) * NY + ypeer(k)
        return rcopy(SA.at[other], SA.at[other], st_s.at[0, n], st_r.at[0, other], here)

    def m_of(k):
        return (m + k) % NM

    def st_m(k):
        return rcopy(SB.at[m], SB.at[m], st_s.at[1, k], st_r.at[1, m], (d, s, m_of(k)))

    def st_m_in(k):
        mm = m_of(k)
        return rcopy(SB.at[mm], SB.at[mm], st_s.at[1, k], st_r.at[1, mm], (d, s, mm))

    SA.at[s * NY + d][...] = STO[...]
    for n in range(15):
        st_yx(n).start()
    for n in range(15):
        st_yx_in(n).wait_recv()
    SB.at[m][...] = stacked(*merge(SA, NX * NY))
    for k in (4, 3, 5, 2, 6, 1, 7):
        st_m(k).start()
    for k in (1, 7, 2, 6, 3, 5, 4):
        st_m_in(k).wait_recv()
    highest, summed, picked = merge(SB, NM)
    logprob = picked - (highest + jnp.log(summed))
    terms = []
    for e in range(2):
        rest = jnp.concatenate([logprob[2 * e:2 * e + 1], logprob[2 * e + 1:2 * e + 2]], axis=1)
        for _ in range(3):
            term = rest.astype(BF).astype(F32)
            terms.append(term)
            rest = rest - term
    row = lax.broadcasted_iota(jnp.int32, (16, 256), 0)
    stack = jnp.zeros((16, 256), F32)
    for j, term in enumerate(terms):
        stack = jnp.where(row == j, term, stack)
    stack = stack.astype(BF)
    slot, position = row_slot(lax.broadcasted_iota(jnp.int32, (256, 32), 0))
    place = lax.broadcasted_iota(jnp.int32, (256, 32), 1)
    results = []
    for i in range(2):
        chosen = source_of[2 * d + i]
        take = ((slot == chosen) & (position == place)
                & (place < live[chosen])).astype(F32).astype(BF)
        got = jnp.dot(stack, take, preferred_element_type=F32)
        results.append([got[j:j + 1] + got[j + 1:j + 2] + got[j + 2:j + 3] for j in (0, 3)])
    for e in range(2):
        first = lax.broadcasted_iota(jnp.int32, (2, 32), 0) == 0
        out.at[e][...] = jnp.where(first, results[0][e], results[1][e])

    @pl.when(s == 0)
    def _():
        for q in range(2):
            for k in range(1, 4):
                eb_z(q, k).wait_send()
            for k in range(4):
                eb_fwd(q, k).wait_send()
        for k in range(1, 4):
            res(k).wait_send()

    @pl.when(s > 0)
    def _():
        for g in range(NY):
            for k in range(1, 4):
                ag_z(g, k).wait_send()
        sums_out().wait_send()
        for n in range(3):
            swap(n).wait_send()

    @pl.when(s < NX - 1)
    def _():
        for g in range(NY):
            hop(g).wait_send()
        hop_raw().wait_send()

    for g in range(NY):
        for k in range(1, 4):
            zred(g, k).wait_send()
        part(g).wait_send()
    for k in range(1, 4):
        ctx(k).wait_send()
    for n in range(15):
        st_yx(n).wait_send()
    for k in range(1, 8):
        st_m(k).wait_send()
    def sent(n, _):
        b, k = n // 4, n % 4

        @pl.when(s == 2 * b + 1)
        def _():
            for j in (1, 2, 3):
                y_x(b, k, j).wait_send()

        for j in (1, 2, 3):
            y_first(b, k, j).wait_send()
        for j in (1, 3):
            for part_no in range(3):
                y_second(b, k, part_no, j).wait_send()
        for half in range(2):
            y_relay(b, k, half).wait_send()
        for j in range(7):
            y_fwd(b, k, j, c).wait_send()
        return 0

    lax.fori_loop(0, 8, sent, 0)


def tables():
    row = np.arange(ROWS)
    position = (row // 8) * 4 + row % 4
    half = HD // 2
    freqs = (ROPE_BASE ** (-np.arange(half) * 2.0 / HD)).astype(np.float32)
    angles = (position.astype(np.float32)[:, None] * freqs[None, :]).astype(np.float64)
    cos, sin = np.cos(angles), np.sin(angles)
    return (np.concatenate([cos, cos], 1).astype(np.float32),
            np.concatenate([-sin, sin], 1).astype(np.float32))


def per_device(
    embeds, targets, lengths, source, attn_gain, w_query, w_key, w_value, w_out, final_gain, head
):
    vocab = head.shape[0]
    cos, sin = tables()
    vmem = pl.BlockSpec(memory_space=pltpu.VMEM)
    hbm = pl.BlockSpec(memory_space=pl.ANY)
    smem = pl.BlockSpec(memory_space=pltpu.SMEM)
    dma = pltpu.SemaphoreType.DMA
    stats = pl.pallas_call(
        kernel,
        out_shape=jax.ShapeDtypeStruct((2, 2, 32), F32),
        in_specs=[hbm, smem, smem] + [hbm] * 10,
        out_specs=vmem,
        scratch_shapes=[
            pltpu.VMEM((2, 4, D), BF),
            pltpu.VMEM((8, 32), jnp.int32),
            pltpu.VMEM((1, D), F32),
            pltpu.VMEM((1, D), F32),
            pltpu.VMEM((ROWS, HD), F32),
            pltpu.VMEM((ROWS, HD), F32),
            pltpu.VMEM((2, 16, 256, 768), BF),
            pltpu.VMEM((QW, 2048), BF),
            pltpu.VMEM((2, 4, vocab, 1024), BF),
            pltpu.VMEM((2, NM, 16, 2048), BF),
            pltpu.VMEM((NY, NM, ROWS, 256), BF),
            pltpu.VMEM((NY, NZ, ROWS, 256), BF),
            pltpu.VMEM((NY, ROWS, 256), BF),
            pltpu.VMEM((4 * ROWS, ROWS), F32),
            pltpu.VMEM((ROWS, 128), F32),
            pltpu.VMEM((2, ROWS, 896), F32),
            pltpu.VMEM((ROWS, 896), F32),
            pltpu.VMEM((NY, ROWS, 256), BF),
            pltpu.VMEM((NY, ROWS, QW), BF),
            pltpu.VMEM((NY, NZ, ROWS, 256), BF),
            pltpu.VMEM((NY, NZ, ROWS, 256), BF),
            pltpu.VMEM((NY, NZ, ROWS, 256), F32),
            pltpu.VMEM((NY, NZ, ROWS, 256), BF),
            pltpu.VMEM((NY, NZ, ROWS, 256), BF),
            pltpu.VMEM((NY, ROWS, 256), BF),
            pltpu.VMEM((2, 4, 2, 4, 4, ROWS, 256), BF),
            pltpu.VMEM((2, vocab, 256), F32),
            pltpu.VMEM((2, NY, ROWS, 128), F32),
            pltpu.VMEM((16, 128), F32),
            pltpu.VMEM((NX * NY, 16, 128), F32),
            pltpu.VMEM((NM, 16, 128), F32),
            dma((20,)),
            dma((3,)), dma((3,)),
            dma, dma,
            dma((2, 8)), dma((2, 8)),
            dma((5,)), dma((5,)),
            dma((4, 8)), dma((4, 8)),
            dma((4,)), dma((4,)),
            dma((4,)), dma((4,)),
            dma((4,)), dma((4,)),
            dma((4, 4)), dma((4, 4)),
            dma((2, 4, 22)), dma((2, 4, 19)),
            dma((2, 16)), dma((2, 16)),
        ],
        compiler_params=pltpu.CompilerParams(
            collective_id=0, has_side_effects=True, vmem_limit_bytes=60 * 1024 * 1024),
        cost_estimate=pl.CostEstimate(flops=8_000_000_000, bytes_accessed=24_000_000,
                                      transcendentals=300_000),
    )(
        embeds, lengths, source, targets, attn_gain, final_gain.reshape(1, D), jnp.asarray(cos), jnp.asarray(sin),
        w_query.reshape(16, 2, 256, 512), w_key.reshape(16, 2, 256, 128),
        w_value.reshape(16, 2, 256, 128), w_out.reshape(512, 2048), head,
    )
    return (stats[0], stats[1])


def solution(mesh):
    return jax.shard_map(
        per_device,
        mesh=mesh,
        in_specs=(
            P("dp", "mp", None),
            P(),
            P(),
            P(),
            P("section", None),
            P("section", None, "mp"),
            P("section", None, "mp"),
            P("section", None, "mp"),
            P("section", "mp", "dp"),
            P(),
            P(("dp", "section", "mp"), None),
        ),
        out_specs=(P("dp", None), P("dp", None)),
        check_vma=False,
    )
```

```python
import jax
import jax.numpy as jnp
import numpy as np
from jax import lax
from jax.experimental import pallas as pl
from jax.experimental.pallas import tpu as pltpu
from jax.sharding import PartitionSpec as P

HD = 128
EPS = 1e-05
ROPE_BASE = 500000.0
NY = 4
NX = 4
NZ = 4
NM = 8
ROWS = 64
D = 8192
QW = 512
MESH = pl.DeviceIdType.MESH
BF = jnp.bfloat16
F32 = jnp.float32


def lane(start, size):
    return pl.ds(pl.multiple_of(start, 128), size)


def kernel(
    emb_in, live, source_of, targets_in, gain, fgain_in, cosine_in, sine_in, wq, wk, wv, wo, head,
    out,
    emb, targets, gains, fgain, cosine, sine, W, WO, HEAD, EB, XE, X, RX, MASK, SS, QA, QR, R, C, PS, PR, PO, ZS, ZR, HP, Y, LT, SQ, WANT, TAKE, STO, SA, SB,
    w_sem, sw_s, sw_r, qr_s, qr_r, eb_s, eb_r, hop_s, hop_r, ag_s, ag_r, res_s, res_r, ctx_s, ctx_r, ps_s, ps_r,
    zz_s, zz_r, y_s, y_r, st_s, st_r,
):
    d = lax.axis_index("dp")
    s = lax.axis_index("section")
    m = lax.axis_index("mp")
    z = m // 2
    c = m % 2
    sib = z * 2 + (1 - c)

    def ypeer(k):
        return (d + k) % NY

    def zpeer(k):
        return ((z + k) % NZ) * 2 + c

    def zother(k):
        return ((z + k) % NZ) * 2 + (1 - c)

    def rcopy(src, dst, ssem, rsem, dev):
        return pltpu.make_async_remote_copy(
            src_ref=src, dst_ref=dst, send_sem=ssem, recv_sem=rsem,
            device_id=dev, device_id_type=MESH,
        )

    here = (d, s, sib)

    barrier = pltpu.get_barrier_semaphore()
    partners = []
    for k in range(1, 4):
        partners.append((ypeer(k), s, m))
        partners.append((d, (s + k) % NX, m))
        partners.append((d, s, zpeer(k)))
        partners.append((d, s, zother(k)))
        partners.append((ypeer(k), (s + 1) % NX, m))
        partners.append((ypeer(k), (s + 3) % NX, m))
        partners.append((ypeer(k), (s + 2) % NX, m))
    partners.append(here)
    for dev in partners:
        pl.semaphore_signal(barrier, inc=1, device_id=dev, device_id_type=MESH)
    small = [
        pltpu.make_async_copy(src, dst, w_sem.at[14 + n])
        for n, (src, dst) in enumerate((
            (emb_in, emb), (gain, gains), (cosine_in, cosine), (sine_in, sine),
            (fgain_in, fgain), (targets_in, targets)))
    ]
    for copy in small:
        copy.start()
    parts = ((wq, pl.ds(0, 512)), (wk, pl.ds(512, 128)), (wv, pl.ds(640, 128)))

    def load(n, first):
        src, lanes = parts[n]
        take = 1 if first else jnp.where(s == 0, 0, c)
        return pltpu.make_async_copy(src.at[:, take], W.at[first, :, :, lanes],
                                     w_sem.at[3 * first + n])

    def swap(n):
        src, lanes = parts[n]
        return rcopy(src.at[:, 1 - c], W.at[1, :, :, lanes], sw_s.at[n], sw_r.at[n], here)

    wo_load = pltpu.make_async_copy(wo, WO, w_sem.at[12])
    for n in range(3):
        load(n, 0).start()

    @pl.when(s == 0)
    def _():
        for n in range(3):
            load(n, 1).start()

    head_load = pltpu.make_async_copy(HEAD, HEAD, w_sem.at[13])

    def row_slot(lanes):
        return (lanes // 64) * 2 + (lanes // 4) % 2, ((lanes // 8) % 8) * 4 + lanes % 4

    def wanted_rows():
        slot, position = row_slot(lax.broadcasted_iota(jnp.int32, (32, 256), 1))
        place = (position == lax.broadcasted_iota(jnp.int32, (32, 256), 0)).astype(BF)
        tokens = targets[...]
        keep = slot[0:8] == lax.broadcasted_iota(jnp.int32, (8, 256), 0)
        parts = []
        for term in (tokens // 256, tokens % 256):
            every = jnp.dot(term.astype(F32).astype(BF), place, preferred_element_type=F32)
            parts.append(jnp.sum(jnp.where(keep, every, 0.0), axis=0, keepdims=True))
        return parts[0] * 256.0 + parts[1]

    def prepare():
        wo_load.start()
        offsets = (0, 3, 1, 2)
        for cc in range(2):
            for j in range(4):
                for i in range(4):
                    g, zz = (offsets[i], offsets[j]) if cc == 0 else (offsets[j], offsets[i])
                    col = ypeer(g) * 2048 + ((z + zz) % NZ) * 512 + cc * 256
                    pltpu.make_async_copy(head.at[:, lane(col, 256)],
                                          HEAD.at[cc, j, :, i * 256:i * 256 + 256],
                                          w_sem.at[13]).start()
        shape = (4 * ROWS, ROWS)
        rq = lax.broadcasted_iota(jnp.int32, shape, 0) % ROWS
        rk = lax.broadcasted_iota(jnp.int32, shape, 1)
        slot_q, slot_k = (rq // 4) % 2, (rk // 4) % 2
        pos_q, pos_k = (rq // 8) * 4 + rq % 4, (rk // 8) * 4 + rk % 4
        live_k = jnp.where(slot_k == 0, live[2 * d], live[2 * d + 1])
        allowed = (slot_q == slot_k) & (pos_k <= pos_q) & (pos_k < live_k)
        MASK[...] = jnp.where(allowed, F32(0.0), F32(-1e30))

        @pl.when(s > 0)
        def _():
            for n in range(3):
                load(n, 0).wait()
                swap(n).wait_recv()
            for copy in small[1:2]:
                copy.wait()
            diagonal = (lax.broadcasted_iota(jnp.int32, (256, 256), 0)
                        == lax.broadcasted_iota(jnp.int32, (256, 256), 1))

            def scale(i, _):
                cols = lane((i // NZ) * 2048 + ((i % NZ) * 2 + c) * 256, 256)
                column = jnp.sum(jnp.where(diagonal, gains[:, cols], 0.0), axis=1, keepdims=True)
                for which in range(2):
                    W.at[which, i][...] = (W[which, i].astype(F32) * column).astype(BF)
                return 0

            lax.fori_loop(0, 16, scale, 0)

        @pl.when(s == 0)
        def _():
            for copy in small[1:2]:
                copy.wait()
        for copy in small[2:]:
            copy.wait()

        WANT[...] = jnp.broadcast_to(wanted_rows(), WANT.shape)
        slot, position = row_slot(lax.broadcasted_iota(jnp.int32, (256, 32), 0))
        place = lax.broadcasted_iota(jnp.int32, (256, 32), 1)
        for i in range(2):
            chosen = source_of[2 * d + i]
            TAKE.at[i][...] = ((slot == chosen) & (position == place)
                               & (place < live[chosen])).astype(F32).astype(BF)

        @pl.when(s > 0)
        def _():
            scale_head()

    def scale_head():
        head_load.wait()

        def off(n):
            return jnp.where(n == 0, 0, jnp.where(n == 1, 3, jnp.where(n == 2, 1, 2)))

        def scale(n, _):
            cc, j, i = n // 16, (n // 4) % 4, n % 4
            g = jnp.where(cc == 0, off(i), off(j))
            zz = jnp.where(cc == 0, off(j), off(i))
            col = ((d + g) % NY) * 2048 + ((z + zz) % NZ) * 512 + cc * 256
            block = HEAD.at[cc, j, :, lane(i * 256, 256)]
            block[...] = (block[...].astype(F32) * fgain[:, lane(col, 256)]).astype(BF)
            return 0

        lax.fori_loop(0, 32, scale, 0)

    small[0].wait()

    @pl.when(s == 0)
    def _():
        rows = jnp.concatenate([emb[0], emb[1]], axis=0).astype(F32)
        for q in range(2):
            EB.at[q, m][...] = jnp.concatenate(
                [rows[:, q * 2048:q * 2048 + 2048], rows[:, q * 2048 + 4096:q * 2048 + 6144]],
                axis=0).astype(BF)

    pl.semaphore_wait(barrier, len(partners))

    @pl.when(s > 0)
    def _():
        for n in range(3):
            swap(n).start()

    def eb_z(q, k):
        return rcopy(EB.at[q, m], EB.at[q, m], eb_s.at[q, k], eb_r.at[q, m], (d, s, zpeer(k)))

    def eb_z_in(q, k):
        mk = zpeer(k)
        return rcopy(EB.at[q, mk], EB.at[q, mk], eb_s.at[q, k], eb_r.at[q, mk], here)

    def eb_fwd(q, k):
        mk = zpeer(k)
        return rcopy(EB.at[q, mk], EB.at[q, mk], eb_s.at[q, 4 + k], eb_r.at[q, mk], here)

    def eb_sib_in(q, k):
        mk = zother(k)
        return rcopy(EB.at[q, mk], EB.at[q, mk], eb_s.at[q, 4 + k], eb_r.at[q, mk], here)

    def hop(g):
        return rcopy(HP.at[g], X.at[d, z], hop_s.at[g], hop_r.at[d], (g, (s + 1) % NX, m))

    def hop_in(g):
        return rcopy(HP.at[g], X.at[g, z], hop_s.at[g], hop_r.at[g], here)

    def hop_raw():
        return rcopy(HP, R, hop_s.at[4], hop_r.at[4], (d, (s + 1) % NX, m))

    def ag_z(g, k):
        return rcopy(X.at[g, z], X.at[g, z], ag_s.at[g, k], ag_r.at[g, z], (d, s, zpeer(k)))

    def ag_z_in(g, k):
        zk = (z + k) % NZ
        return rcopy(X.at[g, zk], X.at[g, zk], ag_s.at[g, k], ag_r.at[g, zk], here)

    def sums_out():
        return rcopy(QA.at[1], QR, qr_s, qr_r, here)

    def res(k):
        g = ypeer(k)
        return rcopy(RX.at[g], R.at[d], res_s.at[k], res_r.at[d], (g, s, m))

    def res_in(k):
        g = ypeer(k)
        return rcopy(RX.at[g], R.at[g], res_s.at[k], res_r.at[g], here)

    def ctx(k):
        return rcopy(C.at[d], C.at[d], ctx_s.at[k], ctx_r.at[d], (ypeer(k), s, m))

    def ctx_in(k):
        g = ypeer(k)
        return rcopy(C.at[g], C.at[g], ctx_s.at[k], ctx_r.at[g], here)

    def part(g):
        return rcopy(PS.at[g], PR.at[g], ps_s.at[g], ps_r.at[g], here)

    def zred(g, k):
        return rcopy(ZS.at[g, k], ZR.at[g, k], zz_s.at[g, k], zz_r.at[g, k], (d, s, zpeer(k)))

    def layer():
        def multiply(x, which, rows, n, start=False):
            w = W[which, pl.ds(rows * NZ, NZ)].reshape(4 * 256, 768)
            term = jnp.dot(x, w, preferred_element_type=F32)
            QA.at[n][:, 0:768] = term if start else QA[n, :, 0:768] + term

        @pl.when(s == 0)
        def _():
            for q in range(2):
                for k in (1, 3, 2):
                    eb_z_in(q, k).wait_recv()
                    eb_fwd(q, k).start()
            QA[...] = jnp.zeros_like(QA)
            QR[...] = jnp.zeros_like(QR)
            SS[...] = jnp.zeros_like(SS)
            for q in range(2):
                for k in range(4):
                    eb_sib_in(q, k).wait_recv()

                def blocks(mm):
                    x = EB[q, :, :, lane(mm * 256, 256)].astype(F32)
                    return [x[:, i * 8:i * 8 + 8, :].reshape(ROWS, 256) for i in range(2)]

                def body(mm, total):
                    for half, xs in enumerate(blocks(mm)):
                        g = half * 2 + q
                        cols = lane(g * 2048 + mm * 256, 256)
                        XE.at[g, mm][...] = (xs * gains[:, cols]).astype(BF)
                        square = xs * xs
                        total = total + square[:, 0:128] + square[:, 128:256]
                    return total

                SS[...] = lax.fori_loop(0, NM, body, SS[...])
                for half, xs in enumerate(blocks(m)):
                    RX.at[half * 2 + q][...] = xs.astype(BF)
                if q == 0:
                    for n in range(3):
                        load(n, 0).wait()
                        load(n, 1).wait()

                def both(i, _):
                    g = 2 * i + q
                    for who in range(2):
                        x = jnp.concatenate([XE[g, 2 * zz + who] for zz in range(NZ)], axis=1)
                        multiply(x, who, g, 0)
                    return 0

                lax.fori_loop(0, 2, both, 0)
            for k in (2, 1, 3):
                res(k).start()
            R.at[d][...] = RX[d]

        @pl.when(s > 0)
        def _():
            def arrived(k):
                g = ypeer(k)
                hop_in(g).wait_recv()
                for j in (2, 1, 3):
                    ag_z(g, j).start()

            def columns(k):
                g = ypeer(k)
                for j in (1, 3, 2):
                    ag_z_in(g, j).wait_recv()
                return jnp.concatenate([X[g, zz] for zz in range(NZ)], axis=1)

            def both(k, start=False):
                x = columns(k)
                multiply(x, 1, ypeer(k), 1, start)
                multiply(x, 0, ypeer(k), 0, start)

            def squares_of(k):
                total = jnp.zeros((ROWS, 128), F32)
                for zz in range(NZ):
                    x = X[ypeer(k), zz].astype(F32)
                    square = x * x
                    total = total + square[:, 0:128] + square[:, 128:256]
                return total

            arrived(0)
            arrived(3)
            arrived(1)
            arrived(2)
            both(0, True)
            squares = squares_of(0)
            both(3)
            squares = squares + squares_of(3)
            both(1)
            squares = squares + squares_of(1)
            x = columns(2)
            multiply(x, 1, ypeer(2), 1)
            squares = squares + squares_of(2)
            QA.at[1][:, 768:896] = squares
            sums_out().start()
            multiply(x, 0, ypeer(2), 0)
            sums_out().wait_recv()
            SS[...] = squares + QR[:, 768:896]

        r = lax.rsqrt(jnp.sum(SS[...], axis=1, keepdims=True) * (1.0 / D) + EPS)
        cos = cosine[...]
        sin = sine[...]

        def summed(first, last):
            return QA[0, :, first:last] + QR[:, first:last]

        def rope(x):
            return (x * cos + pltpu.roll(x, 64, 1) * sin).astype(BF)

        query = jnp.concatenate(
            [rope(summed(j * HD, (j + 1) * HD) * r) for j in range(4)], axis=0)
        key = rope(summed(512, 640) * r)
        value = (summed(640, 768) * r).astype(BF)
        scores = lax.dot_general(query, key, (((1,), (1,)), ((), ())),
                                 preferred_element_type=F32) * (HD ** -0.5)
        scores = scores + MASK[...]
        highest = jnp.max(scores, axis=-1, keepdims=True)
        weights = jnp.exp(scores - highest)
        probs = (weights / jnp.sum(weights, axis=-1, keepdims=True)).astype(BF)
        mixed = jnp.dot(probs, value, preferred_element_type=F32).astype(BF)
        for j in range(4):
            C.at[d][:, j * HD:(j + 1) * HD] = mixed[j * ROWS:(j + 1) * ROWS]
        for k in (2, 1, 3):
            ctx(k).start()

        wo_load.wait()

        def project(g):
            for zz in range(NZ):
                p = jnp.dot(C[g], WO[:, zz * 512:zz * 512 + 512], preferred_element_type=F32)
                low, high = p[:, :256], p[:, 256:]
                PO.at[g, zz][...] = jnp.where(c == 0, low, high)
                PS.at[g, zz][...] = jnp.where(c == 0, high, low).astype(BF)
            part(g).start()

        def pair(g):
            part(g).wait_recv()
            for k in (2, 1, 3):
                zt = (z + k) % NZ
                ZS.at[g, k][...] = (PO[g, zt] + PR[g, zt].astype(F32)).astype(BF)
                zred(g, k).start()

        def total_of(g):
            total = PO[g, z] + PR[g, z].astype(F32) + R[g].astype(F32)
            for k in (1, 3, 2):
                zred(g, k).wait_recv()
                total = total + ZR[g, k].astype(F32)
            HP.at[g][...] = total.astype(BF)

            @pl.when(s < NX - 1)
            def _():
                hop(g).start()

        project(d)

        @pl.when(s == 0)
        def _():
            for k in (1, 3, 2):
                res_in(k).wait_recv()

        @pl.when(s > 0)
        def _():
            hop_raw().wait_recv()

        pair(d)
        for k in (1, 3):
            ctx_in(k).wait_recv()
            project(ypeer(k))
        pair(ypeer(1))
        pair(ypeer(3))
        def own_chunk(k):
            @pl.when(s == NX - 1)
            def _():
                stage_own(1, k, True)
                if k >= 1:
                    stage_first(1, k - 1)
                if k >= 2:
                    stage_second(1, k - 2)

        total_of(d)
        own_chunk(0)
        ctx_in(2).wait_recv()
        project(ypeer(2))
        total_of(ypeer(1))
        pair(ypeer(2))
        own_chunk(1)
        total_of(ypeer(3))
        own_chunk(2)
        total_of(ypeer(2))
        own_chunk(3)

        @pl.when(s < NX - 1)
        def _():
            hop_raw().start()

        @pl.when(s == 1)
        def _():
            def body(k, _):
                stage_own(0, k, True)
                return 0

            lax.fori_loop(0, 4, body, 0)

    def first_dev(k):
        return (jnp.where(c == 0, ypeer(k), d), s, jnp.where(c == 0, m, zpeer(k)))

    def second_dev(k):
        return (jnp.where(c == 0, d, ypeer(k)), s, jnp.where(c == 0, zpeer(k), m))

    def ycopy(src, dst, b, k, i, j, dev):
        return rcopy(src, dst, y_s.at[b, k, i], y_r.at[b, k, j], dev)

    def y_x(b, k, n):
        ref = Y.at[b, k, c, 0, 0]
        return ycopy(ref, ref, b, k, n, 0, (d, (s + n) % NX, m))

    def y_first(b, k, n):
        slot = (1, 3, 2)[n - 1]
        return ycopy(Y.at[b, k, c, 0, 0], Y.at[b, k, c, 0, slot], b, k, 3 + n, slot, first_dev(n))

    sets = (pl.ds(0, 1), pl.ds(1, 2), pl.ds(3, 1))

    def y_second(b, k, part_no, n):
        slot = 1 if n == 1 else 2
        return ycopy(Y.at[b, k, c, 0, sets[part_no]], Y.at[b, k, c, slot, sets[part_no]], b, k,
                     7 + part_no * 2 + (slot - 1), 1 + 3 * slot + part_no, second_dev(n))

    def y_relay(b, k, half):
        slot, n = ((1, 1), (2, 3))[half]
        two = pl.ds(2 * half, 2)
        return ycopy(Y.at[b, k, c, slot, two], Y.at[b, k, c, 3, two], b, k, 13 + half, 10 + half,
                     second_dev(n))

    forwards = ((0, 0, 1), (0, 1, 2), (0, 3, 1), (1, 0, 4), (2, 0, 4), (3, 0, 2), (3, 2, 2))

    def y_fwd(b, k, n, who):
        j, i, size = forwards[n]
        ref = Y.at[b, k, who, j, pl.ds(i, size)]
        return ycopy(ref, ref, b, k, 15 + n, 12 + n, here)

    def chunk_order(step):
        return jnp.where(step == 3, 2, jnp.where(step == 2, 3, step))

    def stage_own(b, k, source):
        if source:
            Y.at[b, k, c, 0, 0][...] = HP[(d + chunk_order(k)) % NY]
            for n in (2, 1, 3):
                y_x(b, k, n).start()
        else:
            y_x(b, k, 1).wait_recv()
        for n in (2, 1, 3):
            y_first(b, k, n).start()
        for n in (1, 3):
            y_second(b, k, 0, n).start()
        y_fwd(b, k, 0, c).start()

    def stage_first(b, k):
        y_first(b, k, 1).wait_recv()
        y_first(b, k, 3).wait_recv()
        for n in (1, 3):
            y_second(b, k, 1, n).start()
        y_fwd(b, k, 1, c).start()
        y_first(b, k, 2).wait_recv()
        for n in (1, 3):
            y_second(b, k, 2, n).start()
        y_fwd(b, k, 2, c).start()

    def stage_second(b, k):
        for part_no in (0, 1):
            y_second(b, k, part_no, 1).wait_recv()
        y_relay(b, k, 0).start()
        for part_no in (1, 2):
            y_second(b, k, part_no, 3).wait_recv()
        y_relay(b, k, 1).start()
        y_second(b, k, 2, 1).wait_recv()
        y_fwd(b, k, 3, c).start()
        y_second(b, k, 0, 3).wait_recv()
        y_fwd(b, k, 4, c).start()

    def stage_last(b, k):
        for half in range(2):
            y_relay(b, k, half).wait_recv()
            y_fwd(b, k, 5 + half, c).start()
        for n in range(7):
            y_fwd(b, k, n, 1 - c).wait_recv()

    def dots(b, cc, j):
        blocks = []
        for g in range(NY):
            row = []
            total = jnp.zeros((ROWS, 128), F32)
            for i in range(4):
                off_j = jnp.where(j == 0, 0, jnp.where(j == 1, 3, jnp.where(j == 2, 1, 2)))
                sender = (d + jnp.where(cc == 0, (0, 3, 1, 2)[i], off_j)) % NY
                k = chunk_order((g - sender + NY) % NY)
                x = Y[b, k, cc, j, i]
                row.append(x)
                wide = x.astype(F32)
                square = wide * wide
                total = total + square[:, 0:128] + square[:, 128:256]
            SQ.at[b, g][...] += total
            blocks.append(jnp.concatenate(row, axis=1))
        pieces = jnp.concatenate(blocks, axis=0)
        LT.at[b][...] += lax.dot_general(HEAD[cc, j], pieces, (((1,), (1,)), ((), ())),
                                         preferred_element_type=F32)

    def layer_sent():
        @pl.when(s == 0)
        def _():
            for q in range(2):
                for k in range(1, 4):
                    eb_z(q, k).wait_send()
                for k in range(4):
                    eb_fwd(q, k).wait_send()
            for k in range(1, 4):
                res(k).wait_send()

        @pl.when(s > 0)
        def _():
            for g in range(NY):
                for k in range(1, 4):
                    ag_z(g, k).wait_send()
            sums_out().wait_send()
            for n in range(3):
                swap(n).wait_send()

        @pl.when(s < NX - 1)
        def _():
            for g in range(NY):
                hop(g).wait_send()
            hop_raw().wait_send()

        for g in range(NY):
            for k in range(1, 4):
                zred(g, k).wait_send()
            part(g).wait_send()
        for k in range(1, 4):
            ctx(k).wait_send()

    def chunk_sent(b, k, source):
        @pl.when(s == source)
        def _():
            for j in (1, 2, 3):
                y_x(b, k, j).wait_send()

        for j in (1, 2, 3):
            y_first(b, k, j).wait_send()
        for j in (1, 3):
            for part_no in range(3):
                y_second(b, k, part_no, j).wait_send()
        for half in range(2):
            y_relay(b, k, half).wait_send()
        for j in range(7):
            y_fwd(b, k, j, c).wait_send()

    def gather(b):
        source = 2 * b + 1
        final = (b == 1) & (s == NX - 1)
        late = (b == 1) & (s >= 2)

        def body(t, _):
            @pl.when((t < 4) & (s != source))
            def _():
                stage_own(b, t, False)

            @pl.when((t >= 1) & (t < 5) & ((t == 4) | jnp.logical_not(final)))
            def _():
                stage_first(b, t - 1)

            @pl.when((t >= 2) & (t < 6) & ((t >= 4) | jnp.logical_not(final)))
            def _():
                stage_second(b, t - 2)

            @pl.when(t >= 3)
            def _():
                stage_last(b, t - 3)
                chunk_sent(b, t - 3, source)

            @pl.when(late & (t == 0))
            def _():
                stage_last(0, 3)
                chunk_sent(0, 3, 1)

            @pl.when(late & (t >= 1) & (t < 5))
            def _():
                j = chunk_order(t - 1)
                dots(0, c, j)
                dots(0, 1 - c, j)
            return 0

        lax.fori_loop(0, 6, body, 0)

    def finish(b):
        @pl.when((b == 1) | (s < 2))
        def _():
            dots(b, c, 0)
            for n in range(3):
                y_fwd(b, 3, n, 1 - c).wait_recv()
            dots(b, 1 - c, 0)
            dots(b, c, 1)
            dots(b, c, 2)
            for half in range(2):
                y_relay(b, 3, half).wait_recv()
                y_fwd(b, 3, 5 + half, c).start()
            for n in (3, 4):
                y_fwd(b, 3, n, 1 - c).wait_recv()
            dots(b, 1 - c, 1)
            dots(b, 1 - c, 2)
            dots(b, c, 3)
            for n in (5, 6):
                y_fwd(b, 3, n, 1 - c).wait_recv()
            dots(b, 1 - c, 3)

        @pl.when((b == 0) & (s < 2))
        def _():
            chunk_sent(0, 3, 1)

        squares = SQ[b].reshape(NY * ROWS, 128)
        top = squares.astype(BF)
        rest = (squares - top.astype(F32)).astype(BF)
        ones = jnp.ones((16, 128), BF)
        nt = (((1,), (1,)), ((), ()))
        sums = (lax.dot_general(ones, top, nt, preferred_element_type=F32)
                + lax.dot_general(ones, rest, nt, preferred_element_type=F32))[0:1]
        r = lax.rsqrt(sums * (1.0 / D) + EPS)
        logits = LT[b] * r
        highest = jnp.max(logits, axis=0, keepdims=True)
        summed = jnp.sum(jnp.exp(logits - highest), axis=0, keepdims=True)
        vocab = HEAD.shape[2]
        first = ((d * NX + s) * NM + m) * vocab
        index = (lax.broadcasted_iota(jnp.int32, logits.shape, 0) + first).astype(F32)
        wanted = WANT[0:1, :]
        picked = jnp.sum(jnp.where(index == wanted, logits, 0.0), axis=0, keepdims=True)
        for n, value in enumerate((highest, summed, picked)):
            for half in range(2):
                STO[pl.ds(n * 4 + b * 2 + half, 1), :] = value[:, half * 128:half * 128 + 128]

    def step(t, _):
        last = s == NX - 1
        place = jnp.where(last, 1, 0)

        @pl.when(t == place)
        def _():
            layer()

        @pl.when(jnp.where(last, (t == 0) | (t == 2), (t == 1) | (t == jnp.where(s < 2, 3, 2))))
        def _():
            gather(jnp.where((t == 0) | (t == 1), 0, 1))

        @pl.when((t == 4) | (t == jnp.where(s < 2, 2, 3)))
        def _():
            @pl.when((t == 2) & (s == 0))
            def _():
                scale_head()
            finish(jnp.where(t == 4, 1, 0))
        return 0

    @pl.when(s == 0)
    def _():
        for q in range(2):
            for k in (2, 1, 3, 0):
                (eb_z(q, k) if k else eb_fwd(q, 0)).start()

    prepare()
    STO[...] = jnp.zeros_like(STO)
    SQ[...] = jnp.zeros_like(SQ)
    LT[...] = jnp.zeros_like(LT)
    lax.fori_loop(0, 5, step, 0)

    def merge(ref, count):
        parts = [ref[j] for j in range(count)]
        highest = parts[0][0:4]
        for p in parts[1:]:
            highest = jnp.maximum(highest, p[0:4])
        summed = jnp.zeros_like(highest)
        picked = jnp.zeros_like(highest)
        for p in parts:
            summed = summed + p[4:8] * jnp.exp(p[0:4] - highest)
            picked = picked + p[8:12]
        return highest, summed, picked

    def stacked(highest, summed, picked):
        return jnp.concatenate([highest, summed, picked, jnp.zeros_like(picked)], axis=0)

    pairs = [(j, k) for j in range(NX) for k in range(NY) if j or k]

    def st_yx(n):
        j, k = pairs[n]
        mine = s * NY + d
        return rcopy(SA.at[mine], SA.at[mine], st_s.at[0, n], st_r.at[0, mine],
                     (ypeer(k), (s + j) % NX, m))

    def st_yx_in(n):
        j, k = pairs[n]
        other = ((s + j) % NX) * NY + ypeer(k)
        return rcopy(SA.at[other], SA.at[other], st_s.at[0, n], st_r.at[0, other], here)

    def m_of(k):
        return (m + k) % NM

    def st_m(k):
        return rcopy(SB.at[m], SB.at[m], st_s.at[1, k], st_r.at[1, m], (d, s, m_of(k)))

    def st_m_in(k):
        mm = m_of(k)
        return rcopy(SB.at[mm], SB.at[mm], st_s.at[1, k], st_r.at[1, mm], (d, s, mm))

    SA.at[s * NY + d][...] = STO[...]
    for n in range(15):
        st_yx(n).start()
    layer_sent()
    chunk_sent(1, 3, NX - 1)
    for n in range(15):
        st_yx_in(n).wait_recv()
    SB.at[m][...] = stacked(*merge(SA, NX * NY))
    for k in (4, 3, 5, 2, 6, 1, 7):
        st_m(k).start()
    for n in range(15):
        st_yx(n).wait_send()
    for k in (1, 7, 2, 6, 3, 5, 4):
        st_m_in(k).wait_recv()
    highest, summed, picked = merge(SB, NM)
    logprob = picked - (highest + jnp.log(summed))
    terms = []
    for e in range(2):
        rest = jnp.concatenate([logprob[2 * e:2 * e + 1], logprob[2 * e + 1:2 * e + 2]], axis=1)
        for _ in range(3):
            term = rest.astype(BF).astype(F32)
            terms.append(term)
            rest = rest - term
    row = lax.broadcasted_iota(jnp.int32, (16, 256), 0)
    stack = jnp.zeros((16, 256), F32)
    for j, term in enumerate(terms):
        stack = jnp.where(row == j, term, stack)
    stack = stack.astype(BF)
    results = []
    for i in range(2):
        got = jnp.dot(stack, TAKE[i], preferred_element_type=F32)
        results.append([got[j:j + 1] + got[j + 1:j + 2] + got[j + 2:j + 3] for j in (0, 3)])
    for e in range(2):
        first = lax.broadcasted_iota(jnp.int32, (2, 32), 0) == 0
        out.at[e][...] = jnp.where(first, results[0][e], results[1][e])
    for k in range(1, 8):
        st_m(k).wait_send()


def tables():
    row = np.arange(ROWS)
    position = (row // 8) * 4 + row % 4
    half = HD // 2
    freqs = (ROPE_BASE ** (-np.arange(half) * 2.0 / HD)).astype(np.float32)
    angles = (position.astype(np.float32)[:, None] * freqs[None, :]).astype(np.float64)
    cos, sin = np.cos(angles), np.sin(angles)
    return (np.concatenate([cos, cos], 1).astype(np.float32),
            np.concatenate([-sin, sin], 1).astype(np.float32))


def per_device(
    embeds, targets, lengths, source, attn_gain, w_query, w_key, w_value, w_out, final_gain, head
):
    vocab = head.shape[0]
    cos, sin = tables()
    vmem = pl.BlockSpec(memory_space=pltpu.VMEM)
    hbm = pl.BlockSpec(memory_space=pl.ANY)
    smem = pl.BlockSpec(memory_space=pltpu.SMEM)
    dma = pltpu.SemaphoreType.DMA
    stats = pl.pallas_call(
        kernel,
        out_shape=jax.ShapeDtypeStruct((2, 2, 32), F32),
        in_specs=[hbm, smem, smem] + [hbm] * 10,
        out_specs=vmem,
        scratch_shapes=[
            pltpu.VMEM((2, 4, D), BF),
            pltpu.VMEM((8, 32), jnp.int32),
            pltpu.VMEM((1, D), F32),
            pltpu.VMEM((1, D), F32),
            pltpu.VMEM((ROWS, HD), F32),
            pltpu.VMEM((ROWS, HD), F32),
            pltpu.VMEM((2, 16, 256, 768), BF),
            pltpu.VMEM((QW, 2048), BF),
            pltpu.VMEM((2, 4, vocab, 1024), BF),
            pltpu.VMEM((2, NM, 16, 2048), BF),
            pltpu.VMEM((NY, NM, ROWS, 256), BF),
            pltpu.VMEM((NY, NZ, ROWS, 256), BF),
            pltpu.VMEM((NY, ROWS, 256), BF),
            pltpu.VMEM((4 * ROWS, ROWS), F32),
            pltpu.VMEM((ROWS, 128), F32),
            pltpu.VMEM((2, ROWS, 896), F32),
            pltpu.VMEM((ROWS, 896), F32),
            pltpu.VMEM((NY, ROWS, 256), BF),
            pltpu.VMEM((NY, ROWS, QW), BF),
            pltpu.VMEM((NY, NZ, ROWS, 256), BF),
            pltpu.VMEM((NY, NZ, ROWS, 256), BF),
            pltpu.VMEM((NY, NZ, ROWS, 256), F32),
            pltpu.VMEM((NY, NZ, ROWS, 256), BF),
            pltpu.VMEM((NY, NZ, ROWS, 256), BF),
            pltpu.VMEM((NY, ROWS, 256), BF),
            pltpu.VMEM((2, 4, 2, 4, 4, ROWS, 256), BF),
            pltpu.VMEM((2, vocab, 256), F32),
            pltpu.VMEM((2, NY, ROWS, 128), F32),
            pltpu.VMEM((8, 256), F32),
            pltpu.VMEM((2, 256, 32), BF),
            pltpu.VMEM((16, 128), F32),
            pltpu.VMEM((NX * NY, 16, 128), F32),
            pltpu.VMEM((NM, 16, 128), F32),
            dma((20,)),
            dma((3,)), dma((3,)),
            dma, dma,
            dma((2, 8)), dma((2, 8)),
            dma((5,)), dma((5,)),
            dma((4, 8)), dma((4, 8)),
            dma((4,)), dma((4,)),
            dma((4,)), dma((4,)),
            dma((4,)), dma((4,)),
            dma((4, 4)), dma((4, 4)),
            dma((2, 4, 22)), dma((2, 4, 19)),
            dma((2, 16)), dma((2, 16)),
        ],
        compiler_params=pltpu.CompilerParams(
            collective_id=0, has_side_effects=True, vmem_limit_bytes=60 * 1024 * 1024),
        cost_estimate=pl.CostEstimate(flops=8_000_000_000, bytes_accessed=24_000_000,
                                      transcendentals=300_000),
    )(
        embeds, lengths, source, targets, attn_gain, final_gain.reshape(1, D), jnp.asarray(cos), jnp.asarray(sin),
        w_query.reshape(16, 2, 256, 512), w_key.reshape(16, 2, 256, 128),
        w_value.reshape(16, 2, 256, 128), w_out.reshape(512, 2048), head,
    )
    return (stats[0], stats[1])


def solution(mesh):
    return jax.shard_map(
        per_device,
        mesh=mesh,
        in_specs=(
            P("dp", "mp", None),
            P(),
            P(),
            P(),
            P("section", None),
            P("section", None, "mp"),
            P("section", None, "mp"),
            P("section", None, "mp"),
            P("section", "mp", "dp"),
            P(),
            P(("dp", "section", "mp"), None),
        ),
        out_specs=(P("dp", None), P("dp", None)),
        check_vma=False,
    )
```

```python
import jax
import jax.numpy as jnp
import numpy as np
from jax import lax
from jax.experimental import pallas as pl
from jax.experimental.pallas import tpu as pltpu
from jax.sharding import PartitionSpec as P

HD = 128
EPS = 1e-05
ROPE_BASE = 500000.0
NY = 4
NX = 4
NZ = 4
NM = 8
ROWS = 64
D = 8192
QW = 512
MESH = pl.DeviceIdType.MESH
BF = jnp.bfloat16
F32 = jnp.float32


def lane(start, size):
    return pl.ds(pl.multiple_of(start, 128), size)


def kernel(
    emb_in, live, source_of, targets_in, gain, fgain_in, cosine_in, sine_in, wq, wk, wv, wo, head,
    out,
    emb, targets, gains, fgain, cosine, sine, W, WO, HEAD, EB, XE, X, RX, MASK, SS, QA, QR, R, C, PS, PR, PO, ZS, ZR, HP, Y, LT, SQ, WANT, TAKE, STO, SA, SB,
    w_sem, sw_s, sw_r, qr_s, qr_r, eb_s, eb_r, hop_s, hop_r, ag_s, ag_r, res_s, res_r, ctx_s, ctx_r, ps_s, ps_r,
    zz_s, zz_r, y_s, y_r, st_s, st_r,
):
    d = lax.axis_index("dp")
    s = lax.axis_index("section")
    m = lax.axis_index("mp")
    z = m // 2
    c = m % 2
    sib = z * 2 + (1 - c)

    def ypeer(k):
        return (d + k) % NY

    def zpeer(k):
        return ((z + k) % NZ) * 2 + c

    def zother(k):
        return ((z + k) % NZ) * 2 + (1 - c)

    def rcopy(src, dst, ssem, rsem, dev):
        return pltpu.make_async_remote_copy(
            src_ref=src, dst_ref=dst, send_sem=ssem, recv_sem=rsem,
            device_id=dev, device_id_type=MESH,
        )

    here = (d, s, sib)

    barrier = pltpu.get_barrier_semaphore()
    partners = []
    for k in range(1, 4):
        partners.append((ypeer(k), s, m))
        partners.append((d, (s + k) % NX, m))
        partners.append((d, s, zpeer(k)))
        partners.append((d, s, zother(k)))
        partners.append((ypeer(k), (s + 1) % NX, m))
        partners.append((ypeer(k), (s + 3) % NX, m))
        partners.append((ypeer(k), (s + 2) % NX, m))
    partners.append(here)
    for dev in partners:
        pl.semaphore_signal(barrier, inc=1, device_id=dev, device_id_type=MESH)
    small = [
        pltpu.make_async_copy(src, dst, w_sem.at[14 + n])
        for n, (src, dst) in enumerate((
            (emb_in, emb), (gain, gains), (cosine_in, cosine), (sine_in, sine),
            (fgain_in, fgain), (targets_in, targets)))
    ]
    for copy in small:
        copy.start()
    parts = ((wq, pl.ds(0, 512)), (wk, pl.ds(512, 128)), (wv, pl.ds(640, 128)))

    def load(n, first):
        src, lanes = parts[n]
        take = 1 if first else jnp.where(s == 0, 0, c)
        return pltpu.make_async_copy(src.at[:, take], W.at[first, :, :, lanes],
                                     w_sem.at[3 * first + n])

    def swap(n):
        src, lanes = parts[n]
        return rcopy(src.at[:, 1 - c], W.at[1, :, :, lanes], sw_s.at[n], sw_r.at[n], here)

    wo_load = pltpu.make_async_copy(wo, WO, w_sem.at[12])
    for n in range(3):
        load(n, 0).start()

    @pl.when(s == 0)
    def _():
        for n in range(3):
            load(n, 1).start()

    head_load = pltpu.make_async_copy(HEAD, HEAD, w_sem.at[13])

    def row_slot(lanes):
        return (lanes // 64) * 2 + (lanes // 4) % 2, ((lanes // 8) % 8) * 4 + lanes % 4

    def wanted_rows():
        slot, position = row_slot(lax.broadcasted_iota(jnp.int32, (32, 256), 1))
        place = (position == lax.broadcasted_iota(jnp.int32, (32, 256), 0)).astype(BF)
        tokens = targets[...]
        keep = slot[0:8] == lax.broadcasted_iota(jnp.int32, (8, 256), 0)
        parts = []
        for term in (tokens // 256, tokens % 256):
            every = jnp.dot(term.astype(F32).astype(BF), place, preferred_element_type=F32)
            parts.append(jnp.sum(jnp.where(keep, every, 0.0), axis=0, keepdims=True))
        return parts[0] * 256.0 + parts[1]

    def prepare():
        wo_load.start()
        offsets = (0, 3, 1, 2)
        for cc in range(2):
            for j in range(4):
                for i in range(4):
                    g, zz = (offsets[i], offsets[j]) if cc == 0 else (offsets[j], offsets[i])
                    col = ypeer(g) * 2048 + ((z + zz) % NZ) * 512 + cc * 256
                    pltpu.make_async_copy(head.at[:, lane(col, 256)],
                                          HEAD.at[cc, j, :, i * 256:i * 256 + 256],
                                          w_sem.at[13]).start()
        shape = (4 * ROWS, ROWS)
        rq = lax.broadcasted_iota(jnp.int32, shape, 0) % ROWS
        rk = lax.broadcasted_iota(jnp.int32, shape, 1)
        slot_q, slot_k = (rq // 4) % 2, (rk // 4) % 2
        pos_q, pos_k = (rq // 8) * 4 + rq % 4, (rk // 8) * 4 + rk % 4
        live_k = jnp.where(slot_k == 0, live[2 * d], live[2 * d + 1])
        allowed = (slot_q == slot_k) & (pos_k <= pos_q) & (pos_k < live_k)
        MASK[...] = jnp.where(allowed, F32(0.0), F32(-1e30))

        @pl.when(s > 0)
        def _():
            for n in range(3):
                load(n, 0).wait()
                swap(n).wait_recv()
            for copy in small[1:2]:
                copy.wait()
            diagonal = (lax.broadcasted_iota(jnp.int32, (256, 256), 0)
                        == lax.broadcasted_iota(jnp.int32, (256, 256), 1))

            def scale(i, _):
                cols = lane((i // NZ) * 2048 + ((i % NZ) * 2 + c) * 256, 256)
                column = jnp.sum(jnp.where(diagonal, gains[:, cols], 0.0), axis=1, keepdims=True)
                for which in range(2):
                    W.at[which, i][...] = (W[which, i].astype(F32) * column).astype(BF)
                return 0

            lax.fori_loop(0, 16, scale, 0)

        @pl.when(s == 0)
        def _():
            for copy in small[1:2]:
                copy.wait()
        for copy in small[2:]:
            copy.wait()

        WANT[...] = jnp.broadcast_to(wanted_rows(), WANT.shape)
        slot, position = row_slot(lax.broadcasted_iota(jnp.int32, (256, 32), 0))
        place = lax.broadcasted_iota(jnp.int32, (256, 32), 1)
        for i in range(2):
            chosen = source_of[2 * d + i]
            TAKE.at[i][...] = ((slot == chosen) & (position == place)
                               & (place < live[chosen])).astype(F32).astype(BF)

        @pl.when(s > 0)
        def _():
            scale_head()

    def scale_head():
        head_load.wait()

        def off(n):
            return jnp.where(n == 0, 0, jnp.where(n == 1, 3, jnp.where(n == 2, 1, 2)))

        def scale(n, _):
            cc, j, i = n // 16, (n // 4) % 4, n % 4
            g = jnp.where(cc == 0, off(i), off(j))
            zz = jnp.where(cc == 0, off(j), off(i))
            col = ((d + g) % NY) * 2048 + ((z + zz) % NZ) * 512 + cc * 256
            block = HEAD.at[cc, j, :, lane(i * 256, 256)]
            block[...] = (block[...].astype(F32) * fgain[:, lane(col, 256)]).astype(BF)
            return 0

        lax.fori_loop(0, 32, scale, 0)

    small[0].wait()

    @pl.when(s == 0)
    def _():
        rows = jnp.concatenate([emb[0], emb[1]], axis=0).astype(F32)
        for q in range(2):
            EB.at[q, m][...] = jnp.concatenate(
                [rows[:, q * 2048:q * 2048 + 2048], rows[:, q * 2048 + 4096:q * 2048 + 6144]],
                axis=0).astype(BF)

    pl.semaphore_wait(barrier, len(partners))

    @pl.when(s > 0)
    def _():
        for n in range(3):
            swap(n).start()

    def eb_z(q, k):
        return rcopy(EB.at[q, m], EB.at[q, m], eb_s.at[q, k], eb_r.at[q, m], (d, s, zpeer(k)))

    def eb_z_in(q, k):
        mk = zpeer(k)
        return rcopy(EB.at[q, mk], EB.at[q, mk], eb_s.at[q, k], eb_r.at[q, mk], here)

    def eb_fwd(q, k):
        mk = zpeer(k)
        return rcopy(EB.at[q, mk], EB.at[q, mk], eb_s.at[q, 4 + k], eb_r.at[q, mk], here)

    def eb_sib_in(q, k):
        mk = zother(k)
        return rcopy(EB.at[q, mk], EB.at[q, mk], eb_s.at[q, 4 + k], eb_r.at[q, mk], here)

    def hop(g):
        return rcopy(HP.at[g], X.at[d, z], hop_s.at[g], hop_r.at[d], (g, (s + 1) % NX, m))

    def hop_in(g):
        return rcopy(HP.at[g], X.at[g, z], hop_s.at[g], hop_r.at[g], here)

    def hop_raw():
        return rcopy(HP, R, hop_s.at[4], hop_r.at[4], (d, (s + 1) % NX, m))

    def ag_z(g, k):
        return rcopy(X.at[g, z], X.at[g, z], ag_s.at[g, k], ag_r.at[g, z], (d, s, zpeer(k)))

    def ag_z_in(g, k):
        zk = (z + k) % NZ
        return rcopy(X.at[g, zk], X.at[g, zk], ag_s.at[g, k], ag_r.at[g, zk], here)

    def sums_out():
        return rcopy(QA.at[1], QR, qr_s, qr_r, here)

    def res(k):
        g = ypeer(k)
        return rcopy(RX.at[g], R.at[d], res_s.at[k], res_r.at[d], (g, s, m))

    def res_in(k):
        g = ypeer(k)
        return rcopy(RX.at[g], R.at[g], res_s.at[k], res_r.at[g], here)

    def ctx(k):
        return rcopy(C.at[d], C.at[d], ctx_s.at[k], ctx_r.at[d], (ypeer(k), s, m))

    def ctx_in(k):
        g = ypeer(k)
        return rcopy(C.at[g], C.at[g], ctx_s.at[k], ctx_r.at[g], here)

    def part(g):
        return rcopy(PS.at[g], PR.at[g], ps_s.at[g], ps_r.at[g], here)

    def zred(g, k):
        return rcopy(ZS.at[g, k], ZR.at[g, k], zz_s.at[g, k], zz_r.at[g, k], (d, s, zpeer(k)))

    def layer():
        def multiply(x, which, rows, n, start=False):
            w = W[which, pl.ds(rows * NZ, NZ)].reshape(4 * 256, 768)
            term = jnp.dot(x, w, preferred_element_type=F32)
            QA.at[n][:, 0:768] = term if start else QA[n, :, 0:768] + term

        @pl.when(s == 0)
        def _():
            for q in range(2):
                for k in (1, 3, 2):
                    eb_z_in(q, k).wait_recv()
                    eb_fwd(q, k).start()
            QA[...] = jnp.zeros_like(QA)
            QR[...] = jnp.zeros_like(QR)
            SS[...] = jnp.zeros_like(SS)
            for q in range(2):
                for k in range(4):
                    eb_sib_in(q, k).wait_recv()

                def blocks(mm):
                    x = EB[q, :, :, lane(mm * 256, 256)].astype(F32)
                    return [x[:, i * 8:i * 8 + 8, :].reshape(ROWS, 256) for i in range(2)]

                def body(mm, total):
                    for half, xs in enumerate(blocks(mm)):
                        g = half * 2 + q
                        cols = lane(g * 2048 + mm * 256, 256)
                        XE.at[g, mm][...] = (xs * gains[:, cols]).astype(BF)
                        square = xs * xs
                        total = total + square[:, 0:128] + square[:, 128:256]
                    return total

                SS[...] = lax.fori_loop(0, NM, body, SS[...])
                for half, xs in enumerate(blocks(m)):
                    RX.at[half * 2 + q][...] = xs.astype(BF)
                if q == 0:
                    for n in range(3):
                        load(n, 0).wait()
                        load(n, 1).wait()

                def both(i, _):
                    g = 2 * i + q
                    for who in range(2):
                        x = jnp.concatenate([XE[g, 2 * zz + who] for zz in range(NZ)], axis=1)
                        multiply(x, who, g, 0)
                    return 0

                lax.fori_loop(0, 2, both, 0)
            for k in (2, 1, 3):
                res(k).start()
            R.at[d][...] = RX[d]

        @pl.when(s > 0)
        def _():
            def arrived(k):
                g = ypeer(k)
                hop_in(g).wait_recv()
                for j in (2, 1, 3):
                    ag_z(g, j).start()

            def columns(k):
                g = ypeer(k)
                for j in (1, 3, 2):
                    ag_z_in(g, j).wait_recv()
                return jnp.concatenate([X[g, zz] for zz in range(NZ)], axis=1)

            def both(k, start=False):
                x = columns(k)
                multiply(x, 1, ypeer(k), 1, start)
                multiply(x, 0, ypeer(k), 0, start)

            def squares_of(k):
                total = jnp.zeros((ROWS, 128), F32)
                for zz in range(NZ):
                    x = X[ypeer(k), zz].astype(F32)
                    square = x * x
                    total = total + square[:, 0:128] + square[:, 128:256]
                return total

            arrived(0)
            arrived(3)
            arrived(1)
            arrived(2)
            both(0, True)
            squares = squares_of(0)
            both(3)
            squares = squares + squares_of(3)
            both(1)
            squares = squares + squares_of(1)
            x = columns(2)
            multiply(x, 1, ypeer(2), 1)
            squares = squares + squares_of(2)
            QA.at[1][:, 768:896] = squares
            sums_out().start()
            multiply(x, 0, ypeer(2), 0)
            sums_out().wait_recv()
            SS[...] = squares + QR[:, 768:896]

        r = lax.rsqrt(jnp.sum(SS[...], axis=1, keepdims=True) * (1.0 / D) + EPS)
        cos = cosine[...]
        sin = sine[...]

        def summed(first, last):
            return QA[0, :, first:last] + QR[:, first:last]

        def rope(x):
            return (x * cos + pltpu.roll(x, 64, 1) * sin).astype(BF)

        query = jnp.concatenate(
            [rope(summed(j * HD, (j + 1) * HD) * r) for j in range(4)], axis=0)
        key = rope(summed(512, 640) * r)
        value = (summed(640, 768) * r).astype(BF)
        scores = lax.dot_general(query, key, (((1,), (1,)), ((), ())),
                                 preferred_element_type=F32) * (HD ** -0.5)
        scores = scores + MASK[...]
        highest = jnp.max(scores, axis=-1, keepdims=True)
        weights = jnp.exp(scores - highest)
        probs = (weights / jnp.sum(weights, axis=-1, keepdims=True)).astype(BF)
        mixed = jnp.dot(probs, value, preferred_element_type=F32).astype(BF)
        for j in range(4):
            C.at[d][:, j * HD:(j + 1) * HD] = mixed[j * ROWS:(j + 1) * ROWS]
        for k in (2, 1, 3):
            ctx(k).start()

        wo_load.wait()

        def project(g):
            for zz in range(NZ):
                p = jnp.dot(C[g], WO[:, zz * 512:zz * 512 + 512], preferred_element_type=F32)
                low, high = p[:, :256], p[:, 256:]
                PO.at[g, zz][...] = jnp.where(c == 0, low, high)
                PS.at[g, zz][...] = jnp.where(c == 0, high, low).astype(BF)
            part(g).start()

        def pair(g):
            part(g).wait_recv()
            for k in (2, 1, 3):
                zt = (z + k) % NZ
                ZS.at[g, k][...] = (PO[g, zt] + PR[g, zt].astype(F32)).astype(BF)
                zred(g, k).start()

        def total_of(g):
            total = PO[g, z] + PR[g, z].astype(F32) + R[g].astype(F32)
            for k in (1, 3, 2):
                zred(g, k).wait_recv()
                total = total + ZR[g, k].astype(F32)
            HP.at[g][...] = total.astype(BF)

            @pl.when(s < NX - 1)
            def _():
                hop(g).start()

        project(d)

        @pl.when(s == 0)
        def _():
            for k in (1, 3, 2):
                res_in(k).wait_recv()

        @pl.when(s > 0)
        def _():
            hop_raw().wait_recv()

        pair(d)
        for k in (1, 3):
            ctx_in(k).wait_recv()
            project(ypeer(k))
        pair(ypeer(1))
        pair(ypeer(3))
        def own_chunk(k):
            @pl.when(s == NX - 1)
            def _():
                stage_own(1, k, True)
                if k >= 1:
                    stage_first(1, k - 1)
                if k >= 2:
                    stage_second(1, k - 2)

        total_of(d)
        own_chunk(0)
        ctx_in(2).wait_recv()
        project(ypeer(2))
        total_of(ypeer(1))
        pair(ypeer(2))
        own_chunk(1)
        total_of(ypeer(3))
        own_chunk(2)
        total_of(ypeer(2))
        own_chunk(3)

        @pl.when(s < NX - 1)
        def _():
            hop_raw().start()

        @pl.when(s == 1)
        def _():
            def body(k, _):
                stage_own(0, k, True)
                return 0

            lax.fori_loop(0, 4, body, 0)

    def first_dev(k):
        return (jnp.where(c == 0, ypeer(k), d), s, jnp.where(c == 0, m, zpeer(k)))

    def second_dev(k):
        return (jnp.where(c == 0, d, ypeer(k)), s, jnp.where(c == 0, zpeer(k), m))

    def ycopy(src, dst, b, k, i, j, dev):
        return rcopy(src, dst, y_s.at[b, k, i], y_r.at[b, k, j], dev)

    def y_x(b, k, n):
        ref = Y.at[b, k, c, 0, 0]
        return ycopy(ref, ref, b, k, n, 0, (d, (s + n) % NX, m))

    def y_first(b, k, n):
        slot = (1, 3, 2)[n - 1]
        return ycopy(Y.at[b, k, c, 0, 0], Y.at[b, k, c, 0, slot], b, k, 3 + n, slot, first_dev(n))

    sets = (pl.ds(0, 1), pl.ds(1, 2), pl.ds(3, 1))

    def y_second(b, k, part_no, n):
        slot = 1 if n == 1 else 2
        return ycopy(Y.at[b, k, c, 0, sets[part_no]], Y.at[b, k, c, slot, sets[part_no]], b, k,
                     7 + part_no * 2 + (slot - 1), 1 + 3 * slot + part_no, second_dev(n))

    def y_relay(b, k, half):
        slot, n = ((1, 1), (2, 3))[half]
        two = pl.ds(2 * half, 2)
        return ycopy(Y.at[b, k, c, slot, two], Y.at[b, k, c, 3, two], b, k, 13 + half, 10 + half,
                     second_dev(n))

    def y_far(k):
        ref = Y.at[0, k, c, 3]
        return ycopy(ref, ref, 0, k, 22, 19, (d, NX - 1 - s, m))

    forwards = ((0, 0, 1), (0, 1, 2), (0, 3, 1), (1, 0, 4), (2, 0, 4), (3, 0, 2), (3, 2, 2))

    def y_fwd(b, k, n, who):
        j, i, size = forwards[n]
        ref = Y.at[b, k, who, j, pl.ds(i, size)]
        return ycopy(ref, ref, b, k, 15 + n, 12 + n, here)

    def chunk_order(step):
        return jnp.where(step == 3, 2, jnp.where(step == 2, 3, step))

    def stage_own(b, k, source):
        if source:
            Y.at[b, k, c, 0, 0][...] = HP[(d + chunk_order(k)) % NY]
            for n in (2, 1, 3):
                y_x(b, k, n).start()
        else:
            y_x(b, k, 1).wait_recv()
        for n in (2, 1, 3):
            y_first(b, k, n).start()
        for n in (1, 3):
            y_second(b, k, 0, n).start()
        y_fwd(b, k, 0, c).start()

    def stage_first(b, k):
        y_first(b, k, 1).wait_recv()
        y_first(b, k, 3).wait_recv()
        for n in (1, 3):
            y_second(b, k, 1, n).start()
        y_fwd(b, k, 1, c).start()
        y_first(b, k, 2).wait_recv()
        for n in (1, 3):
            y_second(b, k, 2, n).start()
        y_fwd(b, k, 2, c).start()

    def relaying(b):
        return (b == 1) | (s < 2)

    def stage_second(b, k):
        for part_no in (0, 1):
            y_second(b, k, part_no, 1).wait_recv()

        @pl.when(relaying(b))
        def _():
            y_relay(b, k, 0).start()

        for part_no in (1, 2):
            y_second(b, k, part_no, 3).wait_recv()

        @pl.when(relaying(b))
        def _():
            y_relay(b, k, 1).start()

        y_second(b, k, 2, 1).wait_recv()
        y_fwd(b, k, 3, c).start()
        y_second(b, k, 0, 3).wait_recv()
        y_fwd(b, k, 4, c).start()

    def opposite(b, k):
        @pl.when(relaying(b))
        def _():
            for half in range(2):
                y_relay(b, k, half).wait_recv()
                y_fwd(b, k, 5 + half, c).start()

            @pl.when(b == 0)
            def _():
                y_far(k).start()

        @pl.when(jnp.logical_not(relaying(b)))
        def _():
            y_far(k).wait_recv()
            for half in range(2):
                y_fwd(b, k, 5 + half, c).start()

    def stage_last(b, k):
        opposite(b, k)
        for n in range(7):
            y_fwd(b, k, n, 1 - c).wait_recv()

    def dots(b, cc, j):
        blocks = []
        for g in range(NY):
            row = []
            total = jnp.zeros((ROWS, 128), F32)
            for i in range(4):
                off_j = jnp.where(j == 0, 0, jnp.where(j == 1, 3, jnp.where(j == 2, 1, 2)))
                sender = (d + jnp.where(cc == 0, (0, 3, 1, 2)[i], off_j)) % NY
                k = chunk_order((g - sender + NY) % NY)
                x = Y[b, k, cc, j, i]
                row.append(x)
                wide = x.astype(F32)
                square = wide * wide
                total = total + square[:, 0:128] + square[:, 128:256]
            SQ.at[b, g][...] += total
            blocks.append(jnp.concatenate(row, axis=1))
        pieces = jnp.concatenate(blocks, axis=0)
        LT.at[b][...] += lax.dot_general(HEAD[cc, j], pieces, (((1,), (1,)), ((), ())),
                                         preferred_element_type=F32)

    def layer_sent():
        @pl.when(s == 0)
        def _():
            for q in range(2):
                for k in range(1, 4):
                    eb_z(q, k).wait_send()
                for k in range(4):
                    eb_fwd(q, k).wait_send()
            for k in range(1, 4):
                res(k).wait_send()

        @pl.when(s > 0)
        def _():
            for g in range(NY):
                for k in range(1, 4):
                    ag_z(g, k).wait_send()
            sums_out().wait_send()
            for n in range(3):
                swap(n).wait_send()

        @pl.when(s < NX - 1)
        def _():
            for g in range(NY):
                hop(g).wait_send()
            hop_raw().wait_send()

        for g in range(NY):
            for k in range(1, 4):
                zred(g, k).wait_send()
            part(g).wait_send()
        for k in range(1, 4):
            ctx(k).wait_send()

    def chunk_sent(b, k, source):
        @pl.when(s == source)
        def _():
            for j in (1, 2, 3):
                y_x(b, k, j).wait_send()

        for j in (1, 2, 3):
            y_first(b, k, j).wait_send()
        for j in (1, 3):
            for part_no in range(3):
                y_second(b, k, part_no, j).wait_send()

        @pl.when(relaying(b))
        def _():
            for half in range(2):
                y_relay(b, k, half).wait_send()

            @pl.when(b == 0)
            def _():
                y_far(k).wait_send()

        for j in range(7):
            y_fwd(b, k, j, c).wait_send()

    def gather(b):
        source = 2 * b + 1
        final = (b == 1) & (s == NX - 1)
        late = (b == 1) & (s >= 2)

        def body(t, _):
            @pl.when((t < 4) & (s != source))
            def _():
                stage_own(b, t, False)

            @pl.when((t >= 1) & (t < 5) & ((t == 4) | jnp.logical_not(final)))
            def _():
                stage_first(b, t - 1)

            @pl.when((t >= 2) & (t < 6) & ((t >= 4) | jnp.logical_not(final)))
            def _():
                stage_second(b, t - 2)

            @pl.when((t >= 3) & relaying(b))
            def _():
                stage_last(b, t - 3)
                chunk_sent(b, t - 3, source)

            @pl.when(late & (t == 0))
            def _():
                def rest(k, _):
                    stage_last(0, k)
                    chunk_sent(0, k, 1)
                    return 0

                lax.fori_loop(0, 4, rest, 0)

            @pl.when(late & (t >= 1) & (t < 5))
            def _():
                j = chunk_order(t - 1)
                dots(0, c, j)
                dots(0, 1 - c, j)
            return 0

        lax.fori_loop(0, 6, body, 0)

    def finish(b):
        @pl.when((b == 1) | (s < 2))
        def _():
            dots(b, c, 0)
            for n in range(3):
                y_fwd(b, 3, n, 1 - c).wait_recv()
            dots(b, 1 - c, 0)
            dots(b, c, 1)
            dots(b, c, 2)
            opposite(b, 3)
            for n in (3, 4):
                y_fwd(b, 3, n, 1 - c).wait_recv()
            dots(b, 1 - c, 1)
            dots(b, 1 - c, 2)
            dots(b, c, 3)
            for n in (5, 6):
                y_fwd(b, 3, n, 1 - c).wait_recv()
            dots(b, 1 - c, 3)

        @pl.when((b == 0) & (s < 2))
        def _():
            chunk_sent(0, 3, 1)

        squares = SQ[b].reshape(NY * ROWS, 128)
        top = squares.astype(BF)
        rest = (squares - top.astype(F32)).astype(BF)
        ones = jnp.ones((16, 128), BF)
        nt = (((1,), (1,)), ((), ()))
        sums = (lax.dot_general(ones, top, nt, preferred_element_type=F32)
                + lax.dot_general(ones, rest, nt, preferred_element_type=F32))[0:1]
        r = lax.rsqrt(sums * (1.0 / D) + EPS)
        logits = LT[b] * r
        highest = jnp.max(logits, axis=0, keepdims=True)
        summed = jnp.sum(jnp.exp(logits - highest), axis=0, keepdims=True)
        vocab = HEAD.shape[2]
        first = ((d * NX + s) * NM + m) * vocab
        index = (lax.broadcasted_iota(jnp.int32, logits.shape, 0) + first).astype(F32)
        wanted = WANT[0:1, :]
        picked = jnp.sum(jnp.where(index == wanted, logits, 0.0), axis=0, keepdims=True)
        for n, value in enumerate((highest, summed, picked)):
            for half in range(2):
                STO[pl.ds(n * 4 + b * 2 + half, 1), :] = value[:, half * 128:half * 128 + 128]

    def step(t, _):
        last = s == NX - 1
        place = jnp.where(last, 1, 0)

        @pl.when(t == place)
        def _():
            layer()

        @pl.when(jnp.where(last, (t == 0) | (t == 2), (t == 1) | (t == jnp.where(s < 2, 3, 2))))
        def _():
            gather(jnp.where((t == 0) | (t == 1), 0, 1))

        @pl.when((t == 4) | (t == jnp.where(s < 2, 2, 3)))
        def _():
            @pl.when((t == 2) & (s == 0))
            def _():
                scale_head()
            finish(jnp.where(t == 4, 1, 0))
        return 0

    @pl.when(s == 0)
    def _():
        for q in range(2):
            for k in (2, 1, 3, 0):
                (eb_z(q, k) if k else eb_fwd(q, 0)).start()

    prepare()
    STO[...] = jnp.zeros_like(STO)
    SQ[...] = jnp.zeros_like(SQ)
    LT[...] = jnp.zeros_like(LT)
    lax.fori_loop(0, 5, step, 0)

    def merge(ref, count):
        parts = [ref[j] for j in range(count)]
        highest = parts[0][0:4]
        for p in parts[1:]:
            highest = jnp.maximum(highest, p[0:4])
        summed = jnp.zeros_like(highest)
        picked = jnp.zeros_like(highest)
        for p in parts:
            summed = summed + p[4:8] * jnp.exp(p[0:4] - highest)
            picked = picked + p[8:12]
        return highest, summed, picked

    def stacked(highest, summed, picked):
        return jnp.concatenate([highest, summed, picked, jnp.zeros_like(picked)], axis=0)

    pairs = [(j, k) for j in range(NX) for k in range(NY) if j or k]

    def st_yx(n):
        j, k = pairs[n]
        mine = s * NY + d
        return rcopy(SA.at[mine], SA.at[mine], st_s.at[0, n], st_r.at[0, mine],
                     (ypeer(k), (s + j) % NX, m))

    def st_yx_in(n):
        j, k = pairs[n]
        other = ((s + j) % NX) * NY + ypeer(k)
        return rcopy(SA.at[other], SA.at[other], st_s.at[0, n], st_r.at[0, other], here)

    def m_of(k):
        return (m + k) % NM

    def st_m(k):
        return rcopy(SB.at[m], SB.at[m], st_s.at[1, k], st_r.at[1, m], (d, s, m_of(k)))

    def st_m_in(k):
        mm = m_of(k)
        return rcopy(SB.at[mm], SB.at[mm], st_s.at[1, k], st_r.at[1, mm], (d, s, mm))

    SA.at[s * NY + d][...] = STO[...]
    for n in range(15):
        st_yx(n).start()
    layer_sent()
    chunk_sent(1, 3, NX - 1)
    for n in range(15):
        st_yx_in(n).wait_recv()
    SB.at[m][...] = stacked(*merge(SA, NX * NY))
    for k in (4, 3, 5, 2, 6, 1, 7):
        st_m(k).start()
    for n in range(15):
        st_yx(n).wait_send()
    for k in (1, 7, 2, 6, 3, 5, 4):
        st_m_in(k).wait_recv()
    highest, summed, picked = merge(SB, NM)
    logprob = picked - (highest + jnp.log(summed))
    terms = []
    for e in range(2):
        rest = jnp.concatenate([logprob[2 * e:2 * e + 1], logprob[2 * e + 1:2 * e + 2]], axis=1)
        for _ in range(3):
            term = rest.astype(BF).astype(F32)
            terms.append(term)
            rest = rest - term
    row = lax.broadcasted_iota(jnp.int32, (16, 256), 0)
    stack = jnp.zeros((16, 256), F32)
    for j, term in enumerate(terms):
        stack = jnp.where(row == j, term, stack)
    stack = stack.astype(BF)
    results = []
    for i in range(2):
        got = jnp.dot(stack, TAKE[i], preferred_element_type=F32)
        results.append([got[j:j + 1] + got[j + 1:j + 2] + got[j + 2:j + 3] for j in (0, 3)])
    for e in range(2):
        first = lax.broadcasted_iota(jnp.int32, (2, 32), 0) == 0
        out.at[e][...] = jnp.where(first, results[0][e], results[1][e])
    for k in range(1, 8):
        st_m(k).wait_send()


def tables():
    row = np.arange(ROWS)
    position = (row // 8) * 4 + row % 4
    half = HD // 2
    freqs = (ROPE_BASE ** (-np.arange(half) * 2.0 / HD)).astype(np.float32)
    angles = (position.astype(np.float32)[:, None] * freqs[None, :]).astype(np.float64)
    cos, sin = np.cos(angles), np.sin(angles)
    return (np.concatenate([cos, cos], 1).astype(np.float32),
            np.concatenate([-sin, sin], 1).astype(np.float32))


def per_device(
    embeds, targets, lengths, source, attn_gain, w_query, w_key, w_value, w_out, final_gain, head
):
    vocab = head.shape[0]
    cos, sin = tables()
    vmem = pl.BlockSpec(memory_space=pltpu.VMEM)
    hbm = pl.BlockSpec(memory_space=pl.ANY)
    smem = pl.BlockSpec(memory_space=pltpu.SMEM)
    dma = pltpu.SemaphoreType.DMA
    stats = pl.pallas_call(
        kernel,
        out_shape=jax.ShapeDtypeStruct((2, 2, 32), F32),
        in_specs=[hbm, smem, smem] + [hbm] * 10,
        out_specs=vmem,
        scratch_shapes=[
            pltpu.VMEM((2, 4, D), BF),
            pltpu.VMEM((8, 32), jnp.int32),
            pltpu.VMEM((1, D), F32),
            pltpu.VMEM((1, D), F32),
            pltpu.VMEM((ROWS, HD), F32),
            pltpu.VMEM((ROWS, HD), F32),
            pltpu.VMEM((2, 16, 256, 768), BF),
            pltpu.VMEM((QW, 2048), BF),
            pltpu.VMEM((2, 4, vocab, 1024), BF),
            pltpu.VMEM((2, NM, 16, 2048), BF),
            pltpu.VMEM((NY, NM, ROWS, 256), BF),
            pltpu.VMEM((NY, NZ, ROWS, 256), BF),
            pltpu.VMEM((NY, ROWS, 256), BF),
            pltpu.VMEM((4 * ROWS, ROWS), F32),
            pltpu.VMEM((ROWS, 128), F32),
            pltpu.VMEM((2, ROWS, 896), F32),
            pltpu.VMEM((ROWS, 896), F32),
            pltpu.VMEM((NY, ROWS, 256), BF),
            pltpu.VMEM((NY, ROWS, QW), BF),
            pltpu.VMEM((NY, NZ, ROWS, 256), BF),
            pltpu.VMEM((NY, NZ, ROWS, 256), BF),
            pltpu.VMEM((NY, NZ, ROWS, 256), F32),
            pltpu.VMEM((NY, NZ, ROWS, 256), BF),
            pltpu.VMEM((NY, NZ, ROWS, 256), BF),
            pltpu.VMEM((NY, ROWS, 256), BF),
            pltpu.VMEM((2, 4, 2, 4, 4, ROWS, 256), BF),
            pltpu.VMEM((2, vocab, 256), F32),
            pltpu.VMEM((2, NY, ROWS, 128), F32),
            pltpu.VMEM((8, 256), F32),
            pltpu.VMEM((2, 256, 32), BF),
            pltpu.VMEM((16, 128), F32),
            pltpu.VMEM((NX * NY, 16, 128), F32),
            pltpu.VMEM((NM, 16, 128), F32),
            dma((20,)),
            dma((3,)), dma((3,)),
            dma, dma,
            dma((2, 8)), dma((2, 8)),
            dma((5,)), dma((5,)),
            dma((4, 8)), dma((4, 8)),
            dma((4,)), dma((4,)),
            dma((4,)), dma((4,)),
            dma((4,)), dma((4,)),
            dma((4, 4)), dma((4, 4)),
            dma((2, 4, 23)), dma((2, 4, 20)),
            dma((2, 16)), dma((2, 16)),
        ],
        compiler_params=pltpu.CompilerParams(
            collective_id=0, has_side_effects=True, vmem_limit_bytes=60 * 1024 * 1024),
        cost_estimate=pl.CostEstimate(flops=8_000_000_000, bytes_accessed=24_000_000,
                                      transcendentals=300_000),
    )(
        embeds, lengths, source, targets, attn_gain, final_gain.reshape(1, D), jnp.asarray(cos), jnp.asarray(sin),
        w_query.reshape(16, 2, 256, 512), w_key.reshape(16, 2, 256, 128),
        w_value.reshape(16, 2, 256, 128), w_out.reshape(512, 2048), head,
    )
    return (stats[0], stats[1])


def solution(mesh):
    return jax.shard_map(
        per_device,
        mesh=mesh,
        in_specs=(
            P("dp", "mp", None),
            P(),
            P(),
            P(),
            P("section", None),
            P("section", None, "mp"),
            P("section", None, "mp"),
            P("section", None, "mp"),
            P("section", "mp", "dp"),
            P(),
            P(("dp", "section", "mp"), None),
        ),
        out_specs=(P("dp", None), P("dp", None)),
        check_vma=False,
    )
```

```python
import jax
import jax.numpy as jnp
import numpy as np
from jax import lax
from jax.experimental import pallas as pl
from jax.experimental.pallas import tpu as pltpu
from jax.sharding import PartitionSpec as P

HD = 128
EPS = 1e-05
ROPE_BASE = 500000.0
NY = 4
NX = 4
NZ = 4
NM = 8
ROWS = 64
D = 8192
QW = 512
MESH = pl.DeviceIdType.MESH
BF = jnp.bfloat16
F32 = jnp.float32


def lane(start, size):
    return pl.ds(pl.multiple_of(start, 128), size)


def kernel(
    emb_in, live, source_of, targets_in, gain, fgain_in, cosine_in, sine_in, wq, wk, wv, wo, head,
    out,
    emb, targets, gains, fgain, cosine, sine, W, WO, HEAD, EB, XE, X, RX, MASK, SS, QA, QR, R, C, PS, PR, PO, ZS, ZR, HP, Y, LT, SQ, WANT, TAKE, STO, SA, SB,
    w_sem, sw_s, sw_r, qr_s, qr_r, eb_s, eb_r, hop_s, hop_r, ag_s, ag_r, res_s, res_r, ctx_s, ctx_r, ps_s, ps_r,
    zz_s, zz_r, y_s, y_r, st_s, st_r,
):
    d = lax.axis_index("dp")
    s = lax.axis_index("section")
    m = lax.axis_index("mp")
    z = m // 2
    c = m % 2
    sib = z * 2 + (1 - c)

    def ypeer(k):
        return (d + k) % NY

    def zpeer(k):
        return ((z + k) % NZ) * 2 + c

    def zother(k):
        return ((z + k) % NZ) * 2 + (1 - c)

    def rcopy(src, dst, ssem, rsem, dev):
        return pltpu.make_async_remote_copy(
            src_ref=src, dst_ref=dst, send_sem=ssem, recv_sem=rsem,
            device_id=dev, device_id_type=MESH,
        )

    here = (d, s, sib)

    barrier = pltpu.get_barrier_semaphore()
    partners = []
    for k in range(1, 4):
        partners.append((ypeer(k), s, m))
        partners.append((d, (s + k) % NX, m))
        partners.append((d, s, zpeer(k)))
        partners.append((d, s, zother(k)))
        partners.append((ypeer(k), (s + 1) % NX, m))
        partners.append((ypeer(k), (s + 3) % NX, m))
        partners.append((ypeer(k), (s + 2) % NX, m))
    partners.append(here)
    for dev in partners:
        pl.semaphore_signal(barrier, inc=1, device_id=dev, device_id_type=MESH)
    small = [
        pltpu.make_async_copy(src, dst, w_sem.at[14 + n])
        for n, (src, dst) in enumerate((
            (emb_in, emb), (gain, gains), (cosine_in, cosine), (sine_in, sine),
            (fgain_in, fgain), (targets_in, targets)))
    ]
    for copy in small:
        copy.start()
    parts = ((wq, pl.ds(0, 512)), (wk, pl.ds(512, 128)), (wv, pl.ds(640, 128)))

    def load(n, first):
        src, lanes = parts[n]
        take = 1 if first else jnp.where(s == 0, 0, c)
        return pltpu.make_async_copy(src.at[:, take], W.at[first, :, :, lanes],
                                     w_sem.at[3 * first + n])

    def swap(n):
        src, lanes = parts[n]
        return rcopy(src.at[:, 1 - c], W.at[1, :, :, lanes], sw_s.at[n], sw_r.at[n], here)

    wo_load = pltpu.make_async_copy(wo, WO, w_sem.at[12])
    for n in range(3):
        load(n, 0).start()

    @pl.when(s == 0)
    def _():
        for n in range(3):
            load(n, 1).start()

    head_load = pltpu.make_async_copy(HEAD, HEAD, w_sem.at[13])

    def row_slot(lanes):
        return (lanes // 64) * 2 + (lanes // 4) % 2, ((lanes // 8) % 8) * 4 + lanes % 4

    def wanted_rows():
        slot, position = row_slot(lax.broadcasted_iota(jnp.int32, (32, 256), 1))
        place = (position == lax.broadcasted_iota(jnp.int32, (32, 256), 0)).astype(BF)
        tokens = targets[...]
        keep = slot[0:8] == lax.broadcasted_iota(jnp.int32, (8, 256), 0)
        parts = []
        for term in (tokens // 256, tokens % 256):
            every = jnp.dot(term.astype(F32).astype(BF), place, preferred_element_type=F32)
            parts.append(jnp.sum(jnp.where(keep, every, 0.0), axis=0, keepdims=True))
        return parts[0] * 256.0 + parts[1]

    def prepare():
        wo_load.start()
        offsets = (0, 3, 1, 2)
        for cc in range(2):
            for j in range(4):
                for i in range(4):
                    g, zz = (offsets[i], offsets[j]) if cc == 0 else (offsets[j], offsets[i])
                    col = ypeer(g) * 2048 + ((z + zz) % NZ) * 512 + cc * 256
                    pltpu.make_async_copy(head.at[:, lane(col, 256)],
                                          HEAD.at[cc, j, :, i * 256:i * 256 + 256],
                                          w_sem.at[13]).start()
        shape = (4 * ROWS, ROWS)
        rq = lax.broadcasted_iota(jnp.int32, shape, 0) % ROWS
        rk = lax.broadcasted_iota(jnp.int32, shape, 1)
        slot_q, slot_k = (rq // 4) % 2, (rk // 4) % 2
        pos_q, pos_k = (rq // 8) * 4 + rq % 4, (rk // 8) * 4 + rk % 4
        live_k = jnp.where(slot_k == 0, live[2 * d], live[2 * d + 1])
        allowed = (slot_q == slot_k) & (pos_k <= pos_q) & (pos_k < live_k)
        MASK[...] = jnp.where(allowed, F32(0.0), F32(-1e30))

        @pl.when(s > 0)
        def _():
            for n in range(3):
                load(n, 0).wait()
                swap(n).wait_recv()
            for copy in small[1:2]:
                copy.wait()
            diagonal = (lax.broadcasted_iota(jnp.int32, (256, 256), 0)
                        == lax.broadcasted_iota(jnp.int32, (256, 256), 1))

            def scale(i, _):
                cols = lane((i // NZ) * 2048 + ((i % NZ) * 2 + c) * 256, 256)
                column = jnp.sum(jnp.where(diagonal, gains[:, cols], 0.0), axis=1, keepdims=True)
                for which in range(2):
                    W.at[which, i][...] = (W[which, i].astype(F32) * column).astype(BF)
                return 0

            lax.fori_loop(0, 16, scale, 0)

        @pl.when(s == 0)
        def _():
            for copy in small[1:2]:
                copy.wait()
        for copy in small[2:]:
            copy.wait()

        WANT[...] = jnp.broadcast_to(wanted_rows(), WANT.shape)
        slot, position = row_slot(lax.broadcasted_iota(jnp.int32, (256, 32), 0))
        place = lax.broadcasted_iota(jnp.int32, (256, 32), 1)
        for i in range(2):
            chosen = source_of[2 * d + i]
            TAKE.at[i][...] = ((slot == chosen) & (position == place)
                               & (place < live[chosen])).astype(F32).astype(BF)

        @pl.when(s > 0)
        def _():
            scale_head()

    def scale_head():
        head_load.wait()

        def off(n):
            return jnp.where(n == 0, 0, jnp.where(n == 1, 3, jnp.where(n == 2, 1, 2)))

        def scale(n, _):
            cc, j, i = n // 16, (n // 4) % 4, n % 4
            g = jnp.where(cc == 0, off(i), off(j))
            zz = jnp.where(cc == 0, off(j), off(i))
            col = ((d + g) % NY) * 2048 + ((z + zz) % NZ) * 512 + cc * 256
            block = HEAD.at[cc, j, :, lane(i * 256, 256)]
            block[...] = (block[...].astype(F32) * fgain[:, lane(col, 256)]).astype(BF)
            return 0

        lax.fori_loop(0, 32, scale, 0)

    small[0].wait()

    @pl.when(s == 0)
    def _():
        rows = jnp.concatenate([emb[0], emb[1]], axis=0).astype(F32)
        for q in range(2):
            EB.at[q, m][...] = jnp.concatenate(
                [rows[:, q * 2048:q * 2048 + 2048], rows[:, q * 2048 + 4096:q * 2048 + 6144]],
                axis=0).astype(BF)

    pl.semaphore_wait(barrier, len(partners))

    @pl.when(s > 0)
    def _():
        for n in range(3):
            swap(n).start()

    def eb_z(q, k):
        return rcopy(EB.at[q, m], EB.at[q, m], eb_s.at[q, k], eb_r.at[q, m], (d, s, zpeer(k)))

    def eb_z_in(q, k):
        mk = zpeer(k)
        return rcopy(EB.at[q, mk], EB.at[q, mk], eb_s.at[q, k], eb_r.at[q, mk], here)

    def eb_fwd(q, k):
        mk = zpeer(k)
        return rcopy(EB.at[q, mk], EB.at[q, mk], eb_s.at[q, 4 + k], eb_r.at[q, mk], here)

    def eb_sib_in(q, k):
        mk = zother(k)
        return rcopy(EB.at[q, mk], EB.at[q, mk], eb_s.at[q, 4 + k], eb_r.at[q, mk], here)

    def hop(g):
        return rcopy(HP.at[g], X.at[d, z], hop_s.at[g], hop_r.at[d], (g, (s + 1) % NX, m))

    def hop_in(g):
        return rcopy(HP.at[g], X.at[g, z], hop_s.at[g], hop_r.at[g], here)

    def hop_raw():
        return rcopy(HP, R, hop_s.at[4], hop_r.at[4], (d, (s + 1) % NX, m))

    def ag_z(g, k):
        return rcopy(X.at[g, z], X.at[g, z], ag_s.at[g, k], ag_r.at[g, z], (d, s, zpeer(k)))

    def ag_z_in(g, k):
        zk = (z + k) % NZ
        return rcopy(X.at[g, zk], X.at[g, zk], ag_s.at[g, k], ag_r.at[g, zk], here)

    def sums_out():
        return rcopy(QA.at[1], QR, qr_s, qr_r, here)

    def res(k):
        g = ypeer(k)
        return rcopy(RX.at[g], R.at[d], res_s.at[k], res_r.at[d], (g, s, m))

    def res_in(k):
        g = ypeer(k)
        return rcopy(RX.at[g], R.at[g], res_s.at[k], res_r.at[g], here)

    def ctx(k):
        return rcopy(C.at[d], C.at[d], ctx_s.at[k], ctx_r.at[d], (ypeer(k), s, m))

    def ctx_in(k):
        g = ypeer(k)
        return rcopy(C.at[g], C.at[g], ctx_s.at[k], ctx_r.at[g], here)

    def part(g):
        return rcopy(PS.at[g], PR.at[g], ps_s.at[g], ps_r.at[g], here)

    def zred(g, k):
        return rcopy(ZS.at[g, k], ZR.at[g, k], zz_s.at[g, k], zz_r.at[g, k], (d, s, zpeer(k)))

    def layer():
        def multiply(x, which, rows, n, start=False):
            w = W[which, pl.ds(rows * NZ, NZ)].reshape(4 * 256, 768)
            term = jnp.dot(x, w, preferred_element_type=F32)
            QA.at[n][:, 0:768] = term if start else QA[n, :, 0:768] + term

        @pl.when(s == 0)
        def _():
            for q in range(2):
                for k in (1, 3, 2):
                    eb_z_in(q, k).wait_recv()
                    eb_fwd(q, k).start()
            QA[...] = jnp.zeros_like(QA)
            QR[...] = jnp.zeros_like(QR)
            SS[...] = jnp.zeros_like(SS)
            for q in range(2):
                for k in range(4):
                    eb_sib_in(q, k).wait_recv()

                def blocks(mm):
                    x = EB[q, :, :, lane(mm * 256, 256)].astype(F32)
                    return [x[:, i * 8:i * 8 + 8, :].reshape(ROWS, 256) for i in range(2)]

                def body(mm, total):
                    for half, xs in enumerate(blocks(mm)):
                        g = half * 2 + q
                        cols = lane(g * 2048 + mm * 256, 256)
                        XE.at[g, mm][...] = (xs * gains[:, cols]).astype(BF)
                        square = xs * xs
                        total = total + square[:, 0:128] + square[:, 128:256]
                    return total

                SS[...] = lax.fori_loop(0, NM, body, SS[...])
                for half, xs in enumerate(blocks(m)):
                    RX.at[half * 2 + q][...] = xs.astype(BF)
                if q == 0:
                    for n in range(3):
                        load(n, 0).wait()
                        load(n, 1).wait()

                def both(i, _):
                    g = 2 * i + q
                    for who in range(2):
                        x = jnp.concatenate([XE[g, 2 * zz + who] for zz in range(NZ)], axis=1)
                        multiply(x, who, g, 0)
                    return 0

                lax.fori_loop(0, 2, both, 0)
            for k in (2, 1, 3):
                res(k).start()
            R.at[d][...] = RX[d]

        @pl.when(s > 0)
        def _():
            def arrived(k):
                g = ypeer(k)
                hop_in(g).wait_recv()
                for j in (2, 1, 3):
                    ag_z(g, j).start()

            def columns(k):
                g = ypeer(k)
                for j in (1, 3, 2):
                    ag_z_in(g, j).wait_recv()
                return jnp.concatenate([X[g, zz] for zz in range(NZ)], axis=1)

            def both(k, start=False):
                x = columns(k)
                multiply(x, 1, ypeer(k), 1, start)
                multiply(x, 0, ypeer(k), 0, start)

            def squares_of(k):
                total = jnp.zeros((ROWS, 128), F32)
                for zz in range(NZ):
                    x = X[ypeer(k), zz].astype(F32)
                    square = x * x
                    total = total + square[:, 0:128] + square[:, 128:256]
                return total

            arrived(0)
            arrived(3)
            arrived(1)
            arrived(2)
            both(0, True)
            squares = squares_of(0)
            both(3)
            squares = squares + squares_of(3)
            both(1)
            squares = squares + squares_of(1)
            x = columns(2)
            multiply(x, 1, ypeer(2), 1)
            squares = squares + squares_of(2)
            QA.at[1][:, 768:896] = squares
            sums_out().start()
            multiply(x, 0, ypeer(2), 0)
            sums_out().wait_recv()
            SS[...] = squares + QR[:, 768:896]

        r = lax.rsqrt(jnp.sum(SS[...], axis=1, keepdims=True) * (1.0 / D) + EPS)
        cos = cosine[...]
        sin = sine[...]

        def summed(first, last):
            return QA[0, :, first:last] + QR[:, first:last]

        def rope(x):
            return (x * cos + pltpu.roll(x, 64, 1) * sin).astype(BF)

        query = jnp.concatenate(
            [rope(summed(j * HD, (j + 1) * HD) * r) for j in range(4)], axis=0)
        key = rope(summed(512, 640) * r)
        value = (summed(640, 768) * r).astype(BF)
        scores = lax.dot_general(query, key, (((1,), (1,)), ((), ())),
                                 preferred_element_type=F32) * (HD ** -0.5)
        scores = scores + MASK[...]
        highest = jnp.max(scores, axis=-1, keepdims=True)
        weights = jnp.exp(scores - highest)
        probs = (weights / jnp.sum(weights, axis=-1, keepdims=True)).astype(BF)
        mixed = jnp.dot(probs, value, preferred_element_type=F32).astype(BF)
        for j in range(4):
            C.at[d][:, j * HD:(j + 1) * HD] = mixed[j * ROWS:(j + 1) * ROWS]
        for k in (2, 1, 3):
            ctx(k).start()

        wo_load.wait()

        def project(g):
            for zz in range(NZ):
                p = jnp.dot(C[g], WO[:, zz * 512:zz * 512 + 512], preferred_element_type=F32)
                low, high = p[:, :256], p[:, 256:]
                PO.at[g, zz][...] = jnp.where(c == 0, low, high)
                PS.at[g, zz][...] = jnp.where(c == 0, high, low).astype(BF)
            part(g).start()

        def pair(g):
            part(g).wait_recv()
            for k in (2, 1, 3):
                zt = (z + k) % NZ
                ZS.at[g, k][...] = (PO[g, zt] + PR[g, zt].astype(F32)).astype(BF)
                zred(g, k).start()

        def total_of(g):
            total = PO[g, z] + PR[g, z].astype(F32) + R[g].astype(F32)
            for k in (1, 3, 2):
                zred(g, k).wait_recv()
                total = total + ZR[g, k].astype(F32)
            HP.at[g][...] = total.astype(BF)

            @pl.when(s < NX - 1)
            def _():
                hop(g).start()

        project(d)

        @pl.when(s == 0)
        def _():
            for k in (1, 3, 2):
                res_in(k).wait_recv()

        @pl.when(s > 0)
        def _():
            hop_raw().wait_recv()

        pair(d)
        for k in (1, 3):
            ctx_in(k).wait_recv()
            project(ypeer(k))
        pair(ypeer(1))
        pair(ypeer(3))
        def own_chunk(k):
            @pl.when(s == NX - 1)
            def _():
                stage_own(1, k, True)
                if k >= 1:
                    stage_first(1, k - 1)
                if k >= 2:
                    stage_second(1, k - 2)

        total_of(d)
        own_chunk(0)
        ctx_in(2).wait_recv()
        project(ypeer(2))
        total_of(ypeer(1))
        pair(ypeer(2))
        own_chunk(1)
        total_of(ypeer(3))
        own_chunk(2)
        total_of(ypeer(2))
        own_chunk(3)

        @pl.when(s < NX - 1)
        def _():
            hop_raw().start()

        @pl.when(s == 1)
        def _():
            def body(k, _):
                stage_own(0, k, True)
                return 0

            lax.fori_loop(0, 4, body, 0)

    def first_dev(k):
        return (jnp.where(c == 0, ypeer(k), d), s, jnp.where(c == 0, m, zpeer(k)))

    def second_dev(k):
        return (jnp.where(c == 0, d, ypeer(k)), s, jnp.where(c == 0, zpeer(k), m))

    def ycopy(src, dst, b, k, i, j, dev):
        return rcopy(src, dst, y_s.at[b, k, i], y_r.at[b, k, j], dev)

    def y_x(b, k, n):
        ref = Y.at[b, k, c, 0, 0]
        return ycopy(ref, ref, b, k, n, 0, (d, (s + n) % NX, m))

    def y_first(b, k, n):
        slot = (1, 3, 2)[n - 1]
        return ycopy(Y.at[b, k, c, 0, 0], Y.at[b, k, c, 0, slot], b, k, 3 + n, slot, first_dev(n))

    sets = (pl.ds(0, 1), pl.ds(1, 2), pl.ds(3, 1))

    def y_second(b, k, part_no, n):
        slot = 1 if n == 1 else 2
        return ycopy(Y.at[b, k, c, 0, sets[part_no]], Y.at[b, k, c, slot, sets[part_no]], b, k,
                     7 + part_no * 2 + (slot - 1), 1 + 3 * slot + part_no, second_dev(n))

    def y_relay(b, k, half):
        slot, n = ((1, 1), (2, 3))[half]
        two = pl.ds(2 * half, 2)
        return ycopy(Y.at[b, k, c, slot, two], Y.at[b, k, c, 3, two], b, k, 13 + half, 10 + half,
                     second_dev(n))

    forwards = ((0, 0, 1), (0, 1, 2), (0, 3, 1), (1, 0, 4), (2, 0, 4), (3, 0, 2), (3, 2, 2))

    def y_fwd(b, k, n, who):
        j, i, size = forwards[n]
        ref = Y.at[b, k, who, j, pl.ds(i, size)]
        return ycopy(ref, ref, b, k, 15 + n, 12 + n, here)

    def chunk_order(step):
        return jnp.where(step == 3, 2, jnp.where(step == 2, 3, step))

    def stage_own(b, k, source):
        if source:
            Y.at[b, k, c, 0, 0][...] = HP[(d + chunk_order(k)) % NY]
            for n in (2, 1, 3):
                y_x(b, k, n).start()
        else:
            y_x(b, k, 1).wait_recv()
        for n in (2, 1, 3):
            y_first(b, k, n).start()
        for n in (1, 3):
            y_second(b, k, 0, n).start()
        y_fwd(b, k, 0, c).start()

    def stage_first(b, k):
        y_first(b, k, 1).wait_recv()
        y_first(b, k, 3).wait_recv()
        for n in (1, 3):
            y_second(b, k, 1, n).start()
        y_fwd(b, k, 1, c).start()
        y_first(b, k, 2).wait_recv()
        for n in (1, 3):
            y_second(b, k, 2, n).start()
        y_fwd(b, k, 2, c).start()

    def stage_second(b, k):
        for part_no in (0, 1):
            y_second(b, k, part_no, 1).wait_recv()
        y_relay(b, k, 0).start()
        for part_no in (1, 2):
            y_second(b, k, part_no, 3).wait_recv()
        y_relay(b, k, 1).start()
        y_second(b, k, 2, 1).wait_recv()
        y_fwd(b, k, 3, c).start()
        y_second(b, k, 0, 3).wait_recv()
        y_fwd(b, k, 4, c).start()

    def opposite(b, k):
        for half in range(2):
            y_relay(b, k, half).wait_recv()
            y_fwd(b, k, 5 + half, c).start()

    def sibling_in(b, k):
        for n in range(7):
            y_fwd(b, k, n, 1 - c).wait_recv()

    def dots(b, cc, j):
        blocks = []
        for g in range(NY):
            row = []
            total = jnp.zeros((ROWS, 128), F32)
            for i in range(4):
                off_j = jnp.where(j == 0, 0, jnp.where(j == 1, 3, jnp.where(j == 2, 1, 2)))
                sender = (d + jnp.where(cc == 0, (0, 3, 1, 2)[i], off_j)) % NY
                k = chunk_order((g - sender + NY) % NY)
                x = Y[b, k, cc, j, i]
                row.append(x)
                wide = x.astype(F32)
                square = wide * wide
                total = total + square[:, 0:128] + square[:, 128:256]
            SQ.at[b, g][...] += total
            blocks.append(jnp.concatenate(row, axis=1))
        pieces = jnp.concatenate(blocks, axis=0)
        LT.at[b][...] += lax.dot_general(HEAD[cc, j], pieces, (((1,), (1,)), ((), ())),
                                         preferred_element_type=F32)

    def layer_sent():
        @pl.when(s == 0)
        def _():
            for q in range(2):
                for k in range(1, 4):
                    eb_z(q, k).wait_send()
                for k in range(4):
                    eb_fwd(q, k).wait_send()
            for k in range(1, 4):
                res(k).wait_send()

        @pl.when(s > 0)
        def _():
            for g in range(NY):
                for k in range(1, 4):
                    ag_z(g, k).wait_send()
            sums_out().wait_send()
            for n in range(3):
                swap(n).wait_send()

        @pl.when(s < NX - 1)
        def _():
            for g in range(NY):
                hop(g).wait_send()
            hop_raw().wait_send()

        for g in range(NY):
            for k in range(1, 4):
                zred(g, k).wait_send()
            part(g).wait_send()
        for k in range(1, 4):
            ctx(k).wait_send()

    def chunk_sent(b, k, source):
        @pl.when(s == source)
        def _():
            for j in (1, 2, 3):
                y_x(b, k, j).wait_send()

        for j in (1, 2, 3):
            y_first(b, k, j).wait_send()
        for j in (1, 3):
            for part_no in range(3):
                y_second(b, k, part_no, j).wait_send()
        for half in range(2):
            y_relay(b, k, half).wait_send()
        for j in range(7):
            y_fwd(b, k, j, c).wait_send()

    def each(count, do):
        def body(k, _):
            do(k)
            return 0

        lax.fori_loop(0, count, body, 0)

    def exit_dots(k):
        j = chunk_order(k)
        dots(0, c, j)
        dots(0, 1 - c, j)

    def gather(b):
        source = 2 * b + 1
        final = (b == 1) & (s == NX - 1)
        others = jnp.logical_not(final)

        def body(t, _):
            @pl.when((t < 4) & (s != source))
            def _():
                stage_own(b, t, False)

            @pl.when((t >= 1) & (t < 5) & ((t == 4) | others))
            def _():
                stage_first(b, t - 1)

            @pl.when((t >= 2) & (t < 6) & ((t >= 4) | others))
            def _():
                stage_second(b, t - 2)

            @pl.when((t >= 3) & ((b == 0) | (t < 6)) & others)
            def _():
                opposite(b, t - 3)

            @pl.when((b == 1) & (s == 2) & (t == 1))
            def _():
                each(4, lambda k: sibling_in(0, k))

            @pl.when((b == 1) & (s == 2) & (t >= 2) & (t < 6))
            def _():
                exit_dots(t - 2)
            return 0

        lax.fori_loop(0, 7, body, 0)

        @pl.when(final)
        def _():
            each(3, lambda k: opposite(1, k))
            each(4, lambda k: sibling_in(0, k))
            each(4, exit_dots)

    def finish(b):
        @pl.when((b == 0) & (s < 2))
        def _():
            each(4, lambda k: sibling_in(0, k))
            each(4, exit_dots)

        @pl.when(b == 1)
        def _():
            dots_order()

        softmax(b)

    def dots_order():
        b = 1
        dots(b, c, 0)
        each(3, lambda k: sibling_in(1, k))
        for n in range(3):
            y_fwd(b, 3, n, 1 - c).wait_recv()
        dots(b, 1 - c, 0)
        opposite(b, 3)
        dots(b, c, 1)
        dots(b, c, 2)
        for n in (3, 4):
            y_fwd(b, 3, n, 1 - c).wait_recv()
        dots(b, 1 - c, 1)
        dots(b, 1 - c, 2)
        dots(b, c, 3)
        for n in (5, 6):
            y_fwd(b, 3, n, 1 - c).wait_recv()
        dots(b, 1 - c, 3)

    def softmax(b):
        squares = SQ[b].reshape(NY * ROWS, 128)
        top = squares.astype(BF)
        rest = (squares - top.astype(F32)).astype(BF)
        ones = jnp.ones((16, 128), BF)
        nt = (((1,), (1,)), ((), ()))
        sums = (lax.dot_general(ones, top, nt, preferred_element_type=F32)
                + lax.dot_general(ones, rest, nt, preferred_element_type=F32))[0:1]
        r = lax.rsqrt(sums * (1.0 / D) + EPS)
        logits = LT[b] * r
        highest = jnp.max(logits, axis=0, keepdims=True)
        summed = jnp.sum(jnp.exp(logits - highest), axis=0, keepdims=True)
        vocab = HEAD.shape[2]
        first = ((d * NX + s) * NM + m) * vocab
        index = (lax.broadcasted_iota(jnp.int32, logits.shape, 0) + first).astype(F32)
        wanted = WANT[0:1, :]
        picked = jnp.sum(jnp.where(index == wanted, logits, 0.0), axis=0, keepdims=True)
        for n, value in enumerate((highest, summed, picked)):
            for half in range(2):
                STO[pl.ds(n * 4 + b * 2 + half, 1), :] = value[:, half * 128:half * 128 + 128]

    def step(t, _):
        last = s == NX - 1
        place = jnp.where(last, 1, 0)

        @pl.when(t == place)
        def _():
            layer()

        @pl.when(jnp.where(last, (t == 0) | (t == 2), (t == 1) | (t == jnp.where(s < 2, 3, 2))))
        def _():
            gather(jnp.where((t == 0) | (t == 1), 0, 1))

        @pl.when((t == 4) | (t == jnp.where(s < 2, 2, 3)))
        def _():
            @pl.when((t == 2) & (s == 0))
            def _():
                scale_head()
            finish(jnp.where(t == 4, 1, 0))
        return 0

    @pl.when(s == 0)
    def _():
        for q in range(2):
            for k in (2, 1, 3, 0):
                (eb_z(q, k) if k else eb_fwd(q, 0)).start()

    prepare()
    STO[...] = jnp.zeros_like(STO)
    SQ[...] = jnp.zeros_like(SQ)
    LT[...] = jnp.zeros_like(LT)
    lax.fori_loop(0, 5, step, 0)

    def merge(ref, count):
        parts = [ref[j] for j in range(count)]
        highest = parts[0][0:4]
        for p in parts[1:]:
            highest = jnp.maximum(highest, p[0:4])
        summed = jnp.zeros_like(highest)
        picked = jnp.zeros_like(highest)
        for p in parts:
            summed = summed + p[4:8] * jnp.exp(p[0:4] - highest)
            picked = picked + p[8:12]
        return highest, summed, picked

    def stacked(highest, summed, picked):
        return jnp.concatenate([highest, summed, picked, jnp.zeros_like(picked)], axis=0)

    pairs = [(j, k) for j in range(NX) for k in range(NY) if j or k]

    def st_yx(n):
        j, k = pairs[n]
        mine = s * NY + d
        return rcopy(SA.at[mine], SA.at[mine], st_s.at[0, n], st_r.at[0, mine],
                     (ypeer(k), (s + j) % NX, m))

    def st_yx_in(n):
        j, k = pairs[n]
        other = ((s + j) % NX) * NY + ypeer(k)
        return rcopy(SA.at[other], SA.at[other], st_s.at[0, n], st_r.at[0, other], here)

    def m_of(k):
        return (m + k) % NM

    def st_m(k):
        return rcopy(SB.at[m], SB.at[m], st_s.at[1, k], st_r.at[1, m], (d, s, m_of(k)))

    def st_m_in(k):
        mm = m_of(k)
        return rcopy(SB.at[mm], SB.at[mm], st_s.at[1, k], st_r.at[1, mm], (d, s, mm))

    SA.at[s * NY + d][...] = STO[...]
    for n in range(15):
        st_yx(n).start()
    layer_sent()
    each(4, lambda k: chunk_sent(0, k, 1))
    each(4, lambda k: chunk_sent(1, k, NX - 1))
    for n in range(15):
        st_yx_in(n).wait_recv()
    SB.at[m][...] = stacked(*merge(SA, NX * NY))
    for k in (4, 3, 5, 2, 6, 1, 7):
        st_m(k).start()
    for n in range(15):
        st_yx(n).wait_send()
    for k in (1, 7, 2, 6, 3, 5, 4):
        st_m_in(k).wait_recv()
    highest, summed, picked = merge(SB, NM)
    logprob = picked - (highest + jnp.log(summed))
    terms = []
    for e in range(2):
        rest = jnp.concatenate([logprob[2 * e:2 * e + 1], logprob[2 * e + 1:2 * e + 2]], axis=1)
        for _ in range(3):
            term = rest.astype(BF).astype(F32)
            terms.append(term)
            rest = rest - term
    row = lax.broadcasted_iota(jnp.int32, (16, 256), 0)
    stack = jnp.zeros((16, 256), F32)
    for j, term in enumerate(terms):
        stack = jnp.where(row == j, term, stack)
    stack = stack.astype(BF)
    results = []
    for i in range(2):
        got = jnp.dot(stack, TAKE[i], preferred_element_type=F32)
        results.append([got[j:j + 1] + got[j + 1:j + 2] + got[j + 2:j + 3] for j in (0, 3)])
    for e in range(2):
        first = lax.broadcasted_iota(jnp.int32, (2, 32), 0) == 0
        out.at[e][...] = jnp.where(first, results[0][e], results[1][e])
    for k in range(1, 8):
        st_m(k).wait_send()


def tables():
    row = np.arange(ROWS)
    position = (row // 8) * 4 + row % 4
    half = HD // 2
    freqs = (ROPE_BASE ** (-np.arange(half) * 2.0 / HD)).astype(np.float32)
    angles = (position.astype(np.float32)[:, None] * freqs[None, :]).astype(np.float64)
    cos, sin = np.cos(angles), np.sin(angles)
    return (np.concatenate([cos, cos], 1).astype(np.float32),
            np.concatenate([-sin, sin], 1).astype(np.float32))


def per_device(
    embeds, targets, lengths, source, attn_gain, w_query, w_key, w_value, w_out, final_gain, head
):
    vocab = head.shape[0]
    cos, sin = tables()
    vmem = pl.BlockSpec(memory_space=pltpu.VMEM)
    hbm = pl.BlockSpec(memory_space=pl.ANY)
    smem = pl.BlockSpec(memory_space=pltpu.SMEM)
    dma = pltpu.SemaphoreType.DMA
    stats = pl.pallas_call(
        kernel,
        out_shape=jax.ShapeDtypeStruct((2, 2, 32), F32),
        in_specs=[hbm, smem, smem] + [hbm] * 10,
        out_specs=vmem,
        scratch_shapes=[
            pltpu.VMEM((2, 4, D), BF),
            pltpu.VMEM((8, 32), jnp.int32),
            pltpu.VMEM((1, D), F32),
            pltpu.VMEM((1, D), F32),
            pltpu.VMEM((ROWS, HD), F32),
            pltpu.VMEM((ROWS, HD), F32),
            pltpu.VMEM((2, 16, 256, 768), BF),
            pltpu.VMEM((QW, 2048), BF),
            pltpu.VMEM((2, 4, vocab, 1024), BF),
            pltpu.VMEM((2, NM, 16, 2048), BF),
            pltpu.VMEM((NY, NM, ROWS, 256), BF),
            pltpu.VMEM((NY, NZ, ROWS, 256), BF),
            pltpu.VMEM((NY, ROWS, 256), BF),
            pltpu.VMEM((4 * ROWS, ROWS), F32),
            pltpu.VMEM((ROWS, 128), F32),
            pltpu.VMEM((2, ROWS, 896), F32),
            pltpu.VMEM((ROWS, 896), F32),
            pltpu.VMEM((NY, ROWS, 256), BF),
            pltpu.VMEM((NY, ROWS, QW), BF),
            pltpu.VMEM((NY, NZ, ROWS, 256), BF),
            pltpu.VMEM((NY, NZ, ROWS, 256), BF),
            pltpu.VMEM((NY, NZ, ROWS, 256), F32),
            pltpu.VMEM((NY, NZ, ROWS, 256), BF),
            pltpu.VMEM((NY, NZ, ROWS, 256), BF),
            pltpu.VMEM((NY, ROWS, 256), BF),
            pltpu.VMEM((2, 4, 2, 4, 4, ROWS, 256), BF),
            pltpu.VMEM((2, vocab, 256), F32),
            pltpu.VMEM((2, NY, ROWS, 128), F32),
            pltpu.VMEM((8, 256), F32),
            pltpu.VMEM((2, 256, 32), BF),
            pltpu.VMEM((16, 128), F32),
            pltpu.VMEM((NX * NY, 16, 128), F32),
            pltpu.VMEM((NM, 16, 128), F32),
            dma((20,)),
            dma((3,)), dma((3,)),
            dma, dma,
            dma((2, 8)), dma((2, 8)),
            dma((5,)), dma((5,)),
            dma((4, 8)), dma((4, 8)),
            dma((4,)), dma((4,)),
            dma((4,)), dma((4,)),
            dma((4,)), dma((4,)),
            dma((4, 4)), dma((4, 4)),
            dma((2, 4, 22)), dma((2, 4, 19)),
            dma((2, 16)), dma((2, 16)),
        ],
        compiler_params=pltpu.CompilerParams(
            collective_id=0, has_side_effects=True, vmem_limit_bytes=60 * 1024 * 1024),
        cost_estimate=pl.CostEstimate(flops=8_000_000_000, bytes_accessed=24_000_000,
                                      transcendentals=300_000),
    )(
        embeds, lengths, source, targets, attn_gain, final_gain.reshape(1, D), jnp.asarray(cos), jnp.asarray(sin),
        w_query.reshape(16, 2, 256, 512), w_key.reshape(16, 2, 256, 128),
        w_value.reshape(16, 2, 256, 128), w_out.reshape(512, 2048), head,
    )
    return (stats[0], stats[1])


def solution(mesh):
    return jax.shard_map(
        per_device,
        mesh=mesh,
        in_specs=(
            P("dp", "mp", None),
            P(),
            P(),
            P(),
            P("section", None),
            P("section", None, "mp"),
            P("section", None, "mp"),
            P("section", None, "mp"),
            P("section", "mp", "dp"),
            P(),
            P(("dp", "section", "mp"), None),
        ),
        out_specs=(P("dp", None), P("dp", None)),
        check_vma=False,
    )
```

```python
import jax
import jax.numpy as jnp
import numpy as np
from jax import lax
from jax.experimental import pallas as pl
from jax.experimental.pallas import tpu as pltpu
from jax.sharding import PartitionSpec as P

HD = 128
EPS = 1e-05
ROPE_BASE = 500000.0
NY = 4
NX = 4
NZ = 4
NM = 8
ROWS = 64
D = 8192
QW = 512
MESH = pl.DeviceIdType.MESH
BF = jnp.bfloat16
F32 = jnp.float32


def lane(start, size):
    return pl.ds(pl.multiple_of(start, 128), size)


def kernel(
    emb_in, live, source_of, targets_in, gain, fgain_in, cosine_in, sine_in, wq, wk, wv, wo, head,
    out,
    emb, targets, gains, fgain, cosine, sine, W, WO, HEAD, EB, XE, X, RX, MASK, SS, QA, QR, R, C, PS, PR, PO, ZS, ZR, HP, Y, LT, SQ, WANT, TAKE, STO, SA, SB,
    w_sem, sw_s, sw_r, qr_s, qr_r, eb_s, eb_r, hop_s, hop_r, ag_s, ag_r, res_s, res_r, ctx_s, ctx_r, ps_s, ps_r,
    zz_s, zz_r, y_s, y_r, st_s, st_r,
):
    d = lax.axis_index("dp")
    s = lax.axis_index("section")
    m = lax.axis_index("mp")
    z = m // 2
    c = m % 2
    sib = z * 2 + (1 - c)

    def ypeer(k):
        return (d + k) % NY

    def zpeer(k):
        return ((z + k) % NZ) * 2 + c

    def zother(k):
        return ((z + k) % NZ) * 2 + (1 - c)

    def rcopy(src, dst, ssem, rsem, dev):
        return pltpu.make_async_remote_copy(
            src_ref=src, dst_ref=dst, send_sem=ssem, recv_sem=rsem,
            device_id=dev, device_id_type=MESH,
        )

    here = (d, s, sib)

    barrier = pltpu.get_barrier_semaphore()
    partners = []
    for k in range(1, 4):
        partners.append((ypeer(k), s, m))
        partners.append((d, (s + k) % NX, m))
        partners.append((d, s, zpeer(k)))
        partners.append((d, s, zother(k)))
        partners.append((ypeer(k), (s + 1) % NX, m))
        partners.append((ypeer(k), (s + 3) % NX, m))
        partners.append((ypeer(k), (s + 2) % NX, m))
    partners.append(here)
    for dev in partners:
        pl.semaphore_signal(barrier, inc=1, device_id=dev, device_id_type=MESH)
    small = [
        pltpu.make_async_copy(src, dst, w_sem.at[14 + n])
        for n, (src, dst) in enumerate((
            (emb_in, emb), (gain, gains), (cosine_in, cosine), (sine_in, sine),
            (fgain_in, fgain), (targets_in, targets)))
    ]
    for copy in small:
        copy.start()
    parts = ((wq, pl.ds(0, 512)), (wk, pl.ds(512, 128)), (wv, pl.ds(640, 128)))

    def load(n, first):
        src, lanes = parts[n]
        take = 1 if first else jnp.where(s == 0, 0, c)
        return pltpu.make_async_copy(src.at[:, take], W.at[first, :, :, lanes],
                                     w_sem.at[3 * first + n])

    def swap(n):
        src, lanes = parts[n]
        return rcopy(src.at[:, 1 - c], W.at[1, :, :, lanes], sw_s.at[n], sw_r.at[n], here)

    wo_load = pltpu.make_async_copy(wo, WO, w_sem.at[12])
    for n in range(3):
        load(n, 0).start()

    @pl.when(s == 0)
    def _():
        for n in range(3):
            load(n, 1).start()

    head_load = pltpu.make_async_copy(HEAD, HEAD, w_sem.at[13])

    def row_slot(lanes):
        return (lanes // 64) * 2 + (lanes // 4) % 2, ((lanes // 8) % 8) * 4 + lanes % 4

    def wanted_rows():
        slot, position = row_slot(lax.broadcasted_iota(jnp.int32, (32, 256), 1))
        place = (position == lax.broadcasted_iota(jnp.int32, (32, 256), 0)).astype(BF)
        tokens = targets[...]
        keep = slot[0:8] == lax.broadcasted_iota(jnp.int32, (8, 256), 0)
        parts = []
        for term in (tokens // 256, tokens % 256):
            every = jnp.dot(term.astype(F32).astype(BF), place, preferred_element_type=F32)
            parts.append(jnp.sum(jnp.where(keep, every, 0.0), axis=0, keepdims=True))
        return parts[0] * 256.0 + parts[1]

    def prepare():
        wo_load.start()
        offsets = (0, 3, 1, 2)
        for cc in range(2):
            for j in range(4):
                for i in range(4):
                    g, zz = (offsets[i], offsets[j]) if cc == 0 else (offsets[j], offsets[i])
                    col = ypeer(g) * 2048 + ((z + zz) % NZ) * 512 + cc * 256
                    pltpu.make_async_copy(head.at[:, lane(col, 256)],
                                          HEAD.at[cc, j, :, i * 256:i * 256 + 256],
                                          w_sem.at[13]).start()
        shape = (4 * ROWS, ROWS)
        rq = lax.broadcasted_iota(jnp.int32, shape, 0) % ROWS
        rk = lax.broadcasted_iota(jnp.int32, shape, 1)
        slot_q, slot_k = (rq // 4) % 2, (rk // 4) % 2
        pos_q, pos_k = (rq // 8) * 4 + rq % 4, (rk // 8) * 4 + rk % 4
        live_k = jnp.where(slot_k == 0, live[2 * d], live[2 * d + 1])
        allowed = (slot_q == slot_k) & (pos_k <= pos_q) & (pos_k < live_k)
        MASK[...] = jnp.where(allowed, F32(0.0), F32(-1e30))

        @pl.when(s > 0)
        def _():
            for n in range(3):
                load(n, 0).wait()
                swap(n).wait_recv()
            for copy in small[1:2]:
                copy.wait()
            diagonal = (lax.broadcasted_iota(jnp.int32, (256, 256), 0)
                        == lax.broadcasted_iota(jnp.int32, (256, 256), 1))

            def scale(i, _):
                cols = lane((i // NZ) * 2048 + ((i % NZ) * 2 + c) * 256, 256)
                column = jnp.sum(jnp.where(diagonal, gains[:, cols], 0.0), axis=1, keepdims=True)
                for which in range(2):
                    W.at[which, i][...] = (W[which, i].astype(F32) * column).astype(BF)
                return 0

            lax.fori_loop(0, 16, scale, 0)

        @pl.when(s == 0)
        def _():
            for copy in small[1:2]:
                copy.wait()
        for copy in small[2:]:
            copy.wait()

        WANT[...] = jnp.broadcast_to(wanted_rows(), WANT.shape)
        slot, position = row_slot(lax.broadcasted_iota(jnp.int32, (256, 32), 0))
        place = lax.broadcasted_iota(jnp.int32, (256, 32), 1)
        for i in range(2):
            chosen = source_of[2 * d + i]
            TAKE.at[i][...] = ((slot == chosen) & (position == place)
                               & (place < live[chosen])).astype(F32).astype(BF)

        @pl.when(s > 0)
        def _():
            scale_head()

    def scale_head():
        head_load.wait()

        def off(n):
            return jnp.where(n == 0, 0, jnp.where(n == 1, 3, jnp.where(n == 2, 1, 2)))

        def scale(n, _):
            cc, j, i = n // 16, (n // 4) % 4, n % 4
            g = jnp.where(cc == 0, off(i), off(j))
            zz = jnp.where(cc == 0, off(j), off(i))
            col = ((d + g) % NY) * 2048 + ((z + zz) % NZ) * 512 + cc * 256
            block = HEAD.at[cc, j, :, lane(i * 256, 256)]
            block[...] = (block[...].astype(F32) * fgain[:, lane(col, 256)]).astype(BF)
            return 0

        lax.fori_loop(0, 32, scale, 0)

    small[0].wait()

    @pl.when(s == 0)
    def _():
        rows = jnp.concatenate([emb[0], emb[1]], axis=0).astype(F32)
        for q in range(2):
            EB.at[q, m][...] = jnp.concatenate(
                [rows[:, q * 2048:q * 2048 + 2048], rows[:, q * 2048 + 4096:q * 2048 + 6144]],
                axis=0).astype(BF)

    pl.semaphore_wait(barrier, len(partners))

    @pl.when(s > 0)
    def _():
        for n in range(3):
            swap(n).start()

    def eb_z(q, k):
        return rcopy(EB.at[q, m], EB.at[q, m], eb_s.at[q, k], eb_r.at[q, m], (d, s, zpeer(k)))

    def eb_z_in(q, k):
        mk = zpeer(k)
        return rcopy(EB.at[q, mk], EB.at[q, mk], eb_s.at[q, k], eb_r.at[q, mk], here)

    def eb_fwd(q, k):
        mk = zpeer(k)
        return rcopy(EB.at[q, mk], EB.at[q, mk], eb_s.at[q, 4 + k], eb_r.at[q, mk], here)

    def eb_sib_in(q, k):
        mk = zother(k)
        return rcopy(EB.at[q, mk], EB.at[q, mk], eb_s.at[q, 4 + k], eb_r.at[q, mk], here)

    def hop(g):
        return rcopy(HP.at[g], X.at[d, z], hop_s.at[g], hop_r.at[d], (g, (s + 1) % NX, m))

    def hop_in(g):
        return rcopy(HP.at[g], X.at[g, z], hop_s.at[g], hop_r.at[g], here)

    def hop_raw():
        return rcopy(HP, R, hop_s.at[4], hop_r.at[4], (d, (s + 1) % NX, m))

    def ag_z(g, k):
        return rcopy(X.at[g, z], X.at[g, z], ag_s.at[g, k], ag_r.at[g, z], (d, s, zpeer(k)))

    def ag_z_in(g, k):
        zk = (z + k) % NZ
        return rcopy(X.at[g, zk], X.at[g, zk], ag_s.at[g, k], ag_r.at[g, zk], here)

    def sums_out():
        return rcopy(QA.at[1], QR, qr_s, qr_r, here)

    def res(k):
        g = ypeer(k)
        return rcopy(RX.at[g], R.at[d], res_s.at[k], res_r.at[d], (g, s, m))

    def res_in(k):
        g = ypeer(k)
        return rcopy(RX.at[g], R.at[g], res_s.at[k], res_r.at[g], here)

    def ctx(k):
        return rcopy(C.at[d], C.at[d], ctx_s.at[k], ctx_r.at[d], (ypeer(k), s, m))

    def ctx_in(k):
        g = ypeer(k)
        return rcopy(C.at[g], C.at[g], ctx_s.at[k], ctx_r.at[g], here)

    def part(g):
        return rcopy(PS.at[g], PR.at[g], ps_s.at[g], ps_r.at[g], here)

    def zred(g, k):
        return rcopy(ZS.at[g, k], ZR.at[g, k], zz_s.at[g, k], zz_r.at[g, k], (d, s, zpeer(k)))

    def layer():
        def multiply(x, which, rows, n, start=False):
            w = W[which, pl.ds(rows * NZ, NZ)].reshape(4 * 256, 768)
            term = jnp.dot(x, w, preferred_element_type=F32)
            QA.at[n][:, 0:768] = term if start else QA[n, :, 0:768] + term

        @pl.when(s == 0)
        def _():
            for q in range(2):
                for k in (1, 3, 2):
                    eb_z_in(q, k).wait_recv()
                    eb_fwd(q, k).start()
            QA[...] = jnp.zeros_like(QA)
            QR[...] = jnp.zeros_like(QR)
            SS[...] = jnp.zeros_like(SS)
            for q in range(2):
                for k in range(4):
                    eb_sib_in(q, k).wait_recv()

                def blocks(mm):
                    x = EB[q, :, :, lane(mm * 256, 256)].astype(F32)
                    return [x[:, i * 8:i * 8 + 8, :].reshape(ROWS, 256) for i in range(2)]

                def body(mm, total):
                    for half, xs in enumerate(blocks(mm)):
                        g = half * 2 + q
                        cols = lane(g * 2048 + mm * 256, 256)
                        XE.at[g, mm][...] = (xs * gains[:, cols]).astype(BF)
                        square = xs * xs
                        total = total + square[:, 0:128] + square[:, 128:256]
                    return total

                SS[...] = lax.fori_loop(0, NM, body, SS[...])
                for half, xs in enumerate(blocks(m)):
                    RX.at[half * 2 + q][...] = xs.astype(BF)
                if q == 0:
                    for n in range(3):
                        load(n, 0).wait()
                        load(n, 1).wait()

                def both(i, _):
                    g = 2 * i + q
                    for who in range(2):
                        x = jnp.concatenate([XE[g, 2 * zz + who] for zz in range(NZ)], axis=1)
                        multiply(x, who, g, 0)
                    return 0

                lax.fori_loop(0, 2, both, 0)
            for k in (2, 1, 3):
                res(k).start()
            R.at[d][...] = RX[d]

        @pl.when(s > 0)
        def _():
            def arrived(k):
                g = ypeer(k)
                hop_in(g).wait_recv()
                for j in (2, 1, 3):
                    ag_z(g, j).start()

            def columns(k):
                g = ypeer(k)
                for j in (1, 3, 2):
                    ag_z_in(g, j).wait_recv()
                return jnp.concatenate([X[g, zz] for zz in range(NZ)], axis=1)

            def both(k, start=False):
                x = columns(k)
                multiply(x, 1, ypeer(k), 1, start)
                multiply(x, 0, ypeer(k), 0, start)

            def squares_of(k):
                total = jnp.zeros((ROWS, 128), F32)
                for zz in range(NZ):
                    x = X[ypeer(k), zz].astype(F32)
                    square = x * x
                    total = total + square[:, 0:128] + square[:, 128:256]
                return total

            arrived(0)
            arrived(3)
            arrived(1)
            arrived(2)
            both(0, True)
            squares = squares_of(0)
            both(3)
            squares = squares + squares_of(3)
            both(1)
            squares = squares + squares_of(1)
            x = columns(2)
            multiply(x, 1, ypeer(2), 1)
            squares = squares + squares_of(2)
            QA.at[1][:, 768:896] = squares
            sums_out().start()
            multiply(x, 0, ypeer(2), 0)
            sums_out().wait_recv()
            SS[...] = squares + QR[:, 768:896]

        r = lax.rsqrt(jnp.sum(SS[...], axis=1, keepdims=True) * (1.0 / D) + EPS)
        cos = cosine[...]
        sin = sine[...]

        def summed(first, last):
            return QA[0, :, first:last] + QR[:, first:last]

        def rope(x):
            return (x * cos + pltpu.roll(x, 64, 1) * sin).astype(BF)

        query = jnp.concatenate(
            [rope(summed(j * HD, (j + 1) * HD) * r) for j in range(4)], axis=0)
        key = rope(summed(512, 640) * r)
        value = (summed(640, 768) * r).astype(BF)
        scores = lax.dot_general(query, key, (((1,), (1,)), ((), ())),
                                 preferred_element_type=F32) * (HD ** -0.5)
        scores = scores + MASK[...]
        highest = jnp.max(scores, axis=-1, keepdims=True)
        weights = jnp.exp(scores - highest)
        probs = (weights / jnp.sum(weights, axis=-1, keepdims=True)).astype(BF)
        mixed = jnp.dot(probs, value, preferred_element_type=F32).astype(BF)
        for j in range(4):
            C.at[d][:, j * HD:(j + 1) * HD] = mixed[j * ROWS:(j + 1) * ROWS]
        for k in (2, 1, 3):
            ctx(k).start()

        wo_load.wait()

        def project(g):
            for zz in range(NZ):
                p = jnp.dot(C[g], WO[:, zz * 512:zz * 512 + 512], preferred_element_type=F32)
                low, high = p[:, :256], p[:, 256:]
                PO.at[g, zz][...] = jnp.where(c == 0, low, high)
                PS.at[g, zz][...] = jnp.where(c == 0, high, low).astype(BF)
            part(g).start()

        def pair(g):
            part(g).wait_recv()
            for k in (2, 1, 3):
                zt = (z + k) % NZ
                ZS.at[g, k][...] = (PO[g, zt] + PR[g, zt].astype(F32)).astype(BF)
                zred(g, k).start()

        def total_of(g):
            total = PO[g, z] + PR[g, z].astype(F32) + R[g].astype(F32)
            for k in (1, 3, 2):
                zred(g, k).wait_recv()
                total = total + ZR[g, k].astype(F32)
            HP.at[g][...] = total.astype(BF)

            @pl.when(s < NX - 1)
            def _():
                hop(g).start()

        project(d)

        @pl.when(s == 0)
        def _():
            for k in (1, 3, 2):
                res_in(k).wait_recv()

        @pl.when(s > 0)
        def _():
            hop_raw().wait_recv()

        pair(d)
        for k in (1, 3):
            ctx_in(k).wait_recv()
            project(ypeer(k))
        pair(ypeer(1))
        pair(ypeer(3))
        def in_last(do):
            @pl.when(s == NX - 1)
            def _():
                do()

        total_of(d)
        in_last(lambda: own_x(1, 0))
        ctx_in(2).wait_recv()
        project(ypeer(2))
        total_of(ypeer(1))
        in_last(lambda: own_x(1, 1))
        pair(ypeer(2))

        def first_two():
            spread(1, 0)
            spread(1, 1)

        in_last(first_two)
        total_of(ypeer(3))

        def third():
            own_x(1, 2)
            spread(1, 2)

        in_last(third)
        total_of(ypeer(2))

        def rest():
            own_x(1, 3)
            spread(1, 3)
            for k in range(3):
                stage_first(1, k)
            for k in range(2):
                stage_second(1, k)

        in_last(rest)

        @pl.when(s < NX - 1)
        def _():
            hop_raw().start()

        @pl.when(s == 1)
        def _():
            def body(k, _):
                own_x(0, k)
                spread(0, k)
                return 0

            lax.fori_loop(0, 4, body, 0)

    def first_dev(k):
        return (jnp.where(c == 0, ypeer(k), d), s, jnp.where(c == 0, m, zpeer(k)))

    def second_dev(k):
        return (jnp.where(c == 0, d, ypeer(k)), s, jnp.where(c == 0, zpeer(k), m))

    def ycopy(src, dst, b, k, i, j, dev):
        return rcopy(src, dst, y_s.at[b, k, i], y_r.at[b, k, j], dev)

    def y_x(b, k, n):
        ref = Y.at[b, k, c, 0, 0]
        return ycopy(ref, ref, b, k, n, 0, (d, (s + n) % NX, m))

    def y_first(b, k, n):
        slot = (1, 3, 2)[n - 1]
        return ycopy(Y.at[b, k, c, 0, 0], Y.at[b, k, c, 0, slot], b, k, 3 + n, slot, first_dev(n))

    sets = (pl.ds(0, 1), pl.ds(1, 2), pl.ds(3, 1))

    def y_second(b, k, part_no, n):
        slot = 1 if n == 1 else 2
        return ycopy(Y.at[b, k, c, 0, sets[part_no]], Y.at[b, k, c, slot, sets[part_no]], b, k,
                     7 + part_no * 2 + (slot - 1), 1 + 3 * slot + part_no, second_dev(n))

    def y_relay(b, k, half):
        slot, n = ((1, 1), (2, 3))[half]
        two = pl.ds(2 * half, 2)
        return ycopy(Y.at[b, k, c, slot, two], Y.at[b, k, c, 3, two], b, k, 13 + half, 10 + half,
                     second_dev(n))

    forwards = ((0, 0, 1), (0, 1, 2), (0, 3, 1), (1, 0, 4), (2, 0, 4), (3, 0, 2), (3, 2, 2))

    def y_fwd(b, k, n, who):
        j, i, size = forwards[n]
        ref = Y.at[b, k, who, j, pl.ds(i, size)]
        return ycopy(ref, ref, b, k, 15 + n, 12 + n, here)

    def chunk_order(step):
        return jnp.where(step == 3, 2, jnp.where(step == 2, 3, step))

    def own_x(b, k):
        Y.at[b, k, c, 0, 0][...] = HP[(d + chunk_order(k)) % NY]
        for n in (2, 1, 3):
            y_x(b, k, n).start()

    def spread(b, k):
        for n in (2, 1, 3):
            y_first(b, k, n).start()
        for n in (1, 3):
            y_second(b, k, 0, n).start()
        y_fwd(b, k, 0, c).start()

    def stage_first(b, k):
        y_first(b, k, 1).wait_recv()
        y_first(b, k, 3).wait_recv()
        for n in (1, 3):
            y_second(b, k, 1, n).start()
        y_fwd(b, k, 1, c).start()
        y_first(b, k, 2).wait_recv()
        for n in (1, 3):
            y_second(b, k, 2, n).start()
        y_fwd(b, k, 2, c).start()

    def stage_second(b, k):
        for part_no in (0, 1):
            y_second(b, k, part_no, 1).wait_recv()
        y_relay(b, k, 0).start()
        for part_no in (1, 2):
            y_second(b, k, part_no, 3).wait_recv()
        y_relay(b, k, 1).start()
        y_second(b, k, 2, 1).wait_recv()
        y_fwd(b, k, 3, c).start()
        y_second(b, k, 0, 3).wait_recv()
        y_fwd(b, k, 4, c).start()

    def opposite(b, k):
        for half in range(2):
            y_relay(b, k, half).wait_recv()
            y_fwd(b, k, 5 + half, c).start()

    def sibling_in(b, k):
        for n in range(7):
            y_fwd(b, k, n, 1 - c).wait_recv()

    def dots(b, cc, j):
        blocks = []
        for g in range(NY):
            row = []
            total = jnp.zeros((ROWS, 128), F32)
            for i in range(4):
                off_j = jnp.where(j == 0, 0, jnp.where(j == 1, 3, jnp.where(j == 2, 1, 2)))
                sender = (d + jnp.where(cc == 0, (0, 3, 1, 2)[i], off_j)) % NY
                k = chunk_order((g - sender + NY) % NY)
                x = Y[b, k, cc, j, i]
                row.append(x)
                wide = x.astype(F32)
                square = wide * wide
                total = total + square[:, 0:128] + square[:, 128:256]
            SQ.at[b, g][...] += total
            blocks.append(jnp.concatenate(row, axis=1))
        pieces = jnp.concatenate(blocks, axis=0)
        LT.at[b][...] += lax.dot_general(HEAD[cc, j], pieces, (((1,), (1,)), ((), ())),
                                         preferred_element_type=F32)

    def layer_sent():
        @pl.when(s == 0)
        def _():
            for q in range(2):
                for k in range(1, 4):
                    eb_z(q, k).wait_send()
                for k in range(4):
                    eb_fwd(q, k).wait_send()
            for k in range(1, 4):
                res(k).wait_send()

        @pl.when(s > 0)
        def _():
            for g in range(NY):
                for k in range(1, 4):
                    ag_z(g, k).wait_send()
            sums_out().wait_send()
            for n in range(3):
                swap(n).wait_send()

        @pl.when(s < NX - 1)
        def _():
            for g in range(NY):
                hop(g).wait_send()
            hop_raw().wait_send()

        for g in range(NY):
            for k in range(1, 4):
                zred(g, k).wait_send()
            part(g).wait_send()
        for k in range(1, 4):
            ctx(k).wait_send()

    def chunk_sent(b, k, source):
        @pl.when(s == source)
        def _():
            for j in (1, 2, 3):
                y_x(b, k, j).wait_send()

        for j in (1, 2, 3):
            y_first(b, k, j).wait_send()
        for j in (1, 3):
            for part_no in range(3):
                y_second(b, k, part_no, j).wait_send()
        for half in range(2):
            y_relay(b, k, half).wait_send()
        for j in range(7):
            y_fwd(b, k, j, c).wait_send()

    def each(count, do):
        def body(k, _):
            do(k)
            return 0

        lax.fori_loop(0, count, body, 0)

    def exit_dots(k):
        j = chunk_order(k)
        dots(0, c, j)
        dots(0, 1 - c, j)

    def gather(b):
        source = 2 * b + 1
        final = (b == 1) & (s == NX - 1)
        others = jnp.logical_not(final)

        def body(t, _):
            @pl.when((t < 4) & (s != source))
            def _():
                y_x(b, t, 1).wait_recv()
                spread(b, t)

            @pl.when((t >= 1) & (t < 5) & ((t == 4) | others))
            def _():
                stage_first(b, t - 1)

            @pl.when((t >= 2) & (t < 6) & ((t >= 4) | others))
            def _():
                stage_second(b, t - 2)

            @pl.when((t >= 3) & ((b == 0) | (t < 6)) & others)
            def _():
                opposite(b, t - 3)

            @pl.when((b == 1) & (s == 2) & (t == 1))
            def _():
                each(4, lambda k: sibling_in(0, k))

            @pl.when((b == 1) & (s == 2) & (t >= 2) & (t < 6))
            def _():
                exit_dots(t - 2)
            return 0

        lax.fori_loop(0, 7, body, 0)

        @pl.when(final)
        def _():
            each(3, lambda k: opposite(1, k))
            each(4, lambda k: sibling_in(0, k))
            each(4, exit_dots)

    def finish(b):
        @pl.when((b == 0) & (s < 2))
        def _():
            each(4, lambda k: sibling_in(0, k))
            each(4, exit_dots)

        @pl.when(b == 1)
        def _():
            dots_order()

        softmax(b)

    def dots_order():
        b = 1
        dots(b, c, 0)
        each(3, lambda k: sibling_in(1, k))
        for n in range(3):
            y_fwd(b, 3, n, 1 - c).wait_recv()
        dots(b, 1 - c, 0)
        opposite(b, 3)
        dots(b, c, 1)
        dots(b, c, 2)
        for n in (3, 4):
            y_fwd(b, 3, n, 1 - c).wait_recv()
        dots(b, 1 - c, 1)
        dots(b, 1 - c, 2)
        dots(b, c, 3)
        for n in (5, 6):
            y_fwd(b, 3, n, 1 - c).wait_recv()
        dots(b, 1 - c, 3)

    def softmax(b):
        squares = SQ[b].reshape(NY * ROWS, 128)
        top = squares.astype(BF)
        rest = (squares - top.astype(F32)).astype(BF)
        ones = jnp.ones((16, 128), BF)
        nt = (((1,), (1,)), ((), ()))
        sums = (lax.dot_general(ones, top, nt, preferred_element_type=F32)
                + lax.dot_general(ones, rest, nt, preferred_element_type=F32))[0:1]
        r = lax.rsqrt(sums * (1.0 / D) + EPS)
        logits = LT[b] * r
        highest = jnp.max(logits, axis=0, keepdims=True)
        summed = jnp.sum(jnp.exp(logits - highest), axis=0, keepdims=True)
        vocab = HEAD.shape[2]
        first = ((d * NX + s) * NM + m) * vocab
        index = (lax.broadcasted_iota(jnp.int32, logits.shape, 0) + first).astype(F32)
        wanted = WANT[0:1, :]
        picked = jnp.sum(jnp.where(index == wanted, logits, 0.0), axis=0, keepdims=True)
        for n, value in enumerate((highest, summed, picked)):
            for half in range(2):
                STO[pl.ds(n * 4 + b * 2 + half, 1), :] = value[:, half * 128:half * 128 + 128]

    def step(t, _):
        last = s == NX - 1
        place = jnp.where(last, 1, 0)

        @pl.when(t == place)
        def _():
            layer()

        @pl.when(jnp.where(last, (t == 0) | (t == 2), (t == 1) | (t == jnp.where(s < 2, 3, 2))))
        def _():
            gather(jnp.where((t == 0) | (t == 1), 0, 1))

        @pl.when((t == 4) | (t == jnp.where(s < 2, 2, 3)))
        def _():
            @pl.when((t == 2) & (s == 0))
            def _():
                scale_head()
            finish(jnp.where(t == 4, 1, 0))
        return 0

    @pl.when(s == 0)
    def _():
        for q in range(2):
            for k in (2, 1, 3, 0):
                (eb_z(q, k) if k else eb_fwd(q, 0)).start()

    prepare()
    STO[...] = jnp.zeros_like(STO)
    SQ[...] = jnp.zeros_like(SQ)
    LT[...] = jnp.zeros_like(LT)
    lax.fori_loop(0, 5, step, 0)

    def merge(ref, count):
        parts = [ref[j] for j in range(count)]
        highest = parts[0][0:4]
        for p in parts[1:]:
            highest = jnp.maximum(highest, p[0:4])
        summed = jnp.zeros_like(highest)
        picked = jnp.zeros_like(highest)
        for p in parts:
            summed = summed + p[4:8] * jnp.exp(p[0:4] - highest)
            picked = picked + p[8:12]
        return highest, summed, picked

    def stacked(highest, summed, picked):
        return jnp.concatenate([highest, summed, picked, jnp.zeros_like(picked)], axis=0)

    pairs = [(j, k) for j in range(NX) for k in range(NY) if j or k]

    def st_yx(n):
        j, k = pairs[n]
        mine = s * NY + d
        return rcopy(SA.at[mine], SA.at[mine], st_s.at[0, n], st_r.at[0, mine],
                     (ypeer(k), (s + j) % NX, m))

    def st_yx_in(n):
        j, k = pairs[n]
        other = ((s + j) % NX) * NY + ypeer(k)
        return rcopy(SA.at[other], SA.at[other], st_s.at[0, n], st_r.at[0, other], here)

    def m_of(k):
        return (m + k) % NM

    def st_m(k):
        return rcopy(SB.at[m], SB.at[m], st_s.at[1, k], st_r.at[1, m], (d, s, m_of(k)))

    def st_m_in(k):
        mm = m_of(k)
        return rcopy(SB.at[mm], SB.at[mm], st_s.at[1, k], st_r.at[1, mm], (d, s, mm))

    SA.at[s * NY + d][...] = STO[...]
    for n in range(15):
        st_yx(n).start()
    layer_sent()
    each(4, lambda k: chunk_sent(0, k, 1))
    each(4, lambda k: chunk_sent(1, k, NX - 1))
    for n in range(15):
        st_yx_in(n).wait_recv()
    SB.at[m][...] = stacked(*merge(SA, NX * NY))
    for k in (4, 3, 5, 2, 6, 1, 7):
        st_m(k).start()
    for n in range(15):
        st_yx(n).wait_send()
    for k in (1, 7, 2, 6, 3, 5, 4):
        st_m_in(k).wait_recv()
    highest, summed, picked = merge(SB, NM)
    logprob = picked - (highest + jnp.log(summed))
    terms = []
    for e in range(2):
        rest = jnp.concatenate([logprob[2 * e:2 * e + 1], logprob[2 * e + 1:2 * e + 2]], axis=1)
        for _ in range(3):
            term = rest.astype(BF).astype(F32)
            terms.append(term)
            rest = rest - term
    row = lax.broadcasted_iota(jnp.int32, (16, 256), 0)
    stack = jnp.zeros((16, 256), F32)
    for j, term in enumerate(terms):
        stack = jnp.where(row == j, term, stack)
    stack = stack.astype(BF)
    results = []
    for i in range(2):
        got = jnp.dot(stack, TAKE[i], preferred_element_type=F32)
        results.append([got[j:j + 1] + got[j + 1:j + 2] + got[j + 2:j + 3] for j in (0, 3)])
    for e in range(2):
        first = lax.broadcasted_iota(jnp.int32, (2, 32), 0) == 0
        out.at[e][...] = jnp.where(first, results[0][e], results[1][e])
    for k in range(1, 8):
        st_m(k).wait_send()


def tables():
    row = np.arange(ROWS)
    position = (row // 8) * 4 + row % 4
    half = HD // 2
    freqs = (ROPE_BASE ** (-np.arange(half) * 2.0 / HD)).astype(np.float32)
    angles = (position.astype(np.float32)[:, None] * freqs[None, :]).astype(np.float64)
    cos, sin = np.cos(angles), np.sin(angles)
    return (np.concatenate([cos, cos], 1).astype(np.float32),
            np.concatenate([-sin, sin], 1).astype(np.float32))


def per_device(
    embeds, targets, lengths, source, attn_gain, w_query, w_key, w_value, w_out, final_gain, head
):
    vocab = head.shape[0]
    cos, sin = tables()
    vmem = pl.BlockSpec(memory_space=pltpu.VMEM)
    hbm = pl.BlockSpec(memory_space=pl.ANY)
    smem = pl.BlockSpec(memory_space=pltpu.SMEM)
    dma = pltpu.SemaphoreType.DMA
    stats = pl.pallas_call(
        kernel,
        out_shape=jax.ShapeDtypeStruct((2, 2, 32), F32),
        in_specs=[hbm, smem, smem] + [hbm] * 10,
        out_specs=vmem,
        scratch_shapes=[
            pltpu.VMEM((2, 4, D), BF),
            pltpu.VMEM((8, 32), jnp.int32),
            pltpu.VMEM((1, D), F32),
            pltpu.VMEM((1, D), F32),
            pltpu.VMEM((ROWS, HD), F32),
            pltpu.VMEM((ROWS, HD), F32),
            pltpu.VMEM((2, 16, 256, 768), BF),
            pltpu.VMEM((QW, 2048), BF),
            pltpu.VMEM((2, 4, vocab, 1024), BF),
            pltpu.VMEM((2, NM, 16, 2048), BF),
            pltpu.VMEM((NY, NM, ROWS, 256), BF),
            pltpu.VMEM((NY, NZ, ROWS, 256), BF),
            pltpu.VMEM((NY, ROWS, 256), BF),
            pltpu.VMEM((4 * ROWS, ROWS), F32),
            pltpu.VMEM((ROWS, 128), F32),
            pltpu.VMEM((2, ROWS, 896), F32),
            pltpu.VMEM((ROWS, 896), F32),
            pltpu.VMEM((NY, ROWS, 256), BF),
            pltpu.VMEM((NY, ROWS, QW), BF),
            pltpu.VMEM((NY, NZ, ROWS, 256), BF),
            pltpu.VMEM((NY, NZ, ROWS, 256), BF),
            pltpu.VMEM((NY, NZ, ROWS, 256), F32),
            pltpu.VMEM((NY, NZ, ROWS, 256), BF),
            pltpu.VMEM((NY, NZ, ROWS, 256), BF),
            pltpu.VMEM((NY, ROWS, 256), BF),
            pltpu.VMEM((2, 4, 2, 4, 4, ROWS, 256), BF),
            pltpu.VMEM((2, vocab, 256), F32),
            pltpu.VMEM((2, NY, ROWS, 128), F32),
            pltpu.VMEM((8, 256), F32),
            pltpu.VMEM((2, 256, 32), BF),
            pltpu.VMEM((16, 128), F32),
            pltpu.VMEM((NX * NY, 16, 128), F32),
            pltpu.VMEM((NM, 16, 128), F32),
            dma((20,)),
            dma((3,)), dma((3,)),
            dma, dma,
            dma((2, 8)), dma((2, 8)),
            dma((5,)), dma((5,)),
            dma((4, 8)), dma((4, 8)),
            dma((4,)), dma((4,)),
            dma((4,)), dma((4,)),
            dma((4,)), dma((4,)),
            dma((4, 4)), dma((4, 4)),
            dma((2, 4, 22)), dma((2, 4, 19)),
            dma((2, 16)), dma((2, 16)),
        ],
        compiler_params=pltpu.CompilerParams(
            collective_id=0, has_side_effects=True, vmem_limit_bytes=60 * 1024 * 1024),
        cost_estimate=pl.CostEstimate(flops=8_000_000_000, bytes_accessed=24_000_000,
                                      transcendentals=300_000),
    )(
        embeds, lengths, source, targets, attn_gain, final_gain.reshape(1, D), jnp.asarray(cos), jnp.asarray(sin),
        w_query.reshape(16, 2, 256, 512), w_key.reshape(16, 2, 256, 128),
        w_value.reshape(16, 2, 256, 128), w_out.reshape(512, 2048), head,
    )
    return (stats[0], stats[1])


def solution(mesh):
    return jax.shard_map(
        per_device,
        mesh=mesh,
        in_specs=(
            P("dp", "mp", None),
            P(),
            P(),
            P(),
            P("section", None),
            P("section", None, "mp"),
            P("section", None, "mp"),
            P("section", None, "mp"),
            P("section", "mp", "dp"),
            P(),
            P(("dp", "section", "mp"), None),
        ),
        out_specs=(P("dp", None), P("dp", None)),
        check_vma=False,
    )
```

```python
import jax
import jax.numpy as jnp
import numpy as np
from jax import lax
from jax.experimental import pallas as pl
from jax.experimental.pallas import tpu as pltpu
from jax.sharding import PartitionSpec as P

HD = 128
EPS = 1e-05
ROPE_BASE = 500000.0
NY = 4
NX = 4
NZ = 4
NM = 8
ROWS = 64
D = 8192
QW = 512
MESH = pl.DeviceIdType.MESH
BF = jnp.bfloat16
F32 = jnp.float32


def lane(start, size):
    return pl.ds(pl.multiple_of(start, 128), size)


def kernel(
    emb_in, live, source_of, targets_in, gain, fgain_in, cosine_in, sine_in, wq, wk, wv, wo, head,
    out,
    emb, targets, gains, fgain, cosine, sine, W, WO, HEAD, EB, XE, X, RX, MASK, SS, QA, QR, R, C, PS, PR, PO, ZS, ZR, HP, Y, LT, SQ, WANT, TAKE, STO, SA, SB,
    w_sem, sw_s, sw_r, qr_s, qr_r, eb_s, eb_r, hop_s, hop_r, ag_s, ag_r, res_s, res_r, ctx_s, ctx_r, ps_s, ps_r,
    zz_s, zz_r, y_s, y_r, st_s, st_r,
):
    d = lax.axis_index("dp")
    s = lax.axis_index("section")
    m = lax.axis_index("mp")
    z = m // 2
    c = m % 2
    sib = z * 2 + (1 - c)

    def ypeer(k):
        return (d + k) % NY

    def zpeer(k):
        return ((z + k) % NZ) * 2 + c

    def zother(k):
        return ((z + k) % NZ) * 2 + (1 - c)

    def rcopy(src, dst, ssem, rsem, dev):
        return pltpu.make_async_remote_copy(
            src_ref=src, dst_ref=dst, send_sem=ssem, recv_sem=rsem,
            device_id=dev, device_id_type=MESH,
        )

    here = (d, s, sib)

    barrier = pltpu.get_barrier_semaphore()
    partners = []
    for k in range(1, 4):
        partners.append((ypeer(k), s, m))
        partners.append((d, (s + k) % NX, m))
        partners.append((d, s, zpeer(k)))
        partners.append((d, s, zother(k)))
        partners.append((ypeer(k), (s + 1) % NX, m))
        partners.append((ypeer(k), (s + 3) % NX, m))
        partners.append((ypeer(k), (s + 2) % NX, m))
    partners.append(here)
    for dev in partners:
        pl.semaphore_signal(barrier, inc=1, device_id=dev, device_id_type=MESH)
    small = [
        pltpu.make_async_copy(src, dst, w_sem.at[14 + n])
        for n, (src, dst) in enumerate((
            (emb_in, emb), (gain, gains), (cosine_in, cosine), (sine_in, sine),
            (fgain_in, fgain), (targets_in, targets)))
    ]
    for copy in small:
        copy.start()
    parts = ((wq, pl.ds(0, 512)), (wk, pl.ds(512, 128)), (wv, pl.ds(640, 128)))

    def load(n, first):
        src, lanes = parts[n]
        take = 1 if first else jnp.where(s == 0, 0, c)
        return pltpu.make_async_copy(src.at[:, take], W.at[first, :, :, lanes],
                                     w_sem.at[3 * first + n])

    def swap(n):
        src, lanes = parts[n]
        return rcopy(src.at[:, 1 - c], W.at[1, :, :, lanes], sw_s.at[n], sw_r.at[n], here)

    wo_load = pltpu.make_async_copy(wo, WO, w_sem.at[12])
    for n in range(3):
        load(n, 0).start()

    @pl.when(s == 0)
    def _():
        for n in range(3):
            load(n, 1).start()

    head_load = pltpu.make_async_copy(HEAD, HEAD, w_sem.at[13])

    def row_slot(lanes):
        return (lanes // 64) * 2 + (lanes // 4) % 2, ((lanes // 8) % 8) * 4 + lanes % 4

    def wanted_rows():
        slot, position = row_slot(lax.broadcasted_iota(jnp.int32, (32, 256), 1))
        place = (position == lax.broadcasted_iota(jnp.int32, (32, 256), 0)).astype(BF)
        tokens = targets[...]
        keep = slot[0:8] == lax.broadcasted_iota(jnp.int32, (8, 256), 0)
        parts = []
        for term in (tokens // 256, tokens % 256):
            every = jnp.dot(term.astype(F32).astype(BF), place, preferred_element_type=F32)
            parts.append(jnp.sum(jnp.where(keep, every, 0.0), axis=0, keepdims=True))
        return parts[0] * 256.0 + parts[1]

    def prepare():
        wo_load.start()
        offsets = (0, 3, 1, 2)
        for cc in range(2):
            for j in range(4):
                for i in range(4):
                    g, zz = (offsets[i], offsets[j]) if cc == 0 else (offsets[j], offsets[i])
                    col = ypeer(g) * 2048 + ((z + zz) % NZ) * 512 + cc * 256
                    pltpu.make_async_copy(head.at[:, lane(col, 256)],
                                          HEAD.at[cc, j, :, i * 256:i * 256 + 256],
                                          w_sem.at[13]).start()
        shape = (4 * ROWS, ROWS)
        rq = lax.broadcasted_iota(jnp.int32, shape, 0) % ROWS
        rk = lax.broadcasted_iota(jnp.int32, shape, 1)
        slot_q, slot_k = (rq // 4) % 2, (rk // 4) % 2
        pos_q, pos_k = (rq // 8) * 4 + rq % 4, (rk // 8) * 4 + rk % 4
        live_k = jnp.where(slot_k == 0, live[2 * d], live[2 * d + 1])
        allowed = (slot_q == slot_k) & (pos_k <= pos_q) & (pos_k < live_k)
        MASK[...] = jnp.where(allowed, F32(0.0), F32(-1e30))

        @pl.when(s > 0)
        def _():
            for n in range(3):
                load(n, 0).wait()
                swap(n).wait_recv()
            for copy in small[1:2]:
                copy.wait()
            diagonal = (lax.broadcasted_iota(jnp.int32, (256, 256), 0)
                        == lax.broadcasted_iota(jnp.int32, (256, 256), 1))

            def scale(i, _):
                cols = lane((i // NZ) * 2048 + ((i % NZ) * 2 + c) * 256, 256)
                column = jnp.sum(jnp.where(diagonal, gains[:, cols], 0.0), axis=1, keepdims=True)
                for which in range(2):
                    W.at[which, i][...] = (W[which, i].astype(F32) * column).astype(BF)
                return 0

            lax.fori_loop(0, 16, scale, 0)

        @pl.when(s == 0)
        def _():
            for copy in small[1:2]:
                copy.wait()
        for copy in small[2:]:
            copy.wait()

        WANT[...] = jnp.broadcast_to(wanted_rows(), WANT.shape)
        slot, position = row_slot(lax.broadcasted_iota(jnp.int32, (256, 32), 0))
        place = lax.broadcasted_iota(jnp.int32, (256, 32), 1)
        for i in range(2):
            chosen = source_of[2 * d + i]
            TAKE.at[i][...] = ((slot == chosen) & (position == place)
                               & (place < live[chosen])).astype(F32).astype(BF)

        @pl.when(s > 0)
        def _():
            scale_head()

    def scale_head():
        head_load.wait()

        def off(n):
            return jnp.where(n == 0, 0, jnp.where(n == 1, 3, jnp.where(n == 2, 1, 2)))

        def scale(n, _):
            cc, j, i = n // 16, (n // 4) % 4, n % 4
            g = jnp.where(cc == 0, off(i), off(j))
            zz = jnp.where(cc == 0, off(j), off(i))
            col = ((d + g) % NY) * 2048 + ((z + zz) % NZ) * 512 + cc * 256
            block = HEAD.at[cc, j, :, lane(i * 256, 256)]
            block[...] = (block[...].astype(F32) * fgain[:, lane(col, 256)]).astype(BF)
            return 0

        lax.fori_loop(0, 32, scale, 0)

    small[0].wait()

    @pl.when(s == 0)
    def _():
        rows = jnp.concatenate([emb[0], emb[1]], axis=0).astype(F32)
        for q in range(2):
            EB.at[q, m][...] = jnp.concatenate(
                [rows[:, q * 2048:q * 2048 + 2048], rows[:, q * 2048 + 4096:q * 2048 + 6144]],
                axis=0).astype(BF)

    pl.semaphore_wait(barrier, len(partners))

    @pl.when(s > 0)
    def _():
        for n in range(3):
            swap(n).start()

    def eb_z(q, k):
        return rcopy(EB.at[q, m], EB.at[q, m], eb_s.at[q, k], eb_r.at[q, m], (d, s, zpeer(k)))

    def eb_z_in(q, k):
        mk = zpeer(k)
        return rcopy(EB.at[q, mk], EB.at[q, mk], eb_s.at[q, k], eb_r.at[q, mk], here)

    def eb_fwd(q, k):
        mk = zpeer(k)
        return rcopy(EB.at[q, mk], EB.at[q, mk], eb_s.at[q, 4 + k], eb_r.at[q, mk], here)

    def eb_sib_in(q, k):
        mk = zother(k)
        return rcopy(EB.at[q, mk], EB.at[q, mk], eb_s.at[q, 4 + k], eb_r.at[q, mk], here)

    def hop(g):
        return rcopy(HP.at[g], X.at[d, z], hop_s.at[g], hop_r.at[d], (g, (s + 1) % NX, m))

    def hop_in(g):
        return rcopy(HP.at[g], X.at[g, z], hop_s.at[g], hop_r.at[g], here)

    def hop_raw():
        return rcopy(HP, R, hop_s.at[4], hop_r.at[4], (d, (s + 1) % NX, m))

    def ag_z(g, k):
        return rcopy(X.at[g, z], X.at[g, z], ag_s.at[g, k], ag_r.at[g, z], (d, s, zpeer(k)))

    def ag_z_in(g, k):
        zk = (z + k) % NZ
        return rcopy(X.at[g, zk], X.at[g, zk], ag_s.at[g, k], ag_r.at[g, zk], here)

    def sums_out():
        return rcopy(QA.at[1], QR, qr_s, qr_r, here)

    def res(k):
        g = ypeer(k)
        return rcopy(RX.at[g], R.at[d], res_s.at[k], res_r.at[d], (g, s, m))

    def res_in(k):
        g = ypeer(k)
        return rcopy(RX.at[g], R.at[g], res_s.at[k], res_r.at[g], here)

    def ctx(k):
        return rcopy(C.at[d], C.at[d], ctx_s.at[k], ctx_r.at[d], (ypeer(k), s, m))

    def ctx_in(k):
        g = ypeer(k)
        return rcopy(C.at[g], C.at[g], ctx_s.at[k], ctx_r.at[g], here)

    def part(g):
        return rcopy(PS.at[g], PR.at[g], ps_s.at[g], ps_r.at[g], here)

    def zred(g, k):
        return rcopy(ZS.at[g, k], ZR.at[g, k], zz_s.at[g, k], zz_r.at[g, k], (d, s, zpeer(k)))

    def layer():
        def multiply(x, which, rows, n, start=False):
            w = W[which, pl.ds(rows * NZ, NZ)].reshape(4 * 256, 768)
            term = jnp.dot(x, w, preferred_element_type=F32)
            QA.at[n][:, 0:768] = term if start else QA[n, :, 0:768] + term

        @pl.when(s == 0)
        def _():
            for q in range(2):
                for k in (1, 3, 2):
                    eb_z_in(q, k).wait_recv()
                    eb_fwd(q, k).start()
            QA[...] = jnp.zeros_like(QA)
            QR[...] = jnp.zeros_like(QR)
            SS[...] = jnp.zeros_like(SS)
            for q in range(2):
                for k in range(4):
                    eb_sib_in(q, k).wait_recv()

                def blocks(mm):
                    x = EB[q, :, :, lane(mm * 256, 256)].astype(F32)
                    return [x[:, i * 8:i * 8 + 8, :].reshape(ROWS, 256) for i in range(2)]

                def body(mm, total):
                    for half, xs in enumerate(blocks(mm)):
                        g = half * 2 + q
                        cols = lane(g * 2048 + mm * 256, 256)
                        XE.at[g, mm][...] = (xs * gains[:, cols]).astype(BF)
                        square = xs * xs
                        total = total + square[:, 0:128] + square[:, 128:256]
                    return total

                SS[...] = lax.fori_loop(0, NM, body, SS[...])
                for half, xs in enumerate(blocks(m)):
                    RX.at[half * 2 + q][...] = xs.astype(BF)
                if q == 0:
                    for n in range(3):
                        load(n, 0).wait()
                        load(n, 1).wait()

                def both(i, _):
                    g = 2 * i + q
                    for who in range(2):
                        x = jnp.concatenate([XE[g, 2 * zz + who] for zz in range(NZ)], axis=1)
                        multiply(x, who, g, 0)
                    return 0

                lax.fori_loop(0, 2, both, 0)
            for k in (2, 1, 3):
                res(k).start()
            R.at[d][...] = RX[d]

        @pl.when(s > 0)
        def _():
            def arrived(k):
                g = ypeer(k)
                hop_in(g).wait_recv()
                for j in (2, 1, 3):
                    ag_z(g, j).start()

            def columns(k):
                g = ypeer(k)
                for j in (1, 3, 2):
                    ag_z_in(g, j).wait_recv()
                return jnp.concatenate([X[g, zz] for zz in range(NZ)], axis=1)

            def both(k, start=False):
                x = columns(k)
                multiply(x, 1, ypeer(k), 1, start)
                multiply(x, 0, ypeer(k), 0, start)

            def squares_of(k):
                total = jnp.zeros((ROWS, 128), F32)
                for zz in range(NZ):
                    x = X[ypeer(k), zz].astype(F32)
                    square = x * x
                    total = total + square[:, 0:128] + square[:, 128:256]
                return total

            arrived(0)
            arrived(3)
            arrived(1)
            arrived(2)
            both(0, True)
            squares = squares_of(0)
            both(3)
            squares = squares + squares_of(3)
            both(1)
            squares = squares + squares_of(1)
            x = columns(2)
            multiply(x, 1, ypeer(2), 1)
            squares = squares + squares_of(2)
            QA.at[1][:, 768:896] = squares
            sums_out().start()
            multiply(x, 0, ypeer(2), 0)
            sums_out().wait_recv()
            SS[...] = squares + QR[:, 768:896]

        r = lax.rsqrt(jnp.sum(SS[...], axis=1, keepdims=True) * (1.0 / D) + EPS)
        cos = cosine[...]
        sin = sine[...]

        def summed(first, last):
            return QA[0, :, first:last] + QR[:, first:last]

        def rope(x):
            return (x * cos + pltpu.roll(x, 64, 1) * sin).astype(BF)

        query = jnp.concatenate(
            [rope(summed(j * HD, (j + 1) * HD) * r) for j in range(4)], axis=0)
        key = rope(summed(512, 640) * r)
        value = (summed(640, 768) * r).astype(BF)
        scores = lax.dot_general(query, key, (((1,), (1,)), ((), ())),
                                 preferred_element_type=F32) * (HD ** -0.5)
        scores = scores + MASK[...]
        highest = jnp.max(scores, axis=-1, keepdims=True)
        weights = jnp.exp(scores - highest)
        probs = (weights / jnp.sum(weights, axis=-1, keepdims=True)).astype(BF)
        mixed = jnp.dot(probs, value, preferred_element_type=F32).astype(BF)
        for j in range(4):
            C.at[d][:, j * HD:(j + 1) * HD] = mixed[j * ROWS:(j + 1) * ROWS]
        for k in (2, 1, 3):
            ctx(k).start()

        @pl.when(s == NX - 1)
        def _():
            each(4, lambda k: stage_second(0, k))


        wo_load.wait()

        def project(g):
            for zz in range(NZ):
                p = jnp.dot(C[g], WO[:, zz * 512:zz * 512 + 512], preferred_element_type=F32)
                low, high = p[:, :256], p[:, 256:]
                PO.at[g, zz][...] = jnp.where(c == 0, low, high)
                PS.at[g, zz][...] = jnp.where(c == 0, high, low).astype(BF)
            part(g).start()

        def pair(g):
            part(g).wait_recv()
            for k in (2, 1, 3):
                zt = (z + k) % NZ
                ZS.at[g, k][...] = (PO[g, zt] + PR[g, zt].astype(F32)).astype(BF)
                zred(g, k).start()

        def total_of(g):
            total = PO[g, z] + PR[g, z].astype(F32) + R[g].astype(F32)
            for k in (1, 3, 2):
                zred(g, k).wait_recv()
                total = total + ZR[g, k].astype(F32)
            HP.at[g][...] = total.astype(BF)

            @pl.when(s < NX - 1)
            def _():
                hop(g).start()

        project(d)

        @pl.when(s == 0)
        def _():
            for k in (1, 3, 2):
                res_in(k).wait_recv()

        @pl.when(s > 0)
        def _():
            hop_raw().wait_recv()

        pair(d)
        for k in (1, 3):
            ctx_in(k).wait_recv()
            project(ypeer(k))
        pair(ypeer(1))
        pair(ypeer(3))
        def in_last(do):
            @pl.when(s == NX - 1)
            def _():
                do()

        total_of(d)
        in_last(lambda: own_x(1, 0))
        ctx_in(2).wait_recv()
        project(ypeer(2))
        total_of(ypeer(1))
        in_last(lambda: own_x(1, 1))
        pair(ypeer(2))

        def first_two():
            spread(1, 0)
            spread(1, 1)

        in_last(first_two)
        total_of(ypeer(3))

        def third():
            own_x(1, 2)
            spread(1, 2)

        in_last(third)
        total_of(ypeer(2))

        def rest():
            own_x(1, 3)
            spread(1, 3)
            for k in range(3):
                stage_first(1, k)
            for k in range(2):
                stage_second(1, k)
            each(4, lambda k: opposite(0, k))

        in_last(rest)

        @pl.when(s < NX - 1)
        def _():
            hop_raw().start()

        @pl.when(s == 1)
        def _():
            def body(k, _):
                own_x(0, k)
                spread(0, k)
                return 0

            lax.fori_loop(0, 4, body, 0)

    def first_dev(k):
        return (jnp.where(c == 0, ypeer(k), d), s, jnp.where(c == 0, m, zpeer(k)))

    def second_dev(k):
        return (jnp.where(c == 0, d, ypeer(k)), s, jnp.where(c == 0, zpeer(k), m))

    def ycopy(src, dst, b, k, i, j, dev):
        return rcopy(src, dst, y_s.at[b, k, i], y_r.at[b, k, j], dev)

    def y_x(b, k, n):
        ref = Y.at[b, k, c, 0, 0]
        return ycopy(ref, ref, b, k, n, 0, (d, (s + n) % NX, m))

    def y_first(b, k, n):
        slot = (1, 3, 2)[n - 1]
        return ycopy(Y.at[b, k, c, 0, 0], Y.at[b, k, c, 0, slot], b, k, 3 + n, slot, first_dev(n))

    sets = (pl.ds(0, 1), pl.ds(1, 2), pl.ds(3, 1))

    def y_second(b, k, part_no, n):
        slot = 1 if n == 1 else 2
        return ycopy(Y.at[b, k, c, 0, sets[part_no]], Y.at[b, k, c, slot, sets[part_no]], b, k,
                     7 + part_no * 2 + (slot - 1), 1 + 3 * slot + part_no, second_dev(n))

    def y_relay(b, k, half):
        slot, n = ((1, 1), (2, 3))[half]
        two = pl.ds(2 * half, 2)
        return ycopy(Y.at[b, k, c, slot, two], Y.at[b, k, c, 3, two], b, k, 13 + half, 10 + half,
                     second_dev(n))

    forwards = ((0, 0, 1), (0, 1, 2), (0, 3, 1), (1, 0, 4), (2, 0, 4), (3, 0, 2), (3, 2, 2))

    def y_fwd(b, k, n, who):
        j, i, size = forwards[n]
        ref = Y.at[b, k, who, j, pl.ds(i, size)]
        return ycopy(ref, ref, b, k, 15 + n, 12 + n, here)

    def chunk_order(step):
        return jnp.where(step == 3, 2, jnp.where(step == 2, 3, step))

    def own_x(b, k):
        Y.at[b, k, c, 0, 0][...] = HP[(d + chunk_order(k)) % NY]
        for n in (2, 1, 3):
            y_x(b, k, n).start()

    def spread(b, k):
        for n in (2, 1, 3):
            y_first(b, k, n).start()
        for n in (1, 3):
            y_second(b, k, 0, n).start()
        y_fwd(b, k, 0, c).start()

    def stage_first(b, k):
        y_first(b, k, 1).wait_recv()
        y_first(b, k, 3).wait_recv()
        for n in (1, 3):
            y_second(b, k, 1, n).start()
        y_fwd(b, k, 1, c).start()
        y_first(b, k, 2).wait_recv()
        for n in (1, 3):
            y_second(b, k, 2, n).start()
        y_fwd(b, k, 2, c).start()

    def stage_second(b, k):
        for part_no in (0, 1):
            y_second(b, k, part_no, 1).wait_recv()
        y_relay(b, k, 0).start()
        for part_no in (1, 2):
            y_second(b, k, part_no, 3).wait_recv()
        y_relay(b, k, 1).start()
        y_second(b, k, 2, 1).wait_recv()
        y_fwd(b, k, 3, c).start()
        y_second(b, k, 0, 3).wait_recv()
        y_fwd(b, k, 4, c).start()

    def opposite(b, k):
        for half in range(2):
            y_relay(b, k, half).wait_recv()
            y_fwd(b, k, 5 + half, c).start()

    def sibling_in(b, k):
        for n in range(7):
            y_fwd(b, k, n, 1 - c).wait_recv()

    def dots(b, cc, j):
        blocks = []
        for g in range(NY):
            row = []
            total = jnp.zeros((ROWS, 128), F32)
            for i in range(4):
                off_j = jnp.where(j == 0, 0, jnp.where(j == 1, 3, jnp.where(j == 2, 1, 2)))
                sender = (d + jnp.where(cc == 0, (0, 3, 1, 2)[i], off_j)) % NY
                k = chunk_order((g - sender + NY) % NY)
                x = Y[b, k, cc, j, i]
                row.append(x)
                wide = x.astype(F32)
                square = wide * wide
                total = total + square[:, 0:128] + square[:, 128:256]
            SQ.at[b, g][...] += total
            blocks.append(jnp.concatenate(row, axis=1))
        pieces = jnp.concatenate(blocks, axis=0)
        LT.at[b][...] += lax.dot_general(HEAD[cc, j], pieces, (((1,), (1,)), ((), ())),
                                         preferred_element_type=F32)

    def layer_sent():
        @pl.when(s == 0)
        def _():
            for q in range(2):
                for k in range(1, 4):
                    eb_z(q, k).wait_send()
                for k in range(4):
                    eb_fwd(q, k).wait_send()
            for k in range(1, 4):
                res(k).wait_send()

        @pl.when(s > 0)
        def _():
            for g in range(NY):
                for k in range(1, 4):
                    ag_z(g, k).wait_send()
            sums_out().wait_send()
            for n in range(3):
                swap(n).wait_send()

        @pl.when(s < NX - 1)
        def _():
            for g in range(NY):
                hop(g).wait_send()
            hop_raw().wait_send()

        for g in range(NY):
            for k in range(1, 4):
                zred(g, k).wait_send()
            part(g).wait_send()
        for k in range(1, 4):
            ctx(k).wait_send()

    def chunk_sent(b, k, source):
        @pl.when(s == source)
        def _():
            for j in (1, 2, 3):
                y_x(b, k, j).wait_send()

        for j in (1, 2, 3):
            y_first(b, k, j).wait_send()
        for j in (1, 3):
            for part_no in range(3):
                y_second(b, k, part_no, j).wait_send()
        for half in range(2):
            y_relay(b, k, half).wait_send()
        for j in range(7):
            y_fwd(b, k, j, c).wait_send()

    def each(count, do):
        def body(k, _):
            do(k)
            return 0

        lax.fori_loop(0, count, body, 0)

    def exit_dots(k):
        j = chunk_order(k)
        dots(0, c, j)
        dots(0, 1 - c, j)

    def gather(b):
        source = 2 * b + 1
        final = (b == 1) & (s == NX - 1)
        others = jnp.logical_not(final)

        def body(t, _):
            @pl.when((t < 4) & (s != source))
            def _():
                y_x(b, t, 1).wait_recv()
                spread(b, t)

            @pl.when((t >= 1) & (t < 5) & ((t == 4) | others))
            def _():
                stage_first(b, t - 1)

            early = (b == 0) & (s == NX - 1)

            @pl.when((t >= 2) & (t < 6) & ((t >= 4) | others) & jnp.logical_not(early))
            def _():
                stage_second(b, t - 2)

            @pl.when((t >= 3) & ((b == 0) | (t < 6)) & others & jnp.logical_not(early))
            def _():
                opposite(b, t - 3)

            @pl.when((b == 1) & (s == 2) & (t == 1))
            def _():
                each(4, lambda k: sibling_in(0, k))

            @pl.when((b == 1) & (s == 2) & (t >= 2) & (t < 6))
            def _():
                exit_dots(t - 2)
            return 0

        lax.fori_loop(0, 7, body, 0)

        @pl.when(final)
        def _():
            each(3, lambda k: opposite(1, k))
            each(4, lambda k: sibling_in(0, k))
            each(4, exit_dots)

    def finish(b):
        @pl.when((b == 0) & (s < 2))
        def _():
            each(4, lambda k: sibling_in(0, k))
            each(4, exit_dots)

        @pl.when(b == 1)
        def _():
            dots_order()

        softmax(b)

    def dots_order():
        b = 1
        dots(b, c, 0)
        each(3, lambda k: sibling_in(1, k))
        for n in range(3):
            y_fwd(b, 3, n, 1 - c).wait_recv()
        dots(b, 1 - c, 0)
        opposite(b, 3)
        dots(b, c, 1)
        dots(b, c, 2)
        for n in (3, 4):
            y_fwd(b, 3, n, 1 - c).wait_recv()
        dots(b, 1 - c, 1)
        dots(b, 1 - c, 2)
        dots(b, c, 3)
        for n in (5, 6):
            y_fwd(b, 3, n, 1 - c).wait_recv()
        dots(b, 1 - c, 3)

    def softmax(b):
        squares = SQ[b].reshape(NY * ROWS, 128)
        top = squares.astype(BF)
        rest = (squares - top.astype(F32)).astype(BF)
        ones = jnp.ones((16, 128), BF)
        nt = (((1,), (1,)), ((), ()))
        sums = (lax.dot_general(ones, top, nt, preferred_element_type=F32)
                + lax.dot_general(ones, rest, nt, preferred_element_type=F32))[0:1]
        r = lax.rsqrt(sums * (1.0 / D) + EPS)
        logits = LT[b] * r
        highest = jnp.max(logits, axis=0, keepdims=True)
        summed = jnp.sum(jnp.exp(logits - highest), axis=0, keepdims=True)
        vocab = HEAD.shape[2]
        first = ((d * NX + s) * NM + m) * vocab
        index = (lax.broadcasted_iota(jnp.int32, logits.shape, 0) + first).astype(F32)
        wanted = WANT[0:1, :]
        picked = jnp.sum(jnp.where(index == wanted, logits, 0.0), axis=0, keepdims=True)
        for n, value in enumerate((highest, summed, picked)):
            for half in range(2):
                STO[pl.ds(n * 4 + b * 2 + half, 1), :] = value[:, half * 128:half * 128 + 128]

    def step(t, _):
        last = s == NX - 1
        place = jnp.where(last, 1, 0)

        @pl.when(t == place)
        def _():
            layer()

        @pl.when(jnp.where(last, (t == 0) | (t == 2), (t == 1) | (t == jnp.where(s < 2, 3, 2))))
        def _():
            gather(jnp.where((t == 0) | (t == 1), 0, 1))

        @pl.when((t == 4) | (t == jnp.where(s < 2, 2, 3)))
        def _():
            @pl.when((t == 2) & (s == 0))
            def _():
                scale_head()
            finish(jnp.where(t == 4, 1, 0))
        return 0

    @pl.when(s == 0)
    def _():
        for q in range(2):
            for k in (2, 1, 3, 0):
                (eb_z(q, k) if k else eb_fwd(q, 0)).start()

    prepare()
    STO[...] = jnp.zeros_like(STO)
    SQ[...] = jnp.zeros_like(SQ)
    LT[...] = jnp.zeros_like(LT)
    lax.fori_loop(0, 5, step, 0)

    def merge(ref, count):
        parts = [ref[j] for j in range(count)]
        highest = parts[0][0:4]
        for p in parts[1:]:
            highest = jnp.maximum(highest, p[0:4])
        summed = jnp.zeros_like(highest)
        picked = jnp.zeros_like(highest)
        for p in parts:
            summed = summed + p[4:8] * jnp.exp(p[0:4] - highest)
            picked = picked + p[8:12]
        return highest, summed, picked

    def stacked(highest, summed, picked):
        return jnp.concatenate([highest, summed, picked, jnp.zeros_like(picked)], axis=0)

    pairs = [(j, k) for j in range(NX) for k in range(NY) if j or k]

    def st_yx(n):
        j, k = pairs[n]
        mine = s * NY + d
        return rcopy(SA.at[mine], SA.at[mine], st_s.at[0, n], st_r.at[0, mine],
                     (ypeer(k), (s + j) % NX, m))

    def st_yx_in(n):
        j, k = pairs[n]
        other = ((s + j) % NX) * NY + ypeer(k)
        return rcopy(SA.at[other], SA.at[other], st_s.at[0, n], st_r.at[0, other], here)

    def m_of(k):
        return (m + k) % NM

    def st_m(k):
        return rcopy(SB.at[m], SB.at[m], st_s.at[1, k], st_r.at[1, m], (d, s, m_of(k)))

    def st_m_in(k):
        mm = m_of(k)
        return rcopy(SB.at[mm], SB.at[mm], st_s.at[1, k], st_r.at[1, mm], (d, s, mm))

    SA.at[s * NY + d][...] = STO[...]
    for n in range(15):
        st_yx(n).start()
    layer_sent()
    each(4, lambda k: chunk_sent(0, k, 1))
    each(4, lambda k: chunk_sent(1, k, NX - 1))
    for n in range(15):
        st_yx_in(n).wait_recv()
    SB.at[m][...] = stacked(*merge(SA, NX * NY))
    for k in (4, 3, 5, 2, 6, 1, 7):
        st_m(k).start()
    for n in range(15):
        st_yx(n).wait_send()
    for k in (1, 7, 2, 6, 3, 5, 4):
        st_m_in(k).wait_recv()
    highest, summed, picked = merge(SB, NM)
    logprob = picked - (highest + jnp.log(summed))
    terms = []
    for e in range(2):
        rest = jnp.concatenate([logprob[2 * e:2 * e + 1], logprob[2 * e + 1:2 * e + 2]], axis=1)
        for _ in range(3):
            term = rest.astype(BF).astype(F32)
            terms.append(term)
            rest = rest - term
    row = lax.broadcasted_iota(jnp.int32, (16, 256), 0)
    stack = jnp.zeros((16, 256), F32)
    for j, term in enumerate(terms):
        stack = jnp.where(row == j, term, stack)
    stack = stack.astype(BF)
    results = []
    for i in range(2):
        got = jnp.dot(stack, TAKE[i], preferred_element_type=F32)
        results.append([got[j:j + 1] + got[j + 1:j + 2] + got[j + 2:j + 3] for j in (0, 3)])
    for e in range(2):
        first = lax.broadcasted_iota(jnp.int32, (2, 32), 0) == 0
        out.at[e][...] = jnp.where(first, results[0][e], results[1][e])
    for k in range(1, 8):
        st_m(k).wait_send()


def tables():
    row = np.arange(ROWS)
    position = (row // 8) * 4 + row % 4
    half = HD // 2
    freqs = (ROPE_BASE ** (-np.arange(half) * 2.0 / HD)).astype(np.float32)
    angles = (position.astype(np.float32)[:, None] * freqs[None, :]).astype(np.float64)
    cos, sin = np.cos(angles), np.sin(angles)
    return (np.concatenate([cos, cos], 1).astype(np.float32),
            np.concatenate([-sin, sin], 1).astype(np.float32))


def per_device(
    embeds, targets, lengths, source, attn_gain, w_query, w_key, w_value, w_out, final_gain, head
):
    vocab = head.shape[0]
    cos, sin = tables()
    vmem = pl.BlockSpec(memory_space=pltpu.VMEM)
    hbm = pl.BlockSpec(memory_space=pl.ANY)
    smem = pl.BlockSpec(memory_space=pltpu.SMEM)
    dma = pltpu.SemaphoreType.DMA
    stats = pl.pallas_call(
        kernel,
        out_shape=jax.ShapeDtypeStruct((2, 2, 32), F32),
        in_specs=[hbm, smem, smem] + [hbm] * 10,
        out_specs=vmem,
        scratch_shapes=[
            pltpu.VMEM((2, 4, D), BF),
            pltpu.VMEM((8, 32), jnp.int32),
            pltpu.VMEM((1, D), F32),
            pltpu.VMEM((1, D), F32),
            pltpu.VMEM((ROWS, HD), F32),
            pltpu.VMEM((ROWS, HD), F32),
            pltpu.VMEM((2, 16, 256, 768), BF),
            pltpu.VMEM((QW, 2048), BF),
            pltpu.VMEM((2, 4, vocab, 1024), BF),
            pltpu.VMEM((2, NM, 16, 2048), BF),
            pltpu.VMEM((NY, NM, ROWS, 256), BF),
            pltpu.VMEM((NY, NZ, ROWS, 256), BF),
            pltpu.VMEM((NY, ROWS, 256), BF),
            pltpu.VMEM((4 * ROWS, ROWS), F32),
            pltpu.VMEM((ROWS, 128), F32),
            pltpu.VMEM((2, ROWS, 896), F32),
            pltpu.VMEM((ROWS, 896), F32),
            pltpu.VMEM((NY, ROWS, 256), BF),
            pltpu.VMEM((NY, ROWS, QW), BF),
            pltpu.VMEM((NY, NZ, ROWS, 256), BF),
            pltpu.VMEM((NY, NZ, ROWS, 256), BF),
            pltpu.VMEM((NY, NZ, ROWS, 256), F32),
            pltpu.VMEM((NY, NZ, ROWS, 256), BF),
            pltpu.VMEM((NY, NZ, ROWS, 256), BF),
            pltpu.VMEM((NY, ROWS, 256), BF),
            pltpu.VMEM((2, 4, 2, 4, 4, ROWS, 256), BF),
            pltpu.VMEM((2, vocab, 256), F32),
            pltpu.VMEM((2, NY, ROWS, 128), F32),
            pltpu.VMEM((8, 256), F32),
            pltpu.VMEM((2, 256, 32), BF),
            pltpu.VMEM((16, 128), F32),
            pltpu.VMEM((NX * NY, 16, 128), F32),
            pltpu.VMEM((NM, 16, 128), F32),
            dma((20,)),
            dma((3,)), dma((3,)),
            dma, dma,
            dma((2, 8)), dma((2, 8)),
            dma((5,)), dma((5,)),
            dma((4, 8)), dma((4, 8)),
            dma((4,)), dma((4,)),
            dma((4,)), dma((4,)),
            dma((4,)), dma((4,)),
            dma((4, 4)), dma((4, 4)),
            dma((2, 4, 22)), dma((2, 4, 19)),
            dma((2, 16)), dma((2, 16)),
        ],
        compiler_params=pltpu.CompilerParams(
            collective_id=0, has_side_effects=True, vmem_limit_bytes=60 * 1024 * 1024),
        cost_estimate=pl.CostEstimate(flops=8_000_000_000, bytes_accessed=24_000_000,
                                      transcendentals=300_000),
    )(
        embeds, lengths, source, targets, attn_gain, final_gain.reshape(1, D), jnp.asarray(cos), jnp.asarray(sin),
        w_query.reshape(16, 2, 256, 512), w_key.reshape(16, 2, 256, 128),
        w_value.reshape(16, 2, 256, 128), w_out.reshape(512, 2048), head,
    )
    return (stats[0], stats[1])


def solution(mesh):
    return jax.shard_map(
        per_device,
        mesh=mesh,
        in_specs=(
            P("dp", "mp", None),
            P(),
            P(),
            P(),
            P("section", None),
            P("section", None, "mp"),
            P("section", None, "mp"),
            P("section", None, "mp"),
            P("section", "mp", "dp"),
            P(),
            P(("dp", "section", "mp"), None),
        ),
        out_specs=(P("dp", None), P("dp", None)),
        check_vma=False,
    )
```

```python
import jax
import jax.numpy as jnp
import numpy as np
from jax import lax
from jax.experimental import pallas as pl
from jax.experimental.pallas import tpu as pltpu
from jax.sharding import PartitionSpec as P

HD = 128
EPS = 1e-05
ROPE_BASE = 500000.0
NY = 4
NX = 4
NZ = 4
NM = 8
ROWS = 64
D = 8192
QW = 512
VOCAB_DEV = 512
MESH = pl.DeviceIdType.MESH
BF = jnp.bfloat16
F32 = jnp.float32


def lane(start, size):
    return pl.ds(pl.multiple_of(start, 128), size)


def kernel(
    emb_in, live, source_of, targets_in, gain, fgain_in, cosine_in, sine_in, wq, wk, wv, wo, head,
    out,
    emb, targets, gains, fgain, cosine, sine, W, WO, HEAD, EB, XE, X, RX, MASK, SS, QA, QR, R, C, PS, PR, PO, ZS, ZR, HP, Y, LT, LR, SQ, WANT, TAKE, STO, SA, SB,
    w_sem, sw_s, sw_r, lt_s, lt_r, qr_s, qr_r, eb_s, eb_r, hop_s, hop_r, ag_s, ag_r, res_s, res_r, ctx_s, ctx_r, ps_s, ps_r,
    zz_s, zz_r, y_s, y_r, st_s, st_r,
):
    d = lax.axis_index("dp")
    s = lax.axis_index("section")
    m = lax.axis_index("mp")
    z = m // 2
    c = m % 2
    sib = z * 2 + (1 - c)

    def ypeer(k):
        return (d + k) % NY

    def zpeer(k):
        return ((z + k) % NZ) * 2 + c

    def zother(k):
        return ((z + k) % NZ) * 2 + (1 - c)

    def rcopy(src, dst, ssem, rsem, dev):
        return pltpu.make_async_remote_copy(
            src_ref=src, dst_ref=dst, send_sem=ssem, recv_sem=rsem,
            device_id=dev, device_id_type=MESH,
        )

    here = (d, s, sib)

    barrier = pltpu.get_barrier_semaphore()
    partners = []
    for k in range(1, 4):
        partners.append((ypeer(k), s, m))
        partners.append((d, (s + k) % NX, m))
        partners.append((d, s, zpeer(k)))
        partners.append((d, s, zother(k)))
        partners.append((ypeer(k), (s + 1) % NX, m))
        partners.append((ypeer(k), (s + 3) % NX, m))
        partners.append((ypeer(k), (s + 2) % NX, m))
    partners.append(here)
    for dev in partners:
        pl.semaphore_signal(barrier, inc=1, device_id=dev, device_id_type=MESH)
    small = [
        pltpu.make_async_copy(src, dst, w_sem.at[14 + n])
        for n, (src, dst) in enumerate((
            (emb_in, emb), (gain, gains), (cosine_in, cosine), (sine_in, sine),
            (fgain_in, fgain), (targets_in, targets)))
    ]
    for copy in small:
        copy.start()
    parts = ((wq, pl.ds(0, 512)), (wk, pl.ds(512, 128)), (wv, pl.ds(640, 128)))

    def load(n, first):
        src, lanes = parts[n]
        take = 1 if first else jnp.where(s == 0, 0, c)
        return pltpu.make_async_copy(src.at[:, take], W.at[first, :, :, lanes],
                                     w_sem.at[3 * first + n])

    def swap(n):
        src, lanes = parts[n]
        return rcopy(src.at[:, 1 - c], W.at[1, :, :, lanes], sw_s.at[n], sw_r.at[n], here)

    wo_load = pltpu.make_async_copy(wo, WO, w_sem.at[12])
    for n in range(3):
        load(n, 0).start()

    @pl.when(s == 0)
    def _():
        for n in range(3):
            load(n, 1).start()

    head_load = pltpu.make_async_copy(HEAD.at[0], HEAD.at[0], w_sem.at[13])
    head_swap = rcopy(HEAD.at[1], HEAD.at[1], sw_s.at[3], sw_r.at[3], here)

    def off(n):
        return jnp.where(n == 0, 0, jnp.where(n == 1, 3, jnp.where(n == 2, 1, 2)))

    def slot_columns(core, j, i):
        g = jnp.where(core == 0, off(i), off(j))
        zz = jnp.where(core == 0, off(j), off(i))
        return lane(((d + g) % NY) * 2048 + ((z + zz) % NZ) * 512 + core * 256, 256)

    def row_slot(lanes):
        return (lanes // 64) * 2 + (lanes // 4) % 2, ((lanes // 8) % 8) * 4 + lanes % 4

    def wanted_rows():
        slot, position = row_slot(lax.broadcasted_iota(jnp.int32, (32, 256), 1))
        place = (position == lax.broadcasted_iota(jnp.int32, (32, 256), 0)).astype(BF)
        tokens = targets[...]
        keep = slot[0:8] == lax.broadcasted_iota(jnp.int32, (8, 256), 0)
        parts = []
        for term in (tokens // 256, tokens % 256):
            every = jnp.dot(term.astype(F32).astype(BF), place, preferred_element_type=F32)
            parts.append(jnp.sum(jnp.where(keep, every, 0.0), axis=0, keepdims=True))
        return parts[0] * 256.0 + parts[1]

    def prepare():
        wo_load.start()
        for j in range(4):
            for i in range(4):
                there = pl.ds(i * 256, 256)
                pltpu.make_async_copy(head.at[:, slot_columns(c, j, i)], HEAD.at[0, j, :, there],
                                      w_sem.at[13]).start()
                rcopy(head.at[:, slot_columns(1 - c, j, i)], HEAD.at[1, j, :, there],
                      sw_s.at[3], sw_r.at[3], here).start()
        shape = (4 * ROWS, ROWS)
        rq = lax.broadcasted_iota(jnp.int32, shape, 0) % ROWS
        rk = lax.broadcasted_iota(jnp.int32, shape, 1)
        slot_q, slot_k = (rq // 4) % 2, (rk // 4) % 2
        pos_q, pos_k = (rq // 8) * 4 + rq % 4, (rk // 8) * 4 + rk % 4
        live_k = jnp.where(slot_k == 0, live[2 * d], live[2 * d + 1])
        allowed = (slot_q == slot_k) & (pos_k <= pos_q) & (pos_k < live_k)
        MASK[...] = jnp.where(allowed, F32(0.0), F32(-1e30))

        @pl.when(s > 0)
        def _():
            for n in range(3):
                load(n, 0).wait()
                swap(n).wait_recv()
            for copy in small[1:2]:
                copy.wait()
            diagonal = (lax.broadcasted_iota(jnp.int32, (256, 256), 0)
                        == lax.broadcasted_iota(jnp.int32, (256, 256), 1))

            def scale(i, _):
                cols = lane((i // NZ) * 2048 + ((i % NZ) * 2 + c) * 256, 256)
                column = jnp.sum(jnp.where(diagonal, gains[:, cols], 0.0), axis=1, keepdims=True)
                for which in range(2):
                    W.at[which, i][...] = (W[which, i].astype(F32) * column).astype(BF)
                return 0

            lax.fori_loop(0, 16, scale, 0)

        @pl.when(s == 0)
        def _():
            for copy in small[1:2]:
                copy.wait()
        for copy in small[2:]:
            copy.wait()

        WANT[...] = jnp.broadcast_to(wanted_rows(), WANT.shape)
        slot, position = row_slot(lax.broadcasted_iota(jnp.int32, (256, 32), 0))
        place = lax.broadcasted_iota(jnp.int32, (256, 32), 1)
        for i in range(2):
            chosen = source_of[2 * d + i]
            TAKE.at[i][...] = ((slot == chosen) & (position == place)
                               & (place < live[chosen])).astype(F32).astype(BF)

        @pl.when(s > 0)
        def _():
            scale_head()

    def scale_head():
        head_load.wait()
        head_swap.wait_recv()

        def scale(n, _):
            cc, j, i = n // 16, (n // 4) % 4, n % 4
            block = HEAD.at[cc, j, :, lane(i * 256, 256)]
            block[...] = (block[...].astype(F32) * fgain[:, slot_columns(c, j, i)]).astype(BF)
            return 0

        lax.fori_loop(0, 32, scale, 0)

    small[0].wait()

    @pl.when(s == 0)
    def _():
        rows = jnp.concatenate([emb[0], emb[1]], axis=0).astype(F32)
        for q in range(2):
            EB.at[q, m][...] = jnp.concatenate(
                [rows[:, q * 2048:q * 2048 + 2048], rows[:, q * 2048 + 4096:q * 2048 + 6144]],
                axis=0).astype(BF)

    pl.semaphore_wait(barrier, len(partners))

    @pl.when(s > 0)
    def _():
        for n in range(3):
            swap(n).start()

    def eb_z(q, k):
        return rcopy(EB.at[q, m], EB.at[q, m], eb_s.at[q, k], eb_r.at[q, m], (d, s, zpeer(k)))

    def eb_z_in(q, k):
        mk = zpeer(k)
        return rcopy(EB.at[q, mk], EB.at[q, mk], eb_s.at[q, k], eb_r.at[q, mk], here)

    def eb_fwd(q, k):
        mk = zpeer(k)
        return rcopy(EB.at[q, mk], EB.at[q, mk], eb_s.at[q, 4 + k], eb_r.at[q, mk], here)

    def eb_sib_in(q, k):
        mk = zother(k)
        return rcopy(EB.at[q, mk], EB.at[q, mk], eb_s.at[q, 4 + k], eb_r.at[q, mk], here)

    def hop(g):
        return rcopy(HP.at[g], X.at[d, z], hop_s.at[g], hop_r.at[d], (g, (s + 1) % NX, m))

    def hop_in(g):
        return rcopy(HP.at[g], X.at[g, z], hop_s.at[g], hop_r.at[g], here)

    def hop_raw():
        return rcopy(HP, R, hop_s.at[4], hop_r.at[4], (d, (s + 1) % NX, m))

    def ag_z(g, k):
        return rcopy(X.at[g, z], X.at[g, z], ag_s.at[g, k], ag_r.at[g, z], (d, s, zpeer(k)))

    def ag_z_in(g, k):
        zk = (z + k) % NZ
        return rcopy(X.at[g, zk], X.at[g, zk], ag_s.at[g, k], ag_r.at[g, zk], here)

    def sums_out():
        return rcopy(QA.at[1], QR, qr_s, qr_r, here)

    def res(k):
        g = ypeer(k)
        return rcopy(RX.at[g], R.at[d], res_s.at[k], res_r.at[d], (g, s, m))

    def res_in(k):
        g = ypeer(k)
        return rcopy(RX.at[g], R.at[g], res_s.at[k], res_r.at[g], here)

    def ctx(k):
        return rcopy(C.at[d], C.at[d], ctx_s.at[k], ctx_r.at[d], (ypeer(k), s, m))

    def ctx_in(k):
        g = ypeer(k)
        return rcopy(C.at[g], C.at[g], ctx_s.at[k], ctx_r.at[g], here)

    def part(g):
        return rcopy(PS.at[g], PR.at[g], ps_s.at[g], ps_r.at[g], here)

    def zred(g, k):
        return rcopy(ZS.at[g, k], ZR.at[g, k], zz_s.at[g, k], zz_r.at[g, k], (d, s, zpeer(k)))

    def layer():
        def multiply(x, which, rows, n, start=False):
            w = W[which, pl.ds(rows * NZ, NZ)].reshape(4 * 256, 768)
            term = jnp.dot(x, w, preferred_element_type=F32)
            QA.at[n][:, 0:768] = term if start else QA[n, :, 0:768] + term

        @pl.when(s == 0)
        def _():
            for q in range(2):
                for k in (1, 3, 2):
                    eb_z_in(q, k).wait_recv()
                    eb_fwd(q, k).start()
            QA[...] = jnp.zeros_like(QA)
            QR[...] = jnp.zeros_like(QR)
            SS[...] = jnp.zeros_like(SS)
            for q in range(2):
                for k in range(4):
                    eb_sib_in(q, k).wait_recv()

                def blocks(mm):
                    x = EB[q, :, :, lane(mm * 256, 256)].astype(F32)
                    return [x[:, i * 8:i * 8 + 8, :].reshape(ROWS, 256) for i in range(2)]

                def body(mm, total):
                    for half, xs in enumerate(blocks(mm)):
                        g = half * 2 + q
                        cols = lane(g * 2048 + mm * 256, 256)
                        XE.at[g, mm][...] = (xs * gains[:, cols]).astype(BF)
                        square = xs * xs
                        total = total + square[:, 0:128] + square[:, 128:256]
                    return total

                SS[...] = lax.fori_loop(0, NM, body, SS[...])
                for half, xs in enumerate(blocks(m)):
                    RX.at[half * 2 + q][...] = xs.astype(BF)
                if q == 0:
                    for n in range(3):
                        load(n, 0).wait()
                        load(n, 1).wait()

                def both(i, _):
                    g = 2 * i + q
                    for who in range(2):
                        x = jnp.concatenate([XE[g, 2 * zz + who] for zz in range(NZ)], axis=1)
                        multiply(x, who, g, 0)
                    return 0

                lax.fori_loop(0, 2, both, 0)
            for k in (2, 1, 3):
                res(k).start()
            R.at[d][...] = RX[d]

        @pl.when(s > 0)
        def _():
            def arrived(k):
                g = ypeer(k)
                hop_in(g).wait_recv()
                for j in (2, 1, 3):
                    ag_z(g, j).start()

            def columns(k):
                g = ypeer(k)
                for j in (1, 3, 2):
                    ag_z_in(g, j).wait_recv()
                return jnp.concatenate([X[g, zz] for zz in range(NZ)], axis=1)

            def both(k, start=False):
                x = columns(k)
                multiply(x, 1, ypeer(k), 1, start)
                multiply(x, 0, ypeer(k), 0, start)

            def squares_of(k):
                total = jnp.zeros((ROWS, 128), F32)
                for zz in range(NZ):
                    x = X[ypeer(k), zz].astype(F32)
                    square = x * x
                    total = total + square[:, 0:128] + square[:, 128:256]
                return total

            arrived(0)
            arrived(3)
            arrived(1)
            arrived(2)
            both(0, True)
            squares = squares_of(0)
            both(3)
            squares = squares + squares_of(3)
            both(1)
            squares = squares + squares_of(1)
            x = columns(2)
            multiply(x, 1, ypeer(2), 1)
            squares = squares + squares_of(2)
            QA.at[1][:, 768:896] = squares
            sums_out().start()
            multiply(x, 0, ypeer(2), 0)
            sums_out().wait_recv()
            SS[...] = squares + QR[:, 768:896]

        r = lax.rsqrt(jnp.sum(SS[...], axis=1, keepdims=True) * (1.0 / D) + EPS)
        cos = cosine[...]
        sin = sine[...]

        def summed(first, last):
            return QA[0, :, first:last] + QR[:, first:last]

        def rope(x):
            return (x * cos + pltpu.roll(x, 64, 1) * sin).astype(BF)

        query = jnp.concatenate(
            [rope(summed(j * HD, (j + 1) * HD) * r) for j in range(4)], axis=0)
        key = rope(summed(512, 640) * r)
        value = (summed(640, 768) * r).astype(BF)
        scores = lax.dot_general(query, key, (((1,), (1,)), ((), ())),
                                 preferred_element_type=F32) * (HD ** -0.5)
        scores = scores + MASK[...]
        highest = jnp.max(scores, axis=-1, keepdims=True)
        weights = jnp.exp(scores - highest)
        probs = (weights / jnp.sum(weights, axis=-1, keepdims=True)).astype(BF)
        mixed = jnp.dot(probs, value, preferred_element_type=F32).astype(BF)
        for j in range(4):
            C.at[d][:, j * HD:(j + 1) * HD] = mixed[j * ROWS:(j + 1) * ROWS]
        for k in (2, 1, 3):
            ctx(k).start()

        wo_load.wait()

        def project(g):
            for zz in range(NZ):
                p = jnp.dot(C[g], WO[:, zz * 512:zz * 512 + 512], preferred_element_type=F32)
                low, high = p[:, :256], p[:, 256:]
                PO.at[g, zz][...] = jnp.where(c == 0, low, high)
                PS.at[g, zz][...] = jnp.where(c == 0, high, low).astype(BF)
            part(g).start()

        def pair(g):
            part(g).wait_recv()
            for k in (2, 1, 3):
                zt = (z + k) % NZ
                ZS.at[g, k][...] = (PO[g, zt] + PR[g, zt].astype(F32)).astype(BF)
                zred(g, k).start()

        def total_of(g):
            total = PO[g, z] + PR[g, z].astype(F32) + R[g].astype(F32)
            for k in (1, 3, 2):
                zred(g, k).wait_recv()
                total = total + ZR[g, k].astype(F32)
            HP.at[g][...] = total.astype(BF)

            @pl.when(s < NX - 1)
            def _():
                hop(g).start()

        project(d)

        @pl.when(s == 0)
        def _():
            for k in (1, 3, 2):
                res_in(k).wait_recv()

        @pl.when(s > 0)
        def _():
            hop_raw().wait_recv()

        pair(d)
        for k in (1, 3):
            ctx_in(k).wait_recv()
            project(ypeer(k))
        pair(ypeer(1))
        pair(ypeer(3))
        def in_last(do):
            @pl.when(s == NX - 1)
            def _():
                do()

        total_of(d)
        in_last(lambda: own_x(1, 0))
        ctx_in(2).wait_recv()
        project(ypeer(2))
        total_of(ypeer(1))
        in_last(lambda: own_x(1, 1))
        pair(ypeer(2))

        def first_two():
            spread(1, 0)
            spread(1, 1)

        in_last(first_two)
        total_of(ypeer(3))

        def third():
            own_x(1, 2)
            spread(1, 2)

        in_last(third)
        total_of(ypeer(2))

        def rest():
            own_x(1, 3)
            spread(1, 3)
            for k in range(3):
                stage_first(1, k)
            for k in range(2):
                stage_second(1, k)

        in_last(rest)

        @pl.when(s < NX - 1)
        def _():
            hop_raw().start()

        @pl.when(s == 1)
        def _():
            def body(k, _):
                own_x(0, k)
                spread(0, k)
                return 0

            lax.fori_loop(0, 4, body, 0)

    def first_dev(k):
        return (jnp.where(c == 0, ypeer(k), d), s, jnp.where(c == 0, m, zpeer(k)))

    def second_dev(k):
        return (jnp.where(c == 0, d, ypeer(k)), s, jnp.where(c == 0, zpeer(k), m))

    def ycopy(src, dst, b, k, i, j, dev):
        return rcopy(src, dst, y_s.at[b, k, i], y_r.at[b, k, j], dev)

    def y_x(b, k, n):
        ref = Y.at[b, k, 0, 0]
        return ycopy(ref, ref, b, k, n, 0, (d, (s + n) % NX, m))

    def y_first(b, k, n):
        slot = (1, 3, 2)[n - 1]
        return ycopy(Y.at[b, k, 0, 0], Y.at[b, k, 0, slot], b, k, 3 + n, slot, first_dev(n))

    sets = (pl.ds(0, 1), pl.ds(1, 2), pl.ds(3, 1))

    def y_second(b, k, part_no, n):
        slot = 1 if n == 1 else 2
        return ycopy(Y.at[b, k, 0, sets[part_no]], Y.at[b, k, slot, sets[part_no]], b, k,
                     7 + part_no * 2 + (slot - 1), 1 + 3 * slot + part_no, second_dev(n))

    def y_relay(b, k, half):
        slot, n = ((1, 1), (2, 3))[half]
        two = pl.ds(2 * half, 2)
        return ycopy(Y.at[b, k, slot, two], Y.at[b, k, 3, two], b, k, 13 + half, 10 + half,
                     second_dev(n))

    def chunk_order(step):
        return jnp.where(step == 3, 2, jnp.where(step == 2, 3, step))

    def own_x(b, k):
        Y.at[b, k, 0, 0][...] = HP[(d + chunk_order(k)) % NY]
        for n in (2, 1, 3):
            y_x(b, k, n).start()

    def spread(b, k):
        for n in (2, 1, 3):
            y_first(b, k, n).start()
        for n in (1, 3):
            y_second(b, k, 0, n).start()

    def stage_first(b, k):
        y_first(b, k, 1).wait_recv()
        y_first(b, k, 3).wait_recv()
        for n in (1, 3):
            y_second(b, k, 1, n).start()
        y_first(b, k, 2).wait_recv()
        for n in (1, 3):
            y_second(b, k, 2, n).start()

    def stage_second(b, k):
        for part_no in (0, 1):
            y_second(b, k, part_no, 1).wait_recv()
        y_relay(b, k, 0).start()
        for part_no in (1, 2):
            y_second(b, k, part_no, 3).wait_recv()
        y_relay(b, k, 1).start()
        y_second(b, k, 2, 1).wait_recv()
        y_second(b, k, 0, 3).wait_recv()

    def opposite(b, k):
        for half in range(2):
            y_relay(b, k, half).wait_recv()

    def dots(b, j, send=False):
        blocks = []
        for g in range(NY):
            row = []
            total = jnp.zeros((ROWS, 128), F32)
            for i in range(4):
                sender = (d + jnp.where(c == 0, (0, 3, 1, 2)[i], off(j))) % NY
                k = chunk_order((g - sender + NY) % NY)
                x = Y[b, k, j, i]
                row.append(x)
                wide = x.astype(F32)
                square = wide * wide
                total = total + square[:, 0:128] + square[:, 128:256]
            SQ.at[b, g][...] += total
            blocks.append(jnp.concatenate(row, axis=1))
        pieces = jnp.concatenate(blocks, axis=0)
        for which in (1, 0):
            LT.at[b, which][0:VOCAB_DEV, :] += lax.dot_general(
                HEAD[which, j], pieces, (((1,), (1,)), ((), ())), preferred_element_type=F32)
            if send and which == 1:
                exchange(b)

    def swap_logits(b):
        return rcopy(LT.at[b, 1], LR.at[b], lt_s.at[b], lt_r.at[b], here)

    def exchange(b):
        squares = SQ[b].reshape(NY * ROWS, 128)
        top = squares.astype(BF)
        rest = (squares - top.astype(F32)).astype(BF)
        ones = jnp.ones((16, 128), BF)
        nt = (((1,), (1,)), ((), ()))
        sums = (lax.dot_general(ones, top, nt, preferred_element_type=F32)
                + lax.dot_general(ones, rest, nt, preferred_element_type=F32))
        LT.at[b, 1][VOCAB_DEV:VOCAB_DEV + 8, :] = sums[0:8]
        swap_logits(b).start()

    def layer_sent():
        @pl.when(s == 0)
        def _():
            for q in range(2):
                for k in range(1, 4):
                    eb_z(q, k).wait_send()
                for k in range(4):
                    eb_fwd(q, k).wait_send()
            for k in range(1, 4):
                res(k).wait_send()

        @pl.when(s > 0)
        def _():
            for g in range(NY):
                for k in range(1, 4):
                    ag_z(g, k).wait_send()
            sums_out().wait_send()
            for n in range(3):
                swap(n).wait_send()

        @pl.when(s < NX - 1)
        def _():
            for g in range(NY):
                hop(g).wait_send()
            hop_raw().wait_send()

        for g in range(NY):
            for k in range(1, 4):
                zred(g, k).wait_send()
            part(g).wait_send()
        for k in range(1, 4):
            ctx(k).wait_send()

    def chunk_sent(b, k, source):
        @pl.when(s == source)
        def _():
            for j in (1, 2, 3):
                y_x(b, k, j).wait_send()

        for j in (1, 2, 3):
            y_first(b, k, j).wait_send()
        for j in (1, 3):
            for part_no in range(3):
                y_second(b, k, part_no, j).wait_send()
        for half in range(2):
            y_relay(b, k, half).wait_send()

    def each(count, do):
        def body(k, _):
            do(k)
            return 0

        lax.fori_loop(0, count, body, 0)

    def exit_dots(n):
        dots(0, n)

    def gather(b):
        source = 2 * b + 1
        final = (b == 1) & (s == NX - 1)
        others = jnp.logical_not(final)

        def body(t, _):
            @pl.when((t < 4) & (s != source))
            def _():
                y_x(b, t, 1).wait_recv()
                spread(b, t)

            @pl.when((t >= 1) & (t < 5) & ((t == 4) | others))
            def _():
                stage_first(b, t - 1)

            @pl.when((t >= 2) & (t < 6) & ((t >= 4) | others))
            def _():
                stage_second(b, t - 2)

            @pl.when((t >= 3) & ((b == 0) | (t < 6)) & others)
            def _():
                opposite(b, t - 3)

            @pl.when((b == 1) & (s == 2) & (t >= 2) & (t < 6))
            def _():
                exit_dots(t - 2)

            @pl.when((b == 1) & (s == 2) & (t == 6))
            def _():
                exchange(0)
            return 0

        lax.fori_loop(0, 7, body, 0)

        @pl.when(final)
        def _():
            each(3, lambda k: opposite(1, k))
            each(4, exit_dots)
            exchange(0)

    def finish(b):
        @pl.when(b == 0)
        def _():
            each(4, exit_dots)
            exchange(0)

        @pl.when(b == 1)
        def _():
            for j in range(3):
                dots(1, j)
            opposite(1, 3)
            dots(1, 3, True)

            @pl.when(s >= 2)
            def _():
                softmax(0)

        softmax(b)

    def softmax(b):
        swap_logits(b).wait_recv()
        last = pl.ds(VOCAB_DEV, 8)
        sums = (LT[b, 1, last] + LR[b, last])[0:1]
        r = lax.rsqrt(sums * (1.0 / D) + EPS)
        logits = (LT[b, 0, 0:VOCAB_DEV] + LR[b, 0:VOCAB_DEV]) * r
        highest = jnp.max(logits, axis=0, keepdims=True)
        summed = jnp.sum(jnp.exp(logits - highest), axis=0, keepdims=True)
        first = ((d * NX + s) * NM + m) * VOCAB_DEV
        index = (lax.broadcasted_iota(jnp.int32, logits.shape, 0) + first).astype(F32)
        wanted = WANT[0:1, :]
        picked = jnp.sum(jnp.where(index == wanted, logits, 0.0), axis=0, keepdims=True)
        for n, value in enumerate((highest, summed, picked)):
            for half in range(2):
                STO[pl.ds(n * 4 + b * 2 + half, 1), :] = value[:, half * 128:half * 128 + 128]

    def step(t, _):
        last = s == NX - 1
        place = jnp.where(last, 1, 0)

        @pl.when(t == place)
        def _():
            layer()

        @pl.when(jnp.where(last, (t == 0) | (t == 2), (t == 1) | (t == jnp.where(s < 2, 3, 2))))
        def _():
            gather(jnp.where((t == 0) | (t == 1), 0, 1))

        @pl.when((t == 4) | ((t == 2) & (s < 2)))
        def _():
            @pl.when((t == 2) & (s == 0))
            def _():
                scale_head()
            finish(jnp.where(t == 4, 1, 0))
        return 0

    @pl.when(s == 0)
    def _():
        for q in range(2):
            for k in (2, 1, 3, 0):
                (eb_z(q, k) if k else eb_fwd(q, 0)).start()

    prepare()
    STO[...] = jnp.zeros_like(STO)
    SQ[...] = jnp.zeros_like(SQ)
    LT[...] = jnp.zeros_like(LT)
    lax.fori_loop(0, 5, step, 0)

    def merge(ref, count):
        parts = [ref[j] for j in range(count)]
        highest = parts[0][0:4]
        for p in parts[1:]:
            highest = jnp.maximum(highest, p[0:4])
        summed = jnp.zeros_like(highest)
        picked = jnp.zeros_like(highest)
        for p in parts:
            summed = summed + p[4:8] * jnp.exp(p[0:4] - highest)
            picked = picked + p[8:12]
        return highest, summed, picked

    def stacked(highest, summed, picked):
        return jnp.concatenate([highest, summed, picked, jnp.zeros_like(picked)], axis=0)

    pairs = [(j, k) for j in range(NX) for k in range(NY) if j or k]

    def st_yx(n):
        j, k = pairs[n]
        mine = s * NY + d
        return rcopy(SA.at[mine], SA.at[mine], st_s.at[0, n], st_r.at[0, mine],
                     (ypeer(k), (s + j) % NX, m))

    def st_yx_in(n):
        j, k = pairs[n]
        other = ((s + j) % NX) * NY + ypeer(k)
        return rcopy(SA.at[other], SA.at[other], st_s.at[0, n], st_r.at[0, other], here)

    def m_of(k):
        return (m + k) % NM

    def st_m(k):
        return rcopy(SB.at[m], SB.at[m], st_s.at[1, k], st_r.at[1, m], (d, s, m_of(k)))

    def st_m_in(k):
        mm = m_of(k)
        return rcopy(SB.at[mm], SB.at[mm], st_s.at[1, k], st_r.at[1, mm], (d, s, mm))

    SA.at[s * NY + d][...] = STO[...]
    for n in range(15):
        st_yx(n).start()
    layer_sent()
    head_swap.wait_send()
    swap_logits(0).wait_send()
    swap_logits(1).wait_send()
    each(4, lambda k: chunk_sent(0, k, 1))
    each(4, lambda k: chunk_sent(1, k, NX - 1))
    for n in range(15):
        st_yx_in(n).wait_recv()
    SB.at[m][...] = stacked(*merge(SA, NX * NY))
    for k in (4, 3, 5, 2, 6, 1, 7):
        st_m(k).start()
    for n in range(15):
        st_yx(n).wait_send()
    for k in (1, 7, 2, 6, 3, 5, 4):
        st_m_in(k).wait_recv()
    highest, summed, picked = merge(SB, NM)
    logprob = picked - (highest + jnp.log(summed))
    terms = []
    for e in range(2):
        rest = jnp.concatenate([logprob[2 * e:2 * e + 1], logprob[2 * e + 1:2 * e + 2]], axis=1)
        for _ in range(3):
            term = rest.astype(BF).astype(F32)
            terms.append(term)
            rest = rest - term
    row = lax.broadcasted_iota(jnp.int32, (16, 256), 0)
    stack = jnp.zeros((16, 256), F32)
    for j, term in enumerate(terms):
        stack = jnp.where(row == j, term, stack)
    stack = stack.astype(BF)
    results = []
    for i in range(2):
        got = jnp.dot(stack, TAKE[i], preferred_element_type=F32)
        results.append([got[j:j + 1] + got[j + 1:j + 2] + got[j + 2:j + 3] for j in (0, 3)])
    for e in range(2):
        first = lax.broadcasted_iota(jnp.int32, (2, 32), 0) == 0
        out.at[e][...] = jnp.where(first, results[0][e], results[1][e])
    for k in range(1, 8):
        st_m(k).wait_send()


def tables():
    row = np.arange(ROWS)
    position = (row // 8) * 4 + row % 4
    half = HD // 2
    freqs = (ROPE_BASE ** (-np.arange(half) * 2.0 / HD)).astype(np.float32)
    angles = (position.astype(np.float32)[:, None] * freqs[None, :]).astype(np.float64)
    cos, sin = np.cos(angles), np.sin(angles)
    return (np.concatenate([cos, cos], 1).astype(np.float32),
            np.concatenate([-sin, sin], 1).astype(np.float32))


def per_device(
    embeds, targets, lengths, source, attn_gain, w_query, w_key, w_value, w_out, final_gain, head
):
    vocab = head.shape[0]
    cos, sin = tables()
    vmem = pl.BlockSpec(memory_space=pltpu.VMEM)
    hbm = pl.BlockSpec(memory_space=pl.ANY)
    smem = pl.BlockSpec(memory_space=pltpu.SMEM)
    dma = pltpu.SemaphoreType.DMA
    stats = pl.pallas_call(
        kernel,
        out_shape=jax.ShapeDtypeStruct((2, 2, 32), F32),
        in_specs=[hbm, smem, smem] + [hbm] * 10,
        out_specs=vmem,
        scratch_shapes=[
            pltpu.VMEM((2, 4, D), BF),
            pltpu.VMEM((8, 32), jnp.int32),
            pltpu.VMEM((1, D), F32),
            pltpu.VMEM((1, D), F32),
            pltpu.VMEM((ROWS, HD), F32),
            pltpu.VMEM((ROWS, HD), F32),
            pltpu.VMEM((2, 16, 256, 768), BF),
            pltpu.VMEM((QW, 2048), BF),
            pltpu.VMEM((2, 4, vocab, 1024), BF),
            pltpu.VMEM((2, NM, 16, 2048), BF),
            pltpu.VMEM((NY, NM, ROWS, 256), BF),
            pltpu.VMEM((NY, NZ, ROWS, 256), BF),
            pltpu.VMEM((NY, ROWS, 256), BF),
            pltpu.VMEM((4 * ROWS, ROWS), F32),
            pltpu.VMEM((ROWS, 128), F32),
            pltpu.VMEM((2, ROWS, 896), F32),
            pltpu.VMEM((ROWS, 896), F32),
            pltpu.VMEM((NY, ROWS, 256), BF),
            pltpu.VMEM((NY, ROWS, QW), BF),
            pltpu.VMEM((NY, NZ, ROWS, 256), BF),
            pltpu.VMEM((NY, NZ, ROWS, 256), BF),
            pltpu.VMEM((NY, NZ, ROWS, 256), F32),
            pltpu.VMEM((NY, NZ, ROWS, 256), BF),
            pltpu.VMEM((NY, NZ, ROWS, 256), BF),
            pltpu.VMEM((NY, ROWS, 256), BF),
            pltpu.VMEM((2, 4, 4, 4, ROWS, 256), BF),
            pltpu.VMEM((2, 2, vocab + 8, 256), F32),
            pltpu.VMEM((2, vocab + 8, 256), F32),
            pltpu.VMEM((2, NY, ROWS, 128), F32),
            pltpu.VMEM((8, 256), F32),
            pltpu.VMEM((2, 256, 32), BF),
            pltpu.VMEM((16, 128), F32),
            pltpu.VMEM((NX * NY, 16, 128), F32),
            pltpu.VMEM((NM, 16, 128), F32),
            dma((20,)),
            dma((4,)), dma((4,)),
            dma((2,)), dma((2,)),
            dma, dma,
            dma((2, 8)), dma((2, 8)),
            dma((5,)), dma((5,)),
            dma((4, 8)), dma((4, 8)),
            dma((4,)), dma((4,)),
            dma((4,)), dma((4,)),
            dma((4,)), dma((4,)),
            dma((4, 4)), dma((4, 4)),
            dma((2, 4, 22)), dma((2, 4, 19)),
            dma((2, 16)), dma((2, 16)),
        ],
        compiler_params=pltpu.CompilerParams(
            collective_id=0, has_side_effects=True, vmem_limit_bytes=60 * 1024 * 1024),
        cost_estimate=pl.CostEstimate(flops=8_000_000_000, bytes_accessed=24_000_000,
                                      transcendentals=300_000),
    )(
        embeds, lengths, source, targets, attn_gain, final_gain.reshape(1, D), jnp.asarray(cos), jnp.asarray(sin),
        w_query.reshape(16, 2, 256, 512), w_key.reshape(16, 2, 256, 128),
        w_value.reshape(16, 2, 256, 128), w_out.reshape(512, 2048), head,
    )
    return (stats[0], stats[1])


def solution(mesh):
    return jax.shard_map(
        per_device,
        mesh=mesh,
        in_specs=(
            P("dp", "mp", None),
            P(),
            P(),
            P(),
            P("section", None),
            P("section", None, "mp"),
            P("section", None, "mp"),
            P("section", None, "mp"),
            P("section", "mp", "dp"),
            P(),
            P(("dp", "section", "mp"), None),
        ),
        out_specs=(P("dp", None), P("dp", None)),
        check_vma=False,
    )
```

```python
import jax
import jax.numpy as jnp
import numpy as np
from jax import lax
from jax.experimental import pallas as pl
from jax.experimental.pallas import tpu as pltpu
from jax.sharding import PartitionSpec as P

HD = 128
EPS = 1e-05
ROPE_BASE = 500000.0
NY = 4
NX = 4
NZ = 4
NM = 8
ROWS = 64
D = 8192
QW = 512
VOCAB_DEV = 512
MESH = pl.DeviceIdType.MESH
BF = jnp.bfloat16
F32 = jnp.float32


def lane(start, size):
    return pl.ds(pl.multiple_of(start, 128), size)


def kernel(
    emb_in, live, source_of, targets_in, gain, fgain_in, cosine_in, sine_in, wq, wk, wv, wo, head,
    out,
    emb, targets, gains, fgain, cosine, sine, W, WO, HEAD, EB, XE, X, RX, MASK, SS, QA, QR, R, C, PS, PR, PO, ZS, ZR, HP, Y, LT, LR, SQ, WANT, TAKE, STO, SA, SB,
    w_sem, sw_s, sw_r, lt_s, lt_r, qr_s, qr_r, eb_s, eb_r, hop_s, hop_r, ag_s, ag_r, res_s, res_r, ctx_s, ctx_r, ps_s, ps_r,
    zz_s, zz_r, y_s, y_r, st_s, st_r,
):
    d = lax.axis_index("dp")
    s = lax.axis_index("section")
    m = lax.axis_index("mp")
    z = m // 2
    c = m % 2
    sib = z * 2 + (1 - c)

    def ypeer(k):
        return (d + k) % NY

    def zpeer(k):
        return ((z + k) % NZ) * 2 + c

    def zother(k):
        return ((z + k) % NZ) * 2 + (1 - c)

    def rcopy(src, dst, ssem, rsem, dev):
        return pltpu.make_async_remote_copy(
            src_ref=src, dst_ref=dst, send_sem=ssem, recv_sem=rsem,
            device_id=dev, device_id_type=MESH,
        )

    here = (d, s, sib)

    barrier = pltpu.get_barrier_semaphore()
    partners = []
    for k in range(1, 4):
        partners.append((ypeer(k), s, m))
        partners.append((d, (s + k) % NX, m))
        partners.append((d, s, zpeer(k)))
        partners.append((d, s, zother(k)))
        partners.append((ypeer(k), (s + 1) % NX, m))
        partners.append((ypeer(k), (s + 3) % NX, m))
        partners.append((ypeer(k), (s + 2) % NX, m))
    partners.append(here)
    for dev in partners:
        pl.semaphore_signal(barrier, inc=1, device_id=dev, device_id_type=MESH)
    small = [
        pltpu.make_async_copy(src, dst, w_sem.at[14 + n])
        for n, (src, dst) in enumerate((
            (emb_in, emb), (gain, gains), (cosine_in, cosine), (sine_in, sine),
            (fgain_in, fgain), (targets_in, targets)))
    ]
    for copy in small:
        copy.start()
    parts = ((wq, pl.ds(0, 512)), (wk, pl.ds(512, 128)), (wv, pl.ds(640, 128)))

    def load(n, first):
        src, lanes = parts[n]
        take = 1 if first else jnp.where(s == 0, 0, c)
        return pltpu.make_async_copy(src.at[:, take], W.at[first, :, :, lanes],
                                     w_sem.at[3 * first + n])

    def swap(n):
        src, lanes = parts[n]
        return rcopy(src.at[:, 1 - c], W.at[1, :, :, lanes], sw_s.at[n], sw_r.at[n], here)

    wo_load = pltpu.make_async_copy(wo, WO, w_sem.at[12])
    @pl.when(s > 0)
    def _():
        for n in range(3):
            load(n, 0).start()

    head_load = pltpu.make_async_copy(HEAD.at[0], HEAD.at[0], w_sem.at[13])
    head_swap = rcopy(HEAD.at[1], HEAD.at[1], sw_s.at[3], sw_r.at[3], here)

    def off(n):
        return jnp.where(n == 0, 0, jnp.where(n == 1, 3, jnp.where(n == 2, 1, 2)))

    def slot_columns(core, j, i):
        g = jnp.where(core == 0, off(i), off(j))
        zz = jnp.where(core == 0, off(j), off(i))
        return lane(((d + g) % NY) * 2048 + ((z + zz) % NZ) * 512 + core * 256, 256)

    def row_slot(lanes):
        return (lanes // 64) * 2 + (lanes // 4) % 2, ((lanes // 8) % 8) * 4 + lanes % 4

    def wanted_rows():
        slot, position = row_slot(lax.broadcasted_iota(jnp.int32, (32, 256), 1))
        place = (position == lax.broadcasted_iota(jnp.int32, (32, 256), 0)).astype(BF)
        tokens = targets[...]
        keep = slot[0:8] == lax.broadcasted_iota(jnp.int32, (8, 256), 0)
        parts = []
        for term in (tokens // 256, tokens % 256):
            every = jnp.dot(term.astype(F32).astype(BF), place, preferred_element_type=F32)
            parts.append(jnp.sum(jnp.where(keep, every, 0.0), axis=0, keepdims=True))
        return parts[0] * 256.0 + parts[1]

    def head_start():
        for j in range(4):
            for i in range(4):
                there = pl.ds(i * 256, 256)
                pltpu.make_async_copy(head.at[:, slot_columns(c, j, i)], HEAD.at[0, j, :, there],
                                      w_sem.at[13]).start()
                rcopy(head.at[:, slot_columns(1 - c, j, i)], HEAD.at[1, j, :, there],
                      sw_s.at[3], sw_r.at[3], here).start()
    def prepare():
        @pl.when(s > 0)
        def _():
            wo_load.start()
            head_start()

        shape = (4 * ROWS, ROWS)
        rq = lax.broadcasted_iota(jnp.int32, shape, 0) % ROWS
        rk = lax.broadcasted_iota(jnp.int32, shape, 1)
        slot_q, slot_k = (rq // 4) % 2, (rk // 4) % 2
        pos_q, pos_k = (rq // 8) * 4 + rq % 4, (rk // 8) * 4 + rk % 4
        live_k = jnp.where(slot_k == 0, live[2 * d], live[2 * d + 1])
        allowed = (slot_q == slot_k) & (pos_k <= pos_q) & (pos_k < live_k)
        MASK[...] = jnp.where(allowed, F32(0.0), F32(-1e30))

        @pl.when(s > 0)
        def _():
            for n in range(3):
                load(n, 0).wait()
                swap(n).wait_recv()
            for copy in small[1:2]:
                copy.wait()
            diagonal = (lax.broadcasted_iota(jnp.int32, (256, 256), 0)
                        == lax.broadcasted_iota(jnp.int32, (256, 256), 1))

            def scale(i, _):
                cols = lane((i // NZ) * 2048 + ((i % NZ) * 2 + c) * 256, 256)
                column = jnp.sum(jnp.where(diagonal, gains[:, cols], 0.0), axis=1, keepdims=True)
                for which in range(2):
                    W.at[which, i][...] = (W[which, i].astype(F32) * column).astype(BF)
                return 0

            lax.fori_loop(0, 16, scale, 0)

        @pl.when(s == 0)
        def _():
            for copy in small[1:2]:
                copy.wait()
        for copy in small[2:]:
            copy.wait()

        WANT[...] = jnp.broadcast_to(wanted_rows(), WANT.shape)
        slot, position = row_slot(lax.broadcasted_iota(jnp.int32, (256, 32), 0))
        place = lax.broadcasted_iota(jnp.int32, (256, 32), 1)
        for i in range(2):
            chosen = source_of[2 * d + i]
            TAKE.at[i][...] = ((slot == chosen) & (position == place)
                               & (place < live[chosen])).astype(F32).astype(BF)

        @pl.when(s > 0)
        def _():
            scale_head()

    def scale_head():
        head_load.wait()
        head_swap.wait_recv()

        def scale(n, _):
            cc, j, i = n // 16, (n // 4) % 4, n % 4
            block = HEAD.at[cc, j, :, lane(i * 256, 256)]
            block[...] = (block[...].astype(F32) * fgain[:, slot_columns(c, j, i)]).astype(BF)
            return 0

        lax.fori_loop(0, 32, scale, 0)

    small[0].wait()

    @pl.when(s == 0)
    def _():
        rows = jnp.concatenate([emb[0], emb[1]], axis=0).astype(F32)
        for q in range(2):
            EB.at[q, m][...] = jnp.concatenate(
                [rows[:, q * 2048:q * 2048 + 2048], rows[:, q * 2048 + 4096:q * 2048 + 6144]],
                axis=0).astype(BF)

    pl.semaphore_wait(barrier, len(partners))

    @pl.when(s > 0)
    def _():
        for n in range(3):
            swap(n).start()

    def eb_z(q, k):
        return rcopy(EB.at[q, m], EB.at[q, m], eb_s.at[q, k], eb_r.at[q, m], (d, s, zpeer(k)))

    def eb_z_in(q, k):
        mk = zpeer(k)
        return rcopy(EB.at[q, mk], EB.at[q, mk], eb_s.at[q, k], eb_r.at[q, mk], here)

    def eb_fwd(q, k):
        mk = zpeer(k)
        return rcopy(EB.at[q, mk], EB.at[q, mk], eb_s.at[q, 4 + k], eb_r.at[q, mk], here)

    def eb_sib_in(q, k):
        mk = zother(k)
        return rcopy(EB.at[q, mk], EB.at[q, mk], eb_s.at[q, 4 + k], eb_r.at[q, mk], here)

    def hop(g):
        return rcopy(HP.at[g], X.at[d, z], hop_s.at[g], hop_r.at[d], (g, (s + 1) % NX, m))

    def hop_in(g):
        return rcopy(HP.at[g], X.at[g, z], hop_s.at[g], hop_r.at[g], here)

    def hop_raw():
        return rcopy(HP, R, hop_s.at[4], hop_r.at[4], (d, (s + 1) % NX, m))

    def ag_z(g, k):
        return rcopy(X.at[g, z], X.at[g, z], ag_s.at[g, k], ag_r.at[g, z], (d, s, zpeer(k)))

    def ag_z_in(g, k):
        zk = (z + k) % NZ
        return rcopy(X.at[g, zk], X.at[g, zk], ag_s.at[g, k], ag_r.at[g, zk], here)

    def sums_out():
        return rcopy(QA.at[1], QR, qr_s, qr_r, here)

    def res(k):
        g = ypeer(k)
        return rcopy(RX.at[g], R.at[d], res_s.at[k], res_r.at[d], (g, s, m))

    def res_in(k):
        g = ypeer(k)
        return rcopy(RX.at[g], R.at[g], res_s.at[k], res_r.at[g], here)

    def ctx(k):
        return rcopy(C.at[d], C.at[d], ctx_s.at[k], ctx_r.at[d], (ypeer(k), s, m))

    def ctx_in(k):
        g = ypeer(k)
        return rcopy(C.at[g], C.at[g], ctx_s.at[k], ctx_r.at[g], here)

    def part(g):
        return rcopy(PS.at[g], PR.at[g], ps_s.at[g], ps_r.at[g], here)

    def zred(g, k):
        return rcopy(ZS.at[g, k], ZR.at[g, k], zz_s.at[g, k], zz_r.at[g, k], (d, s, zpeer(k)))

    def layer():
        def multiply(x, which, rows, n, start=False):
            w = W[which, pl.ds(rows * NZ, NZ)].reshape(4 * 256, 768)
            term = jnp.dot(x, w, preferred_element_type=F32)
            QA.at[n][:, 0:768] = term if start else QA[n, :, 0:768] + term

        @pl.when(s == 0)
        def _():
            for q in range(2):
                for k in (1, 3, 2):
                    eb_z_in(q, k).wait_recv()
                    eb_fwd(q, k).start()
            QA[...] = jnp.zeros_like(QA)
            QR[...] = jnp.zeros_like(QR)
            SS[...] = jnp.zeros_like(SS)
            for q in range(2):
                for k in range(4):
                    eb_sib_in(q, k).wait_recv()

                def blocks(mm):
                    x = EB[q, :, :, lane(mm * 256, 256)].astype(F32)
                    return [x[:, i * 8:i * 8 + 8, :].reshape(ROWS, 256) for i in range(2)]

                def body(mm, total):
                    for half, xs in enumerate(blocks(mm)):
                        g = half * 2 + q
                        cols = lane(g * 2048 + mm * 256, 256)
                        XE.at[g, mm][...] = (xs * gains[:, cols]).astype(BF)
                        square = xs * xs
                        total = total + square[:, 0:128] + square[:, 128:256]
                    return total

                SS[...] = lax.fori_loop(0, NM, body, SS[...])
                for half, xs in enumerate(blocks(m)):
                    RX.at[half * 2 + q][...] = xs.astype(BF)
                if q == 0:
                    for n in range(3):
                        load(n, 0).wait()
                        load(n, 1).wait()

                def both(i, _):
                    g = 2 * i + q
                    for who in range(2):
                        x = jnp.concatenate([XE[g, 2 * zz + who] for zz in range(NZ)], axis=1)
                        multiply(x, who, g, 0)
                    return 0

                lax.fori_loop(0, 2, both, 0)
            for k in (2, 1, 3):
                res(k).start()
            R.at[d][...] = RX[d]

        @pl.when(s > 0)
        def _():
            def arrived(k):
                g = ypeer(k)
                hop_in(g).wait_recv()
                for j in (2, 1, 3):
                    ag_z(g, j).start()

            def columns(k):
                g = ypeer(k)
                for j in (1, 3, 2):
                    ag_z_in(g, j).wait_recv()
                return jnp.concatenate([X[g, zz] for zz in range(NZ)], axis=1)

            def both(k, start=False):
                x = columns(k)
                multiply(x, 1, ypeer(k), 1, start)
                multiply(x, 0, ypeer(k), 0, start)

            def squares_of(k):
                total = jnp.zeros((ROWS, 128), F32)
                for zz in range(NZ):
                    x = X[ypeer(k), zz].astype(F32)
                    square = x * x
                    total = total + square[:, 0:128] + square[:, 128:256]
                return total

            arrived(0)
            arrived(3)
            arrived(1)
            arrived(2)
            both(0, True)
            squares = squares_of(0)
            both(3)
            squares = squares + squares_of(3)
            both(1)
            squares = squares + squares_of(1)
            x = columns(2)
            multiply(x, 1, ypeer(2), 1)
            squares = squares + squares_of(2)
            QA.at[1][:, 768:896] = squares
            sums_out().start()
            multiply(x, 0, ypeer(2), 0)
            sums_out().wait_recv()
            SS[...] = squares + QR[:, 768:896]

        r = lax.rsqrt(jnp.sum(SS[...], axis=1, keepdims=True) * (1.0 / D) + EPS)
        cos = cosine[...]
        sin = sine[...]

        def summed(first, last):
            return QA[0, :, first:last] + QR[:, first:last]

        def rope(x):
            return (x * cos + pltpu.roll(x, 64, 1) * sin).astype(BF)

        query = jnp.concatenate(
            [rope(summed(j * HD, (j + 1) * HD) * r) for j in range(4)], axis=0)
        key = rope(summed(512, 640) * r)
        value = (summed(640, 768) * r).astype(BF)
        scores = lax.dot_general(query, key, (((1,), (1,)), ((), ())),
                                 preferred_element_type=F32) * (HD ** -0.5)
        scores = scores + MASK[...]
        highest = jnp.max(scores, axis=-1, keepdims=True)
        weights = jnp.exp(scores - highest)
        probs = (weights / jnp.sum(weights, axis=-1, keepdims=True)).astype(BF)
        mixed = jnp.dot(probs, value, preferred_element_type=F32).astype(BF)
        for j in range(4):
            C.at[d][:, j * HD:(j + 1) * HD] = mixed[j * ROWS:(j + 1) * ROWS]
        for k in (2, 1, 3):
            ctx(k).start()

        wo_load.wait()

        def project(g):
            for zz in range(NZ):
                p = jnp.dot(C[g], WO[:, zz * 512:zz * 512 + 512], preferred_element_type=F32)
                low, high = p[:, :256], p[:, 256:]
                PO.at[g, zz][...] = jnp.where(c == 0, low, high)
                PS.at[g, zz][...] = jnp.where(c == 0, high, low).astype(BF)
            part(g).start()

        def pair(g):
            part(g).wait_recv()
            for k in (2, 1, 3):
                zt = (z + k) % NZ
                ZS.at[g, k][...] = (PO[g, zt] + PR[g, zt].astype(F32)).astype(BF)
                zred(g, k).start()

        def total_of(g):
            total = PO[g, z] + PR[g, z].astype(F32) + R[g].astype(F32)
            for k in (1, 3, 2):
                zred(g, k).wait_recv()
                total = total + ZR[g, k].astype(F32)
            HP.at[g][...] = total.astype(BF)

            @pl.when(s < NX - 1)
            def _():
                hop(g).start()

        project(d)

        @pl.when(s == 0)
        def _():
            for k in (1, 3, 2):
                res_in(k).wait_recv()

        @pl.when(s > 0)
        def _():
            hop_raw().wait_recv()

        pair(d)
        for k in (1, 3):
            ctx_in(k).wait_recv()
            project(ypeer(k))
        pair(ypeer(1))
        pair(ypeer(3))
        def in_last(do):
            @pl.when(s == NX - 1)
            def _():
                do()

        total_of(d)
        in_last(lambda: own_x(1, 0))
        ctx_in(2).wait_recv()
        project(ypeer(2))
        total_of(ypeer(1))
        in_last(lambda: own_x(1, 1))
        pair(ypeer(2))

        def first_two():
            spread(1, 0)
            spread(1, 1)

        in_last(first_two)
        total_of(ypeer(3))

        def third():
            own_x(1, 2)
            spread(1, 2)

        in_last(third)
        total_of(ypeer(2))

        def rest():
            own_x(1, 3)
            spread(1, 3)
            for k in range(3):
                stage_first(1, k)
            for k in range(2):
                stage_second(1, k)

        in_last(rest)

        @pl.when(s < NX - 1)
        def _():
            hop_raw().start()

        @pl.when(s == 1)
        def _():
            def body(k, _):
                own_x(0, k)
                spread(0, k)
                return 0

            lax.fori_loop(0, 4, body, 0)

    def first_dev(k):
        return (jnp.where(c == 0, ypeer(k), d), s, jnp.where(c == 0, m, zpeer(k)))

    def second_dev(k):
        return (jnp.where(c == 0, d, ypeer(k)), s, jnp.where(c == 0, zpeer(k), m))

    def ycopy(src, dst, b, k, i, j, dev):
        return rcopy(src, dst, y_s.at[b, k, i], y_r.at[b, k, j], dev)

    def y_x(b, k, n):
        ref = Y.at[b, k, 0, 0]
        return ycopy(ref, ref, b, k, n, 0, (d, (s + n) % NX, m))

    def y_first(b, k, n):
        slot = (1, 3, 2)[n - 1]
        return ycopy(Y.at[b, k, 0, 0], Y.at[b, k, 0, slot], b, k, 3 + n, slot, first_dev(n))

    sets = (pl.ds(0, 1), pl.ds(1, 2), pl.ds(3, 1))

    def y_second(b, k, part_no, n):
        slot = 1 if n == 1 else 2
        return ycopy(Y.at[b, k, 0, sets[part_no]], Y.at[b, k, slot, sets[part_no]], b, k,
                     7 + part_no * 2 + (slot - 1), 1 + 3 * slot + part_no, second_dev(n))

    def y_relay(b, k, half):
        slot, n = ((1, 1), (2, 3))[half]
        two = pl.ds(2 * half, 2)
        return ycopy(Y.at[b, k, slot, two], Y.at[b, k, 3, two], b, k, 13 + half, 10 + half,
                     second_dev(n))

    def chunk_order(step):
        return jnp.where(step == 3, 2, jnp.where(step == 2, 3, step))

    def own_x(b, k):
        Y.at[b, k, 0, 0][...] = HP[(d + chunk_order(k)) % NY]
        for n in (2, 1, 3):
            y_x(b, k, n).start()

    def spread(b, k):
        for n in (2, 1, 3):
            y_first(b, k, n).start()
        for n in (1, 3):
            y_second(b, k, 0, n).start()

    def stage_first(b, k):
        y_first(b, k, 1).wait_recv()
        y_first(b, k, 3).wait_recv()
        for n in (1, 3):
            y_second(b, k, 1, n).start()
        y_first(b, k, 2).wait_recv()
        for n in (1, 3):
            y_second(b, k, 2, n).start()

    def stage_second(b, k):
        for part_no in (0, 1):
            y_second(b, k, part_no, 1).wait_recv()
        y_relay(b, k, 0).start()
        for part_no in (1, 2):
            y_second(b, k, part_no, 3).wait_recv()
        y_relay(b, k, 1).start()
        y_second(b, k, 2, 1).wait_recv()
        y_second(b, k, 0, 3).wait_recv()

    def opposite(b, k):
        for half in range(2):
            y_relay(b, k, half).wait_recv()

    def dots(b, j, send=False):
        blocks = []
        for g in range(NY):
            row = []
            total = jnp.zeros((ROWS, 128), F32)
            for i in range(4):
                sender = (d + jnp.where(c == 0, (0, 3, 1, 2)[i], off(j))) % NY
                k = chunk_order((g - sender + NY) % NY)
                x = Y[b, k, j, i]
                row.append(x)
                wide = x.astype(F32)
                square = wide * wide
                total = total + square[:, 0:128] + square[:, 128:256]
            SQ.at[b, g][...] += total
            blocks.append(jnp.concatenate(row, axis=1))
        pieces = jnp.concatenate(blocks, axis=0)
        for which in (1, 0):
            LT.at[b, which][0:VOCAB_DEV, :] += lax.dot_general(
                HEAD[which, j], pieces, (((1,), (1,)), ((), ())), preferred_element_type=F32)
            if send and which == 1:
                exchange(b)

    def swap_logits(b):
        return rcopy(LT.at[b, 1], LR.at[b], lt_s.at[b], lt_r.at[b], here)

    def exchange(b):
        squares = SQ[b].reshape(NY * ROWS, 128)
        top = squares.astype(BF)
        rest = (squares - top.astype(F32)).astype(BF)
        ones = jnp.ones((16, 128), BF)
        nt = (((1,), (1,)), ((), ()))
        sums = (lax.dot_general(ones, top, nt, preferred_element_type=F32)
                + lax.dot_general(ones, rest, nt, preferred_element_type=F32))
        LT.at[b, 1][VOCAB_DEV:VOCAB_DEV + 8, :] = sums[0:8]
        swap_logits(b).start()

    def layer_sent():
        @pl.when(s == 0)
        def _():
            for q in range(2):
                for k in range(1, 4):
                    eb_z(q, k).wait_send()
                for k in range(4):
                    eb_fwd(q, k).wait_send()
            for k in range(1, 4):
                res(k).wait_send()

        @pl.when(s > 0)
        def _():
            for g in range(NY):
                for k in range(1, 4):
                    ag_z(g, k).wait_send()
            sums_out().wait_send()
            for n in range(3):
                swap(n).wait_send()

        @pl.when(s < NX - 1)
        def _():
            for g in range(NY):
                hop(g).wait_send()
            hop_raw().wait_send()

        for g in range(NY):
            for k in range(1, 4):
                zred(g, k).wait_send()
            part(g).wait_send()
        for k in range(1, 4):
            ctx(k).wait_send()

    def chunk_sent(b, k, source):
        @pl.when(s == source)
        def _():
            for j in (1, 2, 3):
                y_x(b, k, j).wait_send()

        for j in (1, 2, 3):
            y_first(b, k, j).wait_send()
        for j in (1, 3):
            for part_no in range(3):
                y_second(b, k, part_no, j).wait_send()
        for half in range(2):
            y_relay(b, k, half).wait_send()

    def each(count, do):
        def body(k, _):
            do(k)
            return 0

        lax.fori_loop(0, count, body, 0)

    def exit_dots(n):
        dots(0, n)

    def gather(b):
        source = 2 * b + 1
        final = (b == 1) & (s == NX - 1)
        others = jnp.logical_not(final)

        def body(t, _):
            @pl.when((t < 4) & (s != source))
            def _():
                y_x(b, t, 1).wait_recv()
                spread(b, t)

            @pl.when((t >= 1) & (t < 5) & ((t == 4) | others))
            def _():
                stage_first(b, t - 1)

            @pl.when((t >= 2) & (t < 6) & ((t >= 4) | others))
            def _():
                stage_second(b, t - 2)

            @pl.when((t >= 3) & ((b == 0) | (t < 6)) & others)
            def _():
                opposite(b, t - 3)

            @pl.when((b == 1) & (s == 2) & (t >= 2) & (t < 6))
            def _():
                exit_dots(t - 2)

            @pl.when((b == 1) & (s == 2) & (t == 6))
            def _():
                exchange(0)
            return 0

        lax.fori_loop(0, 7, body, 0)

        @pl.when(final)
        def _():
            each(3, lambda k: opposite(1, k))
            each(4, exit_dots)
            exchange(0)

    def finish(b):
        @pl.when(b == 0)
        def _():
            each(4, exit_dots)
            exchange(0)

        @pl.when(b == 1)
        def _():
            for j in range(3):
                dots(1, j)
            opposite(1, 3)
            dots(1, 3, True)

            @pl.when(s >= 2)
            def _():
                softmax(0)

        softmax(b)

    def softmax(b):
        swap_logits(b).wait_recv()
        last = pl.ds(VOCAB_DEV, 8)
        sums = (LT[b, 1, last] + LR[b, last])[0:1]
        r = lax.rsqrt(sums * (1.0 / D) + EPS)
        logits = (LT[b, 0, 0:VOCAB_DEV] + LR[b, 0:VOCAB_DEV]) * r
        highest = jnp.max(logits, axis=0, keepdims=True)
        summed = jnp.sum(jnp.exp(logits - highest), axis=0, keepdims=True)
        first = ((d * NX + s) * NM + m) * VOCAB_DEV
        index = (lax.broadcasted_iota(jnp.int32, logits.shape, 0) + first).astype(F32)
        wanted = WANT[0:1, :]
        picked = jnp.sum(jnp.where(index == wanted, logits, 0.0), axis=0, keepdims=True)
        for n, value in enumerate((highest, summed, picked)):
            for half in range(2):
                STO[pl.ds(n * 4 + b * 2 + half, 1), :] = value[:, half * 128:half * 128 + 128]

    def step(t, _):
        last = s == NX - 1
        place = jnp.where(last, 1, 0)

        @pl.when(t == place)
        def _():
            layer()

            @pl.when(s == 0)
            def _():
                head_start()

        @pl.when(jnp.where(last, (t == 0) | (t == 2), (t == 1) | (t == jnp.where(s < 2, 3, 2))))
        def _():
            gather(jnp.where((t == 0) | (t == 1), 0, 1))

        @pl.when((t == 4) | ((t == 2) & (s < 2)))
        def _():
            @pl.when((t == 2) & (s == 0))
            def _():
                scale_head()
            finish(jnp.where(t == 4, 1, 0))
        return 0

    @pl.when(s == 0)
    def _():
        for q in range(2):
            for k in (2, 1, 3, 0):
                (eb_z(q, k) if k else eb_fwd(q, 0)).start()
        for n in range(3):
            load(n, 0).start()
            load(n, 1).start()
        wo_load.start()

    prepare()
    STO[...] = jnp.zeros_like(STO)
    SQ[...] = jnp.zeros_like(SQ)
    LT[...] = jnp.zeros_like(LT)
    lax.fori_loop(0, 5, step, 0)

    def merge(ref, count):
        parts = [ref[j] for j in range(count)]
        highest = parts[0][0:4]
        for p in parts[1:]:
            highest = jnp.maximum(highest, p[0:4])
        summed = jnp.zeros_like(highest)
        picked = jnp.zeros_like(highest)
        for p in parts:
            summed = summed + p[4:8] * jnp.exp(p[0:4] - highest)
            picked = picked + p[8:12]
        return highest, summed, picked

    def stacked(highest, summed, picked):
        return jnp.concatenate([highest, summed, picked, jnp.zeros_like(picked)], axis=0)

    pairs = [(j, k) for j in range(NX) for k in range(NY) if j or k]

    def st_yx(n):
        j, k = pairs[n]
        mine = s * NY + d
        return rcopy(SA.at[mine], SA.at[mine], st_s.at[0, n], st_r.at[0, mine],
                     (ypeer(k), (s + j) % NX, m))

    def st_yx_in(n):
        j, k = pairs[n]
        other = ((s + j) % NX) * NY + ypeer(k)
        return rcopy(SA.at[other], SA.at[other], st_s.at[0, n], st_r.at[0, other], here)

    def m_of(k):
        return (m + k) % NM

    def st_m(k):
        return rcopy(SB.at[m], SB.at[m], st_s.at[1, k], st_r.at[1, m], (d, s, m_of(k)))

    def st_m_in(k):
        mm = m_of(k)
        return rcopy(SB.at[mm], SB.at[mm], st_s.at[1, k], st_r.at[1, mm], (d, s, mm))

    SA.at[s * NY + d][...] = STO[...]
    for n in range(15):
        st_yx(n).start()
    layer_sent()
    head_swap.wait_send()
    swap_logits(0).wait_send()
    swap_logits(1).wait_send()
    each(4, lambda k: chunk_sent(0, k, 1))
    each(4, lambda k: chunk_sent(1, k, NX - 1))
    for n in range(15):
        st_yx_in(n).wait_recv()
    SB.at[m][...] = stacked(*merge(SA, NX * NY))
    for k in (4, 3, 5, 2, 6, 1, 7):
        st_m(k).start()
    for n in range(15):
        st_yx(n).wait_send()
    for k in (1, 7, 2, 6, 3, 5, 4):
        st_m_in(k).wait_recv()
    highest, summed, picked = merge(SB, NM)
    logprob = picked - (highest + jnp.log(summed))
    terms = []
    for e in range(2):
        rest = jnp.concatenate([logprob[2 * e:2 * e + 1], logprob[2 * e + 1:2 * e + 2]], axis=1)
        for _ in range(3):
            term = rest.astype(BF).astype(F32)
            terms.append(term)
            rest = rest - term
    row = lax.broadcasted_iota(jnp.int32, (16, 256), 0)
    stack = jnp.zeros((16, 256), F32)
    for j, term in enumerate(terms):
        stack = jnp.where(row == j, term, stack)
    stack = stack.astype(BF)
    results = []
    for i in range(2):
        got = jnp.dot(stack, TAKE[i], preferred_element_type=F32)
        results.append([got[j:j + 1] + got[j + 1:j + 2] + got[j + 2:j + 3] for j in (0, 3)])
    for e in range(2):
        first = lax.broadcasted_iota(jnp.int32, (2, 32), 0) == 0
        out.at[e][...] = jnp.where(first, results[0][e], results[1][e])
    for k in range(1, 8):
        st_m(k).wait_send()


def tables():
    row = np.arange(ROWS)
    position = (row // 8) * 4 + row % 4
    half = HD // 2
    freqs = (ROPE_BASE ** (-np.arange(half) * 2.0 / HD)).astype(np.float32)
    angles = (position.astype(np.float32)[:, None] * freqs[None, :]).astype(np.float64)
    cos, sin = np.cos(angles), np.sin(angles)
    return (np.concatenate([cos, cos], 1).astype(np.float32),
            np.concatenate([-sin, sin], 1).astype(np.float32))


def per_device(
    embeds, targets, lengths, source, attn_gain, w_query, w_key, w_value, w_out, final_gain, head
):
    vocab = head.shape[0]
    cos, sin = tables()
    vmem = pl.BlockSpec(memory_space=pltpu.VMEM)
    hbm = pl.BlockSpec(memory_space=pl.ANY)
    smem = pl.BlockSpec(memory_space=pltpu.SMEM)
    dma = pltpu.SemaphoreType.DMA
    stats = pl.pallas_call(
        kernel,
        out_shape=jax.ShapeDtypeStruct((2, 2, 32), F32),
        in_specs=[hbm, smem, smem] + [hbm] * 10,
        out_specs=vmem,
        scratch_shapes=[
            pltpu.VMEM((2, 4, D), BF),
            pltpu.VMEM((8, 32), jnp.int32),
            pltpu.VMEM((1, D), F32),
            pltpu.VMEM((1, D), F32),
            pltpu.VMEM((ROWS, HD), F32),
            pltpu.VMEM((ROWS, HD), F32),
            pltpu.VMEM((2, 16, 256, 768), BF),
            pltpu.VMEM((QW, 2048), BF),
            pltpu.VMEM((2, 4, vocab, 1024), BF),
            pltpu.VMEM((2, NM, 16, 2048), BF),
            pltpu.VMEM((NY, NM, ROWS, 256), BF),
            pltpu.VMEM((NY, NZ, ROWS, 256), BF),
            pltpu.VMEM((NY, ROWS, 256), BF),
            pltpu.VMEM((4 * ROWS, ROWS), F32),
            pltpu.VMEM((ROWS, 128), F32),
            pltpu.VMEM((2, ROWS, 896), F32),
            pltpu.VMEM((ROWS, 896), F32),
            pltpu.VMEM((NY, ROWS, 256), BF),
            pltpu.VMEM((NY, ROWS, QW), BF),
            pltpu.VMEM((NY, NZ, ROWS, 256), BF),
            pltpu.VMEM((NY, NZ, ROWS, 256), BF),
            pltpu.VMEM((NY, NZ, ROWS, 256), F32),
            pltpu.VMEM((NY, NZ, ROWS, 256), BF),
            pltpu.VMEM((NY, NZ, ROWS, 256), BF),
            pltpu.VMEM((NY, ROWS, 256), BF),
            pltpu.VMEM((2, 4, 4, 4, ROWS, 256), BF),
            pltpu.VMEM((2, 2, vocab + 8, 256), F32),
            pltpu.VMEM((2, vocab + 8, 256), F32),
            pltpu.VMEM((2, NY, ROWS, 128), F32),
            pltpu.VMEM((8, 256), F32),
            pltpu.VMEM((2, 256, 32), BF),
            pltpu.VMEM((16, 128), F32),
            pltpu.VMEM((NX * NY, 16, 128), F32),
            pltpu.VMEM((NM, 16, 128), F32),
            dma((20,)),
            dma((4,)), dma((4,)),
            dma((2,)), dma((2,)),
            dma, dma,
            dma((2, 8)), dma((2, 8)),
            dma((5,)), dma((5,)),
            dma((4, 8)), dma((4, 8)),
            dma((4,)), dma((4,)),
            dma((4,)), dma((4,)),
            dma((4,)), dma((4,)),
            dma((4, 4)), dma((4, 4)),
            dma((2, 4, 22)), dma((2, 4, 19)),
            dma((2, 16)), dma((2, 16)),
        ],
        compiler_params=pltpu.CompilerParams(
            collective_id=0, has_side_effects=True, vmem_limit_bytes=60 * 1024 * 1024),
        cost_estimate=pl.CostEstimate(flops=8_000_000_000, bytes_accessed=24_000_000,
                                      transcendentals=300_000),
    )(
        embeds, lengths, source, targets, attn_gain, final_gain.reshape(1, D), jnp.asarray(cos), jnp.asarray(sin),
        w_query.reshape(16, 2, 256, 512), w_key.reshape(16, 2, 256, 128),
        w_value.reshape(16, 2, 256, 128), w_out.reshape(512, 2048), head,
    )
    return (stats[0], stats[1])


def solution(mesh):
    return jax.shard_map(
        per_device,
        mesh=mesh,
        in_specs=(
            P("dp", "mp", None),
            P(),
            P(),
            P(),
            P("section", None),
            P("section", None, "mp"),
            P("section", None, "mp"),
            P("section", None, "mp"),
            P("section", "mp", "dp"),
            P(),
            P(("dp", "section", "mp"), None),
        ),
        out_specs=(P("dp", None), P("dp", None)),
        check_vma=False,
    )
```

```python
import jax
import jax.numpy as jnp
import numpy as np
from jax import lax
from jax.experimental import pallas as pl
from jax.experimental.pallas import tpu as pltpu
from jax.sharding import PartitionSpec as P

HD = 128
EPS = 1e-05
ROPE_BASE = 500000.0
NY = 4
NX = 4
NZ = 4
NM = 8
ROWS = 64
D = 8192
QW = 512
VOCAB_DEV = 512
MESH = pl.DeviceIdType.MESH
BF = jnp.bfloat16
F32 = jnp.float32


def lane(start, size):
    return pl.ds(pl.multiple_of(start, 128), size)


def kernel(
    emb_in, live, source_of, targets_in, gain, fgain_in, cosine_in, sine_in, wq, wk, wv, wo, head,
    out,
    emb, targets, gains, fgain, cosine, sine, W, WO, HEAD, EB, XE, X, RX, MASK, SS, QA, QR, R, C, PS, PR, PO, ZS, ZR, HP, Y, LT, LR, SQ, WANT, TAKE, STO, SA, SB,
    w_sem, sw_s, sw_r, lt_s, lt_r, qr_s, qr_r, eb_s, eb_r, hop_s, hop_r, ag_s, ag_r, res_s, res_r, ctx_s, ctx_r, ps_s, ps_r,
    zz_s, zz_r, y_s, y_r, st_s, st_r,
):
    d = lax.axis_index("dp")
    s = lax.axis_index("section")
    m = lax.axis_index("mp")
    z = m // 2
    c = m % 2
    sib = z * 2 + (1 - c)

    def ypeer(k):
        return (d + k) % NY

    def zpeer(k):
        return ((z + k) % NZ) * 2 + c

    def zother(k):
        return ((z + k) % NZ) * 2 + (1 - c)

    def rcopy(src, dst, ssem, rsem, dev):
        return pltpu.make_async_remote_copy(
            src_ref=src, dst_ref=dst, send_sem=ssem, recv_sem=rsem,
            device_id=dev, device_id_type=MESH,
        )

    here = (d, s, sib)

    barrier = pltpu.get_barrier_semaphore()
    partners = []
    for k in range(1, 4):
        partners.append((ypeer(k), s, m))
        partners.append((d, (s + k) % NX, m))
        partners.append((d, s, zpeer(k)))
        partners.append((d, s, zother(k)))
        partners.append((ypeer(k), (s + 1) % NX, m))
        partners.append((ypeer(k), (s + 3) % NX, m))
        partners.append((ypeer(k), (s + 2) % NX, m))
    for k in (1, 3):
        partners.append((d, (s + k) % NX, zpeer(2)))
    partners.append(here)
    for dev in partners:
        pl.semaphore_signal(barrier, inc=1, device_id=dev, device_id_type=MESH)
    small = [
        pltpu.make_async_copy(src, dst, w_sem.at[14 + n])
        for n, (src, dst) in enumerate((
            (emb_in, emb), (gain, gains), (cosine_in, cosine), (sine_in, sine),
            (fgain_in, fgain), (targets_in, targets)))
    ]
    for copy in small:
        copy.start()
    parts = ((wq, pl.ds(0, 512)), (wk, pl.ds(512, 128)), (wv, pl.ds(640, 128)))

    def load(n, first):
        src, lanes = parts[n]
        take = 1 if first else jnp.where(s == 0, 0, c)
        return pltpu.make_async_copy(src.at[:, take], W.at[first, :, :, lanes],
                                     w_sem.at[3 * first + n])

    def swap(n):
        src, lanes = parts[n]
        return rcopy(src.at[:, 1 - c], W.at[1, :, :, lanes], sw_s.at[n], sw_r.at[n], here)

    wo_load = pltpu.make_async_copy(wo, WO, w_sem.at[12])
    @pl.when(s > 0)
    def _():
        for n in range(3):
            load(n, 0).start()

    head_load = pltpu.make_async_copy(HEAD.at[0], HEAD.at[0], w_sem.at[13])
    head_swap = rcopy(HEAD.at[1], HEAD.at[1], sw_s.at[3], sw_r.at[3], here)

    def off(n):
        return jnp.where(n == 0, 0, jnp.where(n == 1, 3, jnp.where(n == 2, 1, 2)))

    def slot_columns(core, j, i):
        g = jnp.where(core == 0, off(i), off(j))
        zz = jnp.where(core == 0, off(j), off(i))
        return lane(((d + g) % NY) * 2048 + ((z + zz) % NZ) * 512 + core * 256, 256)

    def row_slot(lanes):
        return (lanes // 64) * 2 + (lanes // 4) % 2, ((lanes // 8) % 8) * 4 + lanes % 4

    def wanted_rows():
        slot, position = row_slot(lax.broadcasted_iota(jnp.int32, (32, 256), 1))
        place = (position == lax.broadcasted_iota(jnp.int32, (32, 256), 0)).astype(BF)
        tokens = targets[...]
        keep = slot[0:8] == lax.broadcasted_iota(jnp.int32, (8, 256), 0)
        parts = []
        for term in (tokens // 256, tokens % 256):
            every = jnp.dot(term.astype(F32).astype(BF), place, preferred_element_type=F32)
            parts.append(jnp.sum(jnp.where(keep, every, 0.0), axis=0, keepdims=True))
        return parts[0] * 256.0 + parts[1]

    def head_start():
        for j in range(4):
            for i in range(4):
                there = pl.ds(i * 256, 256)
                pltpu.make_async_copy(head.at[:, slot_columns(c, j, i)], HEAD.at[0, j, :, there],
                                      w_sem.at[13]).start()
                rcopy(head.at[:, slot_columns(1 - c, j, i)], HEAD.at[1, j, :, there],
                      sw_s.at[3], sw_r.at[3], here).start()
    def prepare():
        @pl.when(s > 0)
        def _():
            wo_load.start()
            head_start()

        shape = (4 * ROWS, ROWS)
        rq = lax.broadcasted_iota(jnp.int32, shape, 0) % ROWS
        rk = lax.broadcasted_iota(jnp.int32, shape, 1)
        slot_q, slot_k = (rq // 4) % 2, (rk // 4) % 2
        pos_q, pos_k = (rq // 8) * 4 + rq % 4, (rk // 8) * 4 + rk % 4
        live_k = jnp.where(slot_k == 0, live[2 * d], live[2 * d + 1])
        allowed = (slot_q == slot_k) & (pos_k <= pos_q) & (pos_k < live_k)
        MASK[...] = jnp.where(allowed, F32(0.0), F32(-1e30))

        @pl.when(s > 0)
        def _():
            for n in range(3):
                load(n, 0).wait()
                swap(n).wait_recv()
            for copy in small[1:2]:
                copy.wait()
            diagonal = (lax.broadcasted_iota(jnp.int32, (256, 256), 0)
                        == lax.broadcasted_iota(jnp.int32, (256, 256), 1))

            def scale(i, _):
                cols = lane((i // NZ) * 2048 + ((i % NZ) * 2 + c) * 256, 256)
                column = jnp.sum(jnp.where(diagonal, gains[:, cols], 0.0), axis=1, keepdims=True)
                for which in range(2):
                    W.at[which, i][...] = (W[which, i].astype(F32) * column).astype(BF)
                return 0

            lax.fori_loop(0, 16, scale, 0)

        @pl.when(s == 0)
        def _():
            for copy in small[1:2]:
                copy.wait()
        for copy in small[2:]:
            copy.wait()

        WANT[...] = jnp.broadcast_to(wanted_rows(), WANT.shape)
        slot, position = row_slot(lax.broadcasted_iota(jnp.int32, (256, 32), 0))
        place = lax.broadcasted_iota(jnp.int32, (256, 32), 1)
        for i in range(2):
            chosen = source_of[2 * d + i]
            TAKE.at[i][...] = ((slot == chosen) & (position == place)
                               & (place < live[chosen])).astype(F32).astype(BF)

        @pl.when(s > 0)
        def _():
            scale_head()

    def scale_head():
        head_load.wait()
        head_swap.wait_recv()

        def scale(n, _):
            cc, j, i = n // 16, (n // 4) % 4, n % 4
            block = HEAD.at[cc, j, :, lane(i * 256, 256)]
            block[...] = (block[...].astype(F32) * fgain[:, slot_columns(c, j, i)]).astype(BF)
            return 0

        lax.fori_loop(0, 32, scale, 0)

    small[0].wait()

    far_sender = s == jnp.where(c == 0, 1, 3)

    @pl.when((s == 0) | far_sender)
    def _():
        rows = jnp.concatenate([emb[0], emb[1]], axis=0).astype(F32)
        for q in range(2):
            EB.at[q, m][...] = jnp.concatenate(
                [rows[:, q * 2048:q * 2048 + 2048], rows[:, q * 2048 + 4096:q * 2048 + 6144]],
                axis=0).astype(BF)

    pl.semaphore_wait(barrier, len(partners))

    @pl.when(s > 0)
    def _():
        for n in range(3):
            swap(n).start()

    def eb_z(q, k):
        return rcopy(EB.at[q, m], EB.at[q, m], eb_s.at[q, k], eb_r.at[q, m], (d, 0, zpeer(k)))

    def eb_z_in(q, k):
        mk = zpeer(k)
        return rcopy(EB.at[q, mk], EB.at[q, mk], eb_s.at[q, k], eb_r.at[q, mk], here)

    def eb_fwd(q, k):
        mk = zpeer(k)
        return rcopy(EB.at[q, mk], EB.at[q, mk], eb_s.at[q, 4 + k], eb_r.at[q, mk], here)

    def eb_sib_in(q, k):
        mk = zother(k)
        return rcopy(EB.at[q, mk], EB.at[q, mk], eb_s.at[q, 4 + k], eb_r.at[q, mk], here)

    def hop(g):
        return rcopy(HP.at[g], X.at[d, z], hop_s.at[g], hop_r.at[d], (g, (s + 1) % NX, m))

    def hop_in(g):
        return rcopy(HP.at[g], X.at[g, z], hop_s.at[g], hop_r.at[g], here)

    def hop_raw():
        return rcopy(HP, R, hop_s.at[4], hop_r.at[4], (d, (s + 1) % NX, m))

    def ag_z(g, k):
        return rcopy(X.at[g, z], X.at[g, z], ag_s.at[g, k], ag_r.at[g, z], (d, s, zpeer(k)))

    def ag_z_in(g, k):
        zk = (z + k) % NZ
        return rcopy(X.at[g, zk], X.at[g, zk], ag_s.at[g, k], ag_r.at[g, zk], here)

    def sums_out():
        return rcopy(QA.at[1], QR, qr_s, qr_r, here)

    def res(k):
        g = ypeer(k)
        return rcopy(RX.at[g], R.at[d], res_s.at[k], res_r.at[d], (g, s, m))

    def res_in(k):
        g = ypeer(k)
        return rcopy(RX.at[g], R.at[g], res_s.at[k], res_r.at[g], here)

    def ctx(k):
        return rcopy(C.at[d], C.at[d], ctx_s.at[k], ctx_r.at[d], (ypeer(k), s, m))

    def ctx_in(k):
        g = ypeer(k)
        return rcopy(C.at[g], C.at[g], ctx_s.at[k], ctx_r.at[g], here)

    def part(g):
        return rcopy(PS.at[g], PR.at[g], ps_s.at[g], ps_r.at[g], here)

    def zred(g, k):
        return rcopy(ZS.at[g, k], ZR.at[g, k], zz_s.at[g, k], zz_r.at[g, k], (d, s, zpeer(k)))

    def layer():
        def multiply(x, which, rows, n, start=False):
            w = W[which, pl.ds(rows * NZ, NZ)].reshape(4 * 256, 768)
            term = jnp.dot(x, w, preferred_element_type=F32)
            QA.at[n][:, 0:768] = term if start else QA[n, :, 0:768] + term

        @pl.when(s == 0)
        def _():
            for q in range(2):
                for k in (1, 3, 2):
                    eb_z_in(q, k).wait_recv()
                    eb_fwd(q, k).start()
            QA[...] = jnp.zeros_like(QA)
            QR[...] = jnp.zeros_like(QR)
            SS[...] = jnp.zeros_like(SS)
            for q in range(2):
                for k in range(4):
                    eb_sib_in(q, k).wait_recv()

                def blocks(mm):
                    x = EB[q, :, :, lane(mm * 256, 256)].astype(F32)
                    return [x[:, i * 8:i * 8 + 8, :].reshape(ROWS, 256) for i in range(2)]

                def body(mm, total):
                    for half, xs in enumerate(blocks(mm)):
                        g = half * 2 + q
                        cols = lane(g * 2048 + mm * 256, 256)
                        XE.at[g, mm][...] = (xs * gains[:, cols]).astype(BF)
                        square = xs * xs
                        total = total + square[:, 0:128] + square[:, 128:256]
                    return total

                SS[...] = lax.fori_loop(0, NM, body, SS[...])
                for half, xs in enumerate(blocks(m)):
                    RX.at[half * 2 + q][...] = xs.astype(BF)
                if q == 0:
                    for n in range(3):
                        load(n, 0).wait()
                        load(n, 1).wait()

                def both(i, _):
                    g = 2 * i + q
                    for who in range(2):
                        x = jnp.concatenate([XE[g, 2 * zz + who] for zz in range(NZ)], axis=1)
                        multiply(x, who, g, 0)
                    return 0

                lax.fori_loop(0, 2, both, 0)
            for k in (2, 1, 3):
                res(k).start()
            R.at[d][...] = RX[d]

        @pl.when(s > 0)
        def _():
            def arrived(k):
                g = ypeer(k)
                hop_in(g).wait_recv()
                for j in (2, 1, 3):
                    ag_z(g, j).start()

            def columns(k):
                g = ypeer(k)
                for j in (1, 3, 2):
                    ag_z_in(g, j).wait_recv()
                return jnp.concatenate([X[g, zz] for zz in range(NZ)], axis=1)

            def both(k, start=False):
                x = columns(k)
                multiply(x, 1, ypeer(k), 1, start)
                multiply(x, 0, ypeer(k), 0, start)

            def squares_of(k):
                total = jnp.zeros((ROWS, 128), F32)
                for zz in range(NZ):
                    x = X[ypeer(k), zz].astype(F32)
                    square = x * x
                    total = total + square[:, 0:128] + square[:, 128:256]
                return total

            arrived(0)
            arrived(3)
            arrived(1)
            arrived(2)
            both(0, True)
            squares = squares_of(0)
            both(3)
            squares = squares + squares_of(3)
            both(1)
            squares = squares + squares_of(1)
            x = columns(2)
            multiply(x, 1, ypeer(2), 1)
            squares = squares + squares_of(2)
            QA.at[1][:, 768:896] = squares
            sums_out().start()
            multiply(x, 0, ypeer(2), 0)
            sums_out().wait_recv()
            SS[...] = squares + QR[:, 768:896]

        r = lax.rsqrt(jnp.sum(SS[...], axis=1, keepdims=True) * (1.0 / D) + EPS)
        cos = cosine[...]
        sin = sine[...]

        def summed(first, last):
            return QA[0, :, first:last] + QR[:, first:last]

        def rope(x):
            return (x * cos + pltpu.roll(x, 64, 1) * sin).astype(BF)

        query = jnp.concatenate(
            [rope(summed(j * HD, (j + 1) * HD) * r) for j in range(4)], axis=0)
        key = rope(summed(512, 640) * r)
        value = (summed(640, 768) * r).astype(BF)
        scores = lax.dot_general(query, key, (((1,), (1,)), ((), ())),
                                 preferred_element_type=F32) * (HD ** -0.5)
        scores = scores + MASK[...]
        highest = jnp.max(scores, axis=-1, keepdims=True)
        weights = jnp.exp(scores - highest)
        probs = (weights / jnp.sum(weights, axis=-1, keepdims=True)).astype(BF)
        mixed = jnp.dot(probs, value, preferred_element_type=F32).astype(BF)
        for j in range(4):
            C.at[d][:, j * HD:(j + 1) * HD] = mixed[j * ROWS:(j + 1) * ROWS]
        for k in (2, 1, 3):
            ctx(k).start()

        wo_load.wait()

        def project(g):
            for zz in range(NZ):
                p = jnp.dot(C[g], WO[:, zz * 512:zz * 512 + 512], preferred_element_type=F32)
                low, high = p[:, :256], p[:, 256:]
                PO.at[g, zz][...] = jnp.where(c == 0, low, high)
                PS.at[g, zz][...] = jnp.where(c == 0, high, low).astype(BF)
            part(g).start()

        def pair(g):
            part(g).wait_recv()
            for k in (2, 1, 3):
                zt = (z + k) % NZ
                ZS.at[g, k][...] = (PO[g, zt] + PR[g, zt].astype(F32)).astype(BF)
                zred(g, k).start()

        def total_of(g):
            total = PO[g, z] + PR[g, z].astype(F32) + R[g].astype(F32)
            for k in (1, 3, 2):
                zred(g, k).wait_recv()
                total = total + ZR[g, k].astype(F32)
            HP.at[g][...] = total.astype(BF)

            @pl.when(s < NX - 1)
            def _():
                hop(g).start()

        project(d)

        @pl.when(s == 0)
        def _():
            for k in (1, 3, 2):
                res_in(k).wait_recv()

        @pl.when(s > 0)
        def _():
            hop_raw().wait_recv()

        pair(d)
        for k in (1, 3):
            ctx_in(k).wait_recv()
            project(ypeer(k))
        pair(ypeer(1))
        pair(ypeer(3))
        def in_last(do):
            @pl.when(s == NX - 1)
            def _():
                do()

        total_of(d)
        in_last(lambda: own_x(1, 0))
        ctx_in(2).wait_recv()
        project(ypeer(2))
        total_of(ypeer(1))
        in_last(lambda: own_x(1, 1))
        pair(ypeer(2))

        def first_two():
            spread(1, 0)
            spread(1, 1)

        in_last(first_two)
        total_of(ypeer(3))

        def third():
            own_x(1, 2)
            spread(1, 2)

        in_last(third)
        total_of(ypeer(2))

        def rest():
            own_x(1, 3)
            spread(1, 3)
            for k in range(3):
                stage_first(1, k)
            for k in range(2):
                stage_second(1, k)

        in_last(rest)

        @pl.when(s < NX - 1)
        def _():
            hop_raw().start()

        @pl.when(s == 1)
        def _():
            def body(k, _):
                own_x(0, k)
                spread(0, k)
                return 0

            lax.fori_loop(0, 4, body, 0)

    def first_dev(k):
        return (jnp.where(c == 0, ypeer(k), d), s, jnp.where(c == 0, m, zpeer(k)))

    def second_dev(k):
        return (jnp.where(c == 0, d, ypeer(k)), s, jnp.where(c == 0, zpeer(k), m))

    def ycopy(src, dst, b, k, i, j, dev):
        return rcopy(src, dst, y_s.at[b, k, i], y_r.at[b, k, j], dev)

    def y_x(b, k, n):
        ref = Y.at[b, k, 0, 0]
        return ycopy(ref, ref, b, k, n, 0, (d, (s + n) % NX, m))

    def y_first(b, k, n):
        slot = (1, 3, 2)[n - 1]
        return ycopy(Y.at[b, k, 0, 0], Y.at[b, k, 0, slot], b, k, 3 + n, slot, first_dev(n))

    sets = (pl.ds(0, 1), pl.ds(1, 2), pl.ds(3, 1))

    def y_second(b, k, part_no, n):
        slot = 1 if n == 1 else 2
        return ycopy(Y.at[b, k, 0, sets[part_no]], Y.at[b, k, slot, sets[part_no]], b, k,
                     7 + part_no * 2 + (slot - 1), 1 + 3 * slot + part_no, second_dev(n))

    def y_relay(b, k, half):
        slot, n = ((1, 1), (2, 3))[half]
        two = pl.ds(2 * half, 2)
        return ycopy(Y.at[b, k, slot, two], Y.at[b, k, 3, two], b, k, 13 + half, 10 + half,
                     second_dev(n))

    def chunk_order(step):
        return jnp.where(step == 3, 2, jnp.where(step == 2, 3, step))

    def own_x(b, k):
        Y.at[b, k, 0, 0][...] = HP[(d + chunk_order(k)) % NY]
        for n in (2, 1, 3):
            y_x(b, k, n).start()

    def spread(b, k):
        for n in (2, 1, 3):
            y_first(b, k, n).start()
        for n in (1, 3):
            y_second(b, k, 0, n).start()

    def stage_first(b, k):
        y_first(b, k, 1).wait_recv()
        y_first(b, k, 3).wait_recv()
        for n in (1, 3):
            y_second(b, k, 1, n).start()
        y_first(b, k, 2).wait_recv()
        for n in (1, 3):
            y_second(b, k, 2, n).start()

    def stage_second(b, k):
        for part_no in (0, 1):
            y_second(b, k, part_no, 1).wait_recv()
        y_relay(b, k, 0).start()
        for part_no in (1, 2):
            y_second(b, k, part_no, 3).wait_recv()
        y_relay(b, k, 1).start()
        y_second(b, k, 2, 1).wait_recv()
        y_second(b, k, 0, 3).wait_recv()

    def opposite(b, k):
        for half in range(2):
            y_relay(b, k, half).wait_recv()

    def dots(b, j, send=False):
        blocks = []
        for g in range(NY):
            row = []
            total = jnp.zeros((ROWS, 128), F32)
            for i in range(4):
                sender = (d + jnp.where(c == 0, (0, 3, 1, 2)[i], off(j))) % NY
                k = chunk_order((g - sender + NY) % NY)
                x = Y[b, k, j, i]
                row.append(x)
                wide = x.astype(F32)
                square = wide * wide
                total = total + square[:, 0:128] + square[:, 128:256]
            SQ.at[b, g][...] += total
            blocks.append(jnp.concatenate(row, axis=1))
        pieces = jnp.concatenate(blocks, axis=0)
        for which in (1, 0):
            LT.at[b, which][0:VOCAB_DEV, :] += lax.dot_general(
                HEAD[which, j], pieces, (((1,), (1,)), ((), ())), preferred_element_type=F32)
            if send and which == 1:
                exchange(b)

    def swap_logits(b):
        return rcopy(LT.at[b, 1], LR.at[b], lt_s.at[b], lt_r.at[b], here)

    def exchange(b):
        squares = SQ[b].reshape(NY * ROWS, 128)
        top = squares.astype(BF)
        rest = (squares - top.astype(F32)).astype(BF)
        ones = jnp.ones((16, 128), BF)
        nt = (((1,), (1,)), ((), ()))
        sums = (lax.dot_general(ones, top, nt, preferred_element_type=F32)
                + lax.dot_general(ones, rest, nt, preferred_element_type=F32))
        LT.at[b, 1][VOCAB_DEV:VOCAB_DEV + 8, :] = sums[0:8]
        swap_logits(b).start()

    def layer_sent():
        @pl.when(far_sender)
        def _():
            for q in range(2):
                eb_z(q, 2).wait_send()

        @pl.when(s == 0)
        def _():
            for q in range(2):
                for k in (1, 3):
                    eb_z(q, k).wait_send()
                for k in range(4):
                    eb_fwd(q, k).wait_send()
            for k in range(1, 4):
                res(k).wait_send()

        @pl.when(s > 0)
        def _():
            for g in range(NY):
                for k in range(1, 4):
                    ag_z(g, k).wait_send()
            sums_out().wait_send()
            for n in range(3):
                swap(n).wait_send()

        @pl.when(s < NX - 1)
        def _():
            for g in range(NY):
                hop(g).wait_send()
            hop_raw().wait_send()

        for g in range(NY):
            for k in range(1, 4):
                zred(g, k).wait_send()
            part(g).wait_send()
        for k in range(1, 4):
            ctx(k).wait_send()

    def chunk_sent(b, k, source):
        @pl.when(s == source)
        def _():
            for j in (1, 2, 3):
                y_x(b, k, j).wait_send()

        for j in (1, 2, 3):
            y_first(b, k, j).wait_send()
        for j in (1, 3):
            for part_no in range(3):
                y_second(b, k, part_no, j).wait_send()
        for half in range(2):
            y_relay(b, k, half).wait_send()

    def each(count, do):
        def body(k, _):
            do(k)
            return 0

        lax.fori_loop(0, count, body, 0)

    def exit_dots(n):
        dots(0, n)

    def gather(b):
        source = 2 * b + 1
        final = (b == 1) & (s == NX - 1)
        others = jnp.logical_not(final)

        def body(t, _):
            @pl.when((t < 4) & (s != source))
            def _():
                y_x(b, t, 1).wait_recv()
                spread(b, t)

            @pl.when((t >= 1) & (t < 5) & ((t == 4) | others))
            def _():
                stage_first(b, t - 1)

            @pl.when((t >= 2) & (t < 6) & ((t >= 4) | others))
            def _():
                stage_second(b, t - 2)

            @pl.when((t >= 3) & ((b == 0) | (t < 6)) & others)
            def _():
                opposite(b, t - 3)

            @pl.when((b == 1) & (s == 2) & (t >= 2) & (t < 6))
            def _():
                exit_dots(t - 2)

            @pl.when((b == 1) & (s == 2) & (t == 6))
            def _():
                exchange(0)
            return 0

        lax.fori_loop(0, 7, body, 0)

        @pl.when(final)
        def _():
            each(3, lambda k: opposite(1, k))
            each(4, exit_dots)
            exchange(0)

    def finish(b):
        @pl.when(b == 0)
        def _():
            each(4, exit_dots)
            exchange(0)

        @pl.when(b == 1)
        def _():
            for j in range(3):
                dots(1, j)
            opposite(1, 3)
            dots(1, 3, True)

            @pl.when(s >= 2)
            def _():
                softmax(0)

        softmax(b)

    def softmax(b):
        swap_logits(b).wait_recv()
        last = pl.ds(VOCAB_DEV, 8)
        sums = (LT[b, 1, last] + LR[b, last])[0:1]
        r = lax.rsqrt(sums * (1.0 / D) + EPS)
        logits = (LT[b, 0, 0:VOCAB_DEV] + LR[b, 0:VOCAB_DEV]) * r
        highest = jnp.max(logits, axis=0, keepdims=True)
        summed = jnp.sum(jnp.exp(logits - highest), axis=0, keepdims=True)
        first = ((d * NX + s) * NM + m) * VOCAB_DEV
        index = (lax.broadcasted_iota(jnp.int32, logits.shape, 0) + first).astype(F32)
        wanted = WANT[0:1, :]
        picked = jnp.sum(jnp.where(index == wanted, logits, 0.0), axis=0, keepdims=True)
        for n, value in enumerate((highest, summed, picked)):
            for half in range(2):
                STO[pl.ds(n * 4 + b * 2 + half, 1), :] = value[:, half * 128:half * 128 + 128]

    def step(t, _):
        last = s == NX - 1
        place = jnp.where(last, 1, 0)

        @pl.when(t == place)
        def _():
            layer()

            @pl.when(s == 0)
            def _():
                head_start()

        @pl.when(jnp.where(last, (t == 0) | (t == 2), (t == 1) | (t == jnp.where(s < 2, 3, 2))))
        def _():
            gather(jnp.where((t == 0) | (t == 1), 0, 1))

        @pl.when((t == 4) | ((t == 2) & (s < 2)))
        def _():
            @pl.when((t == 2) & (s == 0))
            def _():
                scale_head()
            finish(jnp.where(t == 4, 1, 0))
        return 0

    @pl.when(far_sender)
    def _():
        for q in range(2):
            eb_z(q, 2).start()

    @pl.when(s == 0)
    def _():
        for q in range(2):
            for k in (1, 3, 0):
                (eb_z(q, k) if k else eb_fwd(q, 0)).start()
        for n in range(3):
            load(n, 0).start()
            load(n, 1).start()
        wo_load.start()

    prepare()
    STO[...] = jnp.zeros_like(STO)
    SQ[...] = jnp.zeros_like(SQ)
    LT[...] = jnp.zeros_like(LT)
    lax.fori_loop(0, 5, step, 0)

    def merge(ref, count):
        parts = [ref[j] for j in range(count)]
        highest = parts[0][0:4]
        for p in parts[1:]:
            highest = jnp.maximum(highest, p[0:4])
        summed = jnp.zeros_like(highest)
        picked = jnp.zeros_like(highest)
        for p in parts:
            summed = summed + p[4:8] * jnp.exp(p[0:4] - highest)
            picked = picked + p[8:12]
        return highest, summed, picked

    def stacked(highest, summed, picked):
        return jnp.concatenate([highest, summed, picked, jnp.zeros_like(picked)], axis=0)

    pairs = [(j, k) for j in range(NX) for k in range(NY) if j or k]

    def st_yx(n):
        j, k = pairs[n]
        mine = s * NY + d
        return rcopy(SA.at[mine], SA.at[mine], st_s.at[0, n], st_r.at[0, mine],
                     (ypeer(k), (s + j) % NX, m))

    def st_yx_in(n):
        j, k = pairs[n]
        other = ((s + j) % NX) * NY + ypeer(k)
        return rcopy(SA.at[other], SA.at[other], st_s.at[0, n], st_r.at[0, other], here)

    def m_of(k):
        return (m + k) % NM

    def st_m(k):
        return rcopy(SB.at[m], SB.at[m], st_s.at[1, k], st_r.at[1, m], (d, s, m_of(k)))

    def st_m_in(k):
        mm = m_of(k)
        return rcopy(SB.at[mm], SB.at[mm], st_s.at[1, k], st_r.at[1, mm], (d, s, mm))

    SA.at[s * NY + d][...] = STO[...]
    for n in range(15):
        st_yx(n).start()
    layer_sent()
    head_swap.wait_send()
    swap_logits(0).wait_send()
    swap_logits(1).wait_send()
    each(4, lambda k: chunk_sent(0, k, 1))
    each(4, lambda k: chunk_sent(1, k, NX - 1))
    for n in range(15):
        st_yx_in(n).wait_recv()
    SB.at[m][...] = stacked(*merge(SA, NX * NY))
    for k in (4, 3, 5, 2, 6, 1, 7):
        st_m(k).start()
    for n in range(15):
        st_yx(n).wait_send()
    for k in (1, 7, 2, 6, 3, 5, 4):
        st_m_in(k).wait_recv()
    highest, summed, picked = merge(SB, NM)
    logprob = picked - (highest + jnp.log(summed))
    terms = []
    for e in range(2):
        rest = jnp.concatenate([logprob[2 * e:2 * e + 1], logprob[2 * e + 1:2 * e + 2]], axis=1)
        for _ in range(3):
            term = rest.astype(BF).astype(F32)
            terms.append(term)
            rest = rest - term
    row = lax.broadcasted_iota(jnp.int32, (16, 256), 0)
    stack = jnp.zeros((16, 256), F32)
    for j, term in enumerate(terms):
        stack = jnp.where(row == j, term, stack)
    stack = stack.astype(BF)
    results = []
    for i in range(2):
        got = jnp.dot(stack, TAKE[i], preferred_element_type=F32)
        results.append([got[j:j + 1] + got[j + 1:j + 2] + got[j + 2:j + 3] for j in (0, 3)])
    for e in range(2):
        first = lax.broadcasted_iota(jnp.int32, (2, 32), 0) == 0
        out.at[e][...] = jnp.where(first, results[0][e], results[1][e])
    for k in range(1, 8):
        st_m(k).wait_send()


def tables():
    row = np.arange(ROWS)
    position = (row // 8) * 4 + row % 4
    half = HD // 2
    freqs = (ROPE_BASE ** (-np.arange(half) * 2.0 / HD)).astype(np.float32)
    angles = (position.astype(np.float32)[:, None] * freqs[None, :]).astype(np.float64)
    cos, sin = np.cos(angles), np.sin(angles)
    return (np.concatenate([cos, cos], 1).astype(np.float32),
            np.concatenate([-sin, sin], 1).astype(np.float32))


def per_device(
    embeds, targets, lengths, source, attn_gain, w_query, w_key, w_value, w_out, final_gain, head
):
    vocab = head.shape[0]
    cos, sin = tables()
    vmem = pl.BlockSpec(memory_space=pltpu.VMEM)
    hbm = pl.BlockSpec(memory_space=pl.ANY)
    smem = pl.BlockSpec(memory_space=pltpu.SMEM)
    dma = pltpu.SemaphoreType.DMA
    stats = pl.pallas_call(
        kernel,
        out_shape=jax.ShapeDtypeStruct((2, 2, 32), F32),
        in_specs=[hbm, smem, smem] + [hbm] * 10,
        out_specs=vmem,
        scratch_shapes=[
            pltpu.VMEM((2, 4, D), BF),
            pltpu.VMEM((8, 32), jnp.int32),
            pltpu.VMEM((1, D), F32),
            pltpu.VMEM((1, D), F32),
            pltpu.VMEM((ROWS, HD), F32),
            pltpu.VMEM((ROWS, HD), F32),
            pltpu.VMEM((2, 16, 256, 768), BF),
            pltpu.VMEM((QW, 2048), BF),
            pltpu.VMEM((2, 4, vocab, 1024), BF),
            pltpu.VMEM((2, NM, 16, 2048), BF),
            pltpu.VMEM((NY, NM, ROWS, 256), BF),
            pltpu.VMEM((NY, NZ, ROWS, 256), BF),
            pltpu.VMEM((NY, ROWS, 256), BF),
            pltpu.VMEM((4 * ROWS, ROWS), F32),
            pltpu.VMEM((ROWS, 128), F32),
            pltpu.VMEM((2, ROWS, 896), F32),
            pltpu.VMEM((ROWS, 896), F32),
            pltpu.VMEM((NY, ROWS, 256), BF),
            pltpu.VMEM((NY, ROWS, QW), BF),
            pltpu.VMEM((NY, NZ, ROWS, 256), BF),
            pltpu.VMEM((NY, NZ, ROWS, 256), BF),
            pltpu.VMEM((NY, NZ, ROWS, 256), F32),
            pltpu.VMEM((NY, NZ, ROWS, 256), BF),
            pltpu.VMEM((NY, NZ, ROWS, 256), BF),
            pltpu.VMEM((NY, ROWS, 256), BF),
            pltpu.VMEM((2, 4, 4, 4, ROWS, 256), BF),
            pltpu.VMEM((2, 2, vocab + 8, 256), F32),
            pltpu.VMEM((2, vocab + 8, 256), F32),
            pltpu.VMEM((2, NY, ROWS, 128), F32),
            pltpu.VMEM((8, 256), F32),
            pltpu.VMEM((2, 256, 32), BF),
            pltpu.VMEM((16, 128), F32),
            pltpu.VMEM((NX * NY, 16, 128), F32),
            pltpu.VMEM((NM, 16, 128), F32),
            dma((20,)),
            dma((4,)), dma((4,)),
            dma((2,)), dma((2,)),
            dma, dma,
            dma((2, 8)), dma((2, 8)),
            dma((5,)), dma((5,)),
            dma((4, 8)), dma((4, 8)),
            dma((4,)), dma((4,)),
            dma((4,)), dma((4,)),
            dma((4,)), dma((4,)),
            dma((4, 4)), dma((4, 4)),
            dma((2, 4, 22)), dma((2, 4, 19)),
            dma((2, 16)), dma((2, 16)),
        ],
        compiler_params=pltpu.CompilerParams(
            collective_id=0, has_side_effects=True, vmem_limit_bytes=60 * 1024 * 1024),
        cost_estimate=pl.CostEstimate(flops=8_000_000_000, bytes_accessed=24_000_000,
                                      transcendentals=300_000),
    )(
        embeds, lengths, source, targets, attn_gain, final_gain.reshape(1, D), jnp.asarray(cos), jnp.asarray(sin),
        w_query.reshape(16, 2, 256, 512), w_key.reshape(16, 2, 256, 128),
        w_value.reshape(16, 2, 256, 128), w_out.reshape(512, 2048), head,
    )
    return (stats[0], stats[1])


def solution(mesh):
    return jax.shard_map(
        per_device,
        mesh=mesh,
        in_specs=(
            P("dp", "mp", None),
            P(),
            P(),
            P(),
            P("section", None),
            P("section", None, "mp"),
            P("section", None, "mp"),
            P("section", None, "mp"),
            P("section", "mp", "dp"),
            P(),
            P(("dp", "section", "mp"), None),
        ),
        out_specs=(P("dp", None), P("dp", None)),
        check_vma=False,
    )
```

```python
import jax
import jax.numpy as jnp
import numpy as np
from jax import lax
from jax.experimental import pallas as pl
from jax.experimental.pallas import tpu as pltpu
from jax.sharding import PartitionSpec as P

HD = 128
EPS = 1e-05
ROPE_BASE = 500000.0
NY = 4
NX = 4
NZ = 4
NM = 8
ROWS = 64
D = 8192
QW = 512
VOCAB_DEV = 512
MESH = pl.DeviceIdType.MESH
BF = jnp.bfloat16
F32 = jnp.float32


def lane(start, size):
    return pl.ds(pl.multiple_of(start, 128), size)


def kernel(
    emb_in, live, source_of, targets_in, gain, fgain_in, cosine_in, sine_in, wq, wk, wv, wo, head,
    out,
    emb, targets, gains, fgain, cosine, sine, W, WO, HEAD, EB, XE, X, RX, MASK, SS, QA, QR, R, C, PS, PR, PO, ZS, ZR, HP, Y, LT, LR, SQ, WANT, TAKE, STO, SA, SB,
    w_sem, sw_s, sw_r, lt_s, lt_r, qr_s, qr_r, eb_s, eb_r, hop_s, hop_r, ag_s, ag_r, res_s, res_r, ctx_s, ctx_r, ps_s, ps_r,
    zz_s, zz_r, y_s, y_r, st_s, st_r,
):
    d = lax.axis_index("dp")
    s = lax.axis_index("section")
    m = lax.axis_index("mp")
    z = m // 2
    c = m % 2
    sib = z * 2 + (1 - c)

    def ypeer(k):
        return (d + k) % NY

    def zpeer(k):
        return ((z + k) % NZ) * 2 + c

    def zother(k):
        return ((z + k) % NZ) * 2 + (1 - c)

    def rcopy(src, dst, ssem, rsem, dev):
        return pltpu.make_async_remote_copy(
            src_ref=src, dst_ref=dst, send_sem=ssem, recv_sem=rsem,
            device_id=dev, device_id_type=MESH,
        )

    here = (d, s, sib)

    barrier = pltpu.get_barrier_semaphore()
    partners = []
    for k in range(1, 4):
        partners.append((ypeer(k), s, m))
        partners.append((d, (s + k) % NX, m))
        partners.append((d, s, zpeer(k)))
        partners.append((d, s, zother(k)))
        partners.append((ypeer(k), (s + 1) % NX, m))
        partners.append((ypeer(k), (s + 3) % NX, m))
        partners.append((ypeer(k), (s + 2) % NX, m))
    partners.append(here)
    for dev in partners:
        pl.semaphore_signal(barrier, inc=1, device_id=dev, device_id_type=MESH)
    small = [
        pltpu.make_async_copy(src, dst, w_sem.at[14 + n])
        for n, (src, dst) in enumerate((
            (emb_in, emb), (gain, gains), (cosine_in, cosine), (sine_in, sine),
            (fgain_in, fgain), (targets_in, targets)))
    ]
    for copy in small:
        copy.start()
    parts = ((wq, pl.ds(0, 512)), (wk, pl.ds(512, 128)), (wv, pl.ds(640, 128)))

    def load(n, first):
        src, lanes = parts[n]
        take = 1 if first else jnp.where(s == 0, 0, c)
        return pltpu.make_async_copy(src.at[:, take], W.at[first, :, :, lanes],
                                     w_sem.at[3 * first + n])

    def swap(n):
        src, lanes = parts[n]
        return rcopy(src.at[:, 1 - c], W.at[1, :, :, lanes], sw_s.at[n], sw_r.at[n], here)

    wo_load = pltpu.make_async_copy(wo, WO, w_sem.at[12])
    @pl.when(s > 0)
    def _():
        for n in range(3):
            load(n, 0).start()

    head_load = pltpu.make_async_copy(HEAD.at[0], HEAD.at[0], w_sem.at[13])
    head_swap = rcopy(HEAD.at[1], HEAD.at[1], sw_s.at[3], sw_r.at[3], here)

    def off(n):
        return jnp.where(n == 0, 0, jnp.where(n == 1, 3, jnp.where(n == 2, 1, 2)))

    def slot_columns(core, j, i):
        g = jnp.where(core == 0, off(i), off(j))
        zz = jnp.where(core == 0, off(j), off(i))
        return lane(((d + g) % NY) * 2048 + ((z + zz) % NZ) * 512 + core * 256, 256)

    def row_slot(lanes):
        return (lanes // 64) * 2 + (lanes // 4) % 2, ((lanes // 8) % 8) * 4 + lanes % 4

    def wanted_rows():
        slot, position = row_slot(lax.broadcasted_iota(jnp.int32, (32, 256), 1))
        place = (position == lax.broadcasted_iota(jnp.int32, (32, 256), 0)).astype(BF)
        tokens = targets[...]
        keep = slot[0:8] == lax.broadcasted_iota(jnp.int32, (8, 256), 0)
        parts = []
        for term in (tokens // 256, tokens % 256):
            every = jnp.dot(term.astype(F32).astype(BF), place, preferred_element_type=F32)
            parts.append(jnp.sum(jnp.where(keep, every, 0.0), axis=0, keepdims=True))
        return parts[0] * 256.0 + parts[1]

    def head_start():
        for j in range(4):
            for i in range(4):
                there = pl.ds(i * 256, 256)
                pltpu.make_async_copy(head.at[:, slot_columns(c, j, i)], HEAD.at[0, j, :, there],
                                      w_sem.at[13]).start()
                rcopy(head.at[:, slot_columns(1 - c, j, i)], HEAD.at[1, j, :, there],
                      sw_s.at[3], sw_r.at[3], here).start()
    def prepare():
        @pl.when(s > 0)
        def _():
            wo_load.start()
            head_start()

        shape = (4 * ROWS, ROWS)
        rq = lax.broadcasted_iota(jnp.int32, shape, 0) % ROWS
        rk = lax.broadcasted_iota(jnp.int32, shape, 1)
        slot_q, slot_k = (rq // 4) % 2, (rk // 4) % 2
        pos_q, pos_k = (rq // 8) * 4 + rq % 4, (rk // 8) * 4 + rk % 4
        live_k = jnp.where(slot_k == 0, live[2 * d], live[2 * d + 1])
        allowed = (slot_q == slot_k) & (pos_k <= pos_q) & (pos_k < live_k)
        MASK[...] = jnp.where(allowed, F32(0.0), F32(-1e30))

        @pl.when(s > 0)
        def _():
            for n in range(3):
                load(n, 0).wait()
                swap(n).wait_recv()
            for copy in small[1:2]:
                copy.wait()
            diagonal = (lax.broadcasted_iota(jnp.int32, (256, 256), 0)
                        == lax.broadcasted_iota(jnp.int32, (256, 256), 1))

            def scale(i, _):
                cols = lane((i // NZ) * 2048 + ((i % NZ) * 2 + c) * 256, 256)
                column = jnp.sum(jnp.where(diagonal, gains[:, cols], 0.0), axis=1, keepdims=True)
                for which in range(2):
                    W.at[which, i][...] = (W[which, i].astype(F32) * column).astype(BF)
                return 0

            lax.fori_loop(0, 16, scale, 0)

        @pl.when(s == 0)
        def _():
            for copy in small[1:2]:
                copy.wait()
        for copy in small[2:]:
            copy.wait()

        WANT[...] = jnp.broadcast_to(wanted_rows(), WANT.shape)
        slot, position = row_slot(lax.broadcasted_iota(jnp.int32, (256, 32), 0))
        place = lax.broadcasted_iota(jnp.int32, (256, 32), 1)
        for i in range(2):
            chosen = source_of[2 * d + i]
            TAKE.at[i][...] = ((slot == chosen) & (position == place)
                               & (place < live[chosen])).astype(F32).astype(BF)

        @pl.when(s > 0)
        def _():
            scale_head()

    def scale_head():
        head_load.wait()
        head_swap.wait_recv()

        def scale(n, _):
            cc, j, i = n // 16, (n // 4) % 4, n % 4
            block = HEAD.at[cc, j, :, lane(i * 256, 256)]
            block[...] = (block[...].astype(F32) * fgain[:, slot_columns(c, j, i)]).astype(BF)
            return 0

        lax.fori_loop(0, 32, scale, 0)

    small[0].wait()

    @pl.when(s == 0)
    def _():
        rows = jnp.concatenate([emb[0], emb[1]], axis=0).astype(F32)
        for q in range(2):
            EB.at[q, m][...] = jnp.concatenate(
                [rows[:, q * 2048:q * 2048 + 2048], rows[:, q * 2048 + 4096:q * 2048 + 6144]],
                axis=0).astype(BF)

    pl.semaphore_wait(barrier, len(partners))

    @pl.when(s > 0)
    def _():
        for n in range(3):
            swap(n).start()

    def eb_z(q, k):
        return rcopy(EB.at[q, m], EB.at[q, m], eb_s.at[q, k], eb_r.at[q, m], (d, s, zpeer(k)))

    def eb_z_in(q, k):
        mk = zpeer(k)
        return rcopy(EB.at[q, mk], EB.at[q, mk], eb_s.at[q, k], eb_r.at[q, mk], here)

    def eb_fwd(q, k):
        mk = zpeer(k)
        return rcopy(EB.at[q, mk], EB.at[q, mk], eb_s.at[q, 4 + k], eb_r.at[q, mk], here)

    def eb_sib_in(q, k):
        mk = zother(k)
        return rcopy(EB.at[q, mk], EB.at[q, mk], eb_s.at[q, 4 + k], eb_r.at[q, mk], here)

    def hop(g):
        return rcopy(HP.at[g], X.at[d, z], hop_s.at[g], hop_r.at[d], (g, (s + 1) % NX, m))

    def hop_in(g):
        return rcopy(HP.at[g], X.at[g, z], hop_s.at[g], hop_r.at[g], here)

    def hop_raw():
        return rcopy(HP, R, hop_s.at[4], hop_r.at[4], (d, (s + 1) % NX, m))

    def ag_z(g, k):
        return rcopy(X.at[g, z], X.at[g, z], ag_s.at[g, k], ag_r.at[g, z], (d, s, zpeer(k)))

    def ag_z_in(g, k):
        zk = (z + k) % NZ
        return rcopy(X.at[g, zk], X.at[g, zk], ag_s.at[g, k], ag_r.at[g, zk], here)

    def sums_out():
        return rcopy(QA.at[1], QR, qr_s, qr_r, here)

    def res(k):
        g = ypeer(k)
        return rcopy(RX.at[g], R.at[d], res_s.at[k], res_r.at[d], (g, s, m))

    def res_in(k):
        g = ypeer(k)
        return rcopy(RX.at[g], R.at[g], res_s.at[k], res_r.at[g], here)

    def ctx(k):
        return rcopy(C.at[d], C.at[d], ctx_s.at[k], ctx_r.at[d], (ypeer(k), s, m))

    def ctx_in(k):
        g = ypeer(k)
        return rcopy(C.at[g], C.at[g], ctx_s.at[k], ctx_r.at[g], here)

    def part(g):
        return rcopy(PS.at[g], PR.at[g], ps_s.at[g], ps_r.at[g], here)

    def zred(g, k):
        return rcopy(ZS.at[g, k], ZR.at[g, k], zz_s.at[g, k], zz_r.at[g, k], (d, s, zpeer(k)))

    def layer():
        def multiply(x, which, rows, n, start=False):
            w = W[which, pl.ds(rows * NZ, NZ)].reshape(4 * 256, 768)
            term = jnp.dot(x, w, preferred_element_type=F32)
            QA.at[n][:, 0:768] = term if start else QA[n, :, 0:768] + term

        @pl.when(s == 0)
        def _():
            for q in range(2):
                for k in (1, 3, 2):
                    eb_z_in(q, k).wait_recv()
                    eb_fwd(q, k).start()
            QA[...] = jnp.zeros_like(QA)
            QR[...] = jnp.zeros_like(QR)
            SS[...] = jnp.zeros_like(SS)
            for q in range(2):
                for k in range(4):
                    eb_sib_in(q, k).wait_recv()

                def blocks(mm):
                    x = EB[q, :, :, lane(mm * 256, 256)].astype(F32)
                    return [x[:, i * 8:i * 8 + 8, :].reshape(ROWS, 256) for i in range(2)]

                def body(mm, total):
                    for half, xs in enumerate(blocks(mm)):
                        g = half * 2 + q
                        cols = lane(g * 2048 + mm * 256, 256)
                        XE.at[g, mm][...] = (xs * gains[:, cols]).astype(BF)
                        square = xs * xs
                        total = total + square[:, 0:128] + square[:, 128:256]
                    return total

                SS[...] = lax.fori_loop(0, NM, body, SS[...])
                for half, xs in enumerate(blocks(m)):
                    RX.at[half * 2 + q][...] = xs.astype(BF)
                if q == 0:
                    for n in range(3):
                        load(n, 0).wait()
                        load(n, 1).wait()

                def both(i, _):
                    g = 2 * i + q
                    for who in range(2):
                        x = jnp.concatenate([XE[g, 2 * zz + who] for zz in range(NZ)], axis=1)
                        multiply(x, who, g, 0)
                    return 0

                lax.fori_loop(0, 2, both, 0)
            for k in (2, 1, 3):
                res(k).start()
            R.at[d][...] = RX[d]

        @pl.when(s > 0)
        def _():
            def arrived(k):
                g = ypeer(k)
                hop_in(g).wait_recv()
                for j in (2, 1, 3):
                    ag_z(g, j).start()

            def columns(k):
                g = ypeer(k)
                for j in (1, 3, 2):
                    ag_z_in(g, j).wait_recv()
                return jnp.concatenate([X[g, zz] for zz in range(NZ)], axis=1)

            def both(k, start=False):
                x = columns(k)
                multiply(x, 1, ypeer(k), 1, start)
                multiply(x, 0, ypeer(k), 0, start)

            def squares_of(k):
                total = jnp.zeros((ROWS, 128), F32)
                for zz in range(NZ):
                    x = X[ypeer(k), zz].astype(F32)
                    square = x * x
                    total = total + square[:, 0:128] + square[:, 128:256]
                return total

            arrived(0)
            arrived(3)
            arrived(1)
            arrived(2)
            both(0, True)
            squares = squares_of(0)
            both(3)
            squares = squares + squares_of(3)
            both(1)
            squares = squares + squares_of(1)
            x = columns(2)
            multiply(x, 1, ypeer(2), 1)
            squares = squares + squares_of(2)
            QA.at[1][:, 768:896] = squares
            sums_out().start()
            multiply(x, 0, ypeer(2), 0)
            sums_out().wait_recv()
            SS[...] = squares + QR[:, 768:896]

        r = lax.rsqrt(jnp.sum(SS[...], axis=1, keepdims=True) * (1.0 / D) + EPS)
        cos = cosine[...]
        sin = sine[...]

        def summed(first, last):
            return QA[0, :, first:last] + QR[:, first:last]

        def rope(x):
            return (x * cos + pltpu.roll(x, 64, 1) * sin).astype(BF)

        query = jnp.concatenate(
            [rope(summed(j * HD, (j + 1) * HD) * r) for j in range(4)], axis=0)
        key = rope(summed(512, 640) * r)
        value = (summed(640, 768) * r).astype(BF)
        scores = lax.dot_general(query, key, (((1,), (1,)), ((), ())),
                                 preferred_element_type=F32) * (HD ** -0.5)
        scores = scores + MASK[...]
        highest = jnp.max(scores, axis=-1, keepdims=True)
        weights = jnp.exp(scores - highest)
        probs = (weights / jnp.sum(weights, axis=-1, keepdims=True)).astype(BF)
        mixed = jnp.dot(probs, value, preferred_element_type=F32).astype(BF)
        for j in range(4):
            C.at[d][:, j * HD:(j + 1) * HD] = mixed[j * ROWS:(j + 1) * ROWS]
        for k in (2, 1, 3):
            ctx(k).start()

        wo_load.wait()

        def project(g):
            for zz in range(NZ):
                p = jnp.dot(C[g], WO[:, zz * 512:zz * 512 + 512], preferred_element_type=F32)
                low, high = p[:, :256], p[:, 256:]
                PO.at[g, zz][...] = jnp.where(c == 0, low, high)
                PS.at[g, zz][...] = jnp.where(c == 0, high, low).astype(BF)
            part(g).start()

        def pair(g):
            part(g).wait_recv()
            for k in (2, 1, 3):
                zt = (z + k) % NZ
                ZS.at[g, k][...] = (PO[g, zt] + PR[g, zt].astype(F32)).astype(BF)
                zred(g, k).start()

        def total_of(g):
            total = PO[g, z] + PR[g, z].astype(F32) + R[g].astype(F32)
            for k in (1, 3, 2):
                zred(g, k).wait_recv()
                total = total + ZR[g, k].astype(F32)
            HP.at[g][...] = total.astype(BF)

            @pl.when(s < NX - 1)
            def _():
                hop(g).start()

        project(d)

        @pl.when(s == 0)
        def _():
            for k in (1, 3, 2):
                res_in(k).wait_recv()

        @pl.when(s > 0)
        def _():
            hop_raw().wait_recv()

        pair(d)
        for k in (1, 3):
            ctx_in(k).wait_recv()
            project(ypeer(k))
        pair(ypeer(1))
        pair(ypeer(3))
        def in_last(do):
            @pl.when(s == NX - 1)
            def _():
                do()

        total_of(d)
        in_last(lambda: own_x(1, 0))
        ctx_in(2).wait_recv()
        project(ypeer(2))
        total_of(ypeer(1))
        in_last(lambda: own_x(1, 1))
        pair(ypeer(2))

        def first_two():
            spread(1, 0)
            spread(1, 1)

        in_last(first_two)
        total_of(ypeer(3))

        def third():
            own_x(1, 2)
            spread(1, 2)

        in_last(third)
        total_of(ypeer(2))

        def rest():
            own_x(1, 3)
            spread(1, 3)
            for k in range(3):
                stage_first(1, k)
            for k in range(2):
                stage_second(1, k)

        in_last(rest)

        @pl.when(s < NX - 1)
        def _():
            hop_raw().start()

        @pl.when(s == 1)
        def _():
            def body(k, _):
                own_x(0, k)
                spread(0, k)
                return 0

            lax.fori_loop(0, 4, body, 0)

    def first_dev(k):
        return (jnp.where(c == 0, ypeer(k), d), s, jnp.where(c == 0, m, zpeer(k)))

    def second_dev(k):
        return (jnp.where(c == 0, d, ypeer(k)), s, jnp.where(c == 0, zpeer(k), m))

    def ycopy(src, dst, b, k, i, j, dev):
        return rcopy(src, dst, y_s.at[b, k, i], y_r.at[b, k, j], dev)

    def y_x(b, k, n):
        ref = Y.at[b, k, 0, 0]
        return ycopy(ref, ref, b, k, n, 0, (d, (s + n) % NX, m))

    def y_first(b, k, n):
        slot = (1, 3, 2)[n - 1]
        return ycopy(Y.at[b, k, 0, 0], Y.at[b, k, 0, slot], b, k, 3 + n, slot, first_dev(n))

    sets = (pl.ds(0, 1), pl.ds(1, 2), pl.ds(3, 1))

    def y_second(b, k, part_no, n):
        slot = 1 if n == 1 else 2
        return ycopy(Y.at[b, k, 0, sets[part_no]], Y.at[b, k, slot, sets[part_no]], b, k,
                     7 + part_no * 2 + (slot - 1), 1 + 3 * slot + part_no, second_dev(n))

    def y_relay(b, k, half):
        slot, n = ((1, 1), (2, 3))[half]
        two = pl.ds(2 * half, 2)
        return ycopy(Y.at[b, k, slot, two], Y.at[b, k, 3, two], b, k, 13 + half, 10 + half,
                     second_dev(n))

    def chunk_order(step):
        return jnp.where(step == 3, 2, jnp.where(step == 2, 3, step))

    def own_x(b, k):
        Y.at[b, k, 0, 0][...] = HP[(d + chunk_order(k)) % NY]
        for n in (2, 1, 3):
            y_x(b, k, n).start()

    def spread(b, k):
        for n in (2, 1, 3):
            y_first(b, k, n).start()
        for n in (1, 3):
            y_second(b, k, 0, n).start()

    def stage_first(b, k):
        y_first(b, k, 1).wait_recv()
        y_first(b, k, 3).wait_recv()
        for n in (1, 3):
            y_second(b, k, 1, n).start()
        y_first(b, k, 2).wait_recv()
        for n in (1, 3):
            y_second(b, k, 2, n).start()

    def stage_second(b, k):
        for part_no in (0, 1):
            y_second(b, k, part_no, 1).wait_recv()
        y_relay(b, k, 0).start()
        for part_no in (1, 2):
            y_second(b, k, part_no, 3).wait_recv()
        y_relay(b, k, 1).start()
        y_second(b, k, 2, 1).wait_recv()
        y_second(b, k, 0, 3).wait_recv()

    def opposite(b, k):
        for half in range(2):
            y_relay(b, k, half).wait_recv()

    def dots(b, j, send=False):
        blocks = []
        for g in range(NY):
            row = []
            total = jnp.zeros((ROWS, 128), F32)
            for i in range(4):
                sender = (d + jnp.where(c == 0, (0, 3, 1, 2)[i], off(j))) % NY
                k = chunk_order((g - sender + NY) % NY)
                x = Y[b, k, j, i]
                row.append(x)
                wide = x.astype(F32)
                square = wide * wide
                total = total + square[:, 0:128] + square[:, 128:256]
            SQ.at[b, g][...] += total
            blocks.append(jnp.concatenate(row, axis=1))
        pieces = jnp.concatenate(blocks, axis=0)
        for which in (1, 0):
            LT.at[b, which][0:VOCAB_DEV, :] += lax.dot_general(
                HEAD[which, j], pieces, (((1,), (1,)), ((), ())), preferred_element_type=F32)
            if send and which == 1:
                exchange(b)

    def swap_logits(b):
        return rcopy(LT.at[b, 1], LR.at[b], lt_s.at[b], lt_r.at[b], here)

    def exchange(b):
        squares = SQ[b].reshape(NY * ROWS, 128)
        top = squares.astype(BF)
        rest = (squares - top.astype(F32)).astype(BF)
        ones = jnp.ones((16, 128), BF)
        nt = (((1,), (1,)), ((), ()))
        sums = (lax.dot_general(ones, top, nt, preferred_element_type=F32)
                + lax.dot_general(ones, rest, nt, preferred_element_type=F32))
        LT.at[b, 1][VOCAB_DEV:VOCAB_DEV + 8, :] = sums[0:8]
        swap_logits(b).start()

    def layer_sent():
        @pl.when(s == 0)
        def _():
            for q in range(2):
                for k in range(1, 4):
                    eb_z(q, k).wait_send()
                for k in range(4):
                    eb_fwd(q, k).wait_send()
            for k in range(1, 4):
                res(k).wait_send()

        @pl.when(s > 0)
        def _():
            for g in range(NY):
                for k in range(1, 4):
                    ag_z(g, k).wait_send()
            sums_out().wait_send()
            for n in range(3):
                swap(n).wait_send()

        @pl.when(s < NX - 1)
        def _():
            for g in range(NY):
                hop(g).wait_send()
            hop_raw().wait_send()

        for g in range(NY):
            for k in range(1, 4):
                zred(g, k).wait_send()
            part(g).wait_send()
        for k in range(1, 4):
            ctx(k).wait_send()

    def chunk_sent(b, k, source):
        @pl.when(s == source)
        def _():
            for j in (1, 2, 3):
                y_x(b, k, j).wait_send()

        for j in (1, 2, 3):
            y_first(b, k, j).wait_send()
        for j in (1, 3):
            for part_no in range(3):
                y_second(b, k, part_no, j).wait_send()
        for half in range(2):
            y_relay(b, k, half).wait_send()

    def each(count, do):
        def body(k, _):
            do(k)
            return 0

        lax.fori_loop(0, count, body, 0)

    def exit_dots(n):
        dots(0, n)

    def gather(b):
        source = 2 * b + 1
        final = (b == 1) & (s == NX - 1)
        others = jnp.logical_not(final)

        def body(t, _):
            @pl.when((t < 4) & (s != source))
            def _():
                y_x(b, t, 1).wait_recv()
                spread(b, t)

            @pl.when((t >= 1) & (t < 5) & ((t == 4) | others))
            def _():
                stage_first(b, t - 1)

            @pl.when((t >= 2) & (t < 6) & ((t >= 4) | others))
            def _():
                stage_second(b, t - 2)

            return 0

        lax.fori_loop(0, 6, body, 0)

        @pl.when((b == 1) & (s >= 2))
        def _():
            each(4, lambda k: opposite(0, k))
            each(4, exit_dots)
            exchange(0)

    def finish(b):
        @pl.when(b == 0)
        def _():
            each(4, lambda k: opposite(0, k))
            each(4, exit_dots)
            exchange(0)

        @pl.when(b == 1)
        def _():
            for j in range(3):
                dots(1, j)
            each(4, lambda k: opposite(1, k))
            dots(1, 3, True)

            @pl.when(s >= 2)
            def _():
                softmax(0)

        softmax(b)

    def softmax(b):
        swap_logits(b).wait_recv()
        last = pl.ds(VOCAB_DEV, 8)
        sums = (LT[b, 1, last] + LR[b, last])[0:1]
        r = lax.rsqrt(sums * (1.0 / D) + EPS)
        logits = (LT[b, 0, 0:VOCAB_DEV] + LR[b, 0:VOCAB_DEV]) * r
        highest = jnp.max(logits, axis=0, keepdims=True)
        summed = jnp.sum(jnp.exp(logits - highest), axis=0, keepdims=True)
        first = ((d * NX + s) * NM + m) * VOCAB_DEV
        index = (lax.broadcasted_iota(jnp.int32, logits.shape, 0) + first).astype(F32)
        wanted = WANT[0:1, :]
        picked = jnp.sum(jnp.where(index == wanted, logits, 0.0), axis=0, keepdims=True)
        for n, value in enumerate((highest, summed, picked)):
            for half in range(2):
                STO[pl.ds(n * 4 + b * 2 + half, 1), :] = value[:, half * 128:half * 128 + 128]

    def step(t, _):
        last = s == NX - 1
        place = jnp.where(last, 1, 0)

        @pl.when(t == place)
        def _():
            layer()

            @pl.when(s == 0)
            def _():
                head_start()

        @pl.when(jnp.where(last, (t == 0) | (t == 2), (t == 1) | (t == jnp.where(s < 2, 3, 2))))
        def _():
            gather(jnp.where((t == 0) | (t == 1), 0, 1))

        @pl.when((t == 4) | ((t == 2) & (s < 2)))
        def _():
            @pl.when((t == 2) & (s == 0))
            def _():
                scale_head()
            finish(jnp.where(t == 4, 1, 0))
        return 0

    @pl.when(s == 0)
    def _():
        for q in range(2):
            for k in (2, 1, 3, 0):
                (eb_z(q, k) if k else eb_fwd(q, 0)).start()
        for n in range(3):
            load(n, 0).start()
            load(n, 1).start()
        wo_load.start()

    prepare()
    STO[...] = jnp.zeros_like(STO)
    SQ[...] = jnp.zeros_like(SQ)
    LT[...] = jnp.zeros_like(LT)
    lax.fori_loop(0, 5, step, 0)

    def merge(ref, count):
        parts = [ref[j] for j in range(count)]
        highest = parts[0][0:4]
        for p in parts[1:]:
            highest = jnp.maximum(highest, p[0:4])
        summed = jnp.zeros_like(highest)
        picked = jnp.zeros_like(highest)
        for p in parts:
            summed = summed + p[4:8] * jnp.exp(p[0:4] - highest)
            picked = picked + p[8:12]
        return highest, summed, picked

    def stacked(highest, summed, picked):
        return jnp.concatenate([highest, summed, picked, jnp.zeros_like(picked)], axis=0)

    pairs = [(j, k) for j in range(NX) for k in range(NY) if j or k]

    def st_yx(n):
        j, k = pairs[n]
        mine = s * NY + d
        return rcopy(SA.at[mine], SA.at[mine], st_s.at[0, n], st_r.at[0, mine],
                     (ypeer(k), (s + j) % NX, m))

    def st_yx_in(n):
        j, k = pairs[n]
        other = ((s + j) % NX) * NY + ypeer(k)
        return rcopy(SA.at[other], SA.at[other], st_s.at[0, n], st_r.at[0, other], here)

    def m_of(k):
        return (m + k) % NM

    def st_m(k):
        return rcopy(SB.at[m], SB.at[m], st_s.at[1, k], st_r.at[1, m], (d, s, m_of(k)))

    def st_m_in(k):
        mm = m_of(k)
        return rcopy(SB.at[mm], SB.at[mm], st_s.at[1, k], st_r.at[1, mm], (d, s, mm))

    SA.at[s * NY + d][...] = STO[...]
    for n in range(15):
        st_yx(n).start()
    layer_sent()
    head_swap.wait_send()
    swap_logits(0).wait_send()
    swap_logits(1).wait_send()
    each(4, lambda k: chunk_sent(0, k, 1))
    each(4, lambda k: chunk_sent(1, k, NX - 1))
    for n in range(15):
        st_yx_in(n).wait_recv()
    SB.at[m][...] = stacked(*merge(SA, NX * NY))
    for k in (4, 3, 5, 2, 6, 1, 7):
        st_m(k).start()
    for n in range(15):
        st_yx(n).wait_send()
    for k in (1, 7, 2, 6, 3, 5, 4):
        st_m_in(k).wait_recv()
    highest, summed, picked = merge(SB, NM)
    logprob = picked - (highest + jnp.log(summed))
    terms = []
    for e in range(2):
        rest = jnp.concatenate([logprob[2 * e:2 * e + 1], logprob[2 * e + 1:2 * e + 2]], axis=1)
        for _ in range(3):
            term = rest.astype(BF).astype(F32)
            terms.append(term)
            rest = rest - term
    row = lax.broadcasted_iota(jnp.int32, (16, 256), 0)
    stack = jnp.zeros((16, 256), F32)
    for j, term in enumerate(terms):
        stack = jnp.where(row == j, term, stack)
    stack = stack.astype(BF)
    results = []
    for i in range(2):
        got = jnp.dot(stack, TAKE[i], preferred_element_type=F32)
        results.append([got[j:j + 1] + got[j + 1:j + 2] + got[j + 2:j + 3] for j in (0, 3)])
    for e in range(2):
        first = lax.broadcasted_iota(jnp.int32, (2, 32), 0) == 0
        out.at[e][...] = jnp.where(first, results[0][e], results[1][e])
    for k in range(1, 8):
        st_m(k).wait_send()


def tables():
    row = np.arange(ROWS)
    position = (row // 8) * 4 + row % 4
    half = HD // 2
    freqs = (ROPE_BASE ** (-np.arange(half) * 2.0 / HD)).astype(np.float32)
    angles = (position.astype(np.float32)[:, None] * freqs[None, :]).astype(np.float64)
    cos, sin = np.cos(angles), np.sin(angles)
    return (np.concatenate([cos, cos], 1).astype(np.float32),
            np.concatenate([-sin, sin], 1).astype(np.float32))


def per_device(
    embeds, targets, lengths, source, attn_gain, w_query, w_key, w_value, w_out, final_gain, head
):
    vocab = head.shape[0]
    cos, sin = tables()
    vmem = pl.BlockSpec(memory_space=pltpu.VMEM)
    hbm = pl.BlockSpec(memory_space=pl.ANY)
    smem = pl.BlockSpec(memory_space=pltpu.SMEM)
    dma = pltpu.SemaphoreType.DMA
    stats = pl.pallas_call(
        kernel,
        out_shape=jax.ShapeDtypeStruct((2, 2, 32), F32),
        in_specs=[hbm, smem, smem] + [hbm] * 10,
        out_specs=vmem,
        scratch_shapes=[
            pltpu.VMEM((2, 4, D), BF),
            pltpu.VMEM((8, 32), jnp.int32),
            pltpu.VMEM((1, D), F32),
            pltpu.VMEM((1, D), F32),
            pltpu.VMEM((ROWS, HD), F32),
            pltpu.VMEM((ROWS, HD), F32),
            pltpu.VMEM((2, 16, 256, 768), BF),
            pltpu.VMEM((QW, 2048), BF),
            pltpu.VMEM((2, 4, vocab, 1024), BF),
            pltpu.VMEM((2, NM, 16, 2048), BF),
            pltpu.VMEM((NY, NM, ROWS, 256), BF),
            pltpu.VMEM((NY, NZ, ROWS, 256), BF),
            pltpu.VMEM((NY, ROWS, 256), BF),
            pltpu.VMEM((4 * ROWS, ROWS), F32),
            pltpu.VMEM((ROWS, 128), F32),
            pltpu.VMEM((2, ROWS, 896), F32),
            pltpu.VMEM((ROWS, 896), F32),
            pltpu.VMEM((NY, ROWS, 256), BF),
            pltpu.VMEM((NY, ROWS, QW), BF),
            pltpu.VMEM((NY, NZ, ROWS, 256), BF),
            pltpu.VMEM((NY, NZ, ROWS, 256), BF),
            pltpu.VMEM((NY, NZ, ROWS, 256), F32),
            pltpu.VMEM((NY, NZ, ROWS, 256), BF),
            pltpu.VMEM((NY, NZ, ROWS, 256), BF),
            pltpu.VMEM((NY, ROWS, 256), BF),
            pltpu.VMEM((2, 4, 4, 4, ROWS, 256), BF),
            pltpu.VMEM((2, 2, vocab + 8, 256), F32),
            pltpu.VMEM((2, vocab + 8, 256), F32),
            pltpu.VMEM((2, NY, ROWS, 128), F32),
            pltpu.VMEM((8, 256), F32),
            pltpu.VMEM((2, 256, 32), BF),
            pltpu.VMEM((16, 128), F32),
            pltpu.VMEM((NX * NY, 16, 128), F32),
            pltpu.VMEM((NM, 16, 128), F32),
            dma((20,)),
            dma((4,)), dma((4,)),
            dma((2,)), dma((2,)),
            dma, dma,
            dma((2, 8)), dma((2, 8)),
            dma((5,)), dma((5,)),
            dma((4, 8)), dma((4, 8)),
            dma((4,)), dma((4,)),
            dma((4,)), dma((4,)),
            dma((4,)), dma((4,)),
            dma((4, 4)), dma((4, 4)),
            dma((2, 4, 22)), dma((2, 4, 19)),
            dma((2, 16)), dma((2, 16)),
        ],
        compiler_params=pltpu.CompilerParams(
            collective_id=0, has_side_effects=True, vmem_limit_bytes=60 * 1024 * 1024),
        cost_estimate=pl.CostEstimate(flops=8_000_000_000, bytes_accessed=24_000_000,
                                      transcendentals=300_000),
    )(
        embeds, lengths, source, targets, attn_gain, final_gain.reshape(1, D), jnp.asarray(cos), jnp.asarray(sin),
        w_query.reshape(16, 2, 256, 512), w_key.reshape(16, 2, 256, 128),
        w_value.reshape(16, 2, 256, 128), w_out.reshape(512, 2048), head,
    )
    return (stats[0], stats[1])


def solution(mesh):
    return jax.shard_map(
        per_device,
        mesh=mesh,
        in_specs=(
            P("dp", "mp", None),
            P(),
            P(),
            P(),
            P("section", None),
            P("section", None, "mp"),
            P("section", None, "mp"),
            P("section", None, "mp"),
            P("section", "mp", "dp"),
            P(),
            P(("dp", "section", "mp"), None),
        ),
        out_specs=(P("dp", None), P("dp", None)),
        check_vma=False,
    )
```

```python
import jax
import jax.numpy as jnp
import numpy as np
from jax import lax
from jax.experimental import pallas as pl
from jax.experimental.pallas import tpu as pltpu
from jax.sharding import PartitionSpec as P

HD = 128
EPS = 1e-05
ROPE_BASE = 500000.0
NY = 4
NX = 4
NZ = 4
NM = 8
ROWS = 64
D = 8192
QW = 512
VOCAB_DEV = 512
MESH = pl.DeviceIdType.MESH
BF = jnp.bfloat16
F32 = jnp.float32


def lane(start, size):
    return pl.ds(pl.multiple_of(start, 128), size)


def kernel(
    emb_in, live, source_of, targets_in, gain, fgain_in, cosine_in, sine_in, wq, wk, wv, wo, head,
    out,
    emb, targets, gains, fgain, cosine, sine, W, WO, HEAD, EB, XE, X, RX, MASK, SS, QA, QR, R, C, PS, PR, PO, ZS, ZR, HP, Y, LT, LR, SQ, WANT, TAKE, STO, SA, SB,
    w_sem, sw_s, sw_r, lt_s, lt_r, qr_s, qr_r, eb_s, eb_r, hop_s, hop_r, ag_s, ag_r, res_s, res_r, ctx_s, ctx_r, ps_s, ps_r,
    zz_s, zz_r, y_s, y_r, st_s, st_r,
):
    d = lax.axis_index("dp")
    s = lax.axis_index("section")
    m = lax.axis_index("mp")
    z = m // 2
    c = m % 2
    sib = z * 2 + (1 - c)

    def ypeer(k):
        return (d + k) % NY

    def zpeer(k):
        return ((z + k) % NZ) * 2 + c

    def zother(k):
        return ((z + k) % NZ) * 2 + (1 - c)

    def rcopy(src, dst, ssem, rsem, dev):
        return pltpu.make_async_remote_copy(
            src_ref=src, dst_ref=dst, send_sem=ssem, recv_sem=rsem,
            device_id=dev, device_id_type=MESH,
        )

    here = (d, s, sib)

    barrier = pltpu.get_barrier_semaphore()
    partners = []
    for k in range(1, 4):
        partners.append((ypeer(k), s, m))
        partners.append((d, (s + k) % NX, m))
        partners.append((d, s, zpeer(k)))
        partners.append((d, s, zother(k)))
        partners.append((ypeer(k), (s + 1) % NX, m))
        partners.append((ypeer(k), (s + 3) % NX, m))
        partners.append((ypeer(k), (s + 2) % NX, m))
    partners.append(here)
    for dev in partners:
        pl.semaphore_signal(barrier, inc=1, device_id=dev, device_id_type=MESH)
    small = [
        pltpu.make_async_copy(src, dst, w_sem.at[14 + n])
        for n, (src, dst) in enumerate((
            (emb_in, emb), (gain, gains), (cosine_in, cosine), (sine_in, sine),
            (fgain_in, fgain), (targets_in, targets)))
    ]
    for copy in small:
        copy.start()
    parts = ((wq, pl.ds(0, 512)), (wk, pl.ds(512, 128)), (wv, pl.ds(640, 128)))

    def load(n, first):
        src, lanes = parts[n]
        take = 1 if first else jnp.where(s == 0, 0, c)
        return pltpu.make_async_copy(src.at[:, take], W.at[first, :, :, lanes],
                                     w_sem.at[3 * first + n])

    def swap(n):
        src, lanes = parts[n]
        return rcopy(src.at[:, 1 - c], W.at[1, :, :, lanes], sw_s.at[n], sw_r.at[n], here)

    wo_load = pltpu.make_async_copy(wo, WO, w_sem.at[12])
    @pl.when(s > 0)
    def _():
        for n in range(3):
            load(n, 0).start()

    head_load = pltpu.make_async_copy(HEAD.at[0], HEAD.at[0], w_sem.at[13])
    head_swap = rcopy(HEAD.at[1], HEAD.at[1], sw_s.at[3], sw_r.at[3], here)

    def off(n):
        return jnp.where(n == 0, 0, jnp.where(n == 1, 3, jnp.where(n == 2, 1, 2)))

    def slot_columns(core, j, i):
        g = jnp.where(core == 0, off(i), off(j))
        zz = jnp.where(core == 0, off(j), off(i))
        return lane(((d + g) % NY) * 2048 + ((z + zz) % NZ) * 512 + core * 256, 256)

    def row_slot(lanes):
        return (lanes // 64) * 2 + (lanes // 4) % 2, ((lanes // 8) % 8) * 4 + lanes % 4

    def wanted_rows():
        slot, position = row_slot(lax.broadcasted_iota(jnp.int32, (32, 256), 1))
        place = (position == lax.broadcasted_iota(jnp.int32, (32, 256), 0)).astype(BF)
        tokens = targets[...]
        keep = slot[0:8] == lax.broadcasted_iota(jnp.int32, (8, 256), 0)
        parts = []
        for term in (tokens // 256, tokens % 256):
            every = jnp.dot(term.astype(F32).astype(BF), place, preferred_element_type=F32)
            parts.append(jnp.sum(jnp.where(keep, every, 0.0), axis=0, keepdims=True))
        return parts[0] * 256.0 + parts[1]

    def head_start():
        for j in range(4):
            for i in range(4):
                there = pl.ds(i * 256, 256)
                pltpu.make_async_copy(head.at[:, slot_columns(c, j, i)], HEAD.at[0, j, :, there],
                                      w_sem.at[13]).start()
                rcopy(head.at[:, slot_columns(1 - c, j, i)], HEAD.at[1, j, :, there],
                      sw_s.at[3], sw_r.at[3], here).start()
    def prepare():
        @pl.when(s > 0)
        def _():
            wo_load.start()
            head_start()

        shape = (4 * ROWS, ROWS)
        rq = lax.broadcasted_iota(jnp.int32, shape, 0) % ROWS
        rk = lax.broadcasted_iota(jnp.int32, shape, 1)
        slot_q, slot_k = (rq // 4) % 2, (rk // 4) % 2
        pos_q, pos_k = (rq // 8) * 4 + rq % 4, (rk // 8) * 4 + rk % 4
        live_k = jnp.where(slot_k == 0, live[2 * d], live[2 * d + 1])
        allowed = (slot_q == slot_k) & (pos_k <= pos_q) & (pos_k < live_k)
        MASK[...] = jnp.where(allowed, F32(0.0), F32(-1e30))

        @pl.when(s > 0)
        def _():
            for n in range(3):
                load(n, 0).wait()
                swap(n).wait_recv()
            for copy in small[1:2]:
                copy.wait()
            diagonal = (lax.broadcasted_iota(jnp.int32, (256, 256), 0)
                        == lax.broadcasted_iota(jnp.int32, (256, 256), 1))

            def scale(i, _):
                cols = lane((i // NZ) * 2048 + ((i % NZ) * 2 + c) * 256, 256)
                column = jnp.sum(jnp.where(diagonal, gains[:, cols], 0.0), axis=1, keepdims=True)
                for which in range(2):
                    W.at[which, i][...] = (W[which, i].astype(F32) * column).astype(BF)
                return 0

            lax.fori_loop(0, 16, scale, 0)

        @pl.when(s == 0)
        def _():
            for copy in small[1:2]:
                copy.wait()
        for copy in small[2:]:
            copy.wait()

        WANT[...] = jnp.broadcast_to(wanted_rows(), WANT.shape)
        slot, position = row_slot(lax.broadcasted_iota(jnp.int32, (256, 32), 0))
        place = lax.broadcasted_iota(jnp.int32, (256, 32), 1)
        for i in range(2):
            chosen = source_of[2 * d + i]
            TAKE.at[i][...] = ((slot == chosen) & (position == place)
                               & (place < live[chosen])).astype(F32).astype(BF)

        @pl.when(s > 0)
        def _():
            scale_head()

    def scale_head():
        head_load.wait()
        head_swap.wait_recv()

        def scale(n, _):
            cc, j, i = n // 16, (n // 4) % 4, n % 4
            block = HEAD.at[cc, j, :, lane(i * 256, 256)]
            block[...] = (block[...].astype(F32) * fgain[:, slot_columns(c, j, i)]).astype(BF)
            return 0

        lax.fori_loop(0, 32, scale, 0)

    small[0].wait()

    @pl.when(s == 0)
    def _():
        rows = jnp.concatenate([emb[0], emb[1]], axis=0).astype(F32)
        for q in range(2):
            EB.at[q, m][...] = jnp.concatenate(
                [rows[:, q * 2048:q * 2048 + 2048], rows[:, q * 2048 + 4096:q * 2048 + 6144]],
                axis=0).astype(BF)

    pl.semaphore_wait(barrier, len(partners))

    @pl.when(s > 0)
    def _():
        for n in range(3):
            swap(n).start()

    def eb_z(q, k):
        return rcopy(EB.at[q, m], EB.at[q, m], eb_s.at[q, k], eb_r.at[q, m], (d, s, zpeer(k)))

    def eb_z_in(q, k):
        mk = zpeer(k)
        return rcopy(EB.at[q, mk], EB.at[q, mk], eb_s.at[q, k], eb_r.at[q, mk], here)

    def eb_fwd(q, k):
        mk = zpeer(k)
        return rcopy(EB.at[q, mk], EB.at[q, mk], eb_s.at[q, 4 + k], eb_r.at[q, mk], here)

    def eb_sib_in(q, k):
        mk = zother(k)
        return rcopy(EB.at[q, mk], EB.at[q, mk], eb_s.at[q, 4 + k], eb_r.at[q, mk], here)

    def hop(g):
        return rcopy(HP.at[g], X.at[d, z], hop_s.at[g], hop_r.at[d], (g, (s + 1) % NX, m))

    def hop_in(g):
        return rcopy(HP.at[g], X.at[g, z], hop_s.at[g], hop_r.at[g], here)

    def hop_raw():
        return rcopy(HP, R, hop_s.at[4], hop_r.at[4], (d, (s + 1) % NX, m))

    def ag_z(g, k):
        return rcopy(X.at[g, z], X.at[g, z], ag_s.at[g, k], ag_r.at[g, z], (d, s, zpeer(k)))

    def ag_z_in(g, k):
        zk = (z + k) % NZ
        return rcopy(X.at[g, zk], X.at[g, zk], ag_s.at[g, k], ag_r.at[g, zk], here)

    def sums_out():
        return rcopy(QA.at[1], QR, qr_s, qr_r, here)

    def res(k):
        g = ypeer(k)
        return rcopy(RX.at[g], R.at[d], res_s.at[k], res_r.at[d], (g, s, m))

    def res_in(k):
        g = ypeer(k)
        return rcopy(RX.at[g], R.at[g], res_s.at[k], res_r.at[g], here)

    def ctx(k):
        return rcopy(C.at[d], C.at[d], ctx_s.at[k], ctx_r.at[d], (ypeer(k), s, m))

    def ctx_in(k):
        g = ypeer(k)
        return rcopy(C.at[g], C.at[g], ctx_s.at[k], ctx_r.at[g], here)

    def part(g):
        return rcopy(PS.at[g], PR.at[g], ps_s.at[g], ps_r.at[g], here)

    def zred(g, k):
        return rcopy(ZS.at[g, k], ZR.at[g, k], zz_s.at[g, k], zz_r.at[g, k], (d, s, zpeer(k)))

    def layer():
        def multiply(x, which, rows, n, start=False):
            w = W[which, pl.ds(rows * NZ, NZ)].reshape(4 * 256, 768)
            term = jnp.dot(x, w, preferred_element_type=F32)
            QA.at[n][:, 0:768] = term if start else QA[n, :, 0:768] + term

        @pl.when(s == 0)
        def _():
            for q in range(2):
                for k in (1, 3, 2):
                    eb_z_in(q, k).wait_recv()
                    eb_fwd(q, k).start()
            QA[...] = jnp.zeros_like(QA)
            QR[...] = jnp.zeros_like(QR)
            SS[...] = jnp.zeros_like(SS)
            for q in range(2):
                for k in range(4):
                    eb_sib_in(q, k).wait_recv()

                def blocks(mm):
                    x = EB[q, :, :, lane(mm * 256, 256)].astype(F32)
                    return [x[:, i * 8:i * 8 + 8, :].reshape(ROWS, 256) for i in range(2)]

                def body(mm, total):
                    for half, xs in enumerate(blocks(mm)):
                        g = half * 2 + q
                        cols = lane(g * 2048 + mm * 256, 256)
                        XE.at[g, mm][...] = (xs * gains[:, cols]).astype(BF)
                        square = xs * xs
                        total = total + square[:, 0:128] + square[:, 128:256]
                    return total

                SS[...] = lax.fori_loop(0, NM, body, SS[...])
                for half, xs in enumerate(blocks(m)):
                    RX.at[half * 2 + q][...] = xs.astype(BF)
                if q == 0:
                    for n in range(3):
                        load(n, 0).wait()
                        load(n, 1).wait()

                def both(i, _):
                    g = 2 * i + q
                    for who in range(2):
                        x = jnp.concatenate([XE[g, 2 * zz + who] for zz in range(NZ)], axis=1)
                        multiply(x, who, g, 0)
                    return 0

                lax.fori_loop(0, 2, both, 0)
            for k in (2, 1, 3):
                res(k).start()
            R.at[d][...] = RX[d]

        @pl.when(s > 0)
        def _():
            def arrived(k):
                g = ypeer(k)
                hop_in(g).wait_recv()
                for j in (2, 1, 3):
                    ag_z(g, j).start()

            def columns(k):
                g = ypeer(k)
                for j in (1, 3, 2):
                    ag_z_in(g, j).wait_recv()
                return jnp.concatenate([X[g, zz] for zz in range(NZ)], axis=1)

            def both(k, start=False):
                x = columns(k)
                multiply(x, 1, ypeer(k), 1, start)
                multiply(x, 0, ypeer(k), 0, start)

            def squares_of(k):
                total = jnp.zeros((ROWS, 128), F32)
                for zz in range(NZ):
                    x = X[ypeer(k), zz].astype(F32)
                    square = x * x
                    total = total + square[:, 0:128] + square[:, 128:256]
                return total

            arrived(0)
            arrived(3)
            arrived(1)
            arrived(2)
            both(0, True)
            squares = squares_of(0)
            both(3)
            squares = squares + squares_of(3)
            both(1)
            squares = squares + squares_of(1)
            x = columns(2)
            multiply(x, 1, ypeer(2), 1)
            squares = squares + squares_of(2)
            QA.at[1][:, 768:896] = squares
            sums_out().start()
            multiply(x, 0, ypeer(2), 0)
            sums_out().wait_recv()
            SS[...] = squares + QR[:, 768:896]

        r = lax.rsqrt(jnp.sum(SS[...], axis=1, keepdims=True) * (1.0 / D) + EPS)
        cos = cosine[...]
        sin = sine[...]

        def summed(first, last):
            return QA[0, :, first:last] + QR[:, first:last]

        def rope(x):
            return (x * cos + pltpu.roll(x, 64, 1) * sin).astype(BF)

        query = jnp.concatenate(
            [rope(summed(j * HD, (j + 1) * HD) * r) for j in range(4)], axis=0)
        key = rope(summed(512, 640) * r)
        value = (summed(640, 768) * r).astype(BF)
        scores = lax.dot_general(query, key, (((1,), (1,)), ((), ())),
                                 preferred_element_type=F32) * (HD ** -0.5)
        scores = scores + MASK[...]
        highest = jnp.max(scores, axis=-1, keepdims=True)
        weights = jnp.exp(scores - highest)
        probs = (weights / jnp.sum(weights, axis=-1, keepdims=True)).astype(BF)
        mixed = jnp.dot(probs, value, preferred_element_type=F32).astype(BF)
        for j in range(4):
            C.at[d][:, j * HD:(j + 1) * HD] = mixed[j * ROWS:(j + 1) * ROWS]
        for k in (2, 1, 3):
            ctx(k).start()

        wo_load.wait()

        def project(g):
            for zz in range(NZ):
                p = jnp.dot(C[g], WO[:, zz * 512:zz * 512 + 512], preferred_element_type=F32)
                low, high = p[:, :256], p[:, 256:]
                PO.at[g, zz][...] = jnp.where(c == 0, low, high)
                PS.at[g, zz][...] = jnp.where(c == 0, high, low).astype(BF)
            part(g).start()

        def pair(g):
            part(g).wait_recv()
            for k in (2, 1, 3):
                zt = (z + k) % NZ
                ZS.at[g, k][...] = (PO[g, zt] + PR[g, zt].astype(F32)).astype(BF)
                zred(g, k).start()

        def total_of(g):
            total = PO[g, z] + PR[g, z].astype(F32) + R[g].astype(F32)
            for k in (1, 3, 2):
                zred(g, k).wait_recv()
                total = total + ZR[g, k].astype(F32)
            HP.at[g][...] = total.astype(BF)

            @pl.when(s < NX - 1)
            def _():
                hop(g).start()

        project(d)

        @pl.when(s == 0)
        def _():
            for k in (1, 3, 2):
                res_in(k).wait_recv()

        @pl.when(s > 0)
        def _():
            hop_raw().wait_recv()

        pair(d)
        for k in (1, 3):
            ctx_in(k).wait_recv()
            project(ypeer(k))
        pair(ypeer(1))
        pair(ypeer(3))
        def in_last(do):
            @pl.when(s == NX - 1)
            def _():
                do()

        total_of(d)
        in_last(lambda: own_x(1, 0))
        ctx_in(2).wait_recv()
        project(ypeer(2))
        total_of(ypeer(1))
        in_last(lambda: own_x(1, 1))
        pair(ypeer(2))

        def first_two():
            spread(1, 0)
            spread(1, 1)

        in_last(first_two)
        total_of(ypeer(3))

        def third():
            own_x(1, 2)
            spread(1, 2)

        in_last(third)
        total_of(ypeer(2))

        def rest():
            own_x(1, 3)
            spread(1, 3)
            for k in range(3):
                stage_first(1, k)
            for k in range(2):
                stage_second(1, k)

        in_last(rest)

        @pl.when(s < NX - 1)
        def _():
            hop_raw().start()

        @pl.when(s == 1)
        def _():
            def body(k, _):
                own_x(0, k)
                spread(0, k)
                return 0

            lax.fori_loop(0, 4, body, 0)

    def first_dev(k):
        return (jnp.where(c == 0, ypeer(k), d), s, jnp.where(c == 0, m, zpeer(k)))

    def second_dev(k):
        return (jnp.where(c == 0, d, ypeer(k)), s, jnp.where(c == 0, zpeer(k), m))

    def ycopy(src, dst, b, k, i, j, dev):
        return rcopy(src, dst, y_s.at[b, k, i], y_r.at[b, k, j], dev)

    def y_x(b, k, n):
        ref = Y.at[b, k, 0, 0]
        return ycopy(ref, ref, b, k, n, 0, (d, (s + n) % NX, m))

    def y_first(b, k, n):
        slot = (1, 3, 2)[n - 1]
        return ycopy(Y.at[b, k, 0, 0], Y.at[b, k, 0, slot], b, k, 3 + n, slot, first_dev(n))

    sets = (pl.ds(0, 1), pl.ds(1, 2), pl.ds(3, 1))

    def y_second(b, k, part_no, n):
        slot = 1 if n == 1 else 2
        return ycopy(Y.at[b, k, 0, sets[part_no]], Y.at[b, k, slot, sets[part_no]], b, k,
                     7 + part_no * 2 + (slot - 1), 1 + 3 * slot + part_no, second_dev(n))

    def y_relay(b, k, half):
        slot, n = ((1, 1), (2, 3))[half]
        two = pl.ds(2 * half, 2)
        return ycopy(Y.at[b, k, slot, two], Y.at[b, k, 3, two], b, k, 13 + half, 10 + half,
                     second_dev(n))

    def chunk_order(step):
        return jnp.where(step == 3, 2, jnp.where(step == 2, 3, step))

    def own_x(b, k):
        Y.at[b, k, 0, 0][...] = HP[(d + chunk_order(k)) % NY]
        for n in (2, 1, 3):
            y_x(b, k, n).start()

    def spread(b, k):
        for n in (2, 1, 3):
            y_first(b, k, n).start()
        for n in (1, 3):
            y_second(b, k, 0, n).start()

    def stage_first(b, k):
        y_first(b, k, 1).wait_recv()
        y_first(b, k, 3).wait_recv()
        for n in (1, 3):
            y_second(b, k, 1, n).start()
        y_first(b, k, 2).wait_recv()
        for n in (1, 3):
            y_second(b, k, 2, n).start()

    def stage_second(b, k):
        for part_no in (0, 1):
            y_second(b, k, part_no, 1).wait_recv()
        y_relay(b, k, 0).start()
        for part_no in (1, 2):
            y_second(b, k, part_no, 3).wait_recv()
        y_relay(b, k, 1).start()
        y_second(b, k, 2, 1).wait_recv()
        y_second(b, k, 0, 3).wait_recv()

    def opposite(b, k):
        for half in range(2):
            y_relay(b, k, half).wait_recv()

    def dots(b, j, send=False):
        blocks = []
        for g in range(NY):
            row = []
            total = jnp.zeros((ROWS, 128), F32)
            for i in range(4):
                sender = (d + jnp.where(c == 0, (0, 3, 1, 2)[i], off(j))) % NY
                k = chunk_order((g - sender + NY) % NY)
                x = Y[b, k, j, i]
                row.append(x)
                wide = x.astype(F32)
                square = wide * wide
                total = total + square[:, 0:128] + square[:, 128:256]
            SQ.at[b, g][...] += total
            blocks.append(jnp.concatenate(row, axis=1))
        pieces = jnp.concatenate(blocks, axis=0)
        for which in (1, 0):
            LT.at[b, which][0:VOCAB_DEV, :] += lax.dot_general(
                HEAD[which, j], pieces, (((1,), (1,)), ((), ())), preferred_element_type=F32)
            if send and which == 1:
                exchange(b)

    def swap_logits(b):
        return rcopy(LT.at[b, 1], LR.at[b], lt_s.at[b], lt_r.at[b], here)

    def exchange(b):
        squares = SQ[b].reshape(NY * ROWS, 128)
        top = squares.astype(BF)
        rest = (squares - top.astype(F32)).astype(BF)
        ones = jnp.ones((16, 128), BF)
        nt = (((1,), (1,)), ((), ()))
        sums = (lax.dot_general(ones, top, nt, preferred_element_type=F32)
                + lax.dot_general(ones, rest, nt, preferred_element_type=F32))
        LT.at[b, 1][VOCAB_DEV:VOCAB_DEV + 8, :] = sums[0:8]
        swap_logits(b).start()

    def layer_sent():
        @pl.when(s == 0)
        def _():
            for q in range(2):
                for k in range(1, 4):
                    eb_z(q, k).wait_send()
                for k in range(4):
                    eb_fwd(q, k).wait_send()
            for k in range(1, 4):
                res(k).wait_send()

        @pl.when(s > 0)
        def _():
            for g in range(NY):
                for k in range(1, 4):
                    ag_z(g, k).wait_send()
            sums_out().wait_send()
            for n in range(3):
                swap(n).wait_send()

        @pl.when(s < NX - 1)
        def _():
            for g in range(NY):
                hop(g).wait_send()
            hop_raw().wait_send()

        for g in range(NY):
            for k in range(1, 4):
                zred(g, k).wait_send()
            part(g).wait_send()
        for k in range(1, 4):
            ctx(k).wait_send()

    def chunk_sent(b, k, source):
        @pl.when(s == source)
        def _():
            for j in (1, 2, 3):
                y_x(b, k, j).wait_send()

        for j in (1, 2, 3):
            y_first(b, k, j).wait_send()
        for j in (1, 3):
            for part_no in range(3):
                y_second(b, k, part_no, j).wait_send()
        for half in range(2):
            y_relay(b, k, half).wait_send()

    def each(count, do):
        def body(k, _):
            do(k)
            return 0

        lax.fori_loop(0, count, body, 0)

    def exit_dots(n):
        dots(0, n)

    def gather(b):
        source = 2 * b + 1
        final = (b == 1) & (s == NX - 1)
        others = jnp.logical_not(final)

        def body(t, _):
            @pl.when((t < 4) & (s != source))
            def _():
                y_x(b, t, 1).wait_recv()
                spread(b, t)

            @pl.when((t >= 1) & (t < 5) & ((t == 4) | others))
            def _():
                stage_first(b, t - 1)

            @pl.when((t >= 2) & (t < 6) & ((t >= 4) | others))
            def _():
                stage_second(b, t - 2)

            last = (b == 0) & (s == NX - 1)

            @pl.when((t >= 3) & ((b == 0) | (t < 6)) & others & jnp.logical_not(last))
            def _():
                opposite(b, t - 3)

            @pl.when((b == 1) & (s == 2) & (t >= 2) & (t < 6))
            def _():
                exit_dots(t - 2)

            @pl.when((b == 1) & (s == 2) & (t == 6))
            def _():
                exchange(0)
            return 0

        lax.fori_loop(0, 7, body, 0)

        @pl.when(final)
        def _():
            each(3, lambda k: opposite(1, k))
            each(4, lambda k: opposite(0, k))
            each(4, exit_dots)
            exchange(0)

    def finish(b):
        @pl.when(b == 0)
        def _():
            each(4, exit_dots)
            exchange(0)

        @pl.when(b == 1)
        def _():
            for j in range(3):
                dots(1, j)
            opposite(1, 3)
            dots(1, 3, True)

            @pl.when(s >= 2)
            def _():
                softmax(0)

        softmax(b)

    def softmax(b):
        swap_logits(b).wait_recv()
        last = pl.ds(VOCAB_DEV, 8)
        sums = (LT[b, 1, last] + LR[b, last])[0:1]
        r = lax.rsqrt(sums * (1.0 / D) + EPS)
        logits = (LT[b, 0, 0:VOCAB_DEV] + LR[b, 0:VOCAB_DEV]) * r
        highest = jnp.max(logits, axis=0, keepdims=True)
        summed = jnp.sum(jnp.exp(logits - highest), axis=0, keepdims=True)
        first = ((d * NX + s) * NM + m) * VOCAB_DEV
        index = (lax.broadcasted_iota(jnp.int32, logits.shape, 0) + first).astype(F32)
        wanted = WANT[0:1, :]
        picked = jnp.sum(jnp.where(index == wanted, logits, 0.0), axis=0, keepdims=True)
        for n, value in enumerate((highest, summed, picked)):
            for half in range(2):
                STO[pl.ds(n * 4 + b * 2 + half, 1), :] = value[:, half * 128:half * 128 + 128]

    def step(t, _):
        last = s == NX - 1
        place = jnp.where(last, 1, 0)

        @pl.when(t == place)
        def _():
            layer()

            @pl.when(s == 0)
            def _():
                head_start()

        @pl.when(jnp.where(last, (t == 0) | (t == 2), (t == 1) | (t == jnp.where(s < 2, 3, 2))))
        def _():
            gather(jnp.where((t == 0) | (t == 1), 0, 1))

        @pl.when((t == 4) | ((t == 2) & (s < 2)))
        def _():
            @pl.when((t == 2) & (s == 0))
            def _():
                scale_head()
            finish(jnp.where(t == 4, 1, 0))
        return 0

    @pl.when(s == 0)
    def _():
        for q in range(2):
            for k in (2, 1, 3, 0):
                (eb_z(q, k) if k else eb_fwd(q, 0)).start()
        for n in range(3):
            load(n, 0).start()
            load(n, 1).start()
        wo_load.start()

    prepare()
    STO[...] = jnp.zeros_like(STO)
    SQ[...] = jnp.zeros_like(SQ)
    LT[...] = jnp.zeros_like(LT)
    lax.fori_loop(0, 5, step, 0)

    def merge(ref, count):
        parts = [ref[j] for j in range(count)]
        highest = parts[0][0:4]
        for p in parts[1:]:
            highest = jnp.maximum(highest, p[0:4])
        summed = jnp.zeros_like(highest)
        picked = jnp.zeros_like(highest)
        for p in parts:
            summed = summed + p[4:8] * jnp.exp(p[0:4] - highest)
            picked = picked + p[8:12]
        return highest, summed, picked

    def stacked(highest, summed, picked):
        return jnp.concatenate([highest, summed, picked, jnp.zeros_like(picked)], axis=0)

    pairs = [(j, k) for j in range(NX) for k in range(NY) if j or k]

    def st_yx(n):
        j, k = pairs[n]
        mine = s * NY + d
        return rcopy(SA.at[mine], SA.at[mine], st_s.at[0, n], st_r.at[0, mine],
                     (ypeer(k), (s + j) % NX, m))

    def st_yx_in(n):
        j, k = pairs[n]
        other = ((s + j) % NX) * NY + ypeer(k)
        return rcopy(SA.at[other], SA.at[other], st_s.at[0, n], st_r.at[0, other], here)

    def m_of(k):
        return (m + k) % NM

    def st_m(k):
        return rcopy(SB.at[m], SB.at[m], st_s.at[1, k], st_r.at[1, m], (d, s, m_of(k)))

    def st_m_in(k):
        mm = m_of(k)
        return rcopy(SB.at[mm], SB.at[mm], st_s.at[1, k], st_r.at[1, mm], (d, s, mm))

    SA.at[s * NY + d][...] = STO[...]
    for n in range(15):
        st_yx(n).start()
    layer_sent()
    head_swap.wait_send()
    swap_logits(0).wait_send()
    swap_logits(1).wait_send()
    each(4, lambda k: chunk_sent(0, k, 1))
    each(4, lambda k: chunk_sent(1, k, NX - 1))
    for n in range(15):
        st_yx_in(n).wait_recv()
    SB.at[m][...] = stacked(*merge(SA, NX * NY))
    for k in (4, 3, 5, 2, 6, 1, 7):
        st_m(k).start()
    for n in range(15):
        st_yx(n).wait_send()
    for k in (1, 7, 2, 6, 3, 5, 4):
        st_m_in(k).wait_recv()
    highest, summed, picked = merge(SB, NM)
    logprob = picked - (highest + jnp.log(summed))
    terms = []
    for e in range(2):
        rest = jnp.concatenate([logprob[2 * e:2 * e + 1], logprob[2 * e + 1:2 * e + 2]], axis=1)
        for _ in range(3):
            term = rest.astype(BF).astype(F32)
            terms.append(term)
            rest = rest - term
    row = lax.broadcasted_iota(jnp.int32, (16, 256), 0)
    stack = jnp.zeros((16, 256), F32)
    for j, term in enumerate(terms):
        stack = jnp.where(row == j, term, stack)
    stack = stack.astype(BF)
    results = []
    for i in range(2):
        got = jnp.dot(stack, TAKE[i], preferred_element_type=F32)
        results.append([got[j:j + 1] + got[j + 1:j + 2] + got[j + 2:j + 3] for j in (0, 3)])
    for e in range(2):
        first = lax.broadcasted_iota(jnp.int32, (2, 32), 0) == 0
        out.at[e][...] = jnp.where(first, results[0][e], results[1][e])
    for k in range(1, 8):
        st_m(k).wait_send()


def tables():
    row = np.arange(ROWS)
    position = (row // 8) * 4 + row % 4
    half = HD // 2
    freqs = (ROPE_BASE ** (-np.arange(half) * 2.0 / HD)).astype(np.float32)
    angles = (position.astype(np.float32)[:, None] * freqs[None, :]).astype(np.float64)
    cos, sin = np.cos(angles), np.sin(angles)
    return (np.concatenate([cos, cos], 1).astype(np.float32),
            np.concatenate([-sin, sin], 1).astype(np.float32))


def per_device(
    embeds, targets, lengths, source, attn_gain, w_query, w_key, w_value, w_out, final_gain, head
):
    vocab = head.shape[0]
    cos, sin = tables()
    vmem = pl.BlockSpec(memory_space=pltpu.VMEM)
    hbm = pl.BlockSpec(memory_space=pl.ANY)
    smem = pl.BlockSpec(memory_space=pltpu.SMEM)
    dma = pltpu.SemaphoreType.DMA
    stats = pl.pallas_call(
        kernel,
        out_shape=jax.ShapeDtypeStruct((2, 2, 32), F32),
        in_specs=[hbm, smem, smem] + [hbm] * 10,
        out_specs=vmem,
        scratch_shapes=[
            pltpu.VMEM((2, 4, D), BF),
            pltpu.VMEM((8, 32), jnp.int32),
            pltpu.VMEM((1, D), F32),
            pltpu.VMEM((1, D), F32),
            pltpu.VMEM((ROWS, HD), F32),
            pltpu.VMEM((ROWS, HD), F32),
            pltpu.VMEM((2, 16, 256, 768), BF),
            pltpu.VMEM((QW, 2048), BF),
            pltpu.VMEM((2, 4, vocab, 1024), BF),
            pltpu.VMEM((2, NM, 16, 2048), BF),
            pltpu.VMEM((NY, NM, ROWS, 256), BF),
            pltpu.VMEM((NY, NZ, ROWS, 256), BF),
            pltpu.VMEM((NY, ROWS, 256), BF),
            pltpu.VMEM((4 * ROWS, ROWS), F32),
            pltpu.VMEM((ROWS, 128), F32),
            pltpu.VMEM((2, ROWS, 896), F32),
            pltpu.VMEM((ROWS, 896), F32),
            pltpu.VMEM((NY, ROWS, 256), BF),
            pltpu.VMEM((NY, ROWS, QW), BF),
            pltpu.VMEM((NY, NZ, ROWS, 256), BF),
            pltpu.VMEM((NY, NZ, ROWS, 256), BF),
            pltpu.VMEM((NY, NZ, ROWS, 256), F32),
            pltpu.VMEM((NY, NZ, ROWS, 256), BF),
            pltpu.VMEM((NY, NZ, ROWS, 256), BF),
            pltpu.VMEM((NY, ROWS, 256), BF),
            pltpu.VMEM((2, 4, 4, 4, ROWS, 256), BF),
            pltpu.VMEM((2, 2, vocab + 8, 256), F32),
            pltpu.VMEM((2, vocab + 8, 256), F32),
            pltpu.VMEM((2, NY, ROWS, 128), F32),
            pltpu.VMEM((8, 256), F32),
            pltpu.VMEM((2, 256, 32), BF),
            pltpu.VMEM((16, 128), F32),
            pltpu.VMEM((NX * NY, 16, 128), F32),
            pltpu.VMEM((NM, 16, 128), F32),
            dma((20,)),
            dma((4,)), dma((4,)),
            dma((2,)), dma((2,)),
            dma, dma,
            dma((2, 8)), dma((2, 8)),
            dma((5,)), dma((5,)),
            dma((4, 8)), dma((4, 8)),
            dma((4,)), dma((4,)),
            dma((4,)), dma((4,)),
            dma((4,)), dma((4,)),
            dma((4, 4)), dma((4, 4)),
            dma((2, 4, 22)), dma((2, 4, 19)),
            dma((2, 16)), dma((2, 16)),
        ],
        compiler_params=pltpu.CompilerParams(
            collective_id=0, has_side_effects=True, vmem_limit_bytes=60 * 1024 * 1024),
        cost_estimate=pl.CostEstimate(flops=8_000_000_000, bytes_accessed=24_000_000,
                                      transcendentals=300_000),
    )(
        embeds, lengths, source, targets, attn_gain, final_gain.reshape(1, D), jnp.asarray(cos), jnp.asarray(sin),
        w_query.reshape(16, 2, 256, 512), w_key.reshape(16, 2, 256, 128),
        w_value.reshape(16, 2, 256, 128), w_out.reshape(512, 2048), head,
    )
    return (stats[0], stats[1])


def solution(mesh):
    return jax.shard_map(
        per_device,
        mesh=mesh,
        in_specs=(
            P("dp", "mp", None),
            P(),
            P(),
            P(),
            P("section", None),
            P("section", None, "mp"),
            P("section", None, "mp"),
            P("section", None, "mp"),
            P("section", "mp", "dp"),
            P(),
            P(("dp", "section", "mp"), None),
        ),
        out_specs=(P("dp", None), P("dp", None)),
        check_vma=False,
    )
```
